32 devices in a mesh: section: 2 (over core), seq: 4 (over y, x), wt: 4 (over z).
Axes of the slice: x: 2, y: 2, z: 4, core: 2. Of those that a mesh axis runs over, the one named last changes fastest.
Arguments:
- tokens: float32 [2, 4, 512, 1536], P(None, 'wt', 'seq'), may hold values from -6 to 6
- cotangent: float32 [2, 4, 512, 1536], P(None, 'wt', 'seq'), may hold values from -6 to 6
- norm_gain: float32 [2, 1536], P('section'), may hold values from 0.5 to 1.5
- w_in: bfloat16 [2, 1536, 6448], P('section', 'wt'), may hold values from -0.15625 to 0.15625
- conv_w: float32 [2, 4, 3328], P('section'), may hold values from -3 to 3
- conv_b: float32 [2, 3328], P('section'), may hold values from -2 to 2
- dt_bias: float32 [2, 48], P('section'), may hold values from -5 to -1
- a_log: float32 [2, 48], P('section'), may hold values from -2 to 1.5
- skip_d: float32 [2, 48], P('section'), may hold values from 0.5 to 1.5
- gate_gain: float32 [2, 3072], P('section'), may hold values from 0.5 to 1.5
- w_out: bfloat16 [2, 3072, 1536], P('section', 'wt'), may hold values from -0.109375 to 0.109375
Outputs:
- section_out: float32 [2, 2, 4, 512, 1536], P('section', None, 'wt', 'seq')
- input_grad: float32 [2, 2, 4, 512, 1536], P('section', None, 'wt', 'seq')
- g_norm_gain: float32 [2, 1536], P('section')
- g_w_in: float32 [2, 1536, 6448], P('section', 'wt')
- g_conv_w: float32 [2, 4, 3328], P('section')
- g_conv_b: float32 [2, 3328], P('section')
- g_dt_bias: float32 [2, 48], P('section')
- g_a_log: float32 [2, 48], P('section')
- g_skip_d: float32 [2, 48], P('section')
- g_gate_gain: float32 [2, 3072], P('section')
- g_w_out: float32 [2, 3072, 1536], P('section', 'wt')
The draws below stay inside these ranges and needn't reach their ends.
All inputs are finite; a program needn't handle non-finite values.
Results may differ from the reference program's by a relative error of at most 0.019.
Values may be sent and summed in bfloat16 or wider, within the bound.
A program may use at most 384 MiB of HBM per device.

```python
import jax
import jax.numpy as jnp
from jax import lax

D = 1536
HEADS = 48
HEAD_DIM = 64
STATE = 128
KERNEL = 4
SPAN = 256
MB = 2
INNER = 3072
NIN = 6448
CONV = 3328
LEN = 512
SEQS = 4


def shard_levels(stream_key, shape, split, smallest, high):
    def one(axis_at, shards_of):
        steps = jax.random.uniform(jax.random.fold_in(jax.random.fold_in(stream_key, 6), axis_at), (shards_of,), jnp.float32, smallest / len(split), high / len(split))
        return jnp.repeat(jnp.exp(steps), shape[axis_at] // shards_of).reshape((-1,) + (1,) * (len(shape) - axis_at - 1))

    loudness = one(*split[0])
    for cut in split[1:]:
        loudness = loudness * one(*cut)
    return loudness


def gaussian(key, extent, deviation, reach, pieces=(), kind=jnp.bfloat16):
    gain = shard_levels(key, extent, pieces, -0.22, 0.18) if pieces else 1.0
    result = jax.random.normal(key, extent, jnp.float32) * deviation * gain
    return jnp.minimum(jnp.maximum(result, -reach), reach).astype(kind)


def setup_inputs(seed: int = 0) -> dict:
    seeds = jax.random.split(jax.random.key(seed), 12)
    tokens = gaussian(seeds[0], (MB, SEQS, LEN, D), 1.0, 6.0, ((1, 4), (2, 4)), jnp.float32)
    cotangent = gaussian(seeds[1], (MB, SEQS, LEN, D), 1.0, 6.0, ((1, 4), (2, 4)), jnp.float32)
    norm_gain = jnp.clip(1.0 + 0.1 * jax.random.normal(seeds[2], (2, D), jnp.float32), 0.5, 1.5)
    w_in = gaussian(seeds[3], (2, D, NIN), D ** -0.5, 0.15625, ((0, 2), (1, 4)))
    conv_w = gaussian(seeds[4], (2, KERNEL, CONV), KERNEL ** -0.5, 3.0, ((0, 2),), jnp.float32)
    conv_b = gaussian(seeds[5], (2, CONV), 0.3, 2.0, ((0, 2),), jnp.float32)
    dt_bias = jnp.clip(-5.0 + 4.0 * jax.random.uniform(seeds[6], (2, HEADS), jnp.float32) ** shard_levels(seeds[6], (2, HEADS), ((0, 2),), -0.2, 0.2), -5.0, -1.0)
    a_log = jnp.clip(-2.0 + 3.5 * jax.random.uniform(seeds[7], (2, HEADS), jnp.float32) ** shard_levels(seeds[7], (2, HEADS), ((0, 2),), -0.2, 0.2), -2.0, 1.5)
    skip_d = jnp.clip(0.5 + 1.0 * jax.random.uniform(seeds[8], (2, HEADS), jnp.float32) ** shard_levels(seeds[8], (2, HEADS), ((0, 2),), -0.2, 0.2), 0.5, 1.5)
    gate_gain = jnp.clip(1.0 + 0.1 * jax.random.normal(seeds[9], (2, INNER), jnp.float32), 0.5, 1.5)
    w_out = gaussian(seeds[10], (2, INNER, D), INNER ** -0.5, 0.109375, ((0, 2), (1, 4)))
    return {"tokens": tokens, "cotangent": cotangent, "norm_gain": norm_gain, "w_in": w_in, "conv_w": conv_w, "conv_b": conv_b, "dt_bias": dt_bias, "a_log": a_log, "skip_d": skip_d, "gate_gain": gate_gain, "w_out": w_out}


EPSILON = 1e-05
EXACT_DOT = lax.Precision.HIGHEST

def silu_slope(values):
    sigma = jax.nn.sigmoid(values)
    return sigma * (1.0 + values * (1.0 - sigma))

def conv_silu(seq_in, kernel_w, conv_bias):
    length = seq_in.shape[0]
    padded = jnp.concatenate([jnp.zeros((KERNEL - 1, seq_in.shape[1]), jnp.float32), seq_in], 0)
    conv_sum = conv_bias[None, :] + jnp.zeros_like(seq_in)
    for k in range(KERNEL):
        conv_sum = conv_sum + kernel_w[k][None, :] * padded[k:k + length]
    return jax.nn.silu(conv_sum)

def mixer(x_raw, bc_raw, dt_raw, conv_wx, conv_bx, conv_wbc, conv_bbc, dt_bias, a_log, skip_d):
    x_conv = conv_silu(x_raw, conv_wx, conv_bx)
    bc_conv = conv_silu(bc_raw, conv_wbc, conv_bbc)
    head_count = dt_bias.shape[0]
    length = x_conv.shape[0]
    blocks = length // SPAN
    step_size = jax.nn.softplus(dt_raw + dt_bias[None, :])
    step_rate = -step_size * jnp.exp(a_log)[None, :]
    x_blocks = x_conv.reshape(blocks, SPAN, head_count, HEAD_DIM)
    b_blocks = bc_conv[:, :STATE].reshape(blocks, SPAN, STATE)
    c_blocks = bc_conv[:, STATE:].reshape(blocks, SPAN, STATE)
    step_blocks = step_size.reshape(blocks, SPAN, head_count)
    cum_rate = jnp.cumsum(step_rate.reshape(blocks, SPAN, head_count), axis=1)
    scores = jnp.einsum('ctn,csn->cts', c_blocks, b_blocks, precision=EXACT_DOT)
    row_ids = lax.broadcasted_iota(jnp.int32, (SPAN, SPAN), 0)
    col_ids = lax.broadcasted_iota(jnp.int32, (SPAN, SPAN), 1)
    causal = (row_ids >= col_ids)[None, :, :, None]
    rate_diff = cum_rate[:, :, None, :] - cum_rate[:, None, :, :]
    decay_mat = jnp.where(causal, jnp.exp(jnp.where(causal, rate_diff, 0.0)), 0.0)
    mix_weight = scores[:, :, :, None] * decay_mat * step_blocks[:, None, :, :]
    y_inner = jnp.einsum('ctsh,cshp->cthp', mix_weight, x_blocks, precision=EXACT_DOT)
    last_rate = cum_rate[:, -1, :]
    tail_weight = jnp.exp(last_rate[:, None, :] - cum_rate) * step_blocks
    states = jnp.einsum('csn,cshp->chnp', b_blocks, x_blocks * tail_weight[:, :, :, None], precision=EXACT_DOT)

    def advance(carried, scan_item):
        block_state, block_rate = scan_item
        return (carried * jnp.exp(block_rate)[:, None, None] + block_state, carried)
    _, before = lax.scan(advance, jnp.zeros((head_count, STATE, HEAD_DIM), jnp.float32), (states, last_rate))
    y_outer = jnp.einsum('ctn,chnp->cthp', c_blocks, before, precision=EXACT_DOT) * jnp.exp(cum_rate)[:, :, :, None]
    y_total = y_inner + y_outer + skip_d[None, None, :, None] * x_blocks
    return y_total.reshape(length, head_count * HEAD_DIM)

def section_parts(h_in, params):
    norm_gain, w_in, conv_w, conv_b, dt_bias, a_log, skip_d, gate_gain, w_out = params
    inv_rms = lax.rsqrt(lax.optimization_barrier(jnp.mean(h_in * h_in, axis=-1, keepdims=True)) + EPSILON)
    normed_in = (h_in * inv_rms * norm_gain[None, :]).astype(jnp.bfloat16)
    projected = jnp.dot(normed_in, w_in, preferred_element_type=jnp.float32).astype(jnp.bfloat16)
    gate_raw = projected[:, :INNER]
    x_raw = projected[:, INNER:2 * INNER].astype(jnp.float32)
    bc_raw = projected[:, 2 * INNER:2 * INNER + 2 * STATE].astype(jnp.float32)
    dt_raw = projected[:, 2 * INNER + 2 * STATE:].astype(jnp.float32)
    head_params = (conv_w[:, :INNER], conv_b[:INNER], conv_w[:, INNER:], conv_b[INNER:], dt_bias, a_log, skip_d)
    mixed = mixer(x_raw, bc_raw, dt_raw, *head_params).astype(jnp.bfloat16)
    gate_in = gate_raw.astype(jnp.float32)
    gate_act = jax.nn.silu(gate_in)
    mixed_f = mixed.astype(jnp.float32)
    v = mixed_f * gate_act
    inv_rms2 = lax.rsqrt(lax.optimization_barrier(jnp.mean(v * v, axis=-1, keepdims=True)) + EPSILON)
    normed2 = v * inv_rms2
    normed_out = (normed2 * gate_gain[None, :]).astype(jnp.bfloat16)
    h_out = h_in + jnp.dot(normed_out, w_out, preferred_element_type=jnp.float32)
    return (h_out, (inv_rms, normed_in, x_raw, bc_raw, dt_raw, head_params, gate_in, gate_act, mixed_f, inv_rms2, normed2, normed_out))

def section_forward(h_in, params):
    return section_parts(h_in, params)[0]

def section_backward(h_in, out_grad, params):
    norm_gain, w_in, conv_w, conv_b, dt_bias, a_log, skip_d, gate_gain, w_out = params
    _, kept = section_parts(h_in, params)
    inv_rms, normed_in, x_raw, bc_raw, dt_raw, head_params, gate_in, gate_act, mixed_f, inv_rms2, normed2, normed_out = kept
    out_grad_b = out_grad.astype(jnp.bfloat16)
    g_w_out = lax.dot_general(normed_out, out_grad_b, (((0,), (0,)), ((), ())), preferred_element_type=jnp.float32)
    d_normed = lax.dot_general(out_grad_b, w_out, (((1,), (1,)), ((), ())), preferred_element_type=jnp.float32)
    g_gate = lax.optimization_barrier(jnp.sum(d_normed * normed2, axis=0))
    d_scaled = d_normed * gate_gain[None, :]
    d_v = inv_rms2 * (d_scaled - normed2 * lax.optimization_barrier(jnp.mean(d_scaled * normed2, axis=-1, keepdims=True)))
    d_mixed = (d_v * gate_act).astype(jnp.bfloat16)
    d_gate = d_v * mixed_f * silu_slope(gate_in)
    _, pull = jax.vjp(mixer, x_raw, bc_raw, dt_raw, *head_params)
    grads = pull(d_mixed.astype(jnp.float32))
    d_proj = jnp.concatenate([d_gate, grads[0], grads[1], grads[2]], axis=1).astype(jnp.bfloat16)
    g_w_in = lax.dot_general(normed_in, d_proj, (((0,), (0,)), ((), ())), preferred_element_type=jnp.float32)
    d_in = lax.dot_general(d_proj, w_in, (((1,), (1,)), ((), ())), preferred_element_type=jnp.float32)
    normed_h = h_in * inv_rms
    g_norm = lax.optimization_barrier(jnp.sum(d_in * normed_h, axis=0))
    d_scaled_in = d_in * norm_gain[None, :]
    d_h = out_grad + inv_rms * (d_scaled_in - normed_h * lax.optimization_barrier(jnp.mean(d_scaled_in * normed_h, axis=-1, keepdims=True)))
    g_conv_w = jnp.concatenate([grads[3], grads[5]], axis=1)
    g_conv_b = jnp.concatenate([grads[4], grads[6]], axis=0)
    return (d_h, (g_norm, g_w_in, g_conv_w, g_conv_b, grads[7], grads[8], grads[9], g_gate, g_w_out))

def run_back(params, inputs, grads_out):
    zero_grads = tuple((jnp.zeros(p.shape, jnp.float32) for p in params))

    def back_one(summed, scan_pair):
        d_h, grads = section_backward(scan_pair[0], scan_pair[1], params)
        return (tuple((a + g for a, g in zip(summed, grads))), d_h)
    return lax.scan(back_one, zero_grads, (inputs, grads_out))

def reference(tokens, cotangent, norm_gain, w_in, conv_w, conv_b, dt_bias, a_log, skip_d, gate_gain, w_out):
    stacked = (norm_gain, w_in, conv_w, conv_b, dt_bias, a_log, skip_d, gate_gain, w_out)
    params_low = tuple((p[0] for p in stacked))
    params_top = tuple((p[1] for p in stacked))
    flat_in = tokens.reshape(MB * SEQS, LEN, D)
    mid_out = lax.map(lambda seq_h: section_forward(seq_h, params_low), flat_in)
    top_out = lax.map(lambda seq_h: section_forward(seq_h, params_top), mid_out)
    flat_cot = cotangent.reshape(MB * SEQS, LEN, D)
    grads_top, d_mid = run_back(params_top, mid_out, flat_cot)
    grads_low, d_first = run_back(params_low, flat_in, d_mid)
    section_out = jnp.stack([mid_out, top_out]).reshape(2, MB, SEQS, LEN, D)
    input_grad = jnp.stack([d_first, d_mid]).reshape(2, MB, SEQS, LEN, D)
    both = [jnp.stack([grads_low[i], grads_top[i]]) for i in range(9)]
    return (section_out, input_grad, both[0], both[1], both[2], both[3], both[4], both[5], both[6], both[7], both[8])
```

```python
import functools

import jax
import jax.numpy as jnp
from jax import lax
from jax.experimental import pallas as pl
from jax.experimental.pallas import tpu as pltpu
from jax.sharding import PartitionSpec as P

D = 1536
HEADS = 48
HEAD_DIM = 64
STATE = 128
KERNEL = 4
INNER = 3072
CONV = 3328
EPSILON = 1e-05

Q = 128
F32 = jnp.float32
BF = jnp.bfloat16
VMEM_LIMIT = 48 * 2**20


def dot(a, b, ca, cb, precision=None):
    return lax.dot_general(a, b, (((ca,), (cb,)), ((), ())), precision=precision, preferred_element_type=F32)

def sigmoid(x):
    return 1.0 / (1.0 + jnp.exp(-x))

def softplus(x):
    return jnp.maximum(x, 0.0) + jnp.log1p(jnp.exp(-jnp.abs(x)))

def lane_mask(rows):
    return lax.broadcasted_iota(jnp.int32, (rows, 128), 1) < HEAD_DIM

def spread(cols, pair, mask):
    a = jnp.broadcast_to(cols[:, 2 * pair : 2 * pair + 1], mask.shape)
    b = jnp.broadcast_to(cols[:, 2 * pair + 1 : 2 * pair + 2], mask.shape)
    return jnp.where(mask, a, b)

def split_pair(u, mask):
    zero = jnp.zeros_like(u)
    return jnp.concatenate([jnp.where(mask, u, zero), jnp.where(mask, zero, u)], axis=0)

def conv_tile(proj_ref, cw_ref, pad, proj_at, conv_at, rows):
    pad[0:8, :] = jnp.zeros((8, 128), F32)
    pad[8 : 8 + rows, :] = proj_ref[:, pl.ds(proj_at, 128)].astype(F32)
    pre = jnp.broadcast_to(cw_ref[4:5, pl.ds(conv_at, 128)], (rows, 128))
    for k in range(KERNEL):
        pre = pre + cw_ref[k : k + 1, pl.ds(conv_at, 128)] * pad[5 + k : 5 + k + rows, :]
    return pre

def steps(proj_ref, hp_ref, dt_at):
    raw = proj_ref[:, dt_at : dt_at + 128].astype(F32) + hp_ref[0:1, :]
    return raw, softplus(raw)

def chunk_factors(dt, hp_ref):
    rate = dt * hp_ref[1:2, :]
    rows = lax.broadcasted_iota(jnp.int32, (Q, Q), 0)
    cols = lax.broadcasted_iota(jnp.int32, (Q, Q), 1)
    tri = (rows >= cols).astype(F32)
    cum = dot(tri, rate, 1, 0, lax.Precision.HIGHEST)
    return rate, cum, rows >= cols

def decay_pair(cum, cum_t, causal, pair):
    parts = []
    for h in (2 * pair, 2 * pair + 1):
        diff = jnp.broadcast_to(cum[:, h : h + 1], (Q, Q)) - jnp.broadcast_to(cum_t[h : h + 1, :], (Q, Q))
        parts.append(jnp.exp(jnp.where(causal, diff, -1e30)))
    return jnp.concatenate(parts, axis=1)

def scan_forward(G, proj_ref, cw_ref, hp_ref, gw_ref, vg_ref, ssq_ref, mixed_ref, yp_ref, st_ref, pad, xc, dts, state):
    L = proj_ref.shape[0]
    for tile in range((G + 2 * STATE) // 128):
        pre = conv_tile(proj_ref, cw_ref, pad, G + tile * 128, tile * 128, L)
        xc[:, tile * 128 : tile * 128 + 128] = pre * sigmoid(pre)
    _, dts[...] = steps(proj_ref, hp_ref, 2 * G + 2 * STATE)
    state[...] = jnp.zeros_like(state)
    mask = lane_mask(Q)

    def chunk(c, _):
        at = pl.ds(pl.multiple_of(c * Q, Q), Q)
        dt = dts[at, :]
        rate, cum, causal = chunk_factors(dt, hp_ref)
        cum_t = cum.T
        last = cum[Q - 1 : Q, :]
        e_cum = jnp.exp(cum)
        tail = jnp.exp(last - cum) * dt
        e_last = jnp.broadcast_to(jnp.exp(last), (8, 128))
        b = xc[at, G : G + STATE].astype(BF)
        cc = xc[at, G + STATE : G + 2 * STATE].astype(BF)
        scores = dot(cc, b, 1, 1)
        scores2 = jnp.concatenate([scores, scores], axis=1)
        ssq = jnp.zeros((Q, 1), F32)
        for p in range(G // 128):
            lanes = slice(p * 128, p * 128 + 128)
            x = xc[at, lanes]
            u = (x * spread(dt, p, mask)).astype(BF)
            m = (scores2 * decay_pair(cum, cum_t, causal, p)).astype(BF)
            before = state[:, lanes]
            st_ref[c, :, lanes] = before
            y = dot(m, split_pair(u, mask), 1, 0)
            y = y + dot(cc, before.astype(BF), 1, 0) * spread(e_cum, p, mask)
            yp_ref[at, lanes] = y
            after = dot(b, (x * spread(tail, p, mask)).astype(BF), 0, 0)
            state[:, lanes] = before * spread(e_last, p, mask[0:8])[0:1, :] + after
            mixed = (y + gw_ref[1:2, lanes] * x).astype(BF)
            mixed_ref[at, lanes] = mixed
            gate = proj_ref[at, lanes].astype(F32)
            v = mixed.astype(F32) * (gate * sigmoid(gate))
            vg_ref[at, lanes] = (v * gw_ref[0:1, lanes]).astype(BF)
            ssq = ssq + jnp.sum(v * v, axis=1, keepdims=True)
        ssq_ref[c] = jnp.broadcast_to(ssq, (Q, 128)).T[0:8, :]
        return 0

    lax.fori_loop(0, L // Q, chunk, 0)

def scan_fwd_call(proj, cw, hp, gw):
    L, _ = proj.shape
    G = gw.shape[1]
    nb = L // Q
    vm = pl.BlockSpec(memory_space=pltpu.VMEM)
    return pl.pallas_call(
        functools.partial(scan_forward, G),
        out_shape=(
            jax.ShapeDtypeStruct((L, G), BF),
            jax.ShapeDtypeStruct((nb, 8, 128), F32),
            jax.ShapeDtypeStruct((L, G), BF),
            jax.ShapeDtypeStruct((L, G), F32),
            jax.ShapeDtypeStruct((nb, STATE, G), F32),
        ),
        in_specs=[vm] * 4,
        out_specs=[vm] * 5,
        scratch_shapes=[
            pltpu.VMEM((8 + L, 128), F32),
            pltpu.VMEM((L, G + 2 * STATE), F32),
            pltpu.VMEM((L, 128), F32),
            pltpu.VMEM((STATE, G), F32),
        ],
        compiler_params=pltpu.CompilerParams(vmem_limit_bytes=VMEM_LIMIT),
        cost_estimate=pl.CostEstimate(flops=L * G * 1500, bytes_accessed=L * G * 20, transcendentals=L * G * 4),
        name="scan_forward",
    )(proj, cw, hp, gw)

def scan_backward(G, proj_ref, mixed_ref, yp_ref, st_ref, dn_ref, sc_ref, cw_ref, hp_ref, gw_ref,
                  dproj_ref, no_ref, gg_ref, gc_ref, gh_ref,
                  pad, xc, dts, dy, dxc, dstate, ddt):
    L = proj_ref.shape[0]
    nb = L // Q
    mask = lane_mask(Q)
    for tile in range((G + 2 * STATE) // 128):
        pre = conv_tile(proj_ref, cw_ref, pad, G + tile * 128, tile * 128, L)
        xc[:, tile * 128 : tile * 128 + 128] = pre * sigmoid(pre)
    raw, dts[...] = steps(proj_ref, hp_ref, 2 * G + 2 * STATE)
    dstate[...] = jnp.zeros_like(dstate)
    gg_ref[...] = jnp.zeros_like(gg_ref)
    gh_ref[...] = jnp.zeros_like(gh_ref)

    def chunk(step, _):
        c = nb - 1 - step
        at = pl.ds(pl.multiple_of(c * Q, Q), Q)
        sc = jnp.concatenate([sc_ref[c], jnp.zeros((Q - 8, 128), F32)], axis=0).T
        inv2 = jnp.broadcast_to(sc[:, 0:1], (Q, 128))
        mdot = jnp.broadcast_to(sc[:, 1:2], (Q, 128))
        dt = dts[at, :]
        rate, cum, causal = chunk_factors(dt, hp_ref)
        cum_t = cum.T
        last = cum[Q - 1 : Q, :]
        e_cum = jnp.exp(cum)
        tail = jnp.exp(last - cum)
        e_last = jnp.broadcast_to(jnp.exp(last), (8, 128))
        b = xc[at, G : G + STATE].astype(BF)
        cc = xc[at, G + STATE : G + 2 * STATE].astype(BF)
        scores = dot(cc, b, 1, 1)
        scores2 = jnp.concatenate([scores, scores], axis=1)
        d_scores = jnp.zeros((Q, Q), F32)
        d_b = jnp.zeros((Q, STATE), F32)
        d_c = jnp.zeros((Q, STATE), F32)
        d_cum = jnp.zeros((Q, 128), F32)
        d_dt = jnp.zeros((Q, 128), F32)
        d_last = jnp.zeros((8, 128), F32)
        lane_ids = lax.broadcasted_iota(jnp.int32, (Q, 128), 1)
        for p in range(G // 128):
            lanes = slice(p * 128, p * 128 + 128)
            gate = proj_ref[at, lanes].astype(F32)
            sig = sigmoid(gate)
            act = gate * sig
            mixed = mixed_ref[at, lanes].astype(F32)
            n2 = mixed * act * inv2
            no_ref[at, lanes] = (n2 * gw_ref[0:1, lanes]).astype(BF)
            dn = dn_ref[at, lanes]
            gg_ref[0:1, lanes] += jnp.sum(dn * n2, axis=0, keepdims=True)
            d_v = inv2 * (dn * gw_ref[0:1, lanes] - n2 * mdot)
            dyb = (d_v * act).astype(BF)
            dproj_ref[at, lanes] = (d_v * mixed * (sig * (1.0 + gate * (1.0 - sig)))).astype(BF)
            d_y = dyb.astype(F32)
            x = xc[at, lanes]
            dt_x = spread(dt, p, mask)
            u = (x * dt_x).astype(BF)
            u2 = split_pair(u, mask)
            uf = u.astype(F32)
            dec = decay_pair(cum, cum_t, causal, p)
            m = (scores2 * dec).astype(BF)
            dm = dot(dyb, u2, 1, 1) * dec
            d_scores = d_scores + dm[:, :Q] + dm[:, Q:]
            both = dot(m, dyb, 0, 0)
            du = jnp.where(mask, both[:Q], both[Q:])
            tail_x = spread(tail, p, mask)
            before = st_ref[c, :, lanes]
            after = dstate[:, lanes]
            afterb = after.astype(BF)
            du_out = tail_x * dot(b, afterb, 1, 0)
            du = du + du_out
            dye = (d_y * spread(e_cum, p, mask)).astype(BF)
            d_c = d_c + dot(dye, before.astype(BF), 1, 1)
            d_b = d_b + dot((uf * tail_x).astype(BF), afterb, 1, 1)
            e_last_x = spread(e_last, p, mask[0:8])
            dstate[:, lanes] = after * e_last_x[0:1, :] + dot(cc, dye, 0, 0)
            z3 = jnp.sum(uf * du_out, axis=0, keepdims=True) + e_last_x[0:1, :] * jnp.sum(before * after, axis=0, keepdims=True)
            z1 = d_y * yp_ref[at, lanes] - uf * du
            z2 = x * du
            zero = jnp.zeros_like(z1)
            for half, h in ((True, 2 * p), (False, 2 * p + 1)):
                keep = mask if half else jnp.logical_not(mask)
                here = lane_ids == h
                d_cum = jnp.where(here, jnp.sum(jnp.where(keep, z1, zero), axis=1, keepdims=True), d_cum)
                d_dt = jnp.where(here, jnp.sum(jnp.where(keep, z2, zero), axis=1, keepdims=True), d_dt)
                s3 = jnp.sum(jnp.where(keep[0:8], jnp.broadcast_to(z3, (8, 128)), 0.0), axis=1, keepdims=True)
                d_last = jnp.where(here[0:8], s3, d_last)
            dxc[at, lanes] = dt_x * du + gw_ref[1:2, lanes] * d_y
            gg_ref[1:2, lanes] += jnp.sum(d_y * x, axis=0, keepdims=True)
        dsb = d_scores.astype(BF)
        dxc[at, G : G + STATE] = d_b + dot(dsb, cc, 0, 0)
        dxc[at, G + STATE : G + 2 * STATE] = d_c + dot(dsb, b, 1, 0)
        rows = lax.broadcasted_iota(jnp.int32, (Q, Q), 0)
        cols = lax.broadcasted_iota(jnp.int32, (Q, Q), 1)
        upper = (rows <= cols).astype(F32)
        d_rate = dot(upper, d_cum, 1, 0, lax.Precision.HIGHEST) + d_last[0:1, :]
        d_step = d_dt + d_rate * hp_ref[1:2, :]
        raw_c = proj_ref[at, 2 * G + 2 * STATE : 2 * G + 2 * STATE + 128].astype(F32) + hp_ref[0:1, :]
        d_raw = d_step * sigmoid(raw_c)
        dproj_ref[at, 2 * G + 2 * STATE : 2 * G + 2 * STATE + 128] = d_raw.astype(BF)
        gh_ref[0:1, :] += jnp.sum(d_raw, axis=0, keepdims=True)
        gh_ref[1:2, :] += jnp.sum(d_rate * rate, axis=0, keepdims=True)
        return 0

    lax.fori_loop(0, nb, chunk, 0)

    gc_ref[...] = jnp.zeros_like(gc_ref)
    for tile in range((G + 2 * STATE) // 128):
        lanes = slice(tile * 128, tile * 128 + 128)
        pre = conv_tile(proj_ref, cw_ref, pad, G + tile * 128, tile * 128, L)
        sig = sigmoid(pre)
        d_pre = dxc[:, lanes] * (sig * (1.0 + pre * (1.0 - sig)))
        for k in range(KERNEL):
            gc_ref[k : k + 1, lanes] = jnp.sum(d_pre * pad[5 + k : 5 + k + L, :], axis=0, keepdims=True)
        gc_ref[4:5, lanes] = jnp.sum(d_pre, axis=0, keepdims=True)
        pad[0:L, :] = d_pre
        pad[L : L + 8, :] = jnp.zeros((8, 128), F32)
        d_in = cw_ref[3:4, lanes] * d_pre
        for k in range(KERNEL - 1):
            d_in = d_in + cw_ref[k : k + 1, lanes] * pad[3 - k : 3 - k + L, :]
        dproj_ref[:, G + tile * 128 : G + tile * 128 + 128] = d_in.astype(BF)

def scan_bwd_call(proj, mixed, yp, st, dn, sc, cw, hp, gw):
    L, NC = proj.shape
    G = gw.shape[1]
    vm = pl.BlockSpec(memory_space=pltpu.VMEM)
    CX = G + 2 * STATE
    return pl.pallas_call(
        functools.partial(scan_backward, G),
        out_shape=(
            jax.ShapeDtypeStruct((L, NC), BF),
            jax.ShapeDtypeStruct((L, G), BF),
            jax.ShapeDtypeStruct((8, G), F32),
            jax.ShapeDtypeStruct((8, CX), F32),
            jax.ShapeDtypeStruct((8, 128), F32),
        ),
        in_specs=[vm] * 9,
        out_specs=[vm] * 5,
        scratch_shapes=[
            pltpu.VMEM((8 + L, 128), F32),
            pltpu.VMEM((L, CX), F32),
            pltpu.VMEM((L, 128), F32),
            pltpu.VMEM((8, 128), F32),
            pltpu.VMEM((L, CX), F32),
            pltpu.VMEM((STATE, G), F32),
            pltpu.VMEM((8, 128), F32),
        ],
        compiler_params=pltpu.CompilerParams(vmem_limit_bytes=VMEM_LIMIT),
        cost_estimate=pl.CostEstimate(flops=L * G * 4000, bytes_accessed=L * G * 30, transcendentals=L * G * 6),
        name="scan_backward",
    )(proj, mixed, yp, st, dn, sc, cw, hp, gw)


MESH = pl.DeviceIdType.MESH
VM = pl.BlockSpec(memory_space=pltpu.VMEM)
ANY = pl.BlockSpec(memory_space=pl.ANY)
TILE = 16


def meet(axis, n):
    me = lax.axis_index(axis)
    barrier = pltpu.get_barrier_semaphore()
    for k in range(1, n):
        pl.semaphore_signal(
            barrier, inc=1, device_id={axis: lax.rem(me + k, n)}, device_id_type=MESH
        )
    pl.semaphore_wait(barrier, n - 1)


def send(src, dst, sems, at, axis, peer):
    copy = pltpu.make_async_remote_copy(
        src, dst, sems[0].at[at], sems[1].at[at], device_id={axis: peer}, device_id_type=MESH
    )
    copy.start()
    return copy


def column(row):
    return jnp.broadcast_to(row, (128, 128)).T


def sum_parts(n, part_ref, stat_ref, got, got_stat, sems, stat_sems):
    me = lax.axis_index("seq")
    copies = []
    for k in range(1, n):
        peer = lax.rem(me + k, n)
        copies.append(send(part_ref.at[peer], got.at[k - 1], sems, k - 1, "seq", peer))
        if stat_ref is not None:
            copies.append(
                send(stat_ref.at[peer], got_stat.at[k - 1], stat_sems, k - 1, "seq", peer)
            )
    return copies


def gather_rows(n, own, all_ref, own_stat, stat_ref, sems, stat_sems):
    me = lax.axis_index("seq")
    copies = []
    for k in range(1, n):
        peer = lax.rem(me + k, n)
        copies.append(send(own, all_ref.at[me], sems, k - 1, "seq", peer))
        if stat_ref is not None:
            copies.append(send(own_stat, stat_ref.at[me], stat_sems, k - 1, "seq", peer))
    return copies


def rows_loop(rows, body):
    def step(r, carry):
        body(pl.ds(pl.multiple_of(r * TILE, TILE), TILE))
        return carry

    lax.fori_loop(0, rows // TILE, step, 0)


def total_of(n, part_ref, got, at):
    total = part_ref[lax.axis_index("seq"), at, :].astype(F32)
    for k in range(n - 1):
        total = total + got[k, at, :].astype(F32)
    return total


def start_kernel(n, h_ref, gain_ref, all_ref, own, s0, r0):
    rows = h_ref.shape[0]

    def norm(at):
        h = h_ref[at, :]
        inv = lax.rsqrt(jnp.mean(h * h, axis=1, keepdims=True) + EPSILON)
        own[at, :] = (h * inv * gain_ref[0:1, :]).astype(BF)

    rows_loop(rows, norm)
    meet("seq", n)
    copies = gather_rows(n, own, all_ref, None, None, (s0, r0), None)
    all_ref[lax.axis_index("seq")] = own[...]
    for copy in copies:
        copy.wait()


def start_call(h, gain, n):
    rows = h.shape[0]
    return pl.pallas_call(
        functools.partial(start_kernel, n),
        out_shape=jax.ShapeDtypeStruct((n, rows, D), BF),
        in_specs=[VM, VM],
        out_specs=VM,
        scratch_shapes=[
            pltpu.VMEM((rows, D), BF),
            pltpu.SemaphoreType.DMA((n - 1,)),
            pltpu.SemaphoreType.DMA((n - 1,)),
        ],
        compiler_params=pltpu.CompilerParams(
            collective_id=0, has_side_effects=True, vmem_limit_bytes=VMEM_LIMIT
        ),
        name="start",
    )(h, gain)


def forward_turn_kernel(
    n, last, part_ref, ssq_ref, h_ref, next_ref, hout_ref, pout_ref, all_ref, stat_ref,
    got, got_stat, own, own_stat, cols, mdots, s0, r0, s1, r1, s2, r2, s3, r3
):
    me = lax.axis_index("seq")
    rows = h_ref.shape[0]
    meet("seq", n)
    copies = sum_parts(n, part_ref, ssq_ref, got, got_stat, (s0, r0), (s1, r1))
    for copy in copies:
        copy.wait()
    ssq = ssq_ref[me]
    for k in range(n - 1):
        ssq = ssq + got_stat[k]
    inv2 = lax.rsqrt(ssq * (1.0 / INNER) + EPSILON)
    own_stat[...] = inv2
    cols[...] = column(inv2[0:1, :])

    def finish(at):
        pout = total_of(n, part_ref, got, at) * cols[at, 0:1]
        h = h_ref[at, :] + pout
        hout_ref[at, :] = h
        pout_ref[at, :] = pout
        if last:
            out = next_ref[at, :].astype(BF)
            dots = jnp.sum(out.astype(F32) * pout, axis=1, keepdims=True)
            mdots[at, :] = jnp.broadcast_to(dots * (1.0 / INNER), (TILE, 128))
            own[at, :] = out
        else:
            inv = lax.rsqrt(jnp.mean(h * h, axis=1, keepdims=True) + EPSILON)
            own[at, :] = (h * inv * next_ref[0:1, :]).astype(BF)

    rows_loop(rows, finish)
    if last:
        own_stat[1:2, :] = mdots[...].T[0:1, :]
    copies = gather_rows(n, own, all_ref, own_stat, stat_ref, (s2, r2), (s3, r3))
    all_ref[me] = own[...]
    stat_ref[me] = own_stat[...]
    for copy in copies:
        copy.wait()


def forward_turn(part, ssq, h, following, n, last):
    rows = h.shape[0]
    sems = [pltpu.SemaphoreType.DMA((n - 1,))] * 8
    return pl.pallas_call(
        functools.partial(forward_turn_kernel, n, last),
        out_shape=(
            jax.ShapeDtypeStruct((rows, D), F32),
            jax.ShapeDtypeStruct((rows, D), F32),
            jax.ShapeDtypeStruct((n, rows, D), BF),
            jax.ShapeDtypeStruct((n, 8, 128), F32),
        ),
        in_specs=[VM] * 4,
        out_specs=[VM] * 4,
        scratch_shapes=[
            pltpu.VMEM((n - 1, rows, D), BF),
            pltpu.VMEM((n - 1, 8, 128), F32),
            pltpu.VMEM((rows, D), BF),
            pltpu.VMEM((8, 128), F32),
            pltpu.VMEM((rows, 128), F32),
            pltpu.VMEM((rows, 128), F32),
        ]
        + sems,
        compiler_params=pltpu.CompilerParams(
            collective_id=2 if last else 1, has_side_effects=True, vmem_limit_bytes=VMEM_LIMIT
        ),
        name="forward_end" if last else "forward_turn",
    )(part, ssq, h, following)


def backward_turn_kernel(n, last, *refs):
    if last:
        part_ref, h_ref, og_ref, gain_ref, dh_ref, gn_ref, got, s0, r0 = refs
    else:
        (part_ref, h_ref, og_ref, gain_ref, pout_ref, low_ref, dh_ref, gn_ref, all_ref, stat_ref,
         got, own, own_stat, mdots, s0, r0, s2, r2, s3, r3) = refs
    me = lax.axis_index("seq")
    rows = h_ref.shape[0]
    meet("seq", n)
    for copy in sum_parts(n, part_ref, None, got, None, (s0, r0), None):
        copy.wait()
    gn_ref[...] = jnp.zeros_like(gn_ref)

    def finish(at):
        d_in = total_of(n, part_ref, got, at)
        h = h_ref[at, :]
        inv = lax.rsqrt(jnp.mean(h * h, axis=1, keepdims=True) + EPSILON)
        normed = h * inv
        gn_ref[0:1, :] += jnp.sum(d_in * normed, axis=0, keepdims=True)
        d_s = d_in * gain_ref[0:1, :]
        d_h = og_ref[at, :] + inv * (d_s - normed * jnp.mean(d_s * normed, axis=1, keepdims=True))
        dh_ref[at, :] = d_h
        if not last:
            out = d_h.astype(BF)
            own[at, :] = out
            dots = jnp.sum(out.astype(F32) * pout_ref[at, :], axis=1, keepdims=True)
            mdots[at, :] = jnp.broadcast_to(dots * (1.0 / INNER), (TILE, 128))

    rows_loop(rows, finish)
    if last:
        return
    own_stat[...] = low_ref[...]
    own_stat[1:2, :] = mdots[...].T[0:1, :]
    copies = gather_rows(n, own, all_ref, own_stat, stat_ref, (s2, r2), (s3, r3))
    all_ref[me] = own[...]
    stat_ref[me] = own_stat[...]
    for copy in copies:
        copy.wait()


def backward_turn(part, h, out_grad, gain, below, n):
    rows = h.shape[0]
    last = below is None
    sem = pltpu.SemaphoreType.DMA((n - 1,))
    outs = [jax.ShapeDtypeStruct((rows, D), F32), jax.ShapeDtypeStruct((8, D), F32)]
    scratch = [pltpu.VMEM((n - 1, rows, D), BF)]
    if not last:
        outs += [
            jax.ShapeDtypeStruct((n, rows, D), BF),
            jax.ShapeDtypeStruct((n, 8, 128), F32),
        ]
        scratch += [
            pltpu.VMEM((rows, D), BF),
            pltpu.VMEM((8, 128), F32),
            pltpu.VMEM((rows, 128), F32),
        ]
    args = (part, h, out_grad, gain) + (() if last else below)
    return pl.pallas_call(
        functools.partial(backward_turn_kernel, n, last),
        out_shape=outs,
        in_specs=[VM] * len(args),
        out_specs=[VM] * len(outs),
        scratch_shapes=scratch + [sem] * (2 if last else 6),
        compiler_params=pltpu.CompilerParams(
            collective_id=4 if last else 3, has_side_effects=True, vmem_limit_bytes=VMEM_LIMIT
        ),
        name="backward_end" if last else "backward_turn",
    )(*args)


def swap_kernel(axis, n, scatter, *refs):
    count = (len(refs) - 3) // 2
    sources, targets, (s0, r0, l0) = refs[:count], refs[count : 2 * count], refs[2 * count :]
    me = lax.axis_index(axis)
    meet(axis, n)
    copies = []
    for a in range(count):
        for k in range(1, n):
            peer = lax.rem(me + k, n)
            source = sources[a].at[peer] if scatter else sources[a]
            copies.append(
                send(source, targets[a].at[me], (s0, r0), a * (n - 1) + k - 1, axis, peer)
            )
        mine = sources[a].at[me] if scatter else sources[a]
        local_copy = pltpu.make_async_copy(mine, targets[a].at[me], l0.at[a])
        local_copy.start()
        copies.append(local_copy)
    for copy in copies:
        copy.wait()


def swap(arrays, axis, n, scatter, cid):
    count = len(arrays)
    return pl.pallas_call(
        functools.partial(swap_kernel, axis, n, scatter),
        out_shape=[
            jax.ShapeDtypeStruct(a.shape if scatter else (n,) + a.shape, a.dtype) for a in arrays
        ],
        in_specs=[ANY] * count,
        out_specs=[ANY] * count,
        scratch_shapes=[
            pltpu.SemaphoreType.DMA((count * (n - 1),)),
            pltpu.SemaphoreType.DMA((count * (n - 1),)),
            pltpu.SemaphoreType.DMA((count,)),
        ],
        compiler_params=pltpu.CompilerParams(
            collective_id=cid, has_side_effects=True, vmem_limit_bytes=VMEM_LIMIT
        ),
        name=f"swap_{axis}_{cid}",
    )(*arrays)


def padded(array, size):
    return jnp.pad(array, ((0, 0), (0, size - array.shape[1])))


class Group:
    def __init__(self, n_seq, n_wt):
        self.n_seq, self.n_wt = n_seq, n_wt
        self.heads = HEADS // n_seq
        self.runs = n_wt if HEADS % (n_seq * n_wt) == 0 else 1
        self.run_heads = self.heads // self.runs
        self.chans = self.heads * HEAD_DIM
        self.G = -(-self.chans // 128) * 128
        self.CX = self.G + 2 * STATE
        self.NC = 2 * self.G + 2 * STATE + 128

    def take(self, array, first, width):
        at = lax.axis_index("seq") * self.run_heads * width
        stride = HEADS // self.runs * width
        return [
            lax.dynamic_slice_in_dim(array, first + r * stride + at, self.run_heads * width, 1)
            for r in range(self.runs)
        ]

    def place(self, arrays, width):
        run = self.run_heads * width
        return [
            arrays[g][..., r * run : (r + 1) * run]
            for r in range(self.runs)
            for g in range(self.n_seq)
        ]

    def weight(self, w):
        gate = padded(jnp.concatenate(self.take(w, 0, HEAD_DIM), 1), self.G)
        x = padded(jnp.concatenate(self.take(w, INNER, HEAD_DIM), 1), self.G)
        bc = w[:, 2 * INNER : 2 * INNER + 2 * STATE]
        dt = padded(jnp.concatenate(self.take(w, 2 * INNER + 2 * STATE, 1), 1), 128)
        return jnp.concatenate([gate, x, bc, dt], 1)

    def small(self, norm_gain, conv_w, conv_b, dt_bias, a_log, skip_d, gate_gain):
        conv = jnp.concatenate([conv_w, conv_b[None], jnp.zeros((3, CONV), F32)], 0)
        conv_x = padded(jnp.concatenate(self.take(conv, 0, HEAD_DIM), 1), self.G)
        zero = jnp.zeros((6, HEADS), F32)
        head = jnp.concatenate([dt_bias[None], -jnp.exp(a_log)[None], zero], 0)
        head = padded(jnp.concatenate(self.take(head, 0, 1), 1), 128)
        wide = jnp.concatenate(
            [gate_gain[None], jnp.repeat(skip_d, HEAD_DIM)[None], jnp.zeros((6, INNER), F32)], 0
        )
        wide = padded(jnp.concatenate(self.take(wide, 0, HEAD_DIM), 1), self.G)
        gain = jnp.broadcast_to(norm_gain[None], (8, D))
        return jnp.concatenate([conv_x, conv[:, INNER:], head, wide, gain], 1)

    def parts(self, packed):
        cuts = [0, self.CX, self.CX + 128, self.CX + 128 + self.G, self.CX + 128 + self.G + D]
        return [packed[..., a:b] for a, b in zip(cuts, cuts[1:])]


def local(
    tokens, cotangent, norm_gain, w_in, conv_w, conv_b, dt_bias, a_log, skip_d, gate_gain, w_out
):
    n_seq, n_wt = lax.axis_size("seq"), lax.axis_size("wt")
    core = lax.axis_index("section")
    here = lax.axis_index("seq")
    group = Group(n_seq, n_wt)
    G, rows = group.G, tokens.shape[2]
    length = rows * n_seq

    both = ("section", "wt")
    win = lax.all_gather(group.weight(w_in[0]), both, axis=0, tiled=False)
    win = win.reshape(2, D, group.NC)
    if group.runs == n_wt:
        part = group.chans // n_wt
        piece = lax.dynamic_slice_in_dim(w_out[0], here * part, part, 0)
        wout = lax.all_gather(piece, both, axis=0, tiled=False).reshape(2, group.chans, D)
    else:
        wout = lax.all_gather(w_out[0], both, axis=0, tiled=False).reshape(2, INNER, D)
        wout = lax.dynamic_slice_in_dim(wout, here * group.chans, group.chans, 1)
    wout = jnp.pad(wout, ((0, 0), (0, G - group.chans), (0, 0)))
    packed = group.small(
        norm_gain[0], conv_w[0], conv_b[0], dt_bias[0], a_log[0], skip_d[0], gate_gain[0]
    )
    packed = lax.all_gather(packed, "section", axis=0, tiled=False)
    params = [group.parts(packed[s]) for s in range(2)]

    h0 = lax.dynamic_index_in_dim(tokens, core, 0, keepdims=False)[0]
    last_grad = lax.dynamic_index_in_dim(cotangent, core, 0, keepdims=False)[0]

    def forward(s, normed):
        conv, head, wide, _ = params[s]
        proj = jnp.dot(normed, win[s], preferred_element_type=F32).astype(BF)
        vg, ssq, mixed, yp, states = scan_fwd_call(proj, conv, head, wide)
        part = jnp.dot(vg, wout[s], preferred_element_type=F32).astype(BF)
        return part.reshape(n_seq, rows, D), ssq, (proj, mixed, yp, states)

    def backward(s, normed, kept, grad_b, stats):
        conv, head, wide, _ = params[s]
        proj, mixed, yp, states = kept
        d_normed = dot(grad_b, wout[s], 1, 1)
        d_proj, normed_out, g_wide, g_conv, g_head = scan_bwd_call(
            proj, mixed, yp, states, d_normed, stats, conv, head, wide
        )
        part = dot(d_proj, win[s], 1, 1).astype(BF).reshape(n_seq, rows, D)
        g_out = dot(normed_out, grad_b, 0, 0).astype(BF)
        g_in = dot(normed, d_proj, 0, 0).astype(BF)
        return part, g_in, g_out, (g_conv, g_head, g_wide)

    n0 = start_call(h0, params[0][3], n_seq)
    n0 = n0.reshape(length, D)
    part, ssq, kept0 = forward(0, n0)
    h1, pout0, n1, stat0 = forward_turn(part, ssq, h0, params[1][3], n_seq, False)
    n1 = n1.reshape(length, D)
    part, ssq, kept1 = forward(1, n1)
    h2, pout1, grad_b, stats = forward_turn(part, ssq, h1, last_grad, n_seq, True)
    part, gin1, gout1, small1 = backward(1, n1, kept1, grad_b.reshape(length, D), stats)
    low = lax.dynamic_index_in_dim(stat0, here, 0, keepdims=False)
    d1, gnorm1, grad_b, stats = backward_turn(
        part, h1, last_grad, params[1][3], (pout0, low), n_seq
    )
    part, gin0, gout0, small0 = backward(0, n0, kept0, grad_b.reshape(length, D), stats)
    d0, gnorm0 = backward_turn(part, h0, d1, params[0][3], None, n_seq)

    def to_layer(low_val, top_val):
        own = jnp.where(core == 0, low_val, top_val)
        other = jnp.where(core == 0, top_val, low_val)
        return own, lax.ppermute(other, "section", [(0, 1), (1, 0)])

    own, other = to_layer(gin0, gin1)
    gin = (own.astype(F32) + other.astype(F32)).astype(BF).reshape(n_wt, D // n_wt, group.NC)
    own, other = to_layer(gout0, gout1)
    gout = (own.astype(F32) + other.astype(F32)).astype(BF)
    if group.runs == n_wt:
        gout = gout.reshape(n_wt, G // n_wt, D)
        gin, gout = swap([gin, gout], "wt", n_wt, True, 5)
        gin = jnp.sum(gin.astype(F32), 0).astype(BF)
        gout = jnp.sum(gout.astype(F32), 0).astype(BF)
        gin, gout = swap([gin, gout], "seq", n_seq, False, 6)
        g_out = gout.reshape(INNER // n_wt, D).astype(F32)
    else:
        [gin] = swap([gin], "wt", n_wt, True, 5)
        gin = jnp.sum(gin.astype(F32), 0).astype(BF)
        gout = lax.psum(gout[: group.chans], "wt")
        gin, gout = swap([gin, gout], "seq", n_seq, False, 6)
        mine = INNER // n_wt
        gout = gout.reshape(INNER, D)
        g_out = lax.dynamic_slice_in_dim(gout, lax.axis_index("wt") * mine, mine, 0).astype(F32)
    shards = [gin[g] for g in range(n_seq)]
    shared = jnp.sum(gin[:, :, 2 * G : 2 * G + 2 * STATE].astype(F32), 0)
    g_in = jnp.concatenate(
        [a.astype(F32) for a in group.place([s[:, :G] for s in shards], HEAD_DIM)]
        + [a.astype(F32) for a in group.place([s[:, G : 2 * G] for s in shards], HEAD_DIM)]
        + [shared]
        + [a.astype(F32) for a in group.place([s[:, 2 * G + 2 * STATE :] for s in shards], 1)],
        axis=1,
    )

    packs = jnp.stack(
        [
            jnp.concatenate([*small0, gnorm0], 1),
            jnp.concatenate([*small1, gnorm1], 1),
        ]
    )
    packs = lax.psum(packs, ("section", "wt"))
    packs = lax.dynamic_index_in_dim(packs, core, 0, keepdims=False)
    packs = lax.all_gather(packs, "seq", axis=0, tiled=False)
    conv, head, wide, norm = group.parts(packs)
    conv_all = jnp.concatenate(
        group.place([conv[g, :, : group.chans] for g in range(n_seq)], HEAD_DIM)
        + [jnp.sum(conv[:, :, G:], 0)],
        axis=1,
    )
    head_all = jnp.concatenate(group.place([head[g] for g in range(n_seq)], 1), 1)
    wide_all = jnp.concatenate(
        group.place([wide[g, :, : group.chans] for g in range(n_seq)], HEAD_DIM), 1
    )
    g_skip = jnp.sum(wide_all[1].reshape(HEADS, HEAD_DIM), 1)

    own, other = to_layer(h1, h2)
    section_out = jnp.where(core == 0, jnp.stack([own, other]), jnp.stack([other, own]))
    own, other = to_layer(d0, d1)
    input_grad = jnp.where(core == 0, jnp.stack([own, other]), jnp.stack([other, own]))
    return (
        section_out[None, :, None],
        input_grad[None, :, None],
        jnp.sum(norm[:, 0], 0)[None],
        g_in[None],
        conv_all[None, :KERNEL],
        conv_all[None, KERNEL],
        head_all[None, 0],
        head_all[None, 1],
        g_skip[None],
        wide_all[None, 0],
        g_out[None],
    )


def solution(mesh):
    placed = (
        P(None, "wt", "seq", None),
        P(None, "wt", "seq", None),
        P("section", None),
        P("section", "wt", None),
        P("section", None, None),
        P("section", None),
        P("section", None),
        P("section", None),
        P("section", None),
        P("section", None),
        P("section", "wt", None),
    )
    return jax.shard_map(
        local,
        mesh=mesh,
        in_specs=placed,
        out_specs=(
            P("section", None, "wt", "seq", None),
            P("section", None, "wt", "seq", None),
            P("section", None),
            P("section", "wt", None),
            P("section", None, None),
            P("section", None),
            P("section", None),
            P("section", None),
            P("section", None),
            P("section", None),
            P("section", "wt", None),
        ),
        check_vma=False,
    )
```

```python
import functools

import jax
import jax.numpy as jnp
from jax import lax
from jax.experimental import pallas as pl
from jax.experimental.pallas import tpu as pltpu
from jax.sharding import PartitionSpec as P

D = 1536
HEADS = 48
HEAD_DIM = 64
STATE = 128
KERNEL = 4
INNER = 3072
CONV = 3328
EPSILON = 1e-05

Q = 128
F32 = jnp.float32
BF = jnp.bfloat16
VMEM_LIMIT = 48 * 2**20


def dot(a, b, ca, cb, precision=None):
    return lax.dot_general(a, b, (((ca,), (cb,)), ((), ())), precision=precision, preferred_element_type=F32)

def sigmoid(x):
    return 1.0 / (1.0 + jnp.exp(-x))

def softplus(x):
    return jnp.maximum(x, 0.0) + jnp.log1p(jnp.exp(-jnp.abs(x)))

def lane_mask(rows):
    return lax.broadcasted_iota(jnp.int32, (rows, 128), 1) < HEAD_DIM

def spread(cols, pair, mask):
    a = jnp.broadcast_to(cols[:, 2 * pair : 2 * pair + 1], mask.shape)
    b = jnp.broadcast_to(cols[:, 2 * pair + 1 : 2 * pair + 2], mask.shape)
    return jnp.where(mask, a, b)

def split_pair(u, mask):
    zero = jnp.zeros_like(u)
    return jnp.concatenate([jnp.where(mask, u, zero), jnp.where(mask, zero, u)], axis=0)

def conv_tile(proj_ref, cw_ref, pad, proj_at, conv_at, rows):
    pad[0:8, :] = jnp.zeros((8, 128), F32)
    pad[8 : 8 + rows, :] = proj_ref[:, pl.ds(proj_at, 128)].astype(F32)
    pre = jnp.broadcast_to(cw_ref[4:5, pl.ds(conv_at, 128)], (rows, 128))
    for k in range(KERNEL):
        pre = pre + cw_ref[k : k + 1, pl.ds(conv_at, 128)] * pad[5 + k : 5 + k + rows, :]
    return pre

def steps(proj_ref, hp_ref, dt_at):
    raw = proj_ref[:, dt_at : dt_at + 128].astype(F32) + hp_ref[0:1, :]
    return raw, softplus(raw)

def chunk_factors(dt, hp_ref):
    rate = dt * hp_ref[1:2, :]
    rows = lax.broadcasted_iota(jnp.int32, (Q, Q), 0)
    cols = lax.broadcasted_iota(jnp.int32, (Q, Q), 1)
    tri = (rows >= cols).astype(F32)
    cum = dot(tri, rate, 1, 0, lax.Precision.HIGHEST)
    return rate, cum, rows >= cols

def decay_pair(cum, cum_t, causal, pair):
    parts = []
    for h in (2 * pair, 2 * pair + 1):
        diff = jnp.broadcast_to(cum[:, h : h + 1], (Q, Q)) - jnp.broadcast_to(cum_t[h : h + 1, :], (Q, Q))
        parts.append(jnp.exp(jnp.where(causal, diff, -1e30)))
    return jnp.concatenate(parts, axis=1)

def scan_forward(G, proj_ref, cw_ref, hp_ref, gw_ref, vg_ref, ssq_ref, mixed_ref, yp_ref, st_ref, pad, xc, dts, state):
    L = proj_ref.shape[0]
    for tile in range((G + 2 * STATE) // 128):
        pre = conv_tile(proj_ref, cw_ref, pad, G + tile * 128, tile * 128, L)
        xc[:, tile * 128 : tile * 128 + 128] = pre * sigmoid(pre)
    _, dts[...] = steps(proj_ref, hp_ref, 2 * G + 2 * STATE)
    state[...] = jnp.zeros_like(state)
    mask = lane_mask(Q)

    def chunk(c, _):
        at = pl.ds(pl.multiple_of(c * Q, Q), Q)
        dt = dts[at, :]
        rate, cum, causal = chunk_factors(dt, hp_ref)
        cum_t = cum.T
        last = cum[Q - 1 : Q, :]
        e_cum = jnp.exp(cum)
        tail = jnp.exp(last - cum) * dt
        e_last = jnp.broadcast_to(jnp.exp(last), (8, 128))
        b = xc[at, G : G + STATE].astype(BF)
        cc = xc[at, G + STATE : G + 2 * STATE].astype(BF)
        scores = dot(cc, b, 1, 1)
        scores2 = jnp.concatenate([scores, scores], axis=1)
        ssq = jnp.zeros((Q, 1), F32)
        for p in range(G // 128):
            lanes = slice(p * 128, p * 128 + 128)
            x = xc[at, lanes]
            u = (x * spread(dt, p, mask)).astype(BF)
            m = (scores2 * decay_pair(cum, cum_t, causal, p)).astype(BF)
            before = state[:, lanes]
            st_ref[c, :, lanes] = before
            y = dot(m, split_pair(u, mask), 1, 0)
            y = y + dot(cc, before.astype(BF), 1, 0) * spread(e_cum, p, mask)
            yp_ref[at, lanes] = y
            after = dot(b, (x * spread(tail, p, mask)).astype(BF), 0, 0)
            state[:, lanes] = before * spread(e_last, p, mask[0:8])[0:1, :] + after
            mixed = (y + gw_ref[1:2, lanes] * x).astype(BF)
            mixed_ref[at, lanes] = mixed
            gate = proj_ref[at, lanes].astype(F32)
            v = mixed.astype(F32) * (gate * sigmoid(gate))
            vg_ref[at, lanes] = (v * gw_ref[0:1, lanes]).astype(BF)
            ssq = ssq + jnp.sum(v * v, axis=1, keepdims=True)
        ssq_ref[c] = jnp.broadcast_to(ssq, (Q, 128)).T[0:8, :]
        return 0

    lax.fori_loop(0, L // Q, chunk, 0)

def scan_fwd_call(proj, cw, hp, gw):
    L, _ = proj.shape
    G = gw.shape[1]
    nb = L // Q
    vm = pl.BlockSpec(memory_space=pltpu.VMEM)
    return pl.pallas_call(
        functools.partial(scan_forward, G),
        out_shape=(
            jax.ShapeDtypeStruct((L, G), BF),
            jax.ShapeDtypeStruct((nb, 8, 128), F32),
            jax.ShapeDtypeStruct((L, G), BF),
            jax.ShapeDtypeStruct((L, G), F32),
            jax.ShapeDtypeStruct((nb, STATE, G), F32),
        ),
        in_specs=[vm] * 4,
        out_specs=[vm] * 5,
        scratch_shapes=[
            pltpu.VMEM((8 + L, 128), F32),
            pltpu.VMEM((L, G + 2 * STATE), F32),
            pltpu.VMEM((L, 128), F32),
            pltpu.VMEM((STATE, G), F32),
        ],
        compiler_params=pltpu.CompilerParams(vmem_limit_bytes=VMEM_LIMIT),
        cost_estimate=pl.CostEstimate(flops=L * G * 1500, bytes_accessed=L * G * 20, transcendentals=L * G * 4),
        name="scan_forward",
    )(proj, cw, hp, gw)

def scan_backward(G, proj_ref, mixed_ref, yp_ref, st_ref, dn_ref, sc_ref, cw_ref, hp_ref, gw_ref,
                  dproj_ref, no_ref, gg_ref, gc_ref, gh_ref,
                  pad, xc, dts, dy, dxc, dstate, ddt):
    L = proj_ref.shape[0]
    nb = L // Q
    mask = lane_mask(Q)
    for tile in range((G + 2 * STATE) // 128):
        pre = conv_tile(proj_ref, cw_ref, pad, G + tile * 128, tile * 128, L)
        xc[:, tile * 128 : tile * 128 + 128] = pre * sigmoid(pre)
    raw, dts[...] = steps(proj_ref, hp_ref, 2 * G + 2 * STATE)
    dstate[...] = jnp.zeros_like(dstate)
    gg_ref[...] = jnp.zeros_like(gg_ref)
    gh_ref[...] = jnp.zeros_like(gh_ref)

    def chunk(step, _):
        c = nb - 1 - step
        at = pl.ds(pl.multiple_of(c * Q, Q), Q)
        sc = jnp.concatenate([sc_ref[c], jnp.zeros((Q - 8, 128), F32)], axis=0).T
        inv2 = jnp.broadcast_to(sc[:, 0:1], (Q, 128))
        mdot = jnp.broadcast_to(sc[:, 1:2], (Q, 128))
        dt = dts[at, :]
        rate, cum, causal = chunk_factors(dt, hp_ref)
        cum_t = cum.T
        last = cum[Q - 1 : Q, :]
        e_cum = jnp.exp(cum)
        tail = jnp.exp(last - cum)
        e_last = jnp.broadcast_to(jnp.exp(last), (8, 128))
        b = xc[at, G : G + STATE].astype(BF)
        cc = xc[at, G + STATE : G + 2 * STATE].astype(BF)
        scores = dot(cc, b, 1, 1)
        scores2 = jnp.concatenate([scores, scores], axis=1)
        d_scores = jnp.zeros((Q, Q), F32)
        d_b = jnp.zeros((Q, STATE), F32)
        d_c = jnp.zeros((Q, STATE), F32)
        d_cum = jnp.zeros((Q, 128), F32)
        d_dt = jnp.zeros((Q, 128), F32)
        d_last = jnp.zeros((8, 128), F32)
        lane_ids = lax.broadcasted_iota(jnp.int32, (Q, 128), 1)
        for p in range(G // 128):
            lanes = slice(p * 128, p * 128 + 128)
            gate = proj_ref[at, lanes].astype(F32)
            sig = sigmoid(gate)
            act = gate * sig
            mixed = mixed_ref[at, lanes].astype(F32)
            n2 = mixed * act * inv2
            no_ref[at, lanes] = (n2 * gw_ref[0:1, lanes]).astype(BF)
            dn = dn_ref[at, lanes]
            gg_ref[0:1, lanes] += jnp.sum(dn * n2, axis=0, keepdims=True)
            d_v = inv2 * (dn * gw_ref[0:1, lanes] - n2 * mdot)
            dyb = (d_v * act).astype(BF)
            dproj_ref[at, lanes] = (d_v * mixed * (sig * (1.0 + gate * (1.0 - sig)))).astype(BF)
            d_y = dyb.astype(F32)
            x = xc[at, lanes]
            dt_x = spread(dt, p, mask)
            u = (x * dt_x).astype(BF)
            u2 = split_pair(u, mask)
            uf = u.astype(F32)
            dec = decay_pair(cum, cum_t, causal, p)
            m = (scores2 * dec).astype(BF)
            dm = dot(dyb, u2, 1, 1) * dec
            d_scores = d_scores + dm[:, :Q] + dm[:, Q:]
            both = dot(m, dyb, 0, 0)
            du = jnp.where(mask, both[:Q], both[Q:])
            tail_x = spread(tail, p, mask)
            before = st_ref[c, :, lanes]
            after = dstate[:, lanes]
            afterb = after.astype(BF)
            du_out = tail_x * dot(b, afterb, 1, 0)
            du = du + du_out
            dye = (d_y * spread(e_cum, p, mask)).astype(BF)
            d_c = d_c + dot(dye, before.astype(BF), 1, 1)
            d_b = d_b + dot((uf * tail_x).astype(BF), afterb, 1, 1)
            e_last_x = spread(e_last, p, mask[0:8])
            dstate[:, lanes] = after * e_last_x[0:1, :] + dot(cc, dye, 0, 0)
            z3 = jnp.sum(uf * du_out, axis=0, keepdims=True) + e_last_x[0:1, :] * jnp.sum(before * after, axis=0, keepdims=True)
            z1 = d_y * yp_ref[at, lanes] - uf * du
            z2 = x * du
            zero = jnp.zeros_like(z1)
            for half, h in ((True, 2 * p), (False, 2 * p + 1)):
                keep = mask if half else jnp.logical_not(mask)
                here = lane_ids == h
                d_cum = jnp.where(here, jnp.sum(jnp.where(keep, z1, zero), axis=1, keepdims=True), d_cum)
                d_dt = jnp.where(here, jnp.sum(jnp.where(keep, z2, zero), axis=1, keepdims=True), d_dt)
                s3 = jnp.sum(jnp.where(keep[0:8], jnp.broadcast_to(z3, (8, 128)), 0.0), axis=1, keepdims=True)
                d_last = jnp.where(here[0:8], s3, d_last)
            dxc[at, lanes] = dt_x * du + gw_ref[1:2, lanes] * d_y
            gg_ref[1:2, lanes] += jnp.sum(d_y * x, axis=0, keepdims=True)
        dsb = d_scores.astype(BF)
        dxc[at, G : G + STATE] = d_b + dot(dsb, cc, 0, 0)
        dxc[at, G + STATE : G + 2 * STATE] = d_c + dot(dsb, b, 1, 0)
        rows = lax.broadcasted_iota(jnp.int32, (Q, Q), 0)
        cols = lax.broadcasted_iota(jnp.int32, (Q, Q), 1)
        upper = (rows <= cols).astype(F32)
        d_rate = dot(upper, d_cum, 1, 0, lax.Precision.HIGHEST) + d_last[0:1, :]
        d_step = d_dt + d_rate * hp_ref[1:2, :]
        raw_c = proj_ref[at, 2 * G + 2 * STATE : 2 * G + 2 * STATE + 128].astype(F32) + hp_ref[0:1, :]
        d_raw = d_step * sigmoid(raw_c)
        dproj_ref[at, 2 * G + 2 * STATE : 2 * G + 2 * STATE + 128] = d_raw.astype(BF)
        gh_ref[0:1, :] += jnp.sum(d_raw, axis=0, keepdims=True)
        gh_ref[1:2, :] += jnp.sum(d_rate * rate, axis=0, keepdims=True)
        return 0

    lax.fori_loop(0, nb, chunk, 0)

    gc_ref[...] = jnp.zeros_like(gc_ref)
    for tile in range((G + 2 * STATE) // 128):
        lanes = slice(tile * 128, tile * 128 + 128)
        pre = conv_tile(proj_ref, cw_ref, pad, G + tile * 128, tile * 128, L)
        sig = sigmoid(pre)
        d_pre = dxc[:, lanes] * (sig * (1.0 + pre * (1.0 - sig)))
        for k in range(KERNEL):
            gc_ref[k : k + 1, lanes] = jnp.sum(d_pre * pad[5 + k : 5 + k + L, :], axis=0, keepdims=True)
        gc_ref[4:5, lanes] = jnp.sum(d_pre, axis=0, keepdims=True)
        pad[0:L, :] = d_pre
        pad[L : L + 8, :] = jnp.zeros((8, 128), F32)
        d_in = cw_ref[3:4, lanes] * d_pre
        for k in range(KERNEL - 1):
            d_in = d_in + cw_ref[k : k + 1, lanes] * pad[3 - k : 3 - k + L, :]
        dproj_ref[:, G + tile * 128 : G + tile * 128 + 128] = d_in.astype(BF)

def scan_bwd_call(proj, mixed, yp, st, dn, sc, cw, hp, gw):
    L, NC = proj.shape
    G = gw.shape[1]
    vm = pl.BlockSpec(memory_space=pltpu.VMEM)
    CX = G + 2 * STATE
    return pl.pallas_call(
        functools.partial(scan_backward, G),
        out_shape=(
            jax.ShapeDtypeStruct((L, NC), BF),
            jax.ShapeDtypeStruct((L, G), BF),
            jax.ShapeDtypeStruct((8, G), F32),
            jax.ShapeDtypeStruct((8, CX), F32),
            jax.ShapeDtypeStruct((8, 128), F32),
        ),
        in_specs=[vm] * 9,
        out_specs=[vm] * 5,
        scratch_shapes=[
            pltpu.VMEM((8 + L, 128), F32),
            pltpu.VMEM((L, CX), F32),
            pltpu.VMEM((L, 128), F32),
            pltpu.VMEM((8, 128), F32),
            pltpu.VMEM((L, CX), F32),
            pltpu.VMEM((STATE, G), F32),
            pltpu.VMEM((8, 128), F32),
        ],
        compiler_params=pltpu.CompilerParams(vmem_limit_bytes=VMEM_LIMIT),
        cost_estimate=pl.CostEstimate(flops=L * G * 4000, bytes_accessed=L * G * 30, transcendentals=L * G * 6),
        name="scan_backward",
    )(proj, mixed, yp, st, dn, sc, cw, hp, gw)


MESH = pl.DeviceIdType.MESH
VM = pl.BlockSpec(memory_space=pltpu.VMEM)
ANY = pl.BlockSpec(memory_space=pl.ANY)
TILE = 16


def meet(axis, n):
    me = lax.axis_index(axis)
    barrier = pltpu.get_barrier_semaphore()
    for k in range(1, n):
        pl.semaphore_signal(
            barrier, inc=1, device_id={axis: lax.rem(me + k, n)}, device_id_type=MESH
        )
    pl.semaphore_wait(barrier, n - 1)


def send(src, dst, sems, at, axis, peer):
    copy = pltpu.make_async_remote_copy(
        src, dst, sems[0].at[at], sems[1].at[at], device_id={axis: peer}, device_id_type=MESH
    )
    copy.start()
    return copy


def column(row):
    return jnp.broadcast_to(row, (128, 128)).T


def sum_parts(n, part_ref, stat_ref, got, got_stat, sems, stat_sems):
    me = lax.axis_index("seq")
    copies = []
    for k in range(1, n):
        peer = lax.rem(me + k, n)
        copies.append(send(part_ref.at[peer], got.at[k - 1], sems, k - 1, "seq", peer))
        if stat_ref is not None:
            copies.append(
                send(stat_ref.at[peer], got_stat.at[k - 1], stat_sems, k - 1, "seq", peer)
            )
    return copies


def gather_rows(n, own, all_ref, own_stat, stat_ref, sems, stat_sems):
    me = lax.axis_index("seq")
    copies = []
    for k in range(1, n):
        peer = lax.rem(me + k, n)
        copies.append(send(own, all_ref.at[me], sems, k - 1, "seq", peer))
        if stat_ref is not None:
            copies.append(send(own_stat, stat_ref.at[me], stat_sems, k - 1, "seq", peer))
    return copies


def rows_loop(rows, body):
    def step(r, carry):
        body(pl.ds(pl.multiple_of(r * TILE, TILE), TILE))
        return carry

    lax.fori_loop(0, rows // TILE, step, 0)


def total_of(n, part_ref, got, at):
    total = part_ref[lax.axis_index("seq"), at, :].astype(F32)
    for k in range(n - 1):
        total = total + got[k, at, :].astype(F32)
    return total


def start_kernel(n, h_ref, gain_ref, all_ref, own, s0, r0):
    rows = h_ref.shape[0]

    def norm(at):
        h = h_ref[at, :]
        inv = lax.rsqrt(jnp.mean(h * h, axis=1, keepdims=True) + EPSILON)
        own[at, :] = (h * inv * gain_ref[0:1, :]).astype(BF)

    rows_loop(rows, norm)
    meet("seq", n)
    copies = gather_rows(n, own, all_ref, None, None, (s0, r0), None)
    all_ref[lax.axis_index("seq")] = own[...]
    for copy in copies:
        copy.wait()


def start_call(h, gain, n):
    rows = h.shape[0]
    return pl.pallas_call(
        functools.partial(start_kernel, n),
        out_shape=jax.ShapeDtypeStruct((n, rows, D), BF),
        in_specs=[VM, VM],
        out_specs=VM,
        scratch_shapes=[
            pltpu.VMEM((rows, D), BF),
            pltpu.SemaphoreType.DMA((n - 1,)),
            pltpu.SemaphoreType.DMA((n - 1,)),
        ],
        compiler_params=pltpu.CompilerParams(
            collective_id=0, has_side_effects=True, vmem_limit_bytes=VMEM_LIMIT
        ),
        name="start",
    )(h, gain)


def forward_turn_kernel(
    n, last, part_ref, ssq_ref, h_ref, next_ref, hout_ref, pout_ref, all_ref, stat_ref,
    got, got_stat, own, own_stat, cols, mdots, s0, r0, s1, r1, s2, r2, s3, r3
):
    me = lax.axis_index("seq")
    rows = h_ref.shape[0]
    meet("seq", n)
    copies = sum_parts(n, part_ref, ssq_ref, got, got_stat, (s0, r0), (s1, r1))
    for copy in copies:
        copy.wait()
    ssq = ssq_ref[me]
    for k in range(n - 1):
        ssq = ssq + got_stat[k]
    inv2 = lax.rsqrt(ssq * (1.0 / INNER) + EPSILON)
    own_stat[...] = inv2
    cols[...] = column(inv2[0:1, :])

    def finish(at):
        pout = total_of(n, part_ref, got, at) * cols[at, 0:1]
        h = h_ref[at, :] + pout
        hout_ref[at, :] = h
        pout_ref[at, :] = pout
        if last:
            out = next_ref[at, :].astype(BF)
            dots = jnp.sum(out.astype(F32) * pout, axis=1, keepdims=True)
            mdots[at, :] = jnp.broadcast_to(dots * (1.0 / INNER), (TILE, 128))
            own[at, :] = out
        else:
            inv = lax.rsqrt(jnp.mean(h * h, axis=1, keepdims=True) + EPSILON)
            own[at, :] = (h * inv * next_ref[0:1, :]).astype(BF)

    rows_loop(rows, finish)
    if last:
        own_stat[1:2, :] = mdots[...].T[0:1, :]
    copies = gather_rows(n, own, all_ref, own_stat, stat_ref, (s2, r2), (s3, r3))
    all_ref[me] = own[...]
    stat_ref[me] = own_stat[...]
    for copy in copies:
        copy.wait()


def forward_turn(part, ssq, h, following, n, last):
    rows = h.shape[0]
    sems = [pltpu.SemaphoreType.DMA((n - 1,))] * 8
    return pl.pallas_call(
        functools.partial(forward_turn_kernel, n, last),
        out_shape=(
            jax.ShapeDtypeStruct((rows, D), F32),
            jax.ShapeDtypeStruct((rows, D), F32),
            jax.ShapeDtypeStruct((n, rows, D), BF),
            jax.ShapeDtypeStruct((n, 8, 128), F32),
        ),
        in_specs=[VM] * 4,
        out_specs=[VM] * 4,
        scratch_shapes=[
            pltpu.VMEM((n - 1, rows, D), BF),
            pltpu.VMEM((n - 1, 8, 128), F32),
            pltpu.VMEM((rows, D), BF),
            pltpu.VMEM((8, 128), F32),
            pltpu.VMEM((rows, 128), F32),
            pltpu.VMEM((rows, 128), F32),
        ]
        + sems,
        compiler_params=pltpu.CompilerParams(
            collective_id=2 if last else 1, has_side_effects=True, vmem_limit_bytes=VMEM_LIMIT
        ),
        name="forward_end" if last else "forward_turn",
    )(part, ssq, h, following)


def backward_turn_kernel(n, last, *refs):
    if last:
        part_ref, h_ref, og_ref, gain_ref, dh_ref, gn_ref, got, s0, r0 = refs
    else:
        (part_ref, h_ref, og_ref, gain_ref, pout_ref, low_ref, dh_ref, gn_ref, all_ref, stat_ref,
         got, own, own_stat, mdots, s0, r0, s2, r2, s3, r3) = refs
    me = lax.axis_index("seq")
    rows = h_ref.shape[0]
    meet("seq", n)
    for copy in sum_parts(n, part_ref, None, got, None, (s0, r0), None):
        copy.wait()
    gn_ref[...] = jnp.zeros_like(gn_ref)

    def finish(at):
        d_in = total_of(n, part_ref, got, at)
        h = h_ref[at, :]
        inv = lax.rsqrt(jnp.mean(h * h, axis=1, keepdims=True) + EPSILON)
        normed = h * inv
        gn_ref[0:1, :] += jnp.sum(d_in * normed, axis=0, keepdims=True)
        d_s = d_in * gain_ref[0:1, :]
        d_h = og_ref[at, :] + inv * (d_s - normed * jnp.mean(d_s * normed, axis=1, keepdims=True))
        dh_ref[at, :] = d_h
        if not last:
            out = d_h.astype(BF)
            own[at, :] = out
            dots = jnp.sum(out.astype(F32) * pout_ref[at, :], axis=1, keepdims=True)
            mdots[at, :] = jnp.broadcast_to(dots * (1.0 / INNER), (TILE, 128))

    rows_loop(rows, finish)
    if last:
        return
    own_stat[...] = low_ref[...]
    own_stat[1:2, :] = mdots[...].T[0:1, :]
    copies = gather_rows(n, own, all_ref, own_stat, stat_ref, (s2, r2), (s3, r3))
    all_ref[me] = own[...]
    stat_ref[me] = own_stat[...]
    for copy in copies:
        copy.wait()


def backward_turn(part, h, out_grad, gain, below, n):
    rows = h.shape[0]
    last = below is None
    sem = pltpu.SemaphoreType.DMA((n - 1,))
    outs = [jax.ShapeDtypeStruct((rows, D), F32), jax.ShapeDtypeStruct((8, D), F32)]
    scratch = [pltpu.VMEM((n - 1, rows, D), BF)]
    if not last:
        outs += [
            jax.ShapeDtypeStruct((n, rows, D), BF),
            jax.ShapeDtypeStruct((n, 8, 128), F32),
        ]
        scratch += [
            pltpu.VMEM((rows, D), BF),
            pltpu.VMEM((8, 128), F32),
            pltpu.VMEM((rows, 128), F32),
        ]
    args = (part, h, out_grad, gain) + (() if last else below)
    return pl.pallas_call(
        functools.partial(backward_turn_kernel, n, last),
        out_shape=outs,
        in_specs=[VM] * len(args),
        out_specs=[VM] * len(outs),
        scratch_shapes=scratch + [sem] * (2 if last else 6),
        compiler_params=pltpu.CompilerParams(
            collective_id=4 if last else 3, has_side_effects=True, vmem_limit_bytes=VMEM_LIMIT
        ),
        name="backward_end" if last else "backward_turn",
    )(*args)


def backward_tail_kernel(n, G, *refs):
    ins, outs, scratch = refs[:13], refs[13:20], refs[20:]
    proj, mixed, yp, st, dn, sc, cw, hp, gw, win_ref, h_ref, og_ref, gain_ref = ins
    dproj_ref, no_ref, gg_ref, gc_ref, gh_ref, dh_ref, gn_ref = outs
    part_ref, got, s0, r0 = scratch[7:]
    meet("seq", n)
    scan_backward(
        G, proj, mixed, yp, st, dn, sc, cw, hp, gw, dproj_ref, no_ref, gg_ref, gc_ref, gh_ref,
        *scratch[:7]
    )
    me = lax.axis_index("seq")
    rows = h_ref.shape[0]

    def product(block):
        at = pl.ds(pl.multiple_of(block * rows, rows), rows)

        def tile(t, carry):
            lanes = pl.ds(pl.multiple_of(t * 256, 256), 256)
            part_ref[block, :, lanes] = dot(dproj_ref[at, :], win_ref[lanes, :], 1, 1).astype(BF)
            return carry

        lax.fori_loop(0, D // 256, tile, 0)

    copies = []
    for k in range(1, n):
        peer = lax.rem(me + k, n)
        product(peer)
        copies.append(send(part_ref.at[peer], got.at[k - 1], (s0, r0), k - 1, "seq", peer))
    product(me)
    for copy in copies:
        copy.wait()
    gn_ref[...] = jnp.zeros_like(gn_ref)

    def finish(at):
        d_in = total_of(n, part_ref, got, at)
        h = h_ref[at, :]
        inv = lax.rsqrt(jnp.mean(h * h, axis=1, keepdims=True) + EPSILON)
        normed = h * inv
        gn_ref[0:1, :] += jnp.sum(d_in * normed, axis=0, keepdims=True)
        d_s = d_in * gain_ref[0:1, :]
        dh_ref[at, :] = og_ref[at, :] + inv * (
            d_s - normed * jnp.mean(d_s * normed, axis=1, keepdims=True)
        )

    rows_loop(rows, finish)


def backward_tail(proj, mixed, yp, st, dn, sc, cw, hp, gw, win, h, out_grad, gain, n):
    L, NC = proj.shape
    G = gw.shape[1]
    CX = G + 2 * STATE
    rows = h.shape[0]
    args = (proj, mixed, yp, st, dn, sc, cw, hp, gw, win, h, out_grad, gain)
    return pl.pallas_call(
        functools.partial(backward_tail_kernel, n, G),
        out_shape=(
            jax.ShapeDtypeStruct((L, NC), BF),
            jax.ShapeDtypeStruct((L, G), BF),
            jax.ShapeDtypeStruct((8, G), F32),
            jax.ShapeDtypeStruct((8, CX), F32),
            jax.ShapeDtypeStruct((8, 128), F32),
            jax.ShapeDtypeStruct((rows, D), F32),
            jax.ShapeDtypeStruct((8, D), F32),
        ),
        in_specs=[VM] * len(args),
        out_specs=[VM] * 7,
        scratch_shapes=[
            pltpu.VMEM((8 + L, 128), F32),
            pltpu.VMEM((L, CX), F32),
            pltpu.VMEM((L, 128), F32),
            pltpu.VMEM((8, 128), F32),
            pltpu.VMEM((L, CX), F32),
            pltpu.VMEM((STATE, G), F32),
            pltpu.VMEM((8, 128), F32),
            pltpu.VMEM((n, rows, D), BF),
            pltpu.VMEM((n - 1, rows, D), BF),
            pltpu.SemaphoreType.DMA((n - 1,)),
            pltpu.SemaphoreType.DMA((n - 1,)),
        ],
        compiler_params=pltpu.CompilerParams(
            collective_id=4, has_side_effects=True, vmem_limit_bytes=VMEM_LIMIT
        ),
        name="backward_tail",
    )(*args)


def swap_kernel(axis, n, scatter, *refs):
    count = (len(refs) - 3) // 2
    sources, targets, (s0, r0, l0) = refs[:count], refs[count : 2 * count], refs[2 * count :]
    me = lax.axis_index(axis)
    meet(axis, n)
    copies = []
    for a in range(count):
        for k in range(1, n):
            peer = lax.rem(me + k, n)
            source = sources[a].at[peer] if scatter else sources[a]
            copies.append(
                send(source, targets[a].at[me], (s0, r0), a * (n - 1) + k - 1, axis, peer)
            )
        mine = sources[a].at[me] if scatter else sources[a]
        local_copy = pltpu.make_async_copy(mine, targets[a].at[me], l0.at[a])
        local_copy.start()
        copies.append(local_copy)
    for copy in copies:
        copy.wait()


def swap(arrays, axis, n, scatter, cid):
    count = len(arrays)
    return pl.pallas_call(
        functools.partial(swap_kernel, axis, n, scatter),
        out_shape=[
            jax.ShapeDtypeStruct(a.shape if scatter else (n,) + a.shape, a.dtype) for a in arrays
        ],
        in_specs=[ANY] * count,
        out_specs=[ANY] * count,
        scratch_shapes=[
            pltpu.SemaphoreType.DMA((count * (n - 1),)),
            pltpu.SemaphoreType.DMA((count * (n - 1),)),
            pltpu.SemaphoreType.DMA((count,)),
        ],
        compiler_params=pltpu.CompilerParams(
            collective_id=cid, has_side_effects=True, vmem_limit_bytes=VMEM_LIMIT
        ),
        name=f"swap_{axis}_{cid}",
    )(*arrays)


def padded(array, size):
    return jnp.pad(array, ((0, 0), (0, size - array.shape[1])))


class Group:
    def __init__(self, n_seq, n_wt):
        self.n_seq, self.n_wt = n_seq, n_wt
        self.heads = HEADS // n_seq
        self.runs = n_wt if HEADS % (n_seq * n_wt) == 0 else 1
        self.run_heads = self.heads // self.runs
        self.chans = self.heads * HEAD_DIM
        self.G = -(-self.chans // 128) * 128
        self.CX = self.G + 2 * STATE
        self.NC = 2 * self.G + 2 * STATE + 128

    def take(self, array, first, width):
        at = lax.axis_index("seq") * self.run_heads * width
        stride = HEADS // self.runs * width
        return [
            lax.dynamic_slice_in_dim(array, first + r * stride + at, self.run_heads * width, 1)
            for r in range(self.runs)
        ]

    def place(self, arrays, width):
        run = self.run_heads * width
        return [
            arrays[g][..., r * run : (r + 1) * run]
            for r in range(self.runs)
            for g in range(self.n_seq)
        ]

    def weight(self, w):
        gate = padded(jnp.concatenate(self.take(w, 0, HEAD_DIM), 1), self.G)
        x = padded(jnp.concatenate(self.take(w, INNER, HEAD_DIM), 1), self.G)
        bc = w[:, 2 * INNER : 2 * INNER + 2 * STATE]
        dt = padded(jnp.concatenate(self.take(w, 2 * INNER + 2 * STATE, 1), 1), 128)
        return jnp.concatenate([gate, x, bc, dt], 1)

    def small(self, norm_gain, conv_w, conv_b, dt_bias, a_log, skip_d, gate_gain):
        conv = jnp.concatenate([conv_w, conv_b[None], jnp.zeros((3, CONV), F32)], 0)
        conv_x = padded(jnp.concatenate(self.take(conv, 0, HEAD_DIM), 1), self.G)
        zero = jnp.zeros((6, HEADS), F32)
        head = jnp.concatenate([dt_bias[None], -jnp.exp(a_log)[None], zero], 0)
        head = padded(jnp.concatenate(self.take(head, 0, 1), 1), 128)
        wide = jnp.concatenate(
            [gate_gain[None], jnp.repeat(skip_d, HEAD_DIM)[None], jnp.zeros((6, INNER), F32)], 0
        )
        wide = padded(jnp.concatenate(self.take(wide, 0, HEAD_DIM), 1), self.G)
        gain = jnp.broadcast_to(norm_gain[None], (8, D))
        return jnp.concatenate([conv_x, conv[:, INNER:], head, wide, gain], 1)

    def parts(self, packed):
        cuts = [0, self.CX, self.CX + 128, self.CX + 128 + self.G, self.CX + 128 + self.G + D]
        return [packed[..., a:b] for a, b in zip(cuts, cuts[1:])]


def local(
    tokens, cotangent, norm_gain, w_in, conv_w, conv_b, dt_bias, a_log, skip_d, gate_gain, w_out
):
    n_seq, n_wt = lax.axis_size("seq"), lax.axis_size("wt")
    core = lax.axis_index("section")
    here = lax.axis_index("seq")
    group = Group(n_seq, n_wt)
    G, rows = group.G, tokens.shape[2]
    length = rows * n_seq

    both = ("section", "wt")
    win = lax.all_gather(group.weight(w_in[0]), both, axis=0, tiled=False)
    win = win.reshape(2, D, group.NC)
    if group.runs == n_wt:
        part = group.chans // n_wt
        piece = lax.dynamic_slice_in_dim(w_out[0], here * part, part, 0)
        wout = lax.all_gather(piece, both, axis=0, tiled=False).reshape(2, group.chans, D)
    else:
        wout = lax.all_gather(w_out[0], both, axis=0, tiled=False).reshape(2, INNER, D)
        wout = lax.dynamic_slice_in_dim(wout, here * group.chans, group.chans, 1)
    wout = jnp.pad(wout, ((0, 0), (0, G - group.chans), (0, 0)))
    packed = group.small(
        norm_gain[0], conv_w[0], conv_b[0], dt_bias[0], a_log[0], skip_d[0], gate_gain[0]
    )
    packed = lax.all_gather(packed, "section", axis=0, tiled=False)
    params = [group.parts(packed[s]) for s in range(2)]

    h0 = lax.dynamic_index_in_dim(tokens, core, 0, keepdims=False)[0]
    last_grad = lax.dynamic_index_in_dim(cotangent, core, 0, keepdims=False)[0]

    def forward(s, normed):
        conv, head, wide, _ = params[s]
        proj = jnp.dot(normed, win[s], preferred_element_type=F32).astype(BF)
        vg, ssq, mixed, yp, states = scan_fwd_call(proj, conv, head, wide)
        part = jnp.dot(vg, wout[s], preferred_element_type=F32).astype(BF)
        return part.reshape(n_seq, rows, D), ssq, (proj, mixed, yp, states)

    def backward(s, normed, kept, grad_b, stats):
        conv, head, wide, _ = params[s]
        proj, mixed, yp, states = kept
        d_normed = dot(grad_b, wout[s], 1, 1)
        d_proj, normed_out, g_wide, g_conv, g_head = scan_bwd_call(
            proj, mixed, yp, states, d_normed, stats, conv, head, wide
        )
        part = dot(d_proj, win[s], 1, 1).astype(BF).reshape(n_seq, rows, D)
        g_out = dot(normed_out, grad_b, 0, 0).astype(BF)
        g_in = dot(normed, d_proj, 0, 0).astype(BF)
        return part, g_in, g_out, (g_conv, g_head, g_wide)

    n0 = start_call(h0, params[0][3], n_seq)
    n0 = n0.reshape(length, D)
    part, ssq, kept0 = forward(0, n0)
    h1, pout0, n1, stat0 = forward_turn(part, ssq, h0, params[1][3], n_seq, False)
    n1 = n1.reshape(length, D)
    part, ssq, kept1 = forward(1, n1)
    h2, pout1, grad_b, stats = forward_turn(part, ssq, h1, last_grad, n_seq, True)
    part, gin1, gout1, small1 = backward(1, n1, kept1, grad_b.reshape(length, D), stats)
    low = lax.dynamic_index_in_dim(stat0, here, 0, keepdims=False)
    d1, gnorm1, grad_b, stats = backward_turn(
        part, h1, last_grad, params[1][3], (pout0, low), n_seq
    )
    grad_b = grad_b.reshape(length, D)
    conv, head, wide, _ = params[0]
    d_proj, normed_out, g_wide, g_conv, g_head, d0, gnorm0 = backward_tail(
        *kept0, dot(grad_b, wout[0], 1, 1), stats, conv, head, wide, win[0], h0, d1,
        params[0][3], n_seq
    )
    gout0 = dot(normed_out, grad_b, 0, 0).astype(BF)
    gin0 = dot(n0, d_proj, 0, 0).astype(BF)
    small0 = (g_conv, g_head, g_wide)

    def to_layer(low_val, top_val):
        own = jnp.where(core == 0, low_val, top_val)
        other = jnp.where(core == 0, top_val, low_val)
        return own, lax.ppermute(other, "section", [(0, 1), (1, 0)])

    own, other = to_layer(gin0, gin1)
    gin = (own.astype(F32) + other.astype(F32)).astype(BF).reshape(n_wt, D // n_wt, group.NC)
    own, other = to_layer(gout0, gout1)
    gout = (own.astype(F32) + other.astype(F32)).astype(BF)
    if group.runs == n_wt:
        gout = gout.reshape(n_wt, G // n_wt, D)
        gin, gout = swap([gin, gout], "wt", n_wt, True, 5)
        gin = jnp.sum(gin.astype(F32), 0).astype(BF)
        gout = jnp.sum(gout.astype(F32), 0).astype(BF)
        gin, gout = swap([gin, gout], "seq", n_seq, False, 6)
        g_out = gout.reshape(INNER // n_wt, D).astype(F32)
    else:
        [gin] = swap([gin], "wt", n_wt, True, 5)
        gin = jnp.sum(gin.astype(F32), 0).astype(BF)
        gout = lax.psum(gout[: group.chans], "wt")
        gin, gout = swap([gin, gout], "seq", n_seq, False, 6)
        mine = INNER // n_wt
        gout = gout.reshape(INNER, D)
        g_out = lax.dynamic_slice_in_dim(gout, lax.axis_index("wt") * mine, mine, 0).astype(F32)
    shards = [gin[g] for g in range(n_seq)]
    shared = jnp.sum(gin[:, :, 2 * G : 2 * G + 2 * STATE].astype(F32), 0)
    g_in = jnp.concatenate(
        [a.astype(F32) for a in group.place([s[:, :G] for s in shards], HEAD_DIM)]
        + [a.astype(F32) for a in group.place([s[:, G : 2 * G] for s in shards], HEAD_DIM)]
        + [shared]
        + [a.astype(F32) for a in group.place([s[:, 2 * G + 2 * STATE :] for s in shards], 1)],
        axis=1,
    )

    packs = jnp.stack(
        [
            jnp.concatenate([*small0, gnorm0], 1),
            jnp.concatenate([*small1, gnorm1], 1),
        ]
    )
    packs = lax.psum(packs, ("section", "wt"))
    packs = lax.dynamic_index_in_dim(packs, core, 0, keepdims=False)
    packs = lax.all_gather(packs, "seq", axis=0, tiled=False)
    conv, head, wide, norm = group.parts(packs)
    conv_all = jnp.concatenate(
        group.place([conv[g, :, : group.chans] for g in range(n_seq)], HEAD_DIM)
        + [jnp.sum(conv[:, :, G:], 0)],
        axis=1,
    )
    head_all = jnp.concatenate(group.place([head[g] for g in range(n_seq)], 1), 1)
    wide_all = jnp.concatenate(
        group.place([wide[g, :, : group.chans] for g in range(n_seq)], HEAD_DIM), 1
    )
    g_skip = jnp.sum(wide_all[1].reshape(HEADS, HEAD_DIM), 1)

    own, other = to_layer(h1, h2)
    section_out = jnp.where(core == 0, jnp.stack([own, other]), jnp.stack([other, own]))
    own, other = to_layer(d0, d1)
    input_grad = jnp.where(core == 0, jnp.stack([own, other]), jnp.stack([other, own]))
    return (
        section_out[None, :, None],
        input_grad[None, :, None],
        jnp.sum(norm[:, 0], 0)[None],
        g_in[None],
        conv_all[None, :KERNEL],
        conv_all[None, KERNEL],
        head_all[None, 0],
        head_all[None, 1],
        g_skip[None],
        wide_all[None, 0],
        g_out[None],
    )


def solution(mesh):
    placed = (
        P(None, "wt", "seq", None),
        P(None, "wt", "seq", None),
        P("section", None),
        P("section", "wt", None),
        P("section", None, None),
        P("section", None),
        P("section", None),
        P("section", None),
        P("section", None),
        P("section", None),
        P("section", "wt", None),
    )
    return jax.shard_map(
        local,
        mesh=mesh,
        in_specs=placed,
        out_specs=(
            P("section", None, "wt", "seq", None),
            P("section", None, "wt", "seq", None),
            P("section", None),
            P("section", "wt", None),
            P("section", None, None),
            P("section", None),
            P("section", None),
            P("section", None),
            P("section", None),
            P("section", None),
            P("section", "wt", None),
        ),
        check_vma=False,
    )
```

```python
import functools
from typing import Any, NamedTuple

import jax
import jax.numpy as jnp
from jax import lax
from jax.experimental import pallas as pl
from jax.experimental.pallas import tpu as pltpu
from jax.sharding import PartitionSpec as P

D = 1536
HEADS = 48
HEAD_DIM = 64
STATE = 128
KERNEL = 4
INNER = 3072
CONV = 3328
EPSILON = 1e-05

Q = 128
F32 = jnp.float32
BF = jnp.bfloat16
SEQ, WT, SECTION = "seq", "wt", "section"
FORWARD_VMEM = 56 * 2**20
BACKWARD_VMEM = 60 * 2**20
SMALL_VMEM = 40 * 2**20
MESH = pl.DeviceIdType.MESH
VM = pl.BlockSpec(memory_space=pltpu.VMEM)
ANY = pl.BlockSpec(memory_space=pl.ANY)
TILE = 16


def dot(a, b, ca, cb, precision=None):
    return lax.dot_general(a, b, (((ca,), (cb,)), ((), ())), precision=precision, preferred_element_type=F32)

def sigmoid(x):
    return 1.0 / (1.0 + jnp.exp(-x))

def softplus(x):
    return jnp.maximum(x, 0.0) + jnp.log1p(jnp.exp(-jnp.abs(x)))

def lane_mask(rows):
    return lax.broadcasted_iota(jnp.int32, (rows, 128), 1) < HEAD_DIM

def spread(cols, pair, mask):
    a = jnp.broadcast_to(cols[:, 2 * pair : 2 * pair + 1], mask.shape)
    b = jnp.broadcast_to(cols[:, 2 * pair + 1 : 2 * pair + 2], mask.shape)
    return jnp.where(mask, a, b)

def split_pair(u, mask):
    zero = jnp.zeros_like(u)
    return jnp.concatenate([jnp.where(mask, u, zero), jnp.where(mask, zero, u)], axis=0)

def conv_tile(proj_ref, cw_ref, pad, proj_at, conv_at, rows):
    pad[0:8, :] = jnp.zeros((8, 128), F32)
    pad[8 : 8 + rows, :] = proj_ref[:, pl.ds(proj_at, 128)].astype(F32)
    pre = jnp.broadcast_to(cw_ref[4:5, pl.ds(conv_at, 128)], (rows, 128))
    for k in range(KERNEL):
        pre = pre + cw_ref[k : k + 1, pl.ds(conv_at, 128)] * pad[5 + k : 5 + k + rows, :]
    return pre

def step_inputs(proj_ref, at, hp_ref, sel_ref, dt_at):
    return dot(proj_ref[at, dt_at : dt_at + 128], sel_ref[...], 1, 0) + hp_ref[0:1, :]

def chunk_factors(dt, hp_ref):
    rate = dt * hp_ref[1:2, :]
    rows = lax.broadcasted_iota(jnp.int32, (Q, Q), 0)
    cols = lax.broadcasted_iota(jnp.int32, (Q, Q), 1)
    tri = (rows >= cols).astype(F32)
    cum = dot(tri, rate, 1, 0, lax.Precision.HIGHEST)
    return rate, cum, rows >= cols

def decay_pair(cum, cum_t, causal, pair):
    parts = []
    for h in (2 * pair, 2 * pair + 1):
        diff = jnp.broadcast_to(cum[:, h : h + 1], (Q, Q)) - jnp.broadcast_to(cum_t[h : h + 1, :], (Q, Q))
        parts.append(jnp.exp(jnp.where(causal, diff, -1e30)))
    return jnp.concatenate(parts, axis=1)

def scan_forward(G, proj_ref, cw_ref, hp_ref, gw_ref, sel_ref, mixed_ref, yp_ref, st_ref, pad, xc, dts, state):
    L = proj_ref.shape[0]

    def conv(tile, carry):
        lanes = pl.ds(pl.multiple_of(tile * 128, 128), 128)
        pre = conv_tile(proj_ref, cw_ref, pad, pl.multiple_of(G + tile * 128, 128), lanes.start, L)
        xc[:, lanes] = pre * sigmoid(pre)
        return carry

    lax.fori_loop(0, (G + 2 * STATE) // 128, conv, 0)
    dt_at = 2 * G + 2 * STATE
    dts[...] = softplus(step_inputs(proj_ref, slice(0, L), hp_ref, sel_ref, dt_at))
    state[...] = jnp.zeros_like(state)
    mask = lane_mask(Q)

    def chunk(c, _):
        at = pl.ds(pl.multiple_of(c * Q, Q), Q)
        dt = dts[at, :]
        rate, cum, causal = chunk_factors(dt, hp_ref)
        cum_t = cum.T
        last = cum[Q - 1 : Q, :]
        e_cum = jnp.exp(cum)
        tail = jnp.exp(last - cum) * dt
        e_last = jnp.broadcast_to(jnp.exp(last), (8, 128))
        b = xc[at, G : G + STATE].astype(BF)
        cc = xc[at, G + STATE : G + 2 * STATE].astype(BF)
        scores = dot(cc, b, 1, 1)
        scores2 = jnp.concatenate([scores, scores], axis=1)
        for p in range(G // 128):
            lanes = slice(p * 128, p * 128 + 128)
            x = xc[at, lanes]
            u = (x * spread(dt, p, mask)).astype(BF)
            m = (scores2 * decay_pair(cum, cum_t, causal, p)).astype(BF)
            before = state[:, lanes]
            st_ref[c, :, lanes] = before
            y = dot(m, split_pair(u, mask), 1, 0)
            y = y + dot(cc, before.astype(BF), 1, 0) * spread(e_cum, p, mask)
            yp_ref[at, lanes] = y
            after = dot(b, (x * spread(tail, p, mask)).astype(BF), 0, 0)
            state[:, lanes] = before * spread(e_last, p, mask[0:8])[0:1, :] + after
            mixed_ref[at, lanes] = (y + gw_ref[1:2, lanes] * x).astype(BF)
        return 0

    lax.fori_loop(0, L // Q, chunk, 0)


def gate_forward(G, proj_ref, gw_ref, mixed_ref, vg_ref, ssq_ref):
    def chunk(c, _):
        at = pl.ds(pl.multiple_of(c * Q, Q), Q)
        ssq = jnp.zeros((Q, 1), F32)
        for p in range(G // 128):
            lanes = slice(p * 128, p * 128 + 128)
            gate = proj_ref[at, lanes].astype(F32)
            v = mixed_ref[at, lanes].astype(F32) * (gate * sigmoid(gate))
            vg_ref[at, lanes] = (v * gw_ref[0:1, lanes]).astype(BF)
            ssq = ssq + jnp.sum(v * v, axis=1, keepdims=True)
        ssq_ref[c] = jnp.broadcast_to(ssq, (Q, 128)).T[0:8, :]
        return 0

    lax.fori_loop(0, proj_ref.shape[0] // Q, chunk, 0)


def gate_backward(G, proj_ref, mixed_ref, dn_ref, sc_ref, gw_ref, dy_ref, gg_ref):
    gg_ref[...] = jnp.zeros_like(gg_ref)

    def chunk(c, _):
        at = pl.ds(pl.multiple_of(c * Q, Q), Q)
        sc = jnp.concatenate([sc_ref[c], jnp.zeros((Q - 8, 128), F32)], axis=0).T
        inv2 = jnp.broadcast_to(sc[:, 0:1], (Q, 128))
        mdot = jnp.broadcast_to(sc[:, 1:2], (Q, 128))
        for p in range(G // 128):
            lanes = slice(p * 128, p * 128 + 128)
            gate = proj_ref[at, lanes].astype(F32)
            sig = sigmoid(gate)
            act = gate * sig
            mixed = mixed_ref[at, lanes].astype(F32)
            n2 = mixed * act * inv2
            mixed_ref[at, lanes] = (n2 * gw_ref[0:1, lanes]).astype(BF)
            dn = dn_ref[at, lanes]
            gg_ref[0:1, lanes] += jnp.sum(dn * n2, axis=0, keepdims=True)
            d_v = inv2 * (dn * gw_ref[0:1, lanes] - n2 * mdot)
            dy_ref[at, lanes] = (d_v * act).astype(BF)
            proj_ref[at, lanes] = (d_v * mixed * (sig * (1.0 + gate * (1.0 - sig)))).astype(BF)
        return 0

    lax.fori_loop(0, proj_ref.shape[0] // Q, chunk, 0)


def scan_backward(G, proj_ref, dy_ref, yp_ref, st_ref, cw_ref, hp_ref, gw_ref, sel_ref, gg_ref, gc_ref, gh_ref,
                  pad, xc, dts, dstate):
    L = proj_ref.shape[0]
    nb = L // Q
    mask = lane_mask(Q)

    def conv(tile, carry):
        lanes = pl.ds(pl.multiple_of(tile * 128, 128), 128)
        pre = conv_tile(proj_ref, cw_ref, pad, pl.multiple_of(G + tile * 128, 128), lanes.start, L)
        xc[:, lanes] = pre * sigmoid(pre)
        return carry

    lax.fori_loop(0, (G + 2 * STATE) // 128, conv, 0)
    dt_at = 2 * G + 2 * STATE
    dts[...] = softplus(step_inputs(proj_ref, slice(0, L), hp_ref, sel_ref, dt_at))
    dstate[...] = jnp.zeros_like(dstate)
    gh_ref[...] = jnp.zeros_like(gh_ref)

    def chunk(step, _):
        c = nb - 1 - step
        at = pl.ds(pl.multiple_of(c * Q, Q), Q)
        dt = dts[at, :]
        rate, cum, causal = chunk_factors(dt, hp_ref)
        cum_t = cum.T
        last = cum[Q - 1 : Q, :]
        e_cum = jnp.exp(cum)
        tail = jnp.exp(last - cum)
        e_last = jnp.broadcast_to(jnp.exp(last), (8, 128))
        b = xc[at, G : G + STATE].astype(BF)
        cc = xc[at, G + STATE : G + 2 * STATE].astype(BF)
        scores = dot(cc, b, 1, 1)
        scores2 = jnp.concatenate([scores, scores], axis=1)
        d_scores = jnp.zeros((Q, Q), F32)
        d_b = jnp.zeros((Q, STATE), F32)
        d_c = jnp.zeros((Q, STATE), F32)
        d_cum = jnp.zeros((Q, 128), F32)
        d_dt = jnp.zeros((Q, 128), F32)
        d_last = jnp.zeros((8, 128), F32)
        lane_ids = lax.broadcasted_iota(jnp.int32, (Q, 128), 1)
        for p in range(G // 128):
            lanes = slice(p * 128, p * 128 + 128)
            dyb = dy_ref[at, lanes]
            d_y = dyb.astype(F32)
            x = xc[at, lanes]
            dt_x = spread(dt, p, mask)
            u = (x * dt_x).astype(BF)
            u2 = split_pair(u, mask)
            uf = u.astype(F32)
            dec = decay_pair(cum, cum_t, causal, p)
            m = (scores2 * dec).astype(BF)
            dm = dot(dyb, u2, 1, 1) * dec
            d_scores = d_scores + dm[:, :Q] + dm[:, Q:]
            both = dot(m, dyb, 0, 0)
            du = jnp.where(mask, both[:Q], both[Q:])
            tail_x = spread(tail, p, mask)
            before = st_ref[c, :, lanes]
            after = dstate[:, lanes]
            afterb = after.astype(BF)
            du_out = tail_x * dot(b, afterb, 1, 0)
            du = du + du_out
            dye = (d_y * spread(e_cum, p, mask)).astype(BF)
            d_c = d_c + dot(dye, before.astype(BF), 1, 1)
            d_b = d_b + dot((uf * tail_x).astype(BF), afterb, 1, 1)
            e_last_x = spread(e_last, p, mask[0:8])
            dstate[:, lanes] = after * e_last_x[0:1, :] + dot(cc, dye, 0, 0)
            z3 = jnp.sum(uf * du_out, axis=0, keepdims=True) + e_last_x[0:1, :] * jnp.sum(before * after, axis=0, keepdims=True)
            z1 = d_y * yp_ref[at, lanes] - uf * du
            z2 = x * du
            zero = jnp.zeros_like(z1)
            for half, h in ((True, 2 * p), (False, 2 * p + 1)):
                keep = mask if half else jnp.logical_not(mask)
                here = lane_ids == h
                d_cum = jnp.where(here, jnp.sum(jnp.where(keep, z1, zero), axis=1, keepdims=True), d_cum)
                d_dt = jnp.where(here, jnp.sum(jnp.where(keep, z2, zero), axis=1, keepdims=True), d_dt)
                s3 = jnp.sum(jnp.where(keep[0:8], jnp.broadcast_to(z3, (8, 128)), 0.0), axis=1, keepdims=True)
                d_last = jnp.where(here[0:8], s3, d_last)
            xc[at, lanes] = dt_x * du + gw_ref[1:2, lanes] * d_y
            gg_ref[1:2, lanes] += jnp.sum(d_y * x, axis=0, keepdims=True)
        dsb = d_scores.astype(BF)
        xc[at, G : G + STATE] = d_b + dot(dsb, cc, 0, 0)
        xc[at, G + STATE : G + 2 * STATE] = d_c + dot(dsb, b, 1, 0)
        rows = lax.broadcasted_iota(jnp.int32, (Q, Q), 0)
        cols = lax.broadcasted_iota(jnp.int32, (Q, Q), 1)
        upper = (rows <= cols).astype(F32)
        d_rate = dot(upper, d_cum, 1, 0, lax.Precision.HIGHEST) + d_last[0:1, :]
        d_step = d_dt + d_rate * hp_ref[1:2, :]
        d_raw = d_step * sigmoid(step_inputs(proj_ref, at, hp_ref, sel_ref, dt_at))
        proj_ref[at, dt_at : dt_at + 128] = dot(d_raw.astype(BF), sel_ref[...], 1, 1).astype(BF)
        gh_ref[0:1, :] += jnp.sum(d_raw, axis=0, keepdims=True)
        gh_ref[1:2, :] += jnp.sum(d_rate * rate, axis=0, keepdims=True)
        return 0

    lax.fori_loop(0, nb, chunk, 0)

    gc_ref[...] = jnp.zeros_like(gc_ref)

    def conv_back(tile, carry):
        lanes = pl.ds(pl.multiple_of(tile * 128, 128), 128)
        proj_at = pl.multiple_of(G + tile * 128, 128)
        pre = conv_tile(proj_ref, cw_ref, pad, proj_at, lanes.start, L)
        sig = sigmoid(pre)
        d_pre = xc[:, lanes] * (sig * (1.0 + pre * (1.0 - sig)))
        for k in range(KERNEL):
            gc_ref[k : k + 1, lanes] = jnp.sum(d_pre * pad[5 + k : 5 + k + L, :], axis=0, keepdims=True)
        gc_ref[4:5, lanes] = jnp.sum(d_pre, axis=0, keepdims=True)
        pad[0:L, :] = d_pre
        pad[L : L + 8, :] = jnp.zeros((8, 128), F32)
        d_in = cw_ref[3:4, lanes] * d_pre
        for k in range(KERNEL - 1):
            d_in = d_in + cw_ref[k : k + 1, lanes] * pad[3 - k : 3 - k + L, :]
        proj_ref[:, pl.ds(proj_at, 128)] = d_in.astype(BF)
        return carry

    lax.fori_loop(0, (G + 2 * STATE) // 128, conv_back, 0)


def column(row):
    return jnp.broadcast_to(row, (128, 128)).T


def rows_loop(rows, body):
    def step(r, carry):
        body(pl.ds(pl.multiple_of(r * TILE, TILE), TILE))
        return carry

    lax.fori_loop(0, rows // TILE, step, 0)


def total_of(n, part_ref, got, at):
    total = part_ref[lax.axis_index(SEQ), at, :].astype(F32)
    for k in range(n - 1):
        total = total + got[k, at, :].astype(F32)
    return total


class Group:
    def __init__(self, n_seq, n_wt):
        self.n_seq = n_seq
        self.heads = HEADS // n_seq
        self.runs = n_wt if HEADS % (n_seq * n_wt) == 0 else 1
        self.run_heads = self.heads // self.runs
        self.chans = self.heads * HEAD_DIM
        self.G = -(-self.chans // 128) * 128
        self.CX = self.G + 2 * STATE
        self.NC = 2 * self.G + 2 * STATE + 128
        self.rest = self.G + 2 * STATE + 64
        self.half = (self.G + self.rest) // 2


def head_of(g, here, local_head):
    stride = HEADS // g.runs
    run = local_head // g.run_heads
    return run * stride + here * g.run_heads + (local_head - run * g.run_heads)


def one_hot(found):
    return jnp.where(found, 1.0, 0.0)


def step_select(g, here):
    from_ids = lax.broadcasted_iota(jnp.int32, (128, 128), 0)
    to_ids = lax.broadcasted_iota(jnp.int32, (128, 128), 1)
    return one_hot((from_ids == head_of(g, here, to_ids)) & (to_ids < g.heads))


OUT, GATE, REST = KINDS = range(3)


class Wire:
    def __init__(self, send_sems, recv_sems):
        self.send_sems, self.recv_sems, self.used = send_sems, recv_sems, 0

    def put(self, src, dst, axis, peer):
        copy = pltpu.make_async_remote_copy(
            src, dst, self.send_sems.at[self.used], self.recv_sems.at[self.used],
            device_id={axis: peer}, device_id_type=MESH,
        )
        copy.start()
        self.used += 1
        return copy


class Mover:
    def __init__(self, sems):
        self.sems, self.used = sems, 0

    def put(self, src, dst):
        copy = pltpu.make_async_copy(src, dst, self.sems.at[self.used])
        copy.start()
        self.used += 1
        return copy


def meet_all(axes):
    barrier = pltpu.get_barrier_semaphore()
    count = 0
    for axis, n in axes:
        me = lax.axis_index(axis)
        for k in range(1, n):
            pl.semaphore_signal(
                barrier, inc=1, device_id={axis: lax.rem(me + k, n)}, device_id_type=MESH
            )
        count += n - 1
    pl.semaphore_wait(barrier, count)


def column_tiles(first, last, body):
    whole = (last - first) // 256

    def step(t, carry):
        body(pl.ds(pl.multiple_of(first + t * 256, 128), 256))
        return carry

    lax.fori_loop(0, whole, step, 0)
    if first + whole * 256 < last:
        body(slice(first + whole * 256, last))


class ForwardOuts(NamedTuple):
    sec: Any
    pout: Any
    stat0: Any
    h1: Any
    gb_o: Any
    stats: Any
    packs_o: Any
    wf_o: Any
    of_o: Any
    n_o: Any
    proj_o: Any
    mixed_o: Any
    yp_o: Any
    st_o: Any


class ForwardRefs(NamedTuple):
    tokens: Any
    cotangent: Any
    pack: Any
    w_src: Any
    o_src: Any
    sec: Any
    pout: Any
    stat0: Any
    h1: Any
    gb_o: Any
    stats: Any
    packs_o: Any
    wf_o: Any
    of_o: Any
    n_o: Any
    proj_o: Any
    mixed_o: Any
    yp_o: Any
    st_o: Any
    h0: Any
    cot: Any
    packs: Any
    wf: Any
    of: Any
    normed: Any
    proj: Any
    mixed: Any
    yp: Any
    st: Any
    pad: Any
    xc: Any
    dts: Any
    state: Any
    vg: Any
    ssq: Any
    part: Any
    got: Any
    got_stat: Any
    hbuf: Any
    own_stat: Any
    cols: Any
    mdots: Any
    sel: Any
    ss: Any
    rs: Any
    ls: Any


def forward_kernel(g, n, w, rows, *refs):
    r = ForwardRefs(*refs)
    G, NC = g.G, g.NC
    core, here, shard = lax.axis_index(SECTION), lax.axis_index(SEQ), lax.axis_index(WT)
    sibling = 1 - core
    wire, mover = Wire(r.ss, r.rs), Mover(r.ls)
    wf, of, packs = r.wf, r.of, r.packs
    sends, saves = [], []

    def aligned(at, size):
        return pl.ds(pl.multiple_of(at, 16), size)

    def put(src, dst, axis, peer):
        copy = wire.put(src, dst, axis, peer)
        sends.append(copy)
        return copy

    for layer in range(2):
        for first, last in ((g.chans, G), (G + g.chans, 2 * G), (2 * G + 2 * STATE + HEADS, NC)):
            if first < last:
                wf[layer, first:last, :] = jnp.zeros((last - first, D), BF)
    r.sel[...] = step_select(g, here).astype(BF)
    meet_all(((SEQ, n), (WT, w), (SECTION, 2)))
    o_rows = G // w
    lanes_of = D // w
    mine_o = aligned(shard * o_rows, o_rows)
    piece = here if g.runs == w else shard
    o_own = r.o_src.at[aligned(piece * o_rows, o_rows)]
    mine_lanes = pl.ds(pl.multiple_of(shard * lanes_of, 128), lanes_of)
    width = g.run_heads * HEAD_DIM
    runs = []
    for kind_at, source_at in ((0, 0), (G, INNER)):
        for run in range(g.runs):
            source = source_at + run * (INNER // g.runs) + here * width
            runs.append((source, kind_at + run * width, width))
    runs.append((2 * INNER, 2 * G, 2 * STATE))
    runs.append((2 * INNER + 2 * STATE, 2 * G + 2 * STATE, HEADS))
    siblings = [put(r.pack, packs.at[core], SECTION, sibling)]
    locals_ = [
        mover.put(r.pack, packs.at[core]),
        mover.put(o_own, of.at[core, mine_o]),
        mover.put(r.tokens.at[core, 0], r.h0),
        mover.put(r.cotangent.at[core, 0], r.cot),
    ]
    for source, target, size in runs:
        taken = r.w_src.at[aligned(source, size)]
        siblings.append(put(taken, wf.at[core, target : target + size, mine_lanes], SECTION, sibling))
        locals_.append(mover.put(taken, wf.at[core, target : target + size, mine_lanes]))
    siblings.append(put(o_own, of.at[core, mine_o], SECTION, sibling))

    def part_of(layer, kind, at_shard, at_core):
        if kind == OUT:
            return of.at[layer, aligned(at_shard * o_rows + at_core * (o_rows // 2), o_rows // 2)]
        size = (G if kind == GATE else g.rest) // 2
        first = (0 if kind == GATE else G) + at_core * size
        lanes = pl.ds(pl.multiple_of(at_shard * lanes_of, 128), lanes_of)
        return wf.at[layer, aligned(first, size), lanes]

    def fetch(layer, kind):
        mine = part_of(layer, kind, shard, core)
        return [put(mine, mine, WT, lax.rem(shard + k, w)) for k in range(1, w)]

    def hand_on(copies, layer, kind):
        found = []
        for k, copy in enumerate(copies, 1):
            copy.wait_recv()
            block = part_of(layer, kind, lax.rem(shard + w - k, w), core)
            found.append(put(block, block, SECTION, sibling))
        return found

    def received(copies):
        for copy in copies:
            copy.wait_recv()

    own_rows = aligned(here * rows, rows)

    def gather(layer_ref):
        return [
            wire.put(layer_ref.at[own_rows], layer_ref.at[own_rows], SEQ, lax.rem(here + k, n))
            for k in range(1, n)
        ]

    def save(source, target):
        saves.append(mover.put(source, target))

    def saved():
        while saves:
            saves.pop().wait()

    for copy in locals_:
        copy.wait()
    received(siblings)
    pending = fetch(0, REST)
    gain_at = g.CX + 128 + G

    def norm(at):
        h = r.h0[at, :]
        inv = lax.rsqrt(jnp.mean(h * h, axis=1, keepdims=True) + EPSILON)
        r.normed[pl.ds(pl.multiple_of(here * rows + at.start, TILE), TILE), :] = (
            h * inv * packs[0, 0:1, gain_at:]
        ).astype(BF)

    rows_loop(rows, norm)
    arriving = gather(r.normed)

    for layer in range(2):
        proj, mixed, normed = r.proj, r.mixed, r.normed
        conv = packs.at[layer, :, 0 : g.CX]
        head = packs.at[layer, :, g.CX : g.CX + 128]
        wide = packs.at[layer, :, g.CX + 128 : gain_at]

        def project(lanes):
            proj[:, lanes] = dot(normed[...], wf[layer, lanes, :], 1, 1).astype(BF)

        handed = hand_on(pending, layer, REST)
        pending_gate, pending_o = fetch(layer, GATE), fetch(layer, OUT)
        received(arriving)
        received(handed)
        gathered = arriving
        column_tiles(G, NC, project)
        scan_forward(
            G, proj, conv, head, wide, r.sel, mixed, r.yp, r.st,
            r.pad, r.xc, r.dts, r.state,
        )
        save(mixed, r.mixed_o.at[layer])
        save(r.yp, r.yp_o.at[layer])
        save(r.st, r.st_o.at[layer])
        save(normed, r.n_o.at[layer])
        handed = hand_on(pending_gate, layer, GATE) + hand_on(pending_o, layer, OUT)
        if layer == 0:
            pending = fetch(1, REST)
        received(handed)
        column_tiles(0, G, project)
        save(proj, r.proj_o.at[layer])
        gate_forward(G, proj, wide, mixed, r.vg, r.ssq)

        def out_product(block):
            at = aligned(block * rows, rows)

            def tile(lanes):
                r.part[block, :, lanes] = dot(r.vg[at, :], of[layer, :, lanes], 1, 0).astype(BF)

            column_tiles(0, D, tile)

        saved()
        summing = []
        for k in range(1, n):
            peer = lax.rem(here + k, n)
            out_product(peer)
            summing.append(wire.put(r.part.at[peer], r.got.at[k - 1], SEQ, peer))
            summing.append(wire.put(r.ssq.at[peer], r.got_stat.at[k - 1], SEQ, peer))
        out_product(here)
        for copy in summing:
            copy.wait()
        ssq = r.ssq[here]
        for k in range(n - 1):
            ssq = ssq + r.got_stat[k]
        inv2 = lax.rsqrt(ssq * (1.0 / INNER) + EPSILON)
        r.own_stat[...] = inv2
        r.cols[...] = column(inv2[0:1, :])
        if layer == 0:
            r.stat0[...] = inv2

        def finish(at):
            pout = total_of(n, r.part, r.got, at) * r.cols[at, 0:1]
            whole = pl.ds(pl.multiple_of(here * rows + at.start, TILE), TILE)
            h_in = r.h0[at, :] if layer == 0 else r.hbuf[0, at, :]
            h = h_in + pout
            r.hbuf[layer, at, :] = h
            if layer == 0:
                r.pout[at, :] = pout
                r.h1[at, :] = h
                inv = lax.rsqrt(jnp.mean(h * h, axis=1, keepdims=True) + EPSILON)
                r.normed[whole, :] = (h * inv * packs[1, 0:1, gain_at:]).astype(BF)
            else:
                out = r.cot[at, :].astype(BF)
                dots = jnp.sum(out.astype(F32) * pout, axis=1, keepdims=True)
                r.mdots[at, :] = jnp.broadcast_to(dots * (1.0 / INNER), (TILE, 128))
                r.normed[whole, :] = out

        for copy in gathered:
            copy.wait_send()
        rows_loop(rows, finish)
        if layer == 0:
            arriving = gather(r.normed)
    r.stats[here] = r.own_stat[...]
    r.stats[here, 1:2, :] = r.mdots[...].T[0:1, :]
    arriving = gather(r.normed)
    sends.extend(arriving)
    for k in range(1, n):
        block = r.stats.at[here]
        arriving.append(put(block, block, SEQ, lax.rem(here + k, n)))
    arriving.append(put(r.hbuf.at[1 - core], r.sec.at[core], SECTION, sibling))
    save(r.hbuf.at[core], r.sec.at[core])
    save(packs, r.packs_o)
    save(wf, r.wf_o)
    save(of, r.of_o)
    received(arriving)
    save(r.normed, r.gb_o)
    for copy in sends:
        copy.wait_send()
    saved()


def forward_call(g, n, w, tokens, cotangent, pack, w_src, o_src):
    rows = tokens.shape[2]
    L, G, NC, CX, PK = rows * n, g.G, g.NC, g.CX, pack.shape[1]
    S = jax.ShapeDtypeStruct
    shapes = ForwardOuts(
        sec=S((2, rows, D), F32),
        pout=S((rows, D), F32),
        stat0=S((8, 128), F32),
        h1=S((rows, D), F32),
        gb_o=S((L, D), BF),
        stats=S((n, 8, 128), F32),
        packs_o=S((2, 8, PK), F32),
        wf_o=S((2, NC, D), BF),
        of_o=S((2, G, D), BF),
        n_o=S((2, L, D), BF),
        proj_o=S((2, L, NC), BF),
        mixed_o=S((2, L, G), BF),
        yp_o=S((2, L, G), F32),
        st_o=S((2, L // Q, STATE, G), F32),
    )
    scratch = [
        S((rows, D), F32), S((rows, D), F32), shapes.packs_o, shapes.wf_o, shapes.of_o, S((L, D), BF), S((L, NC), BF), S((L, G), BF),
        S((L, G), F32), S((L // Q, STATE, G), F32), S((8 + L, 128), F32), S((L, CX), F32), S((L, 128), F32), S((STATE, G), F32),
        S((L, G), BF), S((n, 8, 128), F32), S((n, rows, D), BF), S((n - 1, rows, D), BF), S((n - 1, 8, 128), F32),
        S((2, rows, D), F32), S((8, 128), F32), S((rows, 128), F32), S((rows, 128), F32),
        S((128, 128), BF),
    ]
    remote = 4 + 2 * g.runs + 12 * (w - 1) + 8 * (n - 1) + 2
    outs = pl.pallas_call(
        functools.partial(forward_kernel, g, n, w, rows),
        out_shape=list(shapes),
        in_specs=[ANY, ANY, VM, ANY, ANY],
        out_specs=[VM] * 4 + [ANY, VM] + [ANY] * 8,
        scratch_shapes=[pltpu.VMEM(s.shape, s.dtype) for s in scratch]
        + [
            pltpu.SemaphoreType.DMA((remote,)),
            pltpu.SemaphoreType.DMA((remote,)),
            pltpu.SemaphoreType.DMA((22 + 2 * g.runs,)),
        ],
        compiler_params=pltpu.CompilerParams(
            collective_id=0, has_side_effects=True, vmem_limit_bytes=FORWARD_VMEM
        ),
        name="forward",
    )(tokens, cotangent, pack, w_src, o_src)
    return ForwardOuts(*outs)


class BackwardOuts(NamedTuple):
    ig: Any
    gi: Any
    go: Any
    gi_sib: Any
    go_sib: Any
    small: Any
    far: Any


class BackwardRefs(NamedTuple):
    packs_i: Any
    wf_i: Any
    of_i: Any
    n_i: Any
    proj_i: Any
    mixed_i: Any
    yp_i: Any
    st_i: Any
    gb_i: Any
    stats1_i: Any
    stat0_i: Any
    pout_i: Any
    h1_i: Any
    tokens_i: Any
    cotangent_i: Any
    ig: Any
    gi: Any
    go: Any
    gi_sib: Any
    go_sib: Any
    small: Any
    far: Any
    packs: Any
    wf: Any
    of: Any
    n: Any
    proj: Any
    mixed: Any
    yp: Any
    st: Any
    gb: Any
    stats: Any
    pout: Any
    h1: Any
    h0: Any
    cot: Any
    dy: Any
    pad: Any
    xc: Any
    dts: Any
    dstate: Any
    part: Any
    got: Any
    own_stat: Any
    mdots: Any
    grads: Any
    gw: Any
    gout: Any
    sib_w: Any
    sib_o: Any
    z_w: Any
    z_o: Any
    sm: Any
    sm_sib: Any
    sm_z: Any
    sm_own: Any
    sel: Any
    ss: Any
    rs: Any
    ls: Any
    free: Any


def backward_kernel(g, n, w, rows, *refs):
    r = BackwardRefs(*refs)
    G, NC, CX = g.G, g.NC, g.CX
    core, here, shard = lax.axis_index(SECTION), lax.axis_index(SEQ), lax.axis_index(WT)
    sibling = 1 - core
    wire, mover = Wire(r.ss, r.rs), Mover(r.ls)
    o_half, lanes_of = G // (2 * w), D // w
    gain_at = CX + 128 + G

    def aligned(at, size):
        return pl.ds(pl.multiple_of(at, 16), size)

    def load(layer, *pairs):
        return [mover.put(source.at[layer], target) for source, target in pairs]

    first = load(1, (r.of_i, r.of), (r.proj_i, r.proj), (r.mixed_i, r.mixed))
    first += [mover.put(r.packs_i, r.packs), mover.put(r.gb_i, r.gb), mover.put(r.stats1_i, r.stats)]
    later = load(1, (r.n_i, r.n), (r.yp_i, r.yp), (r.st_i, r.st), (r.wf_i, r.wf))
    later += [mover.put(r.pout_i, r.pout), mover.put(r.h1_i, r.h1), mover.put(r.stat0_i, r.own_stat)]
    later += [mover.put(r.tokens_i.at[core, 0], r.h0), mover.put(r.cotangent_i.at[core, 0], r.cot)]
    meet_all(((SEQ, n), (WT, w), (SECTION, 2)))
    r.sm[...] = jnp.zeros_like(r.sm)
    r.sel[...] = step_select(g, here).astype(BF)
    open_sends, record = [], {}
    arrivals = r.got if r.got.shape[0] == n - 1 else r.far

    def put(src, dst, axis, peer):
        copy = wire.put(src, dst, axis, peer)
        open_sends.append(copy)
        return copy

    def rows_of(kind):
        return ((0, G), (0, G), (G, g.rest))[kind]

    def kept(kind):
        return (slice(0, G // (2 * w)), slice(0, G // 2), slice(G // 2, g.half))[kind]

    def buffers(kind):
        if kind == OUT:
            return r.gout, r.sib_o, r.z_o, r.go, r.go_sib
        return r.gw, r.sib_w, r.z_w, r.gi, r.gi_sib

    def block_of(kind, at_shard, at_core):
        if kind == OUT:
            return aligned((2 * at_shard + at_core) * o_half, o_half), slice(0, D)
        first, size = rows_of(kind)
        return (
            aligned(first + at_core * (size // 2), size // 2),
            pl.ds(pl.multiple_of(at_shard * lanes_of, 128), lanes_of),
        )

    def ready(kind):
        for copy in record.pop(kind, ()):
            copy.wait_send()

    def to_sibling(layer, kind):
        grad, sib, _, _, _ = buffers(kind)
        if layer == 0:
            pl.semaphore_wait(r.free.at[kind], 1)
        if kind == OUT:
            pairs = [
                (grad.at[block_of(kind, q, sibling)], sib.at[aligned(q * o_half, o_half)])
                for q in range(w)
            ]
        else:
            first, size = rows_of(kind)
            rows_there = aligned(first + sibling * (size // 2), size // 2)
            pairs = [(grad.at[rows_there], sib.at[kept(kind)])]
        copies = [wire.put(source, target, SECTION, sibling) for source, target in pairs]
        record[kind] = list(copies)
        return copies

    def to_shards(layer, kind, copies):
        grad, sib, z, _, _ = buffers(kind)
        for copy in copies:
            copy.wait_recv()
        if kind == OUT:
            per = o_half // TILE

            def places(t):
                q = t // per
                return (2 * q + core) * o_half + (t - q * per) * TILE, t * TILE

            steps = w * per
        else:
            first, size = rows_of(kind)
            steps = size // 2 // TILE

            def places(t):
                return first + core * (size // 2) + t * TILE, kept(kind).start + t * TILE

        def add(t, carry):
            mine, theirs = (pl.ds(pl.multiple_of(at, TILE), TILE) for at in places(t))
            grad[mine, :] = (grad[mine, :].astype(F32) + sib[theirs, :].astype(F32)).astype(BF)
            return carry

        lax.fori_loop(0, steps, add, 0)
        if layer == 1:
            pl.semaphore_signal(
                r.free.at[kind], inc=1, device_id={SECTION: sibling}, device_id_type=MESH
            )
        found = []
        for k in range(1, w):
            peer = lax.rem(shard + k, w)
            source = grad.at[block_of(kind, peer, core)]
            found.append(wire.put(source, z.at[layer, k - 1, kept(kind)], WT, peer))
        record[kind] += found
        return found

    def to_plane(layer, kind, copies):
        grad, _, z, result, _ = buffers(kind)
        for copy in copies:
            copy.wait_recv()
        at_rows, at_lanes = block_of(kind, shard, core)
        here_rows = kept(kind)

        def add(at):
            mine = pl.ds(pl.multiple_of(at_rows.start + at.start, TILE), TILE)
            there = pl.ds(pl.multiple_of(here_rows.start + at.start, TILE), TILE)
            total = grad[mine, at_lanes].astype(F32)
            for k in range(w - 1):
                total = total + z[layer, k, there, :].astype(F32)
            z[layer, 0, there, :] = total.astype(BF)

        rows_loop(here_rows.stop - here_rows.start, add)
        block, target = z.at[layer, 0, here_rows], result.at[layer, here, here_rows]
        found = [put(block, target, SEQ, lax.rem(here + k, n)) for k in range(1, n)]
        return found, mover.put(block, target)

    def landed(kind, *arrivals):
        _, _, _, result, target = buffers(kind)
        for found, own in arrivals:
            for copy in found:
                copy.wait_recv()
            own.wait()
        return put(result.at[sibling, :, kept(kind)], target.at[:, kept(kind)], SECTION, sibling)

    def done(copies):
        for copy in copies:
            copy.wait()

    arrived = {}
    for layer in (1, 0):
        conv = r.packs.at[layer, :, 0:CX]
        head = r.packs.at[layer, :, CX : CX + 128]
        wide = r.packs.at[layer, :, CX + 128 : gain_at]
        g_conv = r.sm.at[layer, :, 0:CX]
        g_head = r.sm.at[layer, :, CX : CX + 128]
        g_wide = r.sm.at[layer, :, CX + 128 : gain_at]
        g_gain = r.sm.at[layer, :, gain_at : gain_at + D]
        done(first)

        def d_normed(lanes):
            r.xc[:, lanes] = dot(r.gb[...], r.of[lanes, :], 1, 1)

        column_tiles(0, G, d_normed)
        gate_backward(
            G, r.proj, r.mixed, r.xc, r.stats, wide, r.dy, g_wide
        )

        def out_rows(t, carry):
            at = pl.ds(pl.multiple_of(t * 128, 128), 128)
            r.gout[at, :] = dot(r.mixed[:, at], r.gb[...], 0, 0).astype(BF)
            return carry

        def in_rows(first, last):
            def step(t, carry):
                at = pl.ds(pl.multiple_of(t * 128, 128), 128)
                r.gw[at, :] = dot(r.proj[:, at], r.n[...], 0, 0).astype(BF)
                return carry

            lax.fori_loop(first // 128, last // 128, step, 0)

        ready(OUT)
        lax.fori_loop(0, G // 128, out_rows, 0)
        out_sib = to_sibling(layer, OUT)
        done(later)
        ready(GATE)
        in_rows(0, G)
        gate_sib = to_sibling(layer, GATE)
        out_z = to_shards(layer, OUT, out_sib)
        gate_z = to_shards(layer, GATE, gate_sib)
        if layer == 0:
            arrived[1, REST] = to_plane(1, REST, rest_z)
        scan_backward(
            G, r.proj, r.dy, r.yp, r.st, conv, head, wide, r.sel, g_wide, g_conv, g_head,
            r.pad, r.xc, r.dts, r.dstate,
        )
        if layer == 1:
            first = load(0, (r.of_i, r.of), (r.mixed_i, r.mixed))
            later = load(0, (r.yp_i, r.yp), (r.st_i, r.st))

        def in_product(block):
            at = aligned(block * rows, rows)

            def tile(lanes):
                r.part[block, :, lanes] = dot(r.proj[at, :], r.wf[:, lanes], 1, 0).astype(BF)

            column_tiles(0, D, tile)

        summing = []
        for k in range(1, n):
            peer = lax.rem(here + k, n)
            in_product(peer)
            summing.append(wire.put(r.part.at[peer], arrivals.at[k - 1], SEQ, peer))
        in_product(here)
        if layer == 1:
            later += load(0, (r.wf_i, r.wf))
        ready(REST)
        in_rows(G, NC)
        if layer == 1:
            first += load(0, (r.proj_i, r.proj))
            later += load(0, (r.n_i, r.n))
        rest_sib = to_sibling(layer, REST)
        rest_z = to_shards(layer, REST, rest_sib)
        done(summing)
        if arrivals is not r.got:
            done(
                [
                    mover.put(arrivals.at[k - 1], r.part.at[lax.rem(here + k, n)])
                    for k in range(1, n)
                ]
            )

        def finish(at):
            if arrivals is r.got:
                d_in = total_of(n, r.part, r.got, at)
            else:
                d_in = r.part[0, at, :].astype(F32)
                for k in range(1, n):
                    d_in = d_in + r.part[k, at, :].astype(F32)
            h = r.h1[at, :] if layer == 1 else r.h0[at, :]
            above = r.cot[at, :] if layer == 1 else r.grads[1, at, :]
            inv = lax.rsqrt(jnp.mean(h * h, axis=1, keepdims=True) + EPSILON)
            normed = h * inv
            g_gain[0:1, :] += jnp.sum(d_in * normed, axis=0, keepdims=True)
            d_s = d_in * r.packs[layer, 0:1, gain_at:]
            d_h = above + inv * (d_s - normed * jnp.mean(d_s * normed, axis=1, keepdims=True))
            r.grads[layer, at, :] = d_h
            if layer == 1:
                out = d_h.astype(BF)
                whole = pl.ds(pl.multiple_of(here * rows + at.start, TILE), TILE)
                r.gb[whole, :] = out
                dots = jnp.sum(out.astype(F32) * r.pout[at, :], axis=1, keepdims=True)
                r.mdots[at, :] = jnp.broadcast_to(dots * (1.0 / INNER), (TILE, 128))

        rows_loop(rows, finish)
        if layer == 1:
            r.stats[here] = r.own_stat[...]
            r.stats[here, 1:2, :] = r.mdots[...].T[0:1, :]
            own = aligned(here * rows, rows)
            gathering = []
            for k in range(1, n):
                peer = lax.rem(here + k, n)
                gathering.append(put(r.gb.at[own], r.gb.at[own], SEQ, peer))
                gathering.append(put(r.stats.at[here], r.stats.at[here], SEQ, peer))
            arrived[1, OUT] = to_plane(1, OUT, out_z)
            arrived[1, GATE] = to_plane(1, GATE, gate_z)
            for copy in gathering:
                copy.wait_recv()
    ends = [put(r.grads.at[sibling], r.ig.at[core], SECTION, sibling)]
    ends.append(put(r.sm.at[sibling], r.sm_sib, SECTION, sibling))
    local_grad = mover.put(r.grads.at[core], r.ig.at[core])
    arrived[0, OUT] = to_plane(0, OUT, out_z)
    arrived[0, GATE] = to_plane(0, GATE, gate_z)
    ends[1].wait_recv()
    r.sm_own[...] = r.sm[core] + r.sm_sib[...]
    sums = [
        put(r.sm_own, r.sm_z.at[k - 1], WT, lax.rem(shard + k, w)) for k in range(1, w)
    ]
    for copy in sums:
        copy.wait_recv()
    total = r.sm_own[...]
    for k in range(w - 1):
        total = total + r.sm_z[k]
    r.small[here] = total
    sums = [
        put(r.small.at[here], r.small.at[here], SEQ, lax.rem(here + k, n))
        for k in range(1, n)
    ]
    ends.append(landed(OUT, arrived[1, OUT], arrived[0, OUT]))
    ends.append(landed(GATE, arrived[1, GATE], arrived[0, GATE]))
    arrived[0, REST] = to_plane(0, REST, rest_z)
    ends.append(landed(REST, arrived[1, REST], arrived[0, REST]))
    ends[0].wait_recv()
    for copy in ends[2:] + sums:
        copy.wait_recv()
    local_grad.wait()
    for kind in KINDS:
        ready(kind)
    for copy in open_sends:
        copy.wait_send()


def backward_call(g, n, w, fwd, tokens, cotangent):
    rows = tokens.shape[2]
    L, G, NC, CX = rows * n, g.G, g.NC, g.CX
    PK = CX + 128 + G + D
    S = jax.ShapeDtypeStruct
    o_half, lanes_of = G // (2 * w), D // w
    spill = n > 8
    outs = BackwardOuts(
        ig=S((2, rows, D), F32),
        gi=S((2, n, g.half, lanes_of), BF),
        go=S((2, n, o_half, D), BF),
        gi_sib=S((n, g.half, lanes_of), BF),
        go_sib=S((n, o_half, D), BF),
        small=S((n, 8, PK), F32),
        far=S((n - 1, rows, D) if spill else (8, 128), BF),
    )
    scratch = [
        S((2, 8, PK), F32), S((NC, D), BF), S((G, D), BF), S((L, D), BF), S((L, NC), BF), S((L, G), BF),
        S((L, G), F32), S((L // Q, STATE, G), F32), S((L, D), BF), S((n, 8, 128), F32), S((rows, D), F32),
        S((rows, D), F32), S((rows, D), F32), S((rows, D), F32),
        S((L, G), BF), S((8 + L, 128), F32), S((L, CX), F32), S((L, 128), F32), S((STATE, G), F32),
        S((n, rows, D), BF), S((1 if spill else n - 1, rows, D), BF), S((8, 128), F32), S((rows, 128), F32), S((2, rows, D), F32),
        S((NC, D), BF), S((G, D), BF), S((g.half, D), BF), S((G // 2, D), BF),
        S((2, w - 1, g.half, lanes_of), BF),
        S((2, w - 1, o_half, D), BF), S((2, 8, PK), F32), S((8, PK), F32), S((w - 1, 8, PK), F32), S((8, PK), F32),
        S((128, 128), BF),
    ]
    remote = 2 * (3 * (w + w - 1 + n - 1) + n - 1) + 2 * (n - 1) + 5 + (w - 1) + (n - 1)
    args = [
        fwd.packs_o, fwd.wf_o, fwd.of_o, fwd.n_o, fwd.proj_o, fwd.mixed_o, fwd.yp_o, fwd.st_o,
        fwd.gb_o, fwd.stats, fwd.stat0, fwd.pout, fwd.h1, tokens, cotangent,
    ]
    results = pl.pallas_call(
        functools.partial(backward_kernel, g, n, w, rows),
        out_shape=list(outs),
        in_specs=[ANY] * len(args),
        out_specs=[VM, ANY, ANY, ANY, ANY, VM, ANY],
        scratch_shapes=[pltpu.VMEM(s.shape, s.dtype) for s in scratch]
        + [
            pltpu.SemaphoreType.DMA((remote,)),
            pltpu.SemaphoreType.DMA((remote,)),
            pltpu.SemaphoreType.DMA((36 + 2 * n,)),
            pltpu.SemaphoreType.REGULAR((3,)),
        ],
        compiler_params=pltpu.CompilerParams(
            collective_id=1, has_side_effects=True, vmem_limit_bytes=BACKWARD_VMEM
        ),
        name="backward",
    )(*args)
    return BackwardOuts(*results)


def pack_kernel(g, win, conv_ref, bias_ref, dtb_ref, a_ref, skip_ref, gate_ref, norm_ref, pack_ref):
    here = lax.axis_index(SEQ)
    G, width = g.G, g.run_heads * HEAD_DIM
    start = here * width
    base = pl.multiple_of(start // 128 * 128, 128)
    from_ids = lax.broadcasted_iota(jnp.int32, (win, G), 0)
    to_ids = lax.broadcasted_iota(jnp.int32, (win, G), 1)
    exact = lax.Precision.HIGHEST

    def take(ref, rows):
        total = jnp.zeros((rows, G), F32)
        for run in range(g.runs):
            window = ref[0:rows, pl.ds(pl.multiple_of(base + run * (INNER // g.runs), 128), win)]
            inside = (to_ids >= run * width) & (to_ids < (run + 1) * width)
            pick = one_hot(inside & (from_ids == to_ids - run * width + (start - base)))
            total = total + dot(window, pick, 1, 0, exact)
        return total

    head_from = lax.broadcasted_iota(jnp.int32, (HEADS, 128), 0)
    head_to = lax.broadcasted_iota(jnp.int32, (HEADS, 128), 1)
    head_pick = one_hot((head_from == head_of(g, here, head_to)) & (head_to < g.heads))
    wide_from = lax.broadcasted_iota(jnp.int32, (HEADS, G), 0)
    wide_to = lax.broadcasted_iota(jnp.int32, (HEADS, G), 1)
    wide_pick = (wide_from == head_of(g, here, wide_to // HEAD_DIM)) & (wide_to < g.chans)
    head_at, wide_at, gain_at = g.CX, g.CX + 128, g.CX + 128 + G
    pack_ref[...] = jnp.zeros_like(pack_ref)
    pack_ref[0:KERNEL, 0:G] = take(conv_ref, KERNEL)
    pack_ref[4:5, 0:G] = take(bias_ref, 1)
    pack_ref[0:KERNEL, G:head_at] = conv_ref[:, INNER:]
    pack_ref[4:5, G:head_at] = bias_ref[:, INNER:]
    pack_ref[0:1, head_at:wide_at] = dot(dtb_ref[...], head_pick, 1, 0, exact)
    pack_ref[1:2, head_at:wide_at] = dot(-jnp.exp(a_ref[...]), head_pick, 1, 0, exact)
    pack_ref[0:1, wide_at:gain_at] = take(gate_ref, 1)
    pack_ref[1:2, wide_at:gain_at] = dot(skip_ref[...], one_hot(wide_pick), 1, 0, exact)
    pack_ref[0:1, gain_at:] = norm_ref[...]


def pack_call(g, *small):
    win = -(-(g.run_heads * HEAD_DIM + 64) // 128) * 128
    return pl.pallas_call(
        functools.partial(pack_kernel, g, win),
        out_shape=jax.ShapeDtypeStruct((8, g.CX + 128 + g.G + D), F32),
        in_specs=[VM] * len(small),
        out_specs=VM,
        compiler_params=pltpu.CompilerParams(vmem_limit_bytes=SMALL_VMEM),
        name="pack",
    )(*small)


def halves_of_heads(g, ref_of, column_at, head):
    parts = []
    for h in (head, head + 1):
        stride = HEADS // g.runs
        group = h % stride // g.run_heads
        local_head = h // stride * g.run_heads + h % g.run_heads
        value = ref_of(group, slice(column_at + local_head // 2 * 128, column_at + local_head // 2 * 128 + 128))
        parts.append(value if local_head % 2 == h % 2 else pltpu.roll(value, HEAD_DIM, 1))
    lanes = lax.broadcasted_iota(jnp.int32, parts[0].shape, 1)
    return jnp.where(lanes < HEAD_DIM, parts[0], parts[1])


def layout_kernel(g, own_ref, sib_ref, small_ref, g_in_ref, norm_ref, conv_ref, bias_ref, dtb_ref, a_ref, skip_ref, gate_ref):
    n, G = g.n_seq, g.G
    first_core = lax.axis_index(SECTION) == 0

    def copy(groups, kind_at, half_at, half_rows, source, target, size):
        done = 0
        while done < size:
            half, offset = divmod(source + done, half_rows)
            count = min(size - done, half_rows - offset)
            at = slice(half_at + offset, half_at + offset + count)
            total = None
            for group in groups:
                own, sib = own_ref[0, group, at, :], sib_ref[group, at, :]
                value = (jnp.where(first_core, own, sib) if half == 0 else jnp.where(first_core, sib, own)).astype(F32)
                total = value if total is None else total + value
            g_in_ref[target + done : target + done + count, :] = total
            done += count

    width = g.run_heads * HEAD_DIM
    rest = (G, G // 2, g.rest // 2)
    everyone = range(n)
    for run in range(g.runs):
        for group in range(n):
            target = run * (INNER // g.runs) + group * width
            copy([group], 0, 0, G // 2, run * width, target, width)
            copy([group], *rest, run * width, INNER + target, width)
    copy(everyone, *rest, G, 2 * INNER, 2 * STATE)
    copy(everyone, *rest, G + 2 * STATE, 2 * INNER + 2 * STATE, HEADS)

    @pl.when(pl.program_id(0) == 0)
    def _():
        from_ids = lax.broadcasted_iota(jnp.int32, (128, HEADS), 0)
        to_ids = lax.broadcasted_iota(jnp.int32, (128, HEADS), 1)
        picks = [one_hot((to_ids == head_of(g, group, from_ids)) & (from_ids < g.heads)) for group in range(n)]
        exact = lax.Precision.HIGHEST
        head_at, wide_at, gain_at = g.CX, g.CX + 128, g.CX + 128 + G

        def small(group, columns):
            return small_ref[group, :, columns]

        for head in range(0, HEADS, 2):
            at = slice(head * HEAD_DIM, head * HEAD_DIM + 128)
            conv = halves_of_heads(g, small, 0, head)
            conv_ref[:, at] = conv[0:KERNEL]
            bias_ref[:, at] = conv[KERNEL : KERNEL + 1]
            gate_ref[:, at] = halves_of_heads(g, small, wide_at, head)[0:1]
        conv = small(0, slice(G, head_at))
        norm = small(0, slice(gain_at, gain_at + D))
        for group in range(1, n):
            conv = conv + small(group, slice(G, head_at))
            norm = norm + small(group, slice(gain_at, gain_at + D))
        conv_ref[:, INNER:] = conv[0:KERNEL]
        bias_ref[:, INNER:] = conv[KERNEL : KERNEL + 1]
        norm_ref[...] = norm[0:1]
        heads = jnp.zeros((8, HEADS), F32)
        skips = jnp.zeros((8, HEADS), F32)
        wide_from = lax.broadcasted_iota(jnp.int32, (G, HEADS), 0)
        wide_to = lax.broadcasted_iota(jnp.int32, (G, HEADS), 1)
        for group in range(n):
            heads = heads + dot(small(group, slice(head_at, wide_at)), picks[group], 1, 0, exact)
            pick = (wide_to == head_of(g, group, wide_from // HEAD_DIM)) & (wide_from < g.chans)
            skips = skips + dot(small(group, slice(wide_at, gain_at)), one_hot(pick), 1, 0, exact)
        dtb_ref[...] = heads[0:1]
        a_ref[...] = heads[1:2]
        skip_ref[...] = skips[1:2]


def layout_call(g, core, gi, gi_sib, small):
    _, n, half, lanes = gi.shape
    PK = small.shape[2]
    columns = 2 * INNER + 2 * STATE + HEADS
    S = jax.ShapeDtypeStruct
    shapes = (
        S((columns, lanes), F32), S((1, D), F32), S((KERNEL, CONV), F32), S((1, CONV), F32), S((1, HEADS), F32),
        S((1, HEADS), F32), S((1, HEADS), F32), S((1, INNER), F32),
    )
    return pl.pallas_call(
        lambda core_ref, *refs: layout_kernel(g, *refs),
        grid_spec=pltpu.PrefetchScalarGridSpec(
            num_scalar_prefetch=1,
            grid=(lanes // 128,),
            in_specs=[
                pl.BlockSpec((1, n, half, 128), lambda t, c: (c[0], 0, 0, t)),
                pl.BlockSpec((n, half, 128), lambda t, c: (0, 0, t)),
                pl.BlockSpec((n, 8, PK), lambda t, c: (0, 0, 0)),
            ],
            out_specs=[pl.BlockSpec((columns, 128), lambda t, c: (0, t))]
            + [pl.BlockSpec(s.shape, lambda t, c: (0, 0)) for s in shapes[1:]],
        ),
        out_shape=shapes,
        compiler_params=pltpu.CompilerParams(vmem_limit_bytes=SMALL_VMEM),
        name="layout",
    )(core, gi, gi_sib, small)


def widen_kernel(core_ref, own_ref, sib_ref, out_ref):
    mine = pl.program_id(0) == core_ref[0]
    out_ref[...] = jnp.where(mine, own_ref[...], sib_ref[...][None]).astype(F32).reshape(out_ref.shape)


def widen_call(core, go, go_sib):
    _, n, size, columns = go.shape
    return pl.pallas_call(
        widen_kernel,
        grid_spec=pltpu.PrefetchScalarGridSpec(
            num_scalar_prefetch=1,
            grid=(2, n),
            in_specs=[
                pl.BlockSpec((1, 1, size, columns), lambda h, t, c: (c[0], t, 0, 0)),
                pl.BlockSpec((1, size, columns), lambda h, t, c: (t, 0, 0)),
            ],
            out_specs=pl.BlockSpec((1, 1, size, columns), lambda h, t, c: (t, h, 0, 0)),
        ),
        out_shape=jax.ShapeDtypeStruct((n, 2, size, columns), F32),
        compiler_params=pltpu.CompilerParams(vmem_limit_bytes=SMALL_VMEM),
        name="widen",
    )(core, go, go_sib)


def local(
    tokens, cotangent, norm_gain, w_in, conv_w, conv_b, dt_bias, a_log, skip_d, gate_gain, w_out
):
    n_seq, n_wt = lax.axis_size(SEQ), lax.axis_size(WT)
    here = lax.axis_index(SEQ)
    group = Group(n_seq, n_wt)
    core = lax.axis_index(SECTION).reshape(1)
    G = group.G

    pack = pack_call(
        group, conv_w[0], conv_b, dt_bias, a_log, skip_d, gate_gain, norm_gain
    )
    w_src = jnp.swapaxes(w_in[0], 0, 1)
    if group.runs == n_wt:
        o_src = w_out[0]
    else:
        o_src = lax.all_gather(w_out[0], WT, axis=0, tiled=True)
        o_src = lax.dynamic_slice_in_dim(o_src, here * group.chans, group.chans, 0)
        o_src = jnp.pad(o_src, ((0, G - group.chans), (0, 0)))
    fwd = forward_call(group, n_seq, n_wt, tokens, cotangent, pack, w_src, o_src)
    bwd = backward_call(group, n_seq, n_wt, fwd, tokens, cotangent)
    g_in, g_norm, g_conv, g_bias, g_dtb, g_a, g_skip, g_gate = layout_call(
        group, core, bwd.gi, bwd.gi_sib, bwd.small
    )
    g_out = widen_call(core, bwd.go, bwd.go_sib)
    if group.runs == n_wt:
        g_out = g_out.reshape(INNER // n_wt, D)
    else:
        g_out = g_out.astype(BF).reshape(n_seq, G // n_wt, D)
        g_out = lax.all_gather(g_out, WT, axis=1, tiled=True)[:, : group.chans].reshape(INNER, D)
        mine = INNER // n_wt
        g_out = lax.dynamic_slice_in_dim(g_out, lax.axis_index(WT) * mine, mine, 0).astype(F32)
    return (
        fwd.sec[None, :, None],
        bwd.ig[None, :, None],
        g_norm,
        jnp.swapaxes(g_in, 0, 1)[None],
        g_conv[None],
        g_bias,
        g_dtb,
        g_a,
        g_skip,
        g_gate,
        g_out[None],
    )


def solution(mesh):
    placed = (
        P(None, WT, SEQ, None),
        P(None, WT, SEQ, None),
        P(SECTION, None),
        P(SECTION, WT, None),
        P(SECTION, None, None),
        P(SECTION, None),
        P(SECTION, None),
        P(SECTION, None),
        P(SECTION, None),
        P(SECTION, None),
        P(SECTION, WT, None),
    )
    return jax.shard_map(
        local,
        mesh=mesh,
        in_specs=placed,
        out_specs=(
            P(SECTION, None, WT, SEQ, None),
            P(SECTION, None, WT, SEQ, None),
            P(SECTION, None),
            P(SECTION, WT, None),
            P(SECTION, None, None),
            P(SECTION, None),
            P(SECTION, None),
            P(SECTION, None),
            P(SECTION, None),
            P(SECTION, None),
            P(SECTION, WT, None),
        ),
        check_vma=False,
    )
```

```python
import functools
from typing import Any, NamedTuple

import jax
import jax.numpy as jnp
from jax import lax
from jax.experimental import pallas as pl
from jax.experimental.pallas import tpu as pltpu
from jax.sharding import PartitionSpec as P

D = 1536
HEADS = 48
HEAD_DIM = 64
STATE = 128
KERNEL = 4
INNER = 3072
CONV = 3328
EPSILON = 1e-05

Q = 128
F32 = jnp.float32
BF = jnp.bfloat16
SEQ, WT, SECTION = "seq", "wt", "section"
FORWARD_VMEM = 56 * 2**20
BACKWARD_VMEM = 60 * 2**20
SMALL_VMEM = 40 * 2**20
MESH = pl.DeviceIdType.MESH
VM = pl.BlockSpec(memory_space=pltpu.VMEM)
ANY = pl.BlockSpec(memory_space=pl.ANY)
TILE = 16


def dot(a, b, ca, cb, precision=None):
    return lax.dot_general(a, b, (((ca,), (cb,)), ((), ())), precision=precision, preferred_element_type=F32)

def sigmoid(x):
    return 1.0 / (1.0 + jnp.exp(-x))

def softplus(x):
    return jnp.maximum(x, 0.0) + jnp.log1p(jnp.exp(-jnp.abs(x)))

def lane_mask(rows):
    return lax.broadcasted_iota(jnp.int32, (rows, 128), 1) < HEAD_DIM

def spread(cols, pair, mask):
    a = jnp.broadcast_to(cols[:, 2 * pair : 2 * pair + 1], mask.shape)
    b = jnp.broadcast_to(cols[:, 2 * pair + 1 : 2 * pair + 2], mask.shape)
    return jnp.where(mask, a, b)

def split_pair(u, mask):
    zero = jnp.zeros_like(u)
    return jnp.concatenate([jnp.where(mask, u, zero), jnp.where(mask, zero, u)], axis=0)

def conv_tile(proj_ref, cw_ref, pad, proj_at, conv_at, rows):
    pad[0:8, :] = jnp.zeros((8, 128), F32)
    pad[8 : 8 + rows, :] = proj_ref[:, pl.ds(proj_at, 128)].astype(F32)
    pre = jnp.broadcast_to(cw_ref[4:5, pl.ds(conv_at, 128)], (rows, 128))
    for k in range(KERNEL):
        pre = pre + cw_ref[k : k + 1, pl.ds(conv_at, 128)] * pad[5 + k : 5 + k + rows, :]
    return pre

def step_inputs(proj_ref, at, hp_ref, sel_ref, dt_at):
    return dot(proj_ref[at, dt_at : dt_at + 128], sel_ref[...], 1, 0) + hp_ref[0:1, :]

def chunk_factors(dt, hp_ref):
    rate = dt * hp_ref[1:2, :]
    rows = lax.broadcasted_iota(jnp.int32, (Q, Q), 0)
    cols = lax.broadcasted_iota(jnp.int32, (Q, Q), 1)
    tri = (rows >= cols).astype(F32)
    cum = dot(tri, rate, 1, 0, lax.Precision.HIGHEST)
    return rate, cum, rows >= cols

def decay_pair(cum, cum_t, causal, pair):
    parts = []
    for h in (2 * pair, 2 * pair + 1):
        diff = jnp.broadcast_to(cum[:, h : h + 1], (Q, Q)) - jnp.broadcast_to(cum_t[h : h + 1, :], (Q, Q))
        parts.append(jnp.exp(jnp.where(causal, diff, -1e30)))
    return jnp.concatenate(parts, axis=1)

def scan_forward(G, proj_ref, cw_ref, hp_ref, gw_ref, sel_ref, mixed_ref, yp_ref, st_ref, pad, xc, dts, state):
    L = proj_ref.shape[0]

    def conv(tile, carry):
        lanes = pl.ds(pl.multiple_of(tile * 128, 128), 128)
        pre = conv_tile(proj_ref, cw_ref, pad, pl.multiple_of(G + tile * 128, 128), lanes.start, L)
        xc[:, lanes] = pre * sigmoid(pre)
        return carry

    lax.fori_loop(0, (G + 2 * STATE) // 128, conv, 0)
    dt_at = 2 * G + 2 * STATE
    dts[...] = softplus(step_inputs(proj_ref, slice(0, L), hp_ref, sel_ref, dt_at))
    state[...] = jnp.zeros_like(state)
    mask = lane_mask(Q)

    def chunk(c, _):
        at = pl.ds(pl.multiple_of(c * Q, Q), Q)
        dt = dts[at, :]
        rate, cum, causal = chunk_factors(dt, hp_ref)
        cum_t = cum.T
        last = cum[Q - 1 : Q, :]
        e_cum = jnp.exp(cum)
        tail = jnp.exp(last - cum) * dt
        e_last = jnp.broadcast_to(jnp.exp(last), (8, 128))
        b = xc[at, G : G + STATE].astype(BF)
        cc = xc[at, G + STATE : G + 2 * STATE].astype(BF)
        scores = dot(cc, b, 1, 1)
        scores2 = jnp.concatenate([scores, scores], axis=1)
        for p in range(G // 128):
            lanes = slice(p * 128, p * 128 + 128)
            x = xc[at, lanes]
            u = (x * spread(dt, p, mask)).astype(BF)
            m = (scores2 * decay_pair(cum, cum_t, causal, p)).astype(BF)
            before = state[:, lanes]
            st_ref[c, :, lanes] = before
            y = dot(m, split_pair(u, mask), 1, 0)
            y = y + dot(cc, before.astype(BF), 1, 0) * spread(e_cum, p, mask)
            yp_ref[at, lanes] = y
            after = dot(b, (x * spread(tail, p, mask)).astype(BF), 0, 0)
            state[:, lanes] = before * spread(e_last, p, mask[0:8])[0:1, :] + after
            mixed_ref[at, lanes] = (y + gw_ref[1:2, lanes] * x).astype(BF)
        return 0

    lax.fori_loop(0, L // Q, chunk, 0)


def gate_forward(G, proj_ref, gw_ref, mixed_ref, vg_ref, ssq_ref):
    def chunk(c, _):
        at = pl.ds(pl.multiple_of(c * Q, Q), Q)
        ssq = jnp.zeros((Q, 1), F32)
        for p in range(G // 128):
            lanes = slice(p * 128, p * 128 + 128)
            gate = proj_ref[at, lanes].astype(F32)
            v = mixed_ref[at, lanes].astype(F32) * (gate * sigmoid(gate))
            vg_ref[at, lanes] = (v * gw_ref[0:1, lanes]).astype(BF)
            ssq = ssq + jnp.sum(v * v, axis=1, keepdims=True)
        ssq_ref[c] = jnp.broadcast_to(ssq, (Q, 128)).T[0:8, :]
        return 0

    lax.fori_loop(0, proj_ref.shape[0] // Q, chunk, 0)


def gate_backward(G, proj_ref, mixed_ref, dn_ref, sc_ref, gw_ref, dy_ref, gg_ref):
    gg_ref[...] = jnp.zeros_like(gg_ref)

    def chunk(c, _):
        at = pl.ds(pl.multiple_of(c * Q, Q), Q)
        sc = jnp.concatenate([sc_ref[c], jnp.zeros((Q - 8, 128), F32)], axis=0).T
        inv2 = jnp.broadcast_to(sc[:, 0:1], (Q, 128))
        mdot = jnp.broadcast_to(sc[:, 1:2], (Q, 128))
        for p in range(G // 128):
            lanes = slice(p * 128, p * 128 + 128)
            gate = proj_ref[at, lanes].astype(F32)
            sig = sigmoid(gate)
            act = gate * sig
            mixed = mixed_ref[at, lanes].astype(F32)
            n2 = mixed * act * inv2
            mixed_ref[at, lanes] = (n2 * gw_ref[0:1, lanes]).astype(BF)
            dn = dn_ref[at, lanes]
            gg_ref[0:1, lanes] += jnp.sum(dn * n2, axis=0, keepdims=True)
            d_v = inv2 * (dn * gw_ref[0:1, lanes] - n2 * mdot)
            dy_ref[at, lanes] = (d_v * act).astype(BF)
            proj_ref[at, lanes] = (d_v * mixed * (sig * (1.0 + gate * (1.0 - sig)))).astype(BF)
        return 0

    lax.fori_loop(0, proj_ref.shape[0] // Q, chunk, 0)


def scan_backward(G, proj_ref, dy_ref, yp_ref, st_ref, cw_ref, hp_ref, gw_ref, sel_ref, gg_ref, gc_ref, gh_ref,
                  pad, xc, dts, dstate):
    L = proj_ref.shape[0]
    nb = L // Q
    mask = lane_mask(Q)

    def conv(tile, carry):
        lanes = pl.ds(pl.multiple_of(tile * 128, 128), 128)
        pre = conv_tile(proj_ref, cw_ref, pad, pl.multiple_of(G + tile * 128, 128), lanes.start, L)
        xc[:, lanes] = pre * sigmoid(pre)
        return carry

    lax.fori_loop(0, (G + 2 * STATE) // 128, conv, 0)
    dt_at = 2 * G + 2 * STATE
    dts[...] = softplus(step_inputs(proj_ref, slice(0, L), hp_ref, sel_ref, dt_at))
    dstate[...] = jnp.zeros_like(dstate)
    gh_ref[...] = jnp.zeros_like(gh_ref)

    def chunk(step, _):
        c = nb - 1 - step
        at = pl.ds(pl.multiple_of(c * Q, Q), Q)
        dt = dts[at, :]
        rate, cum, causal = chunk_factors(dt, hp_ref)
        cum_t = cum.T
        last = cum[Q - 1 : Q, :]
        e_cum = jnp.exp(cum)
        tail = jnp.exp(last - cum)
        e_last = jnp.broadcast_to(jnp.exp(last), (8, 128))
        b = xc[at, G : G + STATE].astype(BF)
        cc = xc[at, G + STATE : G + 2 * STATE].astype(BF)
        scores = dot(cc, b, 1, 1)
        scores2 = jnp.concatenate([scores, scores], axis=1)
        d_scores = jnp.zeros((Q, Q), F32)
        d_b = jnp.zeros((Q, STATE), F32)
        d_c = jnp.zeros((Q, STATE), F32)
        d_cum = jnp.zeros((Q, 128), F32)
        d_dt = jnp.zeros((Q, 128), F32)
        d_last = jnp.zeros((8, 128), F32)
        lane_ids = lax.broadcasted_iota(jnp.int32, (Q, 128), 1)
        for p in range(G // 128):
            lanes = slice(p * 128, p * 128 + 128)
            dyb = dy_ref[at, lanes]
            d_y = dyb.astype(F32)
            x = xc[at, lanes]
            dt_x = spread(dt, p, mask)
            u = (x * dt_x).astype(BF)
            u2 = split_pair(u, mask)
            uf = u.astype(F32)
            dec = decay_pair(cum, cum_t, causal, p)
            m = (scores2 * dec).astype(BF)
            dm = dot(dyb, u2, 1, 1) * dec
            d_scores = d_scores + dm[:, :Q] + dm[:, Q:]
            both = dot(m, dyb, 0, 0)
            du = jnp.where(mask, both[:Q], both[Q:])
            tail_x = spread(tail, p, mask)
            before = st_ref[c, :, lanes]
            after = dstate[:, lanes]
            afterb = after.astype(BF)
            du_out = tail_x * dot(b, afterb, 1, 0)
            du = du + du_out
            dye = (d_y * spread(e_cum, p, mask)).astype(BF)
            d_c = d_c + dot(dye, before.astype(BF), 1, 1)
            d_b = d_b + dot((uf * tail_x).astype(BF), afterb, 1, 1)
            e_last_x = spread(e_last, p, mask[0:8])
            dstate[:, lanes] = after * e_last_x[0:1, :] + dot(cc, dye, 0, 0)
            z3 = jnp.sum(uf * du_out, axis=0, keepdims=True) + e_last_x[0:1, :] * jnp.sum(before * after, axis=0, keepdims=True)
            z1 = d_y * yp_ref[at, lanes] - uf * du
            z2 = x * du
            zero = jnp.zeros_like(z1)
            for half, h in ((True, 2 * p), (False, 2 * p + 1)):
                keep = mask if half else jnp.logical_not(mask)
                here = lane_ids == h
                d_cum = jnp.where(here, jnp.sum(jnp.where(keep, z1, zero), axis=1, keepdims=True), d_cum)
                d_dt = jnp.where(here, jnp.sum(jnp.where(keep, z2, zero), axis=1, keepdims=True), d_dt)
                s3 = jnp.sum(jnp.where(keep[0:8], jnp.broadcast_to(z3, (8, 128)), 0.0), axis=1, keepdims=True)
                d_last = jnp.where(here[0:8], s3, d_last)
            xc[at, lanes] = dt_x * du + gw_ref[1:2, lanes] * d_y
            gg_ref[1:2, lanes] += jnp.sum(d_y * x, axis=0, keepdims=True)
        dsb = d_scores.astype(BF)
        xc[at, G : G + STATE] = d_b + dot(dsb, cc, 0, 0)
        xc[at, G + STATE : G + 2 * STATE] = d_c + dot(dsb, b, 1, 0)
        rows = lax.broadcasted_iota(jnp.int32, (Q, Q), 0)
        cols = lax.broadcasted_iota(jnp.int32, (Q, Q), 1)
        upper = (rows <= cols).astype(F32)
        d_rate = dot(upper, d_cum, 1, 0, lax.Precision.HIGHEST) + d_last[0:1, :]
        d_step = d_dt + d_rate * hp_ref[1:2, :]
        d_raw = d_step * sigmoid(step_inputs(proj_ref, at, hp_ref, sel_ref, dt_at))
        proj_ref[at, dt_at : dt_at + 128] = dot(d_raw.astype(BF), sel_ref[...], 1, 1).astype(BF)
        gh_ref[0:1, :] += jnp.sum(d_raw, axis=0, keepdims=True)
        gh_ref[1:2, :] += jnp.sum(d_rate * rate, axis=0, keepdims=True)
        return 0

    lax.fori_loop(0, nb, chunk, 0)

    gc_ref[...] = jnp.zeros_like(gc_ref)

    def conv_back(tile, carry):
        lanes = pl.ds(pl.multiple_of(tile * 128, 128), 128)
        proj_at = pl.multiple_of(G + tile * 128, 128)
        pre = conv_tile(proj_ref, cw_ref, pad, proj_at, lanes.start, L)
        sig = sigmoid(pre)
        d_pre = xc[:, lanes] * (sig * (1.0 + pre * (1.0 - sig)))
        for k in range(KERNEL):
            gc_ref[k : k + 1, lanes] = jnp.sum(d_pre * pad[5 + k : 5 + k + L, :], axis=0, keepdims=True)
        gc_ref[4:5, lanes] = jnp.sum(d_pre, axis=0, keepdims=True)
        pad[0:L, :] = d_pre
        pad[L : L + 8, :] = jnp.zeros((8, 128), F32)
        d_in = cw_ref[3:4, lanes] * d_pre
        for k in range(KERNEL - 1):
            d_in = d_in + cw_ref[k : k + 1, lanes] * pad[3 - k : 3 - k + L, :]
        proj_ref[:, pl.ds(proj_at, 128)] = d_in.astype(BF)
        return carry

    lax.fori_loop(0, (G + 2 * STATE) // 128, conv_back, 0)


def column(row):
    return jnp.broadcast_to(row, (128, 128)).T


def rows_loop(rows, body):
    def step(r, carry):
        body(pl.ds(pl.multiple_of(r * TILE, TILE), TILE))
        return carry

    lax.fori_loop(0, rows // TILE, step, 0)


def total_of(n, part_ref, got, at):
    total = part_ref[lax.axis_index(SEQ), at, :].astype(F32)
    for k in range(n - 1):
        total = total + got[k, at, :].astype(F32)
    return total


class Group:
    def __init__(self, n_seq, n_wt):
        self.n_seq = n_seq
        self.heads = HEADS // n_seq
        self.runs = n_wt if HEADS % (n_seq * n_wt) == 0 else 1
        self.run_heads = self.heads // self.runs
        self.chans = self.heads * HEAD_DIM
        self.G = -(-self.chans // 128) * 128
        self.CX = self.G + 2 * STATE
        self.NC = 2 * self.G + 2 * STATE + 128
        self.rest = self.G + 2 * STATE + 64
        self.half = (self.G + self.rest) // 2


def head_of(g, here, local_head):
    stride = HEADS // g.runs
    run = local_head // g.run_heads
    return run * stride + here * g.run_heads + (local_head - run * g.run_heads)


def one_hot(found):
    return jnp.where(found, 1.0, 0.0)


def step_select(g, here):
    from_ids = lax.broadcasted_iota(jnp.int32, (128, 128), 0)
    to_ids = lax.broadcasted_iota(jnp.int32, (128, 128), 1)
    return one_hot((from_ids == head_of(g, here, to_ids)) & (to_ids < g.heads))


OUT, GATE, REST = KINDS = range(3)


class Wire:
    def __init__(self, send_sems, recv_sems):
        self.send_sems, self.recv_sems, self.used = send_sems, recv_sems, 0

    def reserve(self):
        self.used += 1
        return self.used - 1

    def make(self, src, dst, axis, peer, at_send, at_recv):
        return pltpu.make_async_remote_copy(
            src, dst, self.send_sems.at[at_send], self.recv_sems.at[at_recv],
            device_id={axis: peer}, device_id_type=MESH,
        )

    def put(self, src, dst, axis, peer):
        at = self.reserve()
        copy = self.make(src, dst, axis, peer, at, at)
        copy.start()
        return copy


class Maybe:
    def __init__(self, condition, copy):
        self.condition, self.copy = condition, copy

    def start(self):
        pl.when(self.condition)(self.copy.start)
        return self

    def wait_send(self):
        pl.when(self.condition)(self.copy.wait_send)


class Mover:
    def __init__(self, sems):
        self.sems, self.used = sems, 0

    def put(self, src, dst):
        copy = pltpu.make_async_copy(src, dst, self.sems.at[self.used])
        copy.start()
        self.used += 1
        return copy


def meet_all(axes):
    barrier = pltpu.get_barrier_semaphore()
    count = 0
    for axis, n in axes:
        me = lax.axis_index(axis)
        for k in range(1, n):
            pl.semaphore_signal(
                barrier, inc=1, device_id={axis: lax.rem(me + k, n)}, device_id_type=MESH
            )
        count += n - 1
    pl.semaphore_wait(barrier, count)


def column_tiles(first, last, body):
    whole = (last - first) // 256

    def step(t, carry):
        body(pl.ds(pl.multiple_of(first + t * 256, 128), 256))
        return carry

    lax.fori_loop(0, whole, step, 0)
    if first + whole * 256 < last:
        body(slice(first + whole * 256, last))


class ForwardOuts(NamedTuple):
    sec: Any
    pout: Any
    stat0: Any
    h1: Any
    gb_o: Any
    stats: Any
    packs_o: Any
    wf_o: Any
    of_o: Any
    n_o: Any
    proj_o: Any
    mixed_o: Any
    yp_o: Any
    st_o: Any


class ForwardRefs(NamedTuple):
    tokens: Any
    cotangent: Any
    pack: Any
    w_src: Any
    o_src: Any
    sec: Any
    pout: Any
    stat0: Any
    h1: Any
    gb_o: Any
    stats: Any
    packs_o: Any
    wf_o: Any
    of_o: Any
    n_o: Any
    proj_o: Any
    mixed_o: Any
    yp_o: Any
    st_o: Any
    h0: Any
    cot: Any
    packs: Any
    wf: Any
    of: Any
    normed: Any
    proj: Any
    mixed: Any
    yp: Any
    st: Any
    pad: Any
    xc: Any
    dts: Any
    state: Any
    vg: Any
    ssq: Any
    part: Any
    got: Any
    got_stat: Any
    hbuf: Any
    own_stat: Any
    cols: Any
    mdots: Any
    sel: Any
    ss: Any
    rs: Any
    ls: Any


def forward_kernel(g, n, w, rows, *refs):
    r = ForwardRefs(*refs)
    G, NC = g.G, g.NC
    core, here, shard = lax.axis_index(SECTION), lax.axis_index(SEQ), lax.axis_index(WT)
    sibling = 1 - core
    wire, mover = Wire(r.ss, r.rs), Mover(r.ls)
    wf, of, packs = r.wf, r.of, r.packs
    sends, saves = [], []

    def aligned(at, size):
        return pl.ds(pl.multiple_of(at, 16), size)

    def put(src, dst, axis, peer):
        copy = wire.put(src, dst, axis, peer)
        sends.append(copy)
        return copy

    for layer in range(2):
        for first, last in ((g.chans, G), (G + g.chans, 2 * G), (2 * G + 2 * STATE + HEADS, NC)):
            if first < last:
                wf[layer, first:last, :] = jnp.zeros((last - first, D), BF)
    r.sel[...] = step_select(g, here).astype(BF)
    meet_all(((SEQ, n), (WT, w), (SECTION, 2)))
    o_rows = G // w
    lanes_of = D // w
    mine_o = aligned(shard * o_rows, o_rows)
    piece = here if g.runs == w else shard
    o_own = r.o_src.at[aligned(piece * o_rows, o_rows)]
    mine_lanes = pl.ds(pl.multiple_of(shard * lanes_of, 128), lanes_of)
    width = g.run_heads * HEAD_DIM
    runs = []
    for kind_at, source_at in ((0, 0), (G, INNER)):
        for run in range(g.runs):
            source = source_at + run * (INNER // g.runs) + here * width
            runs.append((source, kind_at + run * width, width))
    runs.append((2 * INNER, 2 * G, 2 * STATE))
    runs.append((2 * INNER + 2 * STATE, 2 * G + 2 * STATE, HEADS))
    siblings = [put(r.pack, packs.at[core], SECTION, sibling)]
    locals_ = [
        mover.put(r.pack, packs.at[core]),
        mover.put(o_own, of.at[core, mine_o]),
        mover.put(r.tokens.at[core, 0], r.h0),
        mover.put(r.cotangent.at[core, 0], r.cot),
    ]
    for source, target, size in runs:
        taken = r.w_src.at[aligned(source, size)]
        siblings.append(put(taken, wf.at[core, target : target + size, mine_lanes], SECTION, sibling))
        locals_.append(mover.put(taken, wf.at[core, target : target + size, mine_lanes]))
    siblings.append(put(o_own, of.at[core, mine_o], SECTION, sibling))

    def part_of(layer, kind, at_shard, at_core):
        if kind == OUT:
            return of.at[layer, aligned(at_shard * o_rows + at_core * (o_rows // 2), o_rows // 2)]
        size = (G if kind == GATE else g.rest) // 2
        first = (0 if kind == GATE else G) + at_core * size
        lanes = pl.ds(pl.multiple_of(at_shard * lanes_of, 128), lanes_of)
        return wf.at[layer, aligned(first, size), lanes]

    line = w == 4

    def fetch(layer, kind):
        mine = part_of(layer, kind, shard, core)
        at = [wire.reserve() for _ in range(w)]
        copies = [
            wire.make(mine, mine, WT, lax.rem(shard + k, w), at[k], at[k]) for k in range(1, w)
        ]
        if line:
            copies[1].start()
            sends.append(copies[1])
            sends.append(Maybe(shard != w - 1, copies[0]).start())
            sends.append(Maybe(shard != 0, copies[2]).start())
        else:
            for copy in copies:
                copy.start()
            sends.extend(copies)
        return copies, at

    def hand_on(fetched, layer, kind, then=None):
        copies, at = fetched
        found = []
        for k in (2, 1, 3) if line else range(1, w):
            copies[k - 1].wait_recv()
            block = part_of(layer, kind, lax.rem(shard + w - k, w), core)
            if line and k == 2:
                up = wire.make(block, block, WT, lax.rem(shard + 1, w), at[0], at[3])
                down = wire.make(block, block, WT, lax.rem(shard + w - 1, w), at[0], at[1])
                sends.append(Maybe(shard == 2, up).start())
                sends.append(Maybe(shard == 1, down).start())
            if k == 2 and then is not None:
                then()
            found.append(put(block, block, SECTION, sibling))
        return found

    def received(copies):
        for copy in copies:
            copy.wait_recv()

    own_rows = aligned(here * rows, rows)

    def gather(layer_ref):
        return [
            wire.put(layer_ref.at[own_rows], layer_ref.at[own_rows], SEQ, lax.rem(here + k, n))
            for k in range(1, n)
        ]

    def save(source, target):
        saves.append(mover.put(source, target))

    def saved():
        while saves:
            saves.pop().wait()

    for copy in locals_:
        copy.wait()
    received(siblings)
    pending = fetch(0, REST)
    gain_at = g.CX + 128 + G

    def norm(at):
        h = r.h0[at, :]
        inv = lax.rsqrt(jnp.mean(h * h, axis=1, keepdims=True) + EPSILON)
        r.normed[pl.ds(pl.multiple_of(here * rows + at.start, TILE), TILE), :] = (
            h * inv * packs[0, 0:1, gain_at:]
        ).astype(BF)

    rows_loop(rows, norm)
    arriving = gather(r.normed)

    for layer in range(2):
        proj, mixed, normed = r.proj, r.mixed, r.normed
        conv = packs.at[layer, :, 0 : g.CX]
        head = packs.at[layer, :, g.CX : g.CX + 128]
        wide = packs.at[layer, :, g.CX + 128 : gain_at]

        def project(lanes):
            proj[:, lanes] = dot(normed[...], wf[layer, lanes, :], 1, 1).astype(BF)

        coming = []

        def fetch_others():
            coming.extend([fetch(layer, GATE), fetch(layer, OUT)])

        def fetch_above():
            coming.append(fetch(1, REST))

        handed = hand_on(pending, layer, REST, fetch_others)
        received(arriving)
        received(handed)
        gathered = arriving
        column_tiles(G, NC, project)
        scan_forward(
            G, proj, conv, head, wide, r.sel, mixed, r.yp, r.st,
            r.pad, r.xc, r.dts, r.state,
        )
        save(mixed, r.mixed_o.at[layer])
        save(r.yp, r.yp_o.at[layer])
        save(r.st, r.st_o.at[layer])
        save(normed, r.n_o.at[layer])
        handed = hand_on(coming[0], layer, GATE)
        handed += hand_on(coming[1], layer, OUT, fetch_above if layer == 0 else None)
        pending = coming[-1]
        received(handed)
        column_tiles(0, G, project)
        save(proj, r.proj_o.at[layer])
        gate_forward(G, proj, wide, mixed, r.vg, r.ssq)

        def out_product(block):
            at = aligned(block * rows, rows)

            def tile(lanes):
                r.part[block, :, lanes] = dot(r.vg[at, :], of[layer, :, lanes], 1, 0).astype(BF)

            column_tiles(0, D, tile)

        saved()
        summing = []
        for k in range(1, n):
            peer = lax.rem(here + k, n)
            out_product(peer)
            summing.append(wire.put(r.part.at[peer], r.got.at[k - 1], SEQ, peer))
            summing.append(wire.put(r.ssq.at[peer], r.got_stat.at[k - 1], SEQ, peer))
        out_product(here)
        for copy in summing:
            copy.wait()
        ssq = r.ssq[here]
        for k in range(n - 1):
            ssq = ssq + r.got_stat[k]
        inv2 = lax.rsqrt(ssq * (1.0 / INNER) + EPSILON)
        r.own_stat[...] = inv2
        r.cols[...] = column(inv2[0:1, :])
        if layer == 0:
            r.stat0[...] = inv2

        def finish(at):
            pout = total_of(n, r.part, r.got, at) * r.cols[at, 0:1]
            whole = pl.ds(pl.multiple_of(here * rows + at.start, TILE), TILE)
            h_in = r.h0[at, :] if layer == 0 else r.hbuf[0, at, :]
            h = h_in + pout
            r.hbuf[layer, at, :] = h
            if layer == 0:
                r.pout[at, :] = pout
                r.h1[at, :] = h
                inv = lax.rsqrt(jnp.mean(h * h, axis=1, keepdims=True) + EPSILON)
                r.normed[whole, :] = (h * inv * packs[1, 0:1, gain_at:]).astype(BF)
            else:
                out = r.cot[at, :].astype(BF)
                dots = jnp.sum(out.astype(F32) * pout, axis=1, keepdims=True)
                r.mdots[at, :] = jnp.broadcast_to(dots * (1.0 / INNER), (TILE, 128))
                r.normed[whole, :] = out

        for copy in gathered:
            copy.wait_send()
        rows_loop(rows, finish)
        if layer == 0:
            arriving = gather(r.normed)
    r.stats[here] = r.own_stat[...]
    r.stats[here, 1:2, :] = r.mdots[...].T[0:1, :]
    arriving = gather(r.normed)
    sends.extend(arriving)
    for k in range(1, n):
        block = r.stats.at[here]
        arriving.append(put(block, block, SEQ, lax.rem(here + k, n)))
    arriving.append(put(r.hbuf.at[1 - core], r.sec.at[core], SECTION, sibling))
    save(r.hbuf.at[core], r.sec.at[core])
    save(packs, r.packs_o)
    save(wf, r.wf_o)
    save(of, r.of_o)
    received(arriving)
    save(r.normed, r.gb_o)
    for copy in sends:
        copy.wait_send()
    saved()


def forward_call(g, n, w, tokens, cotangent, pack, w_src, o_src):
    rows = tokens.shape[2]
    L, G, NC, CX, PK = rows * n, g.G, g.NC, g.CX, pack.shape[1]
    S = jax.ShapeDtypeStruct
    shapes = ForwardOuts(
        sec=S((2, rows, D), F32),
        pout=S((rows, D), F32),
        stat0=S((8, 128), F32),
        h1=S((rows, D), F32),
        gb_o=S((L, D), BF),
        stats=S((n, 8, 128), F32),
        packs_o=S((2, 8, PK), F32),
        wf_o=S((2, NC, D), BF),
        of_o=S((2, G, D), BF),
        n_o=S((2, L, D), BF),
        proj_o=S((2, L, NC), BF),
        mixed_o=S((2, L, G), BF),
        yp_o=S((2, L, G), F32),
        st_o=S((2, L // Q, STATE, G), F32),
    )
    scratch = [
        S((rows, D), F32), S((rows, D), F32), shapes.packs_o, shapes.wf_o, shapes.of_o, S((L, D), BF), S((L, NC), BF), S((L, G), BF),
        S((L, G), F32), S((L // Q, STATE, G), F32), S((8 + L, 128), F32), S((L, CX), F32), S((L, 128), F32), S((STATE, G), F32),
        S((L, G), BF), S((n, 8, 128), F32), S((n, rows, D), BF), S((n - 1, rows, D), BF), S((n - 1, 8, 128), F32),
        S((2, rows, D), F32), S((8, 128), F32), S((rows, 128), F32), S((rows, 128), F32),
        S((128, 128), BF),
    ]
    remote = 4 + 2 * g.runs + 6 * w + 6 * (w - 1) + 8 * (n - 1) + 2
    outs = pl.pallas_call(
        functools.partial(forward_kernel, g, n, w, rows),
        out_shape=list(shapes),
        in_specs=[ANY, ANY, VM, ANY, ANY],
        out_specs=[VM] * 4 + [ANY, VM] + [ANY] * 8,
        scratch_shapes=[pltpu.VMEM(s.shape, s.dtype) for s in scratch]
        + [
            pltpu.SemaphoreType.DMA((remote,)),
            pltpu.SemaphoreType.DMA((remote,)),
            pltpu.SemaphoreType.DMA((22 + 2 * g.runs,)),
        ],
        compiler_params=pltpu.CompilerParams(
            collective_id=0, has_side_effects=True, vmem_limit_bytes=FORWARD_VMEM
        ),
        name="forward",
    )(tokens, cotangent, pack, w_src, o_src)
    return ForwardOuts(*outs)


class BackwardOuts(NamedTuple):
    ig: Any
    gi: Any
    go: Any
    gi_sib: Any
    go_sib: Any
    small: Any
    far: Any


class BackwardRefs(NamedTuple):
    packs_i: Any
    wf_i: Any
    of_i: Any
    n_i: Any
    proj_i: Any
    mixed_i: Any
    yp_i: Any
    st_i: Any
    gb_i: Any
    stats1_i: Any
    stat0_i: Any
    pout_i: Any
    h1_i: Any
    tokens_i: Any
    cotangent_i: Any
    ig: Any
    gi: Any
    go: Any
    gi_sib: Any
    go_sib: Any
    small: Any
    far: Any
    packs: Any
    wf: Any
    of: Any
    n: Any
    proj: Any
    mixed: Any
    yp: Any
    st: Any
    gb: Any
    stats: Any
    pout: Any
    h1: Any
    h0: Any
    cot: Any
    dy: Any
    pad: Any
    xc: Any
    dts: Any
    dstate: Any
    part: Any
    got: Any
    own_stat: Any
    mdots: Any
    grads: Any
    gw: Any
    gout: Any
    sib_w: Any
    sib_o: Any
    z_w: Any
    z_o: Any
    relay_w: Any
    relay_o: Any
    sm: Any
    sm_sib: Any
    sm_z: Any
    sm_own: Any
    sel: Any
    ss: Any
    rs: Any
    ls: Any
    free: Any


def backward_kernel(g, n, w, rows, *refs):
    r = BackwardRefs(*refs)
    G, NC, CX = g.G, g.NC, g.CX
    core, here, shard = lax.axis_index(SECTION), lax.axis_index(SEQ), lax.axis_index(WT)
    sibling = 1 - core
    wire, mover = Wire(r.ss, r.rs), Mover(r.ls)
    o_half, lanes_of = G // (2 * w), D // w
    gain_at = CX + 128 + G

    def aligned(at, size):
        return pl.ds(pl.multiple_of(at, 16), size)

    def load(layer, *pairs):
        return [mover.put(source.at[layer], target) for source, target in pairs]

    first = load(1, (r.of_i, r.of), (r.proj_i, r.proj), (r.mixed_i, r.mixed))
    first += [mover.put(r.packs_i, r.packs), mover.put(r.gb_i, r.gb), mover.put(r.stats1_i, r.stats)]
    later = load(1, (r.n_i, r.n), (r.yp_i, r.yp), (r.st_i, r.st), (r.wf_i, r.wf))
    later += [mover.put(r.pout_i, r.pout), mover.put(r.h1_i, r.h1), mover.put(r.stat0_i, r.own_stat)]
    later += [mover.put(r.tokens_i.at[core, 0], r.h0), mover.put(r.cotangent_i.at[core, 0], r.cot)]
    meet_all(((SEQ, n), (WT, w), (SECTION, 2)))
    r.sm[...] = jnp.zeros_like(r.sm)
    r.sel[...] = step_select(g, here).astype(BF)
    open_sends, record = [], {}
    line = w == 4
    arrivals = r.got if r.got.shape[0] == n - 1 else r.far

    def put(src, dst, axis, peer):
        copy = wire.put(src, dst, axis, peer)
        open_sends.append(copy)
        return copy

    def rows_of(kind):
        return ((0, G), (0, G), (G, g.rest))[kind]

    def kept(kind):
        return (slice(0, G // (2 * w)), slice(0, G // 2), slice(G // 2, g.half))[kind]

    def buffers(kind):
        if kind == OUT:
            return r.gout, r.sib_o, r.z_o, r.go, r.go_sib
        return r.gw, r.sib_w, r.z_w, r.gi, r.gi_sib

    def block_of(kind, at_shard, at_core):
        if kind == OUT:
            return aligned((2 * at_shard + at_core) * o_half, o_half), slice(0, D)
        first, size = rows_of(kind)
        return (
            aligned(first + at_core * (size // 2), size // 2),
            pl.ds(pl.multiple_of(at_shard * lanes_of, 128), lanes_of),
        )

    def ready(kind):
        for copy in record.pop(kind, ()):
            copy.wait_send()

    def to_sibling(layer, kind):
        grad, sib, _, _, _ = buffers(kind)
        if layer == 0:
            pl.semaphore_wait(r.free.at[kind], 1)
        if kind == OUT:
            pairs = [
                (grad.at[block_of(kind, q, sibling)], sib.at[aligned(q * o_half, o_half)])
                for q in range(w)
            ]
        else:
            first, size = rows_of(kind)
            rows_there = aligned(first + sibling * (size // 2), size // 2)
            pairs = [(grad.at[rows_there], sib.at[kept(kind)])]
        copies = [wire.put(source, target, SECTION, sibling) for source, target in pairs]
        record[kind] = list(copies)
        return copies

    def to_shards(layer, kind, copies):
        grad, sib, z, _, _ = buffers(kind)
        for copy in copies:
            copy.wait_recv()
        if kind == OUT:
            per = o_half // TILE

            def places(t):
                q = t // per
                return (2 * q + core) * o_half + (t - q * per) * TILE, t * TILE

            steps = w * per
        else:
            first, size = rows_of(kind)
            steps = size // 2 // TILE

            def places(t):
                return first + core * (size // 2) + t * TILE, kept(kind).start + t * TILE

        def add(t, carry):
            mine, theirs = (pl.ds(pl.multiple_of(at, TILE), TILE) for at in places(t))
            grad[mine, :] = (grad[mine, :].astype(F32) + sib[theirs, :].astype(F32)).astype(BF)
            return carry

        lax.fori_loop(0, steps, add, 0)
        if layer == 1:
            pl.semaphore_signal(
                r.free.at[kind], inc=1, device_id={SECTION: sibling}, device_id_type=MESH
            )
        at = [wire.reserve() for _ in range(w)]
        found = []
        for k in range(1, w):
            peer = lax.rem(shard + k, w)
            source = grad.at[block_of(kind, peer, core)]
            found.append(wire.make(source, z.at[layer, k - 1, kept(kind)], WT, peer, at[k], at[k]))
        if not line:
            for copy in found:
                copy.start()
            record[kind] += found
            return found, None
        buffer = (r.relay_o if kind == OUT else r.relay_w).at[layer, kept(kind)]
        up = wire.make(grad.at[block_of(kind, w - 1, core)], buffer, WT, 1, at[0], at[0])
        down = wire.make(grad.at[block_of(kind, 0, core)], buffer, WT, w - 2, at[0], at[0])
        inner = (shard == 1) | (shard == 2)
        record[kind] += [
            Maybe(shard == 0, up).start(),
            Maybe(shard == w - 1, down).start(),
            Maybe(jnp.logical_not(inner), found[1]).start(),
            Maybe(shard != w - 1, found[0]).start(),
            Maybe(shard != 0, found[2]).start(),
        ]
        arriving = wire.make(buffer, buffer, WT, lax.rem(shard + 1, w), at[0], at[0])
        return found, arriving

    def relay(layer, kind, moving):
        found, arriving = moving
        if not line:
            return
        grad, buffer = (r.gout, r.relay_o) if kind == OUT else (r.gw, r.relay_w)
        rows_here = kept(kind)

        @pl.when((shard == 1) | (shard == 2))
        def _():
            arriving.wait_recv()
            at_rows, at_lanes = block_of(kind, lax.rem(shard + 2, w), core)

            def add(at):
                mine = pl.ds(pl.multiple_of(at_rows.start + at.start, TILE), TILE)
                there = pl.ds(pl.multiple_of(rows_here.start + at.start, TILE), TILE)
                total = grad[mine, at_lanes].astype(F32) + buffer[layer, there, :].astype(F32)
                grad[mine, at_lanes] = total.astype(BF)

            rows_loop(rows_here.stop - rows_here.start, add)
            found[1].start()

        record[kind].append(Maybe((shard == 1) | (shard == 2), found[1]))

    def to_plane(layer, kind, moving):
        grad, _, z, result, _ = buffers(kind)
        copies, _ = moving
        if line:
            pl.when(shard != 0)(copies[0].wait_recv)
            copies[1].wait_recv()
            pl.when(shard != w - 1)(copies[2].wait_recv)
        else:
            for copy in copies:
                copy.wait_recv()
        at_rows, at_lanes = block_of(kind, shard, core)
        here_rows = kept(kind)

        def add(at):
            mine = pl.ds(pl.multiple_of(at_rows.start + at.start, TILE), TILE)
            there = pl.ds(pl.multiple_of(here_rows.start + at.start, TILE), TILE)
            total = grad[mine, at_lanes].astype(F32)
            for k in range(w - 1):
                total = total + z[layer, k, there, :].astype(F32)
            z[layer, 1, there, :] = total.astype(BF)

        def add_end(at, near):
            mine = pl.ds(pl.multiple_of(at_rows.start + at.start, TILE), TILE)
            there = pl.ds(pl.multiple_of(here_rows.start + at.start, TILE), TILE)
            total = grad[mine, at_lanes].astype(F32)
            total = total + z[layer, 1, there, :].astype(F32) + z[layer, near, there, :].astype(F32)
            z[layer, 1, there, :] = total.astype(BF)

        count = here_rows.stop - here_rows.start
        if line:

            @pl.when(shard == 0)
            def _():
                rows_loop(count, lambda at: add_end(at, 2))

            @pl.when(shard == w - 1)
            def _():
                rows_loop(count, lambda at: add_end(at, 0))

            @pl.when((shard == 1) | (shard == 2))
            def _():
                rows_loop(count, add)
        else:
            rows_loop(count, add)
        block, target = z.at[layer, 1, here_rows], result.at[layer, here, here_rows]
        found = [put(block, target, SEQ, lax.rem(here + k, n)) for k in range(1, n)]
        return found, mover.put(block, target)

    def landed(kind, *arrivals):
        _, _, _, result, target = buffers(kind)
        for found, own in arrivals:
            for copy in found:
                copy.wait_recv()
            own.wait()
        return put(result.at[sibling, :, kept(kind)], target.at[:, kept(kind)], SECTION, sibling)

    def done(copies):
        for copy in copies:
            copy.wait()

    arrived = {}
    for layer in (1, 0):
        conv = r.packs.at[layer, :, 0:CX]
        head = r.packs.at[layer, :, CX : CX + 128]
        wide = r.packs.at[layer, :, CX + 128 : gain_at]
        g_conv = r.sm.at[layer, :, 0:CX]
        g_head = r.sm.at[layer, :, CX : CX + 128]
        g_wide = r.sm.at[layer, :, CX + 128 : gain_at]
        g_gain = r.sm.at[layer, :, gain_at : gain_at + D]
        done(first)

        def d_normed(lanes):
            r.xc[:, lanes] = dot(r.gb[...], r.of[lanes, :], 1, 1)

        column_tiles(0, G, d_normed)
        gate_backward(
            G, r.proj, r.mixed, r.xc, r.stats, wide, r.dy, g_wide
        )

        def out_rows(t, carry):
            at = pl.ds(pl.multiple_of(t * 128, 128), 128)
            r.gout[at, :] = dot(r.mixed[:, at], r.gb[...], 0, 0).astype(BF)
            return carry

        def in_rows(first, last):
            def step(t, carry):
                at = pl.ds(pl.multiple_of(t * 128, 128), 128)
                r.gw[at, :] = dot(r.proj[:, at], r.n[...], 0, 0).astype(BF)
                return carry

            lax.fori_loop(first // 128, last // 128, step, 0)

        ready(OUT)
        lax.fori_loop(0, G // 128, out_rows, 0)
        out_sib = to_sibling(layer, OUT)
        done(later)
        ready(GATE)
        in_rows(0, G)
        gate_sib = to_sibling(layer, GATE)
        out_z = to_shards(layer, OUT, out_sib)
        gate_z = to_shards(layer, GATE, gate_sib)
        if layer == 0:
            arrived[1, REST] = to_plane(1, REST, rest_z)
        scan_backward(
            G, r.proj, r.dy, r.yp, r.st, conv, head, wide, r.sel, g_wide, g_conv, g_head,
            r.pad, r.xc, r.dts, r.dstate,
        )
        relay(layer, OUT, out_z)
        relay(layer, GATE, gate_z)
        if layer == 1:
            first = load(0, (r.of_i, r.of), (r.mixed_i, r.mixed))
            later = load(0, (r.yp_i, r.yp), (r.st_i, r.st))

        def in_product(block):
            at = aligned(block * rows, rows)

            def tile(lanes):
                r.part[block, :, lanes] = dot(r.proj[at, :], r.wf[:, lanes], 1, 0).astype(BF)

            column_tiles(0, D, tile)

        summing = []
        for k in range(1, n):
            peer = lax.rem(here + k, n)
            in_product(peer)
            summing.append(wire.put(r.part.at[peer], arrivals.at[k - 1], SEQ, peer))
        in_product(here)
        if layer == 1:
            later += load(0, (r.wf_i, r.wf))
        ready(REST)
        in_rows(G, NC)
        if layer == 1:
            first += load(0, (r.proj_i, r.proj))
            later += load(0, (r.n_i, r.n))
        rest_sib = to_sibling(layer, REST)
        rest_z = to_shards(layer, REST, rest_sib)
        done(summing)
        if arrivals is not r.got:
            done(
                [
                    mover.put(arrivals.at[k - 1], r.part.at[lax.rem(here + k, n)])
                    for k in range(1, n)
                ]
            )

        def finish(at):
            if arrivals is r.got:
                d_in = total_of(n, r.part, r.got, at)
            else:
                d_in = r.part[0, at, :].astype(F32)
                for k in range(1, n):
                    d_in = d_in + r.part[k, at, :].astype(F32)
            h = r.h1[at, :] if layer == 1 else r.h0[at, :]
            above = r.cot[at, :] if layer == 1 else r.grads[1, at, :]
            inv = lax.rsqrt(jnp.mean(h * h, axis=1, keepdims=True) + EPSILON)
            normed = h * inv
            g_gain[0:1, :] += jnp.sum(d_in * normed, axis=0, keepdims=True)
            d_s = d_in * r.packs[layer, 0:1, gain_at:]
            d_h = above + inv * (d_s - normed * jnp.mean(d_s * normed, axis=1, keepdims=True))
            r.grads[layer, at, :] = d_h
            if layer == 1:
                out = d_h.astype(BF)
                whole = pl.ds(pl.multiple_of(here * rows + at.start, TILE), TILE)
                r.gb[whole, :] = out
                dots = jnp.sum(out.astype(F32) * r.pout[at, :], axis=1, keepdims=True)
                r.mdots[at, :] = jnp.broadcast_to(dots * (1.0 / INNER), (TILE, 128))

        rows_loop(rows, finish)
        if layer == 1:
            r.stats[here] = r.own_stat[...]
            r.stats[here, 1:2, :] = r.mdots[...].T[0:1, :]
            own = aligned(here * rows, rows)
            gathering = []
            for k in range(1, n):
                peer = lax.rem(here + k, n)
                gathering.append(put(r.gb.at[own], r.gb.at[own], SEQ, peer))
                gathering.append(put(r.stats.at[here], r.stats.at[here], SEQ, peer))
            relay(1, REST, rest_z)
            arrived[1, OUT] = to_plane(1, OUT, out_z)
            arrived[1, GATE] = to_plane(1, GATE, gate_z)
            for copy in gathering:
                copy.wait_recv()
    ends = [put(r.grads.at[sibling], r.ig.at[core], SECTION, sibling)]
    ends.append(put(r.sm.at[sibling], r.sm_sib, SECTION, sibling))
    local_grad = mover.put(r.grads.at[core], r.ig.at[core])
    relay(0, REST, rest_z)
    arrived[0, OUT] = to_plane(0, OUT, out_z)
    arrived[0, GATE] = to_plane(0, GATE, gate_z)
    ends[1].wait_recv()
    r.sm_own[...] = r.sm[core] + r.sm_sib[...]
    sums = [
        put(r.sm_own, r.sm_z.at[k - 1], WT, lax.rem(shard + k, w)) for k in range(1, w)
    ]
    for copy in sums:
        copy.wait_recv()
    total = r.sm_own[...]
    for k in range(w - 1):
        total = total + r.sm_z[k]
    r.small[here] = total
    sums = [
        put(r.small.at[here], r.small.at[here], SEQ, lax.rem(here + k, n))
        for k in range(1, n)
    ]
    ends.append(landed(OUT, arrived[1, OUT], arrived[0, OUT]))
    ends.append(landed(GATE, arrived[1, GATE], arrived[0, GATE]))
    arrived[0, REST] = to_plane(0, REST, rest_z)
    ends.append(landed(REST, arrived[1, REST], arrived[0, REST]))
    ends[0].wait_recv()
    for copy in ends[2:] + sums:
        copy.wait_recv()
    local_grad.wait()
    for kind in KINDS:
        ready(kind)
    for copy in open_sends:
        copy.wait_send()


def backward_call(g, n, w, fwd, tokens, cotangent):
    rows = tokens.shape[2]
    L, G, NC, CX = rows * n, g.G, g.NC, g.CX
    PK = CX + 128 + G + D
    S = jax.ShapeDtypeStruct
    o_half, lanes_of = G // (2 * w), D // w
    spill = n > 8
    outs = BackwardOuts(
        ig=S((2, rows, D), F32),
        gi=S((2, n, g.half, lanes_of), BF),
        go=S((2, n, o_half, D), BF),
        gi_sib=S((n, g.half, lanes_of), BF),
        go_sib=S((n, o_half, D), BF),
        small=S((n, 8, PK), F32),
        far=S((n - 1, rows, D) if spill else (8, 128), BF),
    )
    scratch = [
        S((2, 8, PK), F32), S((NC, D), BF), S((G, D), BF), S((L, D), BF), S((L, NC), BF), S((L, G), BF),
        S((L, G), F32), S((L // Q, STATE, G), F32), S((L, D), BF), S((n, 8, 128), F32), S((rows, D), F32),
        S((rows, D), F32), S((rows, D), F32), S((rows, D), F32),
        S((L, G), BF), S((8 + L, 128), F32), S((L, CX), F32), S((L, 128), F32), S((STATE, G), F32),
        S((n, rows, D), BF), S((1 if spill else n - 1, rows, D), BF), S((8, 128), F32), S((rows, 128), F32), S((2, rows, D), F32),
        S((NC, D), BF), S((G, D), BF), S((g.half, D), BF), S((G // 2, D), BF),
        S((2, w - 1, g.half, lanes_of), BF),
        S((2, w - 1, o_half, D), BF), S((2, g.half, lanes_of), BF), S((2, o_half, D), BF), S((2, 8, PK), F32), S((8, PK), F32), S((w - 1, 8, PK), F32), S((8, PK), F32),
        S((128, 128), BF),
    ]
    remote = 2 * (3 * (w + w + n - 1) + n - 1) + 2 * (n - 1) + 5 + (w - 1) + (n - 1)
    args = [
        fwd.packs_o, fwd.wf_o, fwd.of_o, fwd.n_o, fwd.proj_o, fwd.mixed_o, fwd.yp_o, fwd.st_o,
        fwd.gb_o, fwd.stats, fwd.stat0, fwd.pout, fwd.h1, tokens, cotangent,
    ]
    results = pl.pallas_call(
        functools.partial(backward_kernel, g, n, w, rows),
        out_shape=list(outs),
        in_specs=[ANY] * len(args),
        out_specs=[VM, ANY, ANY, ANY, ANY, VM, ANY],
        scratch_shapes=[pltpu.VMEM(s.shape, s.dtype) for s in scratch]
        + [
            pltpu.SemaphoreType.DMA((remote,)),
            pltpu.SemaphoreType.DMA((remote,)),
            pltpu.SemaphoreType.DMA((36 + 2 * n,)),
            pltpu.SemaphoreType.REGULAR((3,)),
        ],
        compiler_params=pltpu.CompilerParams(
            collective_id=1, has_side_effects=True, vmem_limit_bytes=BACKWARD_VMEM
        ),
        name="backward",
    )(*args)
    return BackwardOuts(*results)


def pack_kernel(g, win, conv_ref, bias_ref, dtb_ref, a_ref, skip_ref, gate_ref, norm_ref, pack_ref):
    here = lax.axis_index(SEQ)
    G, width = g.G, g.run_heads * HEAD_DIM
    start = here * width
    base = pl.multiple_of(start // 128 * 128, 128)
    from_ids = lax.broadcasted_iota(jnp.int32, (win, G), 0)
    to_ids = lax.broadcasted_iota(jnp.int32, (win, G), 1)
    exact = lax.Precision.HIGHEST

    def take(ref, rows):
        total = jnp.zeros((rows, G), F32)
        for run in range(g.runs):
            window = ref[0:rows, pl.ds(pl.multiple_of(base + run * (INNER // g.runs), 128), win)]
            inside = (to_ids >= run * width) & (to_ids < (run + 1) * width)
            pick = one_hot(inside & (from_ids == to_ids - run * width + (start - base)))
            total = total + dot(window, pick, 1, 0, exact)
        return total

    head_from = lax.broadcasted_iota(jnp.int32, (HEADS, 128), 0)
    head_to = lax.broadcasted_iota(jnp.int32, (HEADS, 128), 1)
    head_pick = one_hot((head_from == head_of(g, here, head_to)) & (head_to < g.heads))
    wide_from = lax.broadcasted_iota(jnp.int32, (HEADS, G), 0)
    wide_to = lax.broadcasted_iota(jnp.int32, (HEADS, G), 1)
    wide_pick = (wide_from == head_of(g, here, wide_to // HEAD_DIM)) & (wide_to < g.chans)
    head_at, wide_at, gain_at = g.CX, g.CX + 128, g.CX + 128 + G
    pack_ref[...] = jnp.zeros_like(pack_ref)
    pack_ref[0:KERNEL, 0:G] = take(conv_ref, KERNEL)
    pack_ref[4:5, 0:G] = take(bias_ref, 1)
    pack_ref[0:KERNEL, G:head_at] = conv_ref[:, INNER:]
    pack_ref[4:5, G:head_at] = bias_ref[:, INNER:]
    pack_ref[0:1, head_at:wide_at] = dot(dtb_ref[...], head_pick, 1, 0, exact)
    pack_ref[1:2, head_at:wide_at] = dot(-jnp.exp(a_ref[...]), head_pick, 1, 0, exact)
    pack_ref[0:1, wide_at:gain_at] = take(gate_ref, 1)
    pack_ref[1:2, wide_at:gain_at] = dot(skip_ref[...], one_hot(wide_pick), 1, 0, exact)
    pack_ref[0:1, gain_at:] = norm_ref[...]


def pack_call(g, *small):
    win = -(-(g.run_heads * HEAD_DIM + 64) // 128) * 128
    return pl.pallas_call(
        functools.partial(pack_kernel, g, win),
        out_shape=jax.ShapeDtypeStruct((8, g.CX + 128 + g.G + D), F32),
        in_specs=[VM] * len(small),
        out_specs=VM,
        compiler_params=pltpu.CompilerParams(vmem_limit_bytes=SMALL_VMEM),
        name="pack",
    )(*small)


def halves_of_heads(g, ref_of, column_at, head):
    parts = []
    for h in (head, head + 1):
        stride = HEADS // g.runs
        group = h % stride // g.run_heads
        local_head = h // stride * g.run_heads + h % g.run_heads
        value = ref_of(group, slice(column_at + local_head // 2 * 128, column_at + local_head // 2 * 128 + 128))
        parts.append(value if local_head % 2 == h % 2 else pltpu.roll(value, HEAD_DIM, 1))
    lanes = lax.broadcasted_iota(jnp.int32, parts[0].shape, 1)
    return jnp.where(lanes < HEAD_DIM, parts[0], parts[1])


def layout_kernel(g, own_ref, sib_ref, small_ref, g_in_ref, norm_ref, conv_ref, bias_ref, dtb_ref, a_ref, skip_ref, gate_ref):
    n, G = g.n_seq, g.G
    first_core = lax.axis_index(SECTION) == 0

    def copy(groups, kind_at, half_at, half_rows, source, target, size):
        done = 0
        while done < size:
            half, offset = divmod(source + done, half_rows)
            count = min(size - done, half_rows - offset)
            at = slice(half_at + offset, half_at + offset + count)
            total = None
            for group in groups:
                own, sib = own_ref[0, group, at, :], sib_ref[group, at, :]
                value = (jnp.where(first_core, own, sib) if half == 0 else jnp.where(first_core, sib, own)).astype(F32)
                total = value if total is None else total + value
            g_in_ref[target + done : target + done + count, :] = total
            done += count

    width = g.run_heads * HEAD_DIM
    rest = (G, G // 2, g.rest // 2)
    everyone = range(n)
    for run in range(g.runs):
        for group in range(n):
            target = run * (INNER // g.runs) + group * width
            copy([group], 0, 0, G // 2, run * width, target, width)
            copy([group], *rest, run * width, INNER + target, width)
    copy(everyone, *rest, G, 2 * INNER, 2 * STATE)
    copy(everyone, *rest, G + 2 * STATE, 2 * INNER + 2 * STATE, HEADS)

    @pl.when(pl.program_id(0) == 0)
    def _():
        from_ids = lax.broadcasted_iota(jnp.int32, (128, HEADS), 0)
        to_ids = lax.broadcasted_iota(jnp.int32, (128, HEADS), 1)
        picks = [one_hot((to_ids == head_of(g, group, from_ids)) & (from_ids < g.heads)) for group in range(n)]
        exact = lax.Precision.HIGHEST
        head_at, wide_at, gain_at = g.CX, g.CX + 128, g.CX + 128 + G

        def small(group, columns):
            return small_ref[group, :, columns]

        for head in range(0, HEADS, 2):
            at = slice(head * HEAD_DIM, head * HEAD_DIM + 128)
            conv = halves_of_heads(g, small, 0, head)
            conv_ref[:, at] = conv[0:KERNEL]
            bias_ref[:, at] = conv[KERNEL : KERNEL + 1]
            gate_ref[:, at] = halves_of_heads(g, small, wide_at, head)[0:1]
        conv = small(0, slice(G, head_at))
        norm = small(0, slice(gain_at, gain_at + D))
        for group in range(1, n):
            conv = conv + small(group, slice(G, head_at))
            norm = norm + small(group, slice(gain_at, gain_at + D))
        conv_ref[:, INNER:] = conv[0:KERNEL]
        bias_ref[:, INNER:] = conv[KERNEL : KERNEL + 1]
        norm_ref[...] = norm[0:1]
        heads = jnp.zeros((8, HEADS), F32)
        skips = jnp.zeros((8, HEADS), F32)
        wide_from = lax.broadcasted_iota(jnp.int32, (G, HEADS), 0)
        wide_to = lax.broadcasted_iota(jnp.int32, (G, HEADS), 1)
        for group in range(n):
            heads = heads + dot(small(group, slice(head_at, wide_at)), picks[group], 1, 0, exact)
            pick = (wide_to == head_of(g, group, wide_from // HEAD_DIM)) & (wide_from < g.chans)
            skips = skips + dot(small(group, slice(wide_at, gain_at)), one_hot(pick), 1, 0, exact)
        dtb_ref[...] = heads[0:1]
        a_ref[...] = heads[1:2]
        skip_ref[...] = skips[1:2]


def layout_call(g, core, gi, gi_sib, small):
    _, n, half, lanes = gi.shape
    PK = small.shape[2]
    columns = 2 * INNER + 2 * STATE + HEADS
    S = jax.ShapeDtypeStruct
    shapes = (
        S((columns, lanes), F32), S((1, D), F32), S((KERNEL, CONV), F32), S((1, CONV), F32), S((1, HEADS), F32),
        S((1, HEADS), F32), S((1, HEADS), F32), S((1, INNER), F32),
    )
    return pl.pallas_call(
        lambda core_ref, *refs: layout_kernel(g, *refs),
        grid_spec=pltpu.PrefetchScalarGridSpec(
            num_scalar_prefetch=1,
            grid=(lanes // 128,),
            in_specs=[
                pl.BlockSpec((1, n, half, 128), lambda t, c: (c[0], 0, 0, t)),
                pl.BlockSpec((n, half, 128), lambda t, c: (0, 0, t)),
                pl.BlockSpec((n, 8, PK), lambda t, c: (0, 0, 0)),
            ],
            out_specs=[pl.BlockSpec((columns, 128), lambda t, c: (0, t))]
            + [pl.BlockSpec(s.shape, lambda t, c: (0, 0)) for s in shapes[1:]],
        ),
        out_shape=shapes,
        compiler_params=pltpu.CompilerParams(vmem_limit_bytes=SMALL_VMEM),
        name="layout",
    )(core, gi, gi_sib, small)


def widen_kernel(core_ref, own_ref, sib_ref, out_ref):
    mine = pl.program_id(0) == core_ref[0]
    out_ref[...] = jnp.where(mine, own_ref[...], sib_ref[...][None]).astype(F32).reshape(out_ref.shape)


def widen_call(core, go, go_sib):
    _, n, size, columns = go.shape
    return pl.pallas_call(
        widen_kernel,
        grid_spec=pltpu.PrefetchScalarGridSpec(
            num_scalar_prefetch=1,
            grid=(2, n),
            in_specs=[
                pl.BlockSpec((1, 1, size, columns), lambda h, t, c: (c[0], t, 0, 0)),
                pl.BlockSpec((1, size, columns), lambda h, t, c: (t, 0, 0)),
            ],
            out_specs=pl.BlockSpec((1, 1, size, columns), lambda h, t, c: (t, h, 0, 0)),
        ),
        out_shape=jax.ShapeDtypeStruct((n, 2, size, columns), F32),
        compiler_params=pltpu.CompilerParams(vmem_limit_bytes=SMALL_VMEM),
        name="widen",
    )(core, go, go_sib)


def local(
    tokens, cotangent, norm_gain, w_in, conv_w, conv_b, dt_bias, a_log, skip_d, gate_gain, w_out
):
    n_seq, n_wt = lax.axis_size(SEQ), lax.axis_size(WT)
    here = lax.axis_index(SEQ)
    group = Group(n_seq, n_wt)
    core = lax.axis_index(SECTION).reshape(1)
    G = group.G

    pack = pack_call(
        group, conv_w[0], conv_b, dt_bias, a_log, skip_d, gate_gain, norm_gain
    )
    w_src = jnp.swapaxes(w_in[0], 0, 1)
    if group.runs == n_wt:
        o_src = w_out[0]
    else:
        o_src = lax.all_gather(w_out[0], WT, axis=0, tiled=True)
        o_src = lax.dynamic_slice_in_dim(o_src, here * group.chans, group.chans, 0)
        o_src = jnp.pad(o_src, ((0, G - group.chans), (0, 0)))
    fwd = forward_call(group, n_seq, n_wt, tokens, cotangent, pack, w_src, o_src)
    bwd = backward_call(group, n_seq, n_wt, fwd, tokens, cotangent)
    g_in, g_norm, g_conv, g_bias, g_dtb, g_a, g_skip, g_gate = layout_call(
        group, core, bwd.gi, bwd.gi_sib, bwd.small
    )
    g_out = widen_call(core, bwd.go, bwd.go_sib)
    if group.runs == n_wt:
        g_out = g_out.reshape(INNER // n_wt, D)
    else:
        g_out = g_out.astype(BF).reshape(n_seq, G // n_wt, D)
        g_out = lax.all_gather(g_out, WT, axis=1, tiled=True)[:, : group.chans].reshape(INNER, D)
        mine = INNER // n_wt
        g_out = lax.dynamic_slice_in_dim(g_out, lax.axis_index(WT) * mine, mine, 0).astype(F32)
    return (
        fwd.sec[None, :, None],
        bwd.ig[None, :, None],
        g_norm,
        jnp.swapaxes(g_in, 0, 1)[None],
        g_conv[None],
        g_bias,
        g_dtb,
        g_a,
        g_skip,
        g_gate,
        g_out[None],
    )


def solution(mesh):
    placed = (
        P(None, WT, SEQ, None),
        P(None, WT, SEQ, None),
        P(SECTION, None),
        P(SECTION, WT, None),
        P(SECTION, None, None),
        P(SECTION, None),
        P(SECTION, None),
        P(SECTION, None),
        P(SECTION, None),
        P(SECTION, None),
        P(SECTION, WT, None),
    )
    return jax.shard_map(
        local,
        mesh=mesh,
        in_specs=placed,
        out_specs=(
            P(SECTION, None, WT, SEQ, None),
            P(SECTION, None, WT, SEQ, None),
            P(SECTION, None),
            P(SECTION, WT, None),
            P(SECTION, None, None),
            P(SECTION, None),
            P(SECTION, None),
            P(SECTION, None),
            P(SECTION, None),
            P(SECTION, None),
            P(SECTION, WT, None),
        ),
        check_vma=False,
    )
```

```python
import functools
from typing import Any, NamedTuple

import jax
import jax.numpy as jnp
from jax import lax
from jax.experimental import pallas as pl
from jax.experimental.pallas import tpu as pltpu
from jax.sharding import PartitionSpec as P

D = 1536
HEADS = 48
HEAD_DIM = 64
STATE = 128
KERNEL = 4
INNER = 3072
CONV = 3328
EPSILON = 1e-05

Q = 128
F32 = jnp.float32
BF = jnp.bfloat16
SEQ, WT, SECTION = "seq", "wt", "section"
FORWARD_VMEM = 56 * 2**20
BACKWARD_VMEM = 62 * 2**20
SMALL_VMEM = 60 * 2**20
MESH = pl.DeviceIdType.MESH
VM = pl.BlockSpec(memory_space=pltpu.VMEM)
ANY = pl.BlockSpec(memory_space=pl.ANY)
TILE = 16


def dot(a, b, ca, cb, precision=None):
    return lax.dot_general(a, b, (((ca,), (cb,)), ((), ())), precision=precision, preferred_element_type=F32)

def sigmoid(x):
    return 1.0 / (1.0 + jnp.exp(-x))

def softplus(x):
    return jnp.maximum(x, 0.0) + jnp.log1p(jnp.exp(-jnp.abs(x)))

def lane_mask(rows):
    return lax.broadcasted_iota(jnp.int32, (rows, 128), 1) < HEAD_DIM

def spread(cols, pair, mask):
    a = jnp.broadcast_to(cols[:, 2 * pair : 2 * pair + 1], mask.shape)
    b = jnp.broadcast_to(cols[:, 2 * pair + 1 : 2 * pair + 2], mask.shape)
    return jnp.where(mask, a, b)

def split_pair(u, mask):
    zero = jnp.zeros_like(u)
    return jnp.concatenate([jnp.where(mask, u, zero), jnp.where(mask, zero, u)], axis=0)

def conv_tile(proj_ref, cw_ref, pad, proj_at, conv_at, rows):
    pad[0:8, :] = jnp.zeros((8, 128), F32)
    pad[8 : 8 + rows, :] = proj_ref[:, pl.ds(proj_at, 128)].astype(F32)
    pre = jnp.broadcast_to(cw_ref[4:5, pl.ds(conv_at, 128)], (rows, 128))
    for k in range(KERNEL):
        pre = pre + cw_ref[k : k + 1, pl.ds(conv_at, 128)] * pad[5 + k : 5 + k + rows, :]
    return pre

def step_inputs(proj_ref, at, hp_ref, sel_ref, dt_at):
    return dot(proj_ref[at, dt_at : dt_at + 128], sel_ref[...], 1, 0) + hp_ref[0:1, :]

def chunk_factors(dt, hp_ref):
    rate = dt * hp_ref[1:2, :]
    rows = lax.broadcasted_iota(jnp.int32, (Q, Q), 0)
    cols = lax.broadcasted_iota(jnp.int32, (Q, Q), 1)
    tri = (rows >= cols).astype(F32)
    cum = dot(tri, rate, 1, 0, lax.Precision.HIGHEST)
    return rate, cum, rows >= cols

def decay_pair(cum, cum_t, causal, pair):
    parts = []
    for h in (2 * pair, 2 * pair + 1):
        diff = jnp.broadcast_to(cum[:, h : h + 1], (Q, Q)) - jnp.broadcast_to(cum_t[h : h + 1, :], (Q, Q))
        parts.append(jnp.exp(jnp.where(causal, diff, -1e30)))
    return jnp.concatenate(parts, axis=1)

def scan_forward(G, proj_ref, cw_ref, hp_ref, gw_ref, sel_ref, mixed_ref, yp_ref, st_ref, pad, xc, dts, state):
    L = proj_ref.shape[0]

    def conv(tile, carry):
        lanes = pl.ds(pl.multiple_of(tile * 128, 128), 128)
        pre = conv_tile(proj_ref, cw_ref, pad, pl.multiple_of(G + tile * 128, 128), lanes.start, L)
        xc[:, lanes] = pre * sigmoid(pre)
        return carry

    lax.fori_loop(0, (G + 2 * STATE) // 128, conv, 0)
    dt_at = 2 * G + 2 * STATE
    dts[...] = softplus(step_inputs(proj_ref, slice(0, L), hp_ref, sel_ref, dt_at))
    state[...] = jnp.zeros_like(state)
    mask = lane_mask(Q)

    def chunk(c, _):
        at = pl.ds(pl.multiple_of(c * Q, Q), Q)
        dt = dts[at, :]
        rate, cum, causal = chunk_factors(dt, hp_ref)
        cum_t = cum.T
        last = cum[Q - 1 : Q, :]
        e_cum = jnp.exp(cum)
        tail = jnp.exp(last - cum) * dt
        e_last = jnp.broadcast_to(jnp.exp(last), (8, 128))
        b = xc[at, G : G + STATE].astype(BF)
        cc = xc[at, G + STATE : G + 2 * STATE].astype(BF)
        scores = dot(cc, b, 1, 1)
        scores2 = jnp.concatenate([scores, scores], axis=1)
        for p in range(G // 128):
            lanes = slice(p * 128, p * 128 + 128)
            x = xc[at, lanes]
            u = (x * spread(dt, p, mask)).astype(BF)
            m = (scores2 * decay_pair(cum, cum_t, causal, p)).astype(BF)
            before = state[:, lanes]
            st_ref[c, :, lanes] = before
            y = dot(m, split_pair(u, mask), 1, 0)
            y = y + dot(cc, before.astype(BF), 1, 0) * spread(e_cum, p, mask)
            yp_ref[at, lanes] = y
            after = dot(b, (x * spread(tail, p, mask)).astype(BF), 0, 0)
            state[:, lanes] = before * spread(e_last, p, mask[0:8])[0:1, :] + after
            mixed_ref[at, lanes] = (y + gw_ref[1:2, lanes] * x).astype(BF)
        return 0

    lax.fori_loop(0, L // Q, chunk, 0)


def gate_forward(G, proj_ref, gw_ref, mixed_ref, vg_ref, ssq_ref):
    def chunk(c, _):
        at = pl.ds(pl.multiple_of(c * Q, Q), Q)
        ssq = jnp.zeros((Q, 1), F32)
        for p in range(G // 128):
            lanes = slice(p * 128, p * 128 + 128)
            gate = proj_ref[at, lanes].astype(F32)
            v = mixed_ref[at, lanes].astype(F32) * (gate * sigmoid(gate))
            vg_ref[at, lanes] = (v * gw_ref[0:1, lanes]).astype(BF)
            ssq = ssq + jnp.sum(v * v, axis=1, keepdims=True)
        ssq_ref[c] = jnp.broadcast_to(ssq, (Q, 128)).T[0:8, :]
        return 0

    lax.fori_loop(0, proj_ref.shape[0] // Q, chunk, 0)


def gate_backward(G, proj_ref, mixed_ref, dn_ref, sc_ref, gw_ref, dy_ref, gg_ref):
    gg_ref[...] = jnp.zeros_like(gg_ref)

    def chunk(c, _):
        at = pl.ds(pl.multiple_of(c * Q, Q), Q)
        sc = jnp.concatenate([sc_ref[c], jnp.zeros((Q - 8, 128), F32)], axis=0).T
        inv2 = jnp.broadcast_to(sc[:, 0:1], (Q, 128))
        mdot = jnp.broadcast_to(sc[:, 1:2], (Q, 128))
        for p in range(G // 128):
            lanes = slice(p * 128, p * 128 + 128)
            gate = proj_ref[at, lanes].astype(F32)
            sig = sigmoid(gate)
            act = gate * sig
            mixed = mixed_ref[at, lanes].astype(F32)
            n2 = mixed * act * inv2
            mixed_ref[at, lanes] = (n2 * gw_ref[0:1, lanes]).astype(BF)
            dn = dn_ref[at, lanes]
            gg_ref[0:1, lanes] += jnp.sum(dn * n2, axis=0, keepdims=True)
            d_v = inv2 * (dn * gw_ref[0:1, lanes] - n2 * mdot)
            dy_ref[at, lanes] = (d_v * act).astype(BF)
            proj_ref[at, lanes] = (d_v * mixed * (sig * (1.0 + gate * (1.0 - sig)))).astype(BF)
        return 0

    lax.fori_loop(0, proj_ref.shape[0] // Q, chunk, 0)


def scan_backward(G, proj_ref, dy_ref, yp_ref, st_ref, cw_ref, hp_ref, gw_ref, sel_ref, gg_ref, gc_ref, gh_ref,
                  pad, xc, dts, dstate, serve):
    L = proj_ref.shape[0]
    nb = L // Q
    mask = lane_mask(Q)

    def conv(tile, carry):
        lanes = pl.ds(pl.multiple_of(tile * 128, 128), 128)
        pre = conv_tile(proj_ref, cw_ref, pad, pl.multiple_of(G + tile * 128, 128), lanes.start, L)
        xc[:, lanes] = pre * sigmoid(pre)
        return carry

    lax.fori_loop(0, (G + 2 * STATE) // 128, conv, 0)
    dt_at = 2 * G + 2 * STATE
    dts[...] = softplus(step_inputs(proj_ref, slice(0, L), hp_ref, sel_ref, dt_at))
    dstate[...] = jnp.zeros_like(dstate)
    gh_ref[...] = jnp.zeros_like(gh_ref)

    def chunk(step, _):
        c = nb - 1 - step
        pl.when(step == nb // 4)(serve)
        at = pl.ds(pl.multiple_of(c * Q, Q), Q)
        dt = dts[at, :]
        rate, cum, causal = chunk_factors(dt, hp_ref)
        cum_t = cum.T
        last = cum[Q - 1 : Q, :]
        e_cum = jnp.exp(cum)
        tail = jnp.exp(last - cum)
        e_last = jnp.broadcast_to(jnp.exp(last), (8, 128))
        b = xc[at, G : G + STATE].astype(BF)
        cc = xc[at, G + STATE : G + 2 * STATE].astype(BF)
        scores = dot(cc, b, 1, 1)
        scores2 = jnp.concatenate([scores, scores], axis=1)
        d_scores = jnp.zeros((Q, Q), F32)
        d_b = jnp.zeros((Q, STATE), F32)
        d_c = jnp.zeros((Q, STATE), F32)
        d_cum = jnp.zeros((Q, 128), F32)
        d_dt = jnp.zeros((Q, 128), F32)
        d_last = jnp.zeros((8, 128), F32)
        lane_ids = lax.broadcasted_iota(jnp.int32, (Q, 128), 1)
        for p in range(G // 128):
            lanes = slice(p * 128, p * 128 + 128)
            dyb = dy_ref[at, lanes]
            d_y = dyb.astype(F32)
            x = xc[at, lanes]
            dt_x = spread(dt, p, mask)
            u = (x * dt_x).astype(BF)
            u2 = split_pair(u, mask)
            uf = u.astype(F32)
            dec = decay_pair(cum, cum_t, causal, p)
            m = (scores2 * dec).astype(BF)
            dm = dot(dyb, u2, 1, 1) * dec
            d_scores = d_scores + dm[:, :Q] + dm[:, Q:]
            both = dot(m, dyb, 0, 0)
            du = jnp.where(mask, both[:Q], both[Q:])
            tail_x = spread(tail, p, mask)
            before = st_ref[c, :, lanes]
            after = dstate[:, lanes]
            afterb = after.astype(BF)
            du_out = tail_x * dot(b, afterb, 1, 0)
            du = du + du_out
            dye = (d_y * spread(e_cum, p, mask)).astype(BF)
            d_c = d_c + dot(dye, before.astype(BF), 1, 1)
            d_b = d_b + dot((uf * tail_x).astype(BF), afterb, 1, 1)
            e_last_x = spread(e_last, p, mask[0:8])
            dstate[:, lanes] = after * e_last_x[0:1, :] + dot(cc, dye, 0, 0)
            z3 = jnp.sum(uf * du_out, axis=0, keepdims=True) + e_last_x[0:1, :] * jnp.sum(before * after, axis=0, keepdims=True)
            z1 = d_y * yp_ref[at, lanes] - uf * du
            z2 = x * du
            zero = jnp.zeros_like(z1)
            for half, h in ((True, 2 * p), (False, 2 * p + 1)):
                keep = mask if half else jnp.logical_not(mask)
                here = lane_ids == h
                d_cum = jnp.where(here, jnp.sum(jnp.where(keep, z1, zero), axis=1, keepdims=True), d_cum)
                d_dt = jnp.where(here, jnp.sum(jnp.where(keep, z2, zero), axis=1, keepdims=True), d_dt)
                s3 = jnp.sum(jnp.where(keep[0:8], jnp.broadcast_to(z3, (8, 128)), 0.0), axis=1, keepdims=True)
                d_last = jnp.where(here[0:8], s3, d_last)
            xc[at, lanes] = dt_x * du + gw_ref[1:2, lanes] * d_y
            gg_ref[1:2, lanes] += jnp.sum(d_y * x, axis=0, keepdims=True)
        dsb = d_scores.astype(BF)
        xc[at, G : G + STATE] = d_b + dot(dsb, cc, 0, 0)
        xc[at, G + STATE : G + 2 * STATE] = d_c + dot(dsb, b, 1, 0)
        rows = lax.broadcasted_iota(jnp.int32, (Q, Q), 0)
        cols = lax.broadcasted_iota(jnp.int32, (Q, Q), 1)
        upper = (rows <= cols).astype(F32)
        d_rate = dot(upper, d_cum, 1, 0, lax.Precision.HIGHEST) + d_last[0:1, :]
        d_step = d_dt + d_rate * hp_ref[1:2, :]
        d_raw = d_step * sigmoid(step_inputs(proj_ref, at, hp_ref, sel_ref, dt_at))
        proj_ref[at, dt_at : dt_at + 128] = dot(d_raw.astype(BF), sel_ref[...], 1, 1).astype(BF)
        gh_ref[0:1, :] += jnp.sum(d_raw, axis=0, keepdims=True)
        gh_ref[1:2, :] += jnp.sum(d_rate * rate, axis=0, keepdims=True)
        return 0

    lax.fori_loop(0, nb, chunk, 0)

    gc_ref[...] = jnp.zeros_like(gc_ref)

    def conv_back(tile, carry):
        lanes = pl.ds(pl.multiple_of(tile * 128, 128), 128)
        proj_at = pl.multiple_of(G + tile * 128, 128)
        pre = conv_tile(proj_ref, cw_ref, pad, proj_at, lanes.start, L)
        sig = sigmoid(pre)
        d_pre = xc[:, lanes] * (sig * (1.0 + pre * (1.0 - sig)))
        for k in range(KERNEL):
            gc_ref[k : k + 1, lanes] = jnp.sum(d_pre * pad[5 + k : 5 + k + L, :], axis=0, keepdims=True)
        gc_ref[4:5, lanes] = jnp.sum(d_pre, axis=0, keepdims=True)
        pad[0:L, :] = d_pre
        pad[L : L + 8, :] = jnp.zeros((8, 128), F32)
        d_in = cw_ref[3:4, lanes] * d_pre
        for k in range(KERNEL - 1):
            d_in = d_in + cw_ref[k : k + 1, lanes] * pad[3 - k : 3 - k + L, :]
        proj_ref[:, pl.ds(proj_at, 128)] = d_in.astype(BF)
        return carry

    lax.fori_loop(0, (G + 2 * STATE) // 128, conv_back, 0)


def column(row):
    return jnp.broadcast_to(row, (128, 128)).T


def rows_loop(rows, body):
    def step(r, carry):
        body(pl.ds(pl.multiple_of(r * TILE, TILE), TILE))
        return carry

    lax.fori_loop(0, rows // TILE, step, 0)


def total_of(n, part_ref, got, at):
    total = part_ref[lax.axis_index(SEQ), at, :].astype(F32)
    for k in range(n - 1):
        total = total + got[k, at, :].astype(F32)
    return total


class Group:
    def __init__(self, n_seq, n_wt):
        self.n_seq = n_seq
        self.heads = HEADS // n_seq
        self.runs = n_wt if HEADS % (n_seq * n_wt) == 0 else 1
        self.run_heads = self.heads // self.runs
        self.chans = self.heads * HEAD_DIM
        self.G = -(-self.chans // 128) * 128
        self.CX = self.G + 2 * STATE
        self.NC = 2 * self.G + 2 * STATE + 128
        self.rest = self.G + 2 * STATE + 64
        self.half = (self.G + self.rest) // 2


def head_of(g, here, local_head):
    stride = HEADS // g.runs
    run = local_head // g.run_heads
    return run * stride + here * g.run_heads + (local_head - run * g.run_heads)


def one_hot(found):
    return jnp.where(found, 1.0, 0.0)


def step_select(g, here):
    from_ids = lax.broadcasted_iota(jnp.int32, (128, 128), 0)
    to_ids = lax.broadcasted_iota(jnp.int32, (128, 128), 1)
    return one_hot((from_ids == head_of(g, here, to_ids)) & (to_ids < g.heads))


OUT, GATE, REST = KINDS = range(3)


class Wire:
    def __init__(self, send_sems, recv_sems):
        self.send_sems, self.recv_sems, self.used = send_sems, recv_sems, 0

    def reserve(self):
        self.used += 1
        return self.used - 1

    def make(self, src, dst, axis, peer, at_send, at_recv):
        return pltpu.make_async_remote_copy(
            src, dst, self.send_sems.at[at_send], self.recv_sems.at[at_recv],
            device_id={axis: peer}, device_id_type=MESH,
        )

    def put(self, src, dst, axis, peer):
        at = self.reserve()
        copy = self.make(src, dst, axis, peer, at, at)
        copy.start()
        return copy


class Maybe:
    def __init__(self, condition, copy):
        self.condition, self.copy = condition, copy

    def start(self):
        pl.when(self.condition)(self.copy.start)
        return self

    def wait_send(self):
        pl.when(self.condition)(self.copy.wait_send)


class PlaneGather:
    def __init__(self, put, n, here, source, block):
        self.put, self.block, self.plane = put, block, n == 4
        mine = block(here, None)
        if not self.plane:
            self.copies = [put(source, mine, SEQ, lax.rem(here + k, n)) for k in range(1, n)]
            return
        self.x = here + 1 - 2 * lax.rem(here, 2)
        self.y = lax.rem(here + 2, 4)
        self.copies = [put(source, mine, SEQ, self.x), put(source, mine, SEQ, self.y)]

    def forward(self):
        if self.plane:
            for copy, group, half, peer in (
                (self.copies[0], self.x, 0, self.y),
                (self.copies[1], self.y, 1, self.x),
            ):
                copy.wait_recv()
                part = self.block(group, half)
                self.copies.append(self.put(part, part, SEQ, peer))

    def wait_recv(self):
        for copy in self.copies[2:] if self.plane else self.copies:
            copy.wait_recv()

    def wait_send(self):
        for copy in self.copies:
            copy.wait_send()


class Mover:
    def __init__(self, sems):
        self.sems, self.used = sems, 0

    def put(self, src, dst):
        copy = pltpu.make_async_copy(src, dst, self.sems.at[self.used])
        copy.start()
        self.used += 1
        return copy


def meet_all(axes):
    barrier = pltpu.get_barrier_semaphore()
    count = 0
    for axis, n in axes:
        me = lax.axis_index(axis)
        for k in range(1, n):
            pl.semaphore_signal(
                barrier, inc=1, device_id={axis: lax.rem(me + k, n)}, device_id_type=MESH
            )
        count += n - 1
    pl.semaphore_wait(barrier, count)


def column_tiles(first, last, body):
    whole = (last - first) // 256

    def step(t, carry):
        body(pl.ds(pl.multiple_of(first + t * 256, 128), 256))
        return carry

    lax.fori_loop(0, whole, step, 0)
    if first + whole * 256 < last:
        body(slice(first + whole * 256, last))


class ForwardOuts(NamedTuple):
    sec: Any
    pout: Any
    stat0: Any
    h1: Any
    gb_o: Any
    stats: Any
    packs_o: Any
    wf_o: Any
    of_o: Any
    n_o: Any
    proj_o: Any
    mixed_o: Any
    yp_o: Any
    st_o: Any


class ForwardRefs(NamedTuple):
    tokens: Any
    cotangent: Any
    conv_w: Any
    conv_b: Any
    dt_bias: Any
    a_log: Any
    skip_d: Any
    gate_gain: Any
    norm_gain: Any
    w_src: Any
    o_src: Any
    sec: Any
    pout: Any
    stat0: Any
    h1: Any
    gb_o: Any
    stats: Any
    packs_o: Any
    wf_o: Any
    of_o: Any
    n_o: Any
    proj_o: Any
    mixed_o: Any
    yp_o: Any
    st_o: Any
    h0: Any
    cot: Any
    packs: Any
    wf: Any
    of: Any
    normed: Any
    proj: Any
    mixed: Any
    yp: Any
    st: Any
    pad: Any
    xc: Any
    dts: Any
    state: Any
    vg: Any
    ssq: Any
    part: Any
    got: Any
    got_stat: Any
    hbuf: Any
    own_stat: Any
    cols: Any
    mdots: Any
    sel: Any
    pack: Any
    ss: Any
    rs: Any
    ls: Any


def forward_kernel(g, n, w, rows, *refs):
    r = ForwardRefs(*refs)
    G, NC = g.G, g.NC
    core, here, shard = lax.axis_index(SECTION), lax.axis_index(SEQ), lax.axis_index(WT)
    sibling = 1 - core
    wire, mover = Wire(r.ss, r.rs), Mover(r.ls)
    wf, of, packs = r.wf, r.of, r.packs
    sends, saves = [], []

    def aligned(at, size):
        return pl.ds(pl.multiple_of(at, 16), size)

    def put(src, dst, axis, peer):
        copy = wire.put(src, dst, axis, peer)
        sends.append(copy)
        return copy

    for layer in range(2):
        for first, last in ((g.chans, G), (G + g.chans, 2 * G), (2 * G + 2 * STATE + HEADS, NC)):
            if first < last:
                wf[layer, first:last, :] = jnp.zeros((last - first, D), BF)
    r.sel[...] = step_select(g, here).astype(BF)
    pack_small(g, here, r.conv_w, r.conv_b, r.dt_bias, r.a_log, r.skip_d, r.gate_gain, r.norm_gain, r.pack)
    meet_all(((SEQ, n), (WT, w), (SECTION, 2)))
    o_rows = G // w
    lanes_of = D // w
    mine_o = aligned(shard * o_rows, o_rows)
    piece = here if g.runs == w else shard
    o_own = r.o_src.at[aligned(piece * o_rows, o_rows)]
    mine_lanes = pl.ds(pl.multiple_of(shard * lanes_of, 128), lanes_of)
    width = g.run_heads * HEAD_DIM
    runs = []
    for kind_at, source_at in ((0, 0), (G, INNER)):
        for run in range(g.runs):
            source = source_at + run * (INNER // g.runs) + here * width
            runs.append((source, kind_at + run * width, width))
    runs.append((2 * INNER, 2 * G, 2 * STATE))
    runs.append((2 * INNER + 2 * STATE, 2 * G + 2 * STATE, HEADS))
    siblings = [put(r.pack, packs.at[core], SECTION, sibling)]
    locals_ = [
        mover.put(r.pack, packs.at[core]),
        mover.put(o_own, of.at[core, mine_o]),
        mover.put(r.tokens.at[core, 0], r.h0),
        mover.put(r.cotangent.at[core, 0], r.cot),
    ]
    for source, target, size in runs:
        taken = r.w_src.at[aligned(source, size)]
        siblings.append(put(taken, wf.at[core, target : target + size, mine_lanes], SECTION, sibling))
        locals_.append(mover.put(taken, wf.at[core, target : target + size, mine_lanes]))
    siblings.append(put(o_own, of.at[core, mine_o], SECTION, sibling))

    def part_of(layer, kind, at_shard, at_core):
        if kind == OUT:
            return of.at[layer, aligned(at_shard * o_rows + at_core * (o_rows // 2), o_rows // 2)]
        size = (G if kind == GATE else g.rest) // 2
        first = (0 if kind == GATE else G) + at_core * size
        lanes = pl.ds(pl.multiple_of(at_shard * lanes_of, 128), lanes_of)
        return wf.at[layer, aligned(first, size), lanes]

    line = w == 4

    def fetch(layer, kind):
        mine = part_of(layer, kind, shard, core)
        at = [wire.reserve() for _ in range(w)]
        copies = [
            wire.make(mine, mine, WT, lax.rem(shard + k, w), at[k], at[k]) for k in range(1, w)
        ]
        if line:
            copies[1].start()
            sends.append(copies[1])
            sends.append(Maybe(shard != w - 1, copies[0]).start())
            sends.append(Maybe(shard != 0, copies[2]).start())
        else:
            for copy in copies:
                copy.start()
            sends.extend(copies)
        return copies, at

    def far_part(fetched, layer, kind):
        if not line:
            return []
        at = fetched[1]
        fetched[0][1].wait_recv()
        block = part_of(layer, kind, lax.rem(shard + 2, w), core)
        up = wire.make(block, block, WT, lax.rem(shard + 1, w), at[0], at[3])
        down = wire.make(block, block, WT, lax.rem(shard + w - 1, w), at[0], at[1])
        sends.append(Maybe(shard == 2, up).start())
        sends.append(Maybe(shard == 1, down).start())
        return [put(block, block, SECTION, sibling)]

    def near_parts(fetched, layer, kind):
        found = []
        for k in (1, 3) if line else range(1, w):
            fetched[0][k - 1].wait_recv()
            block = part_of(layer, kind, lax.rem(shard + w - k, w), core)
            found.append(put(block, block, SECTION, sibling))
        return found

    def received(copies):
        for copy in copies:
            copy.wait_recv()

    own_rows = aligned(here * rows, rows)

    def gather(whole):
        def block(group, half):
            size = rows if half is None else rows // 2
            return whole.at[aligned(group * rows + (half or 0) * size, size)]

        return PlaneGather(wire.put, n, here, block(here, None), block)

    def save(source, target):
        saves.append(mover.put(source, target))

    def saved():
        while saves:
            saves.pop().wait()

    for copy in locals_:
        copy.wait()
    received(siblings)
    pending = fetch(0, REST)
    gain_at = g.CX + 128 + G

    def norm(at):
        h = r.h0[at, :]
        inv = lax.rsqrt(jnp.mean(h * h, axis=1, keepdims=True) + EPSILON)
        r.normed[pl.ds(pl.multiple_of(here * rows + at.start, TILE), TILE), :] = (
            h * inv * packs[0, 0:1, gain_at:]
        ).astype(BF)

    rows_loop(rows, norm)
    arriving = gather(r.normed)
    handed = far_part(pending, 0, REST)
    coming = [fetch(0, GATE), fetch(0, OUT)]
    arriving.forward()
    handed += near_parts(pending, 0, REST)

    for layer in range(2):
        proj, mixed, normed = r.proj, r.mixed, r.normed
        conv = packs.at[layer, :, 0 : g.CX]
        head = packs.at[layer, :, g.CX : g.CX + 128]
        wide = packs.at[layer, :, g.CX + 128 : gain_at]

        def project(lanes):
            proj[:, lanes] = dot(normed[...], wf[layer, lanes, :], 1, 1).astype(BF)

        arriving.wait_recv()
        received(handed)
        gathered = arriving
        column_tiles(G, NC, project)
        scan_forward(
            G, proj, conv, head, wide, r.sel, mixed, r.yp, r.st,
            r.pad, r.xc, r.dts, r.state,
        )
        save(mixed, r.mixed_o.at[layer])
        save(r.yp, r.yp_o.at[layer])
        save(r.st, r.st_o.at[layer])
        save(normed, r.n_o.at[layer])
        handed = far_part(coming[0], layer, GATE) + far_part(coming[1], layer, OUT)
        handed += near_parts(coming[0], layer, GATE) + near_parts(coming[1], layer, OUT)
        if layer == 0:
            pending = fetch(1, REST)
        received(handed)
        column_tiles(0, G, project)
        save(proj, r.proj_o.at[layer])
        gate_forward(G, proj, wide, mixed, r.vg, r.ssq)

        def out_product(block):
            at = aligned(block * rows, rows)

            def tile(lanes):
                r.part[block, :, lanes] = dot(r.vg[at, :], of[layer, :, lanes], 1, 0).astype(BF)

            column_tiles(0, D, tile)

        saved()
        gathered.wait_send()
        summing = []
        for k in range(1, n):
            peer = lax.rem(here + k, n)
            out_product(peer)
            summing.append(wire.put(r.part.at[peer], r.got.at[k - 1], SEQ, peer))
            summing.append(wire.put(r.ssq.at[peer], r.got_stat.at[k - 1], SEQ, peer))
        out_product(here)
        for copy in summing:
            copy.wait()
        if layer == 0:
            handed = far_part(pending, 1, REST)
            coming = [fetch(1, GATE), fetch(1, OUT)]
        ssq = r.ssq[here]
        for k in range(n - 1):
            ssq = ssq + r.got_stat[k]
        inv2 = lax.rsqrt(ssq * (1.0 / INNER) + EPSILON)
        r.own_stat[...] = inv2
        r.cols[...] = column(inv2[0:1, :])
        if layer == 0:
            r.stat0[...] = inv2

        def finish(at):
            pout = total_of(n, r.part, r.got, at) * r.cols[at, 0:1]
            whole = pl.ds(pl.multiple_of(here * rows + at.start, TILE), TILE)
            h_in = r.h0[at, :] if layer == 0 else r.hbuf[0, at, :]
            h = h_in + pout
            r.hbuf[layer, at, :] = h
            if layer == 0:
                r.pout[at, :] = pout
                r.h1[at, :] = h
                inv = lax.rsqrt(jnp.mean(h * h, axis=1, keepdims=True) + EPSILON)
                r.normed[whole, :] = (h * inv * packs[1, 0:1, gain_at:]).astype(BF)
            else:
                out = r.cot[at, :].astype(BF)
                dots = jnp.sum(out.astype(F32) * pout, axis=1, keepdims=True)
                r.mdots[at, :] = jnp.broadcast_to(dots * (1.0 / INNER), (TILE, 128))
                r.normed[whole, :] = out

        rows_loop(rows, finish)
        if layer == 0:
            arriving = gather(r.normed)
            arriving.forward()
            handed += near_parts(pending, 1, REST)
    r.stats[here] = r.own_stat[...]
    r.stats[here, 1:2, :] = r.mdots[...].T[0:1, :]
    last_rows = gather(r.normed)
    arriving = []
    for k in range(1, n):
        block = r.stats.at[here]
        arriving.append(put(block, block, SEQ, lax.rem(here + k, n)))
    arriving.append(put(r.hbuf.at[1 - core], r.sec.at[core], SECTION, sibling))
    save(r.hbuf.at[core], r.sec.at[core])
    save(packs, r.packs_o)
    save(wf, r.wf_o)
    save(of, r.of_o)
    last_rows.forward()
    last_rows.wait_recv()
    received(arriving)
    save(r.normed, r.gb_o)
    last_rows.wait_send()
    for copy in sends:
        copy.wait_send()
    saved()


def forward_call(g, n, w, tokens, cotangent, small, w_src, o_src):
    rows = tokens.shape[2]
    L, G, NC, CX, PK = rows * n, g.G, g.NC, g.CX, g.CX + 128 + g.G + D
    S = jax.ShapeDtypeStruct
    shapes = ForwardOuts(
        sec=S((2, rows, D), F32),
        pout=S((rows, D), F32),
        stat0=S((8, 128), F32),
        h1=S((rows, D), F32),
        gb_o=S((L, D), BF),
        stats=S((n, 8, 128), F32),
        packs_o=S((2, 8, PK), F32),
        wf_o=S((2, NC, D), BF),
        of_o=S((2, G, D), BF),
        n_o=S((2, L, D), BF),
        proj_o=S((2, L, NC), BF),
        mixed_o=S((2, L, G), BF),
        yp_o=S((2, L, G), F32),
        st_o=S((2, L // Q, STATE, G), F32),
    )
    scratch = [
        S((rows, D), F32), S((rows, D), F32), shapes.packs_o, shapes.wf_o, shapes.of_o, S((L, D), BF), S((L, NC), BF), S((L, G), BF),
        S((L, G), F32), S((L // Q, STATE, G), F32), S((8 + L, 128), F32), S((L, CX), F32), S((L, 128), F32), S((STATE, G), F32),
        S((L, G), BF), S((n, 8, 128), F32), S((n, rows, D), BF), S((n - 1, rows, D), BF), S((n - 1, 8, 128), F32),
        S((2, rows, D), F32), S((8, 128), F32), S((rows, 128), F32), S((rows, 128), F32),
        S((128, 128), BF), S((8, PK), F32),
    ]
    remote = 4 + 2 * g.runs + 6 * w + 6 * (w - 1) + 3 + 8 * (n - 1) + 2
    outs = pl.pallas_call(
        functools.partial(forward_kernel, g, n, w, rows),
        out_shape=list(shapes),
        in_specs=[ANY, ANY] + [VM] * len(small) + [ANY, ANY],
        out_specs=[VM] * 4 + [ANY, VM] + [ANY] * 8,
        scratch_shapes=[pltpu.VMEM(s.shape, s.dtype) for s in scratch]
        + [
            pltpu.SemaphoreType.DMA((remote,)),
            pltpu.SemaphoreType.DMA((remote,)),
            pltpu.SemaphoreType.DMA((22 + 2 * g.runs,)),
        ],
        compiler_params=pltpu.CompilerParams(
            collective_id=0, has_side_effects=True, vmem_limit_bytes=FORWARD_VMEM
        ),
        name="forward",
    )(tokens, cotangent, *small, w_src, o_src)
    return ForwardOuts(*outs)


class BackwardOuts(NamedTuple):
    ig: Any
    gi: Any
    go: Any
    gi_sib: Any
    go_sib: Any
    small: Any
    far: Any
    late: Any


class BackwardRefs(NamedTuple):
    packs_i: Any
    wf_i: Any
    of_i: Any
    n_i: Any
    proj_i: Any
    mixed_i: Any
    yp_i: Any
    st_i: Any
    gb_i: Any
    stats1_i: Any
    stat0_i: Any
    pout_i: Any
    h1_i: Any
    tokens_i: Any
    cotangent_i: Any
    ig: Any
    gi: Any
    go: Any
    gi_sib: Any
    go_sib: Any
    small: Any
    far: Any
    late: Any
    packs: Any
    wf: Any
    of: Any
    n: Any
    proj: Any
    mixed: Any
    yp: Any
    st: Any
    gb: Any
    stats: Any
    pout: Any
    h1: Any
    h0: Any
    cot: Any
    dy: Any
    pad: Any
    xc: Any
    dts: Any
    dstate: Any
    part: Any
    got: Any
    own_stat: Any
    mdots: Any
    grads: Any
    gw: Any
    gout: Any
    sib_w: Any
    sib_o: Any
    z_w: Any
    z_o: Any
    relay_w: Any
    relay_o: Any
    sm: Any
    sm_sib: Any
    sm_z: Any
    sm_own: Any
    sel: Any
    gain: Any
    gain_z: Any
    gain_sum: Any
    ss: Any
    rs: Any
    ls: Any
    free: Any


def backward_kernel(g, n, w, rows, *refs):
    r = BackwardRefs(*refs)
    G, NC, CX = g.G, g.NC, g.CX
    core, here, shard = lax.axis_index(SECTION), lax.axis_index(SEQ), lax.axis_index(WT)
    sibling = 1 - core
    wire, mover = Wire(r.ss, r.rs), Mover(r.ls)
    o_half, lanes_of = G // (2 * w), D // w
    gain_at = CX + 128 + G

    def aligned(at, size):
        return pl.ds(pl.multiple_of(at, 16), size)

    def load(layer, *pairs):
        return [mover.put(source.at[layer], target) for source, target in pairs]

    first = load(1, (r.of_i, r.of), (r.proj_i, r.proj), (r.mixed_i, r.mixed))
    first += [mover.put(r.packs_i, r.packs), mover.put(r.gb_i, r.gb), mover.put(r.stats1_i, r.stats)]
    later = load(1, (r.n_i, r.n), (r.yp_i, r.yp), (r.st_i, r.st), (r.wf_i, r.wf))
    later += [mover.put(r.pout_i, r.pout), mover.put(r.h1_i, r.h1), mover.put(r.stat0_i, r.own_stat)]
    later += [mover.put(r.tokens_i.at[core, 0], r.h0), mover.put(r.cotangent_i.at[core, 0], r.cot)]
    meet_all(((SEQ, n), (WT, w), (SECTION, 2)))
    r.sm[...] = jnp.zeros_like(r.sm)
    r.sel[...] = step_select(g, here).astype(BF)
    r.gain[here] = jnp.zeros((8, D), F32)
    open_sends, record = [], {}
    line = w == 4
    arrivals = r.got if r.got.shape[0] == n - 1 else r.far

    def put(src, dst, axis, peer):
        copy = wire.put(src, dst, axis, peer)
        open_sends.append(copy)
        return copy

    def rows_of(kind):
        return ((0, G), (0, G), (G, g.rest))[kind]

    def kept(kind):
        return (slice(0, G // (2 * w)), slice(0, G // 2), slice(G // 2, g.half))[kind]

    def buffers(kind):
        if kind == OUT:
            return r.gout, r.sib_o, r.z_o, r.go, r.go_sib
        return r.gw, r.sib_w, r.z_w, r.gi, r.gi_sib

    def block_of(kind, at_shard, at_core):
        if kind == OUT:
            return aligned((2 * at_shard + at_core) * o_half, o_half), slice(0, D)
        first, size = rows_of(kind)
        return (
            aligned(first + at_core * (size // 2), size // 2),
            pl.ds(pl.multiple_of(at_shard * lanes_of, 128), lanes_of),
        )

    def ready(kind):
        for copy in record.pop(kind, ()):
            copy.wait_send()

    def to_sibling(layer, kind):
        grad, sib, _, _, _ = buffers(kind)
        if layer == 0:
            pl.semaphore_wait(r.free.at[kind], 1)
        if kind == OUT:
            pairs = [
                (grad.at[block_of(kind, q, sibling)], sib.at[aligned(q * o_half, o_half)])
                for q in range(w)
            ]
        else:
            first, size = rows_of(kind)
            rows_there = aligned(first + sibling * (size // 2), size // 2)
            pairs = [(grad.at[rows_there], sib.at[kept(kind)])]
        copies = [wire.put(source, target, SECTION, sibling) for source, target in pairs]
        record[kind] = list(copies)
        return copies

    def to_shards(layer, kind, copies):
        grad, sib, z, _, _ = buffers(kind)
        for copy in copies:
            copy.wait_recv()
        if kind == OUT:
            per = o_half // TILE

            def places(t):
                q = t // per
                return (2 * q + core) * o_half + (t - q * per) * TILE, t * TILE

            steps = w * per
        else:
            first, size = rows_of(kind)
            steps = size // 2 // TILE

            def places(t):
                return first + core * (size // 2) + t * TILE, kept(kind).start + t * TILE

        def add(t, carry):
            mine, theirs = (pl.ds(pl.multiple_of(at, TILE), TILE) for at in places(t))
            grad[mine, :] = (grad[mine, :].astype(F32) + sib[theirs, :].astype(F32)).astype(BF)
            return carry

        lax.fori_loop(0, steps, add, 0)
        if layer == 1:
            pl.semaphore_signal(
                r.free.at[kind], inc=1, device_id={SECTION: sibling}, device_id_type=MESH
            )
        at = [wire.reserve() for _ in range(w)]
        found = []
        for k in range(1, w):
            peer = lax.rem(shard + k, w)
            source = grad.at[block_of(kind, peer, core)]
            found.append(wire.make(source, z.at[layer, k - 1, kept(kind)], WT, peer, at[k], at[k]))
        if not line:
            for copy in found:
                copy.start()
            record[kind] += found
            return found, None
        buffer = (r.relay_o if kind == OUT else r.relay_w).at[layer, kept(kind)]
        up = wire.make(grad.at[block_of(kind, w - 1, core)], buffer, WT, 1, at[0], at[0])
        down = wire.make(grad.at[block_of(kind, 0, core)], buffer, WT, w - 2, at[0], at[0])
        inner = (shard == 1) | (shard == 2)
        first = [
            Maybe(shard == 0, up),
            Maybe(shard == w - 1, down),
            Maybe(inner, found[0]),
            Maybe(inner, found[2]),
        ]
        others = [
            Maybe(jnp.logical_not(inner), found[1]),
            Maybe(shard == 0, found[0]),
            Maybe(shard == w - 1, found[2]),
        ]
        record[kind] += [*first, *others, Maybe(inner, found[1])]
        for copy in first:
            copy.start()
        waiting.extend(others)
        arriving = wire.make(buffer, buffer, WT, lax.rem(shard + 1, w), at[0], at[0])
        return found, arriving

    def relay(layer, kind, moving):
        found, arriving = moving
        if not line:
            return
        grad, buffer = (r.gout, r.relay_o) if kind == OUT else (r.gw, r.relay_w)
        rows_here = kept(kind)

        @pl.when((shard == 1) | (shard == 2))
        def _():
            arriving.wait_recv()
            at_rows, at_lanes = block_of(kind, lax.rem(shard + 2, w), core)

            def add(at):
                mine = pl.ds(pl.multiple_of(at_rows.start + at.start, TILE), TILE)
                there = pl.ds(pl.multiple_of(rows_here.start + at.start, TILE), TILE)
                total = grad[mine, at_lanes].astype(F32) + buffer[layer, there, :].astype(F32)
                grad[mine, at_lanes] = total.astype(BF)

            rows_loop(rows_here.stop - rows_here.start, add)
            found[1].start()

    def to_plane(layer, kind, moving):
        grad, _, z, result, _ = buffers(kind)
        copies, _ = moving
        if line:
            pl.when(shard != 0)(copies[0].wait_recv)
            copies[1].wait_recv()
            pl.when(shard != w - 1)(copies[2].wait_recv)
        else:
            for copy in copies:
                copy.wait_recv()
        at_rows, at_lanes = block_of(kind, shard, core)
        here_rows = kept(kind)

        def add(at):
            mine = pl.ds(pl.multiple_of(at_rows.start + at.start, TILE), TILE)
            there = pl.ds(pl.multiple_of(here_rows.start + at.start, TILE), TILE)
            total = grad[mine, at_lanes].astype(F32)
            for k in range(w - 1):
                total = total + z[layer, k, there, :].astype(F32)
            z[layer, 1, there, :] = total.astype(BF)

        def add_end(at, near):
            mine = pl.ds(pl.multiple_of(at_rows.start + at.start, TILE), TILE)
            there = pl.ds(pl.multiple_of(here_rows.start + at.start, TILE), TILE)
            total = grad[mine, at_lanes].astype(F32)
            total = total + z[layer, 1, there, :].astype(F32) + z[layer, near, there, :].astype(F32)
            z[layer, 1, there, :] = total.astype(BF)

        count = here_rows.stop - here_rows.start
        if line:

            @pl.when(shard == 0)
            def _():
                rows_loop(count, lambda at: add_end(at, 2))

            @pl.when(shard == w - 1)
            def _():
                rows_loop(count, lambda at: add_end(at, 0))

            @pl.when((shard == 1) | (shard == 2))
            def _():
                rows_loop(count, add)
        else:
            rows_loop(count, add)
        def target(group, half):
            size = here_rows.stop - here_rows.start
            if half is None:
                return result.at[layer, group, here_rows]
            first = here_rows.start + half * (size // 2)
            return result.at[layer, group, first : first + size // 2]

        block = z.at[layer, 1, here_rows]
        return PlaneGather(put, n, here, block, target), mover.put(block, target(here, None))

    def landed(kind, *arrivals):
        _, _, _, result, target = buffers(kind)
        for found, own in arrivals:
            found.wait_recv()
            own.wait()
        return put(result.at[sibling, :, kept(kind)], target.at[:, kept(kind)], SECTION, sibling)

    def done(copies):
        for copy in copies:
            copy.wait()

    arrived, waiting = {}, []
    for layer in (1, 0):
        conv = r.packs.at[layer, :, 0:CX]
        head = r.packs.at[layer, :, CX : CX + 128]
        wide = r.packs.at[layer, :, CX + 128 : gain_at]
        g_conv = r.sm.at[layer, :, 0:CX]
        g_head = r.sm.at[layer, :, CX : CX + 128]
        g_wide = r.sm.at[layer, :, CX + 128 : gain_at]
        g_gain = r.sm.at[layer, :, gain_at : gain_at + D] if layer == 1 else r.gain.at[here]
        done(first)

        def d_normed(lanes):
            r.xc[:, lanes] = dot(r.gb[...], r.of[lanes, :], 1, 1)

        column_tiles(0, G, d_normed)
        gate_backward(
            G, r.proj, r.mixed, r.xc, r.stats, wide, r.dy, g_wide
        )

        def out_rows(t, carry):
            at = pl.ds(pl.multiple_of(t * 128, 128), 128)
            r.gout[at, :] = dot(r.mixed[:, at], r.gb[...], 0, 0).astype(BF)
            return carry

        def in_rows(first, last):
            def step(t, carry):
                at = pl.ds(pl.multiple_of(t * 128, 128), 128)
                r.gw[at, :] = dot(r.proj[:, at], r.n[...], 0, 0).astype(BF)
                return carry

            lax.fori_loop(first // 128, last // 128, step, 0)

        ready(OUT)
        lax.fori_loop(0, G // 128, out_rows, 0)
        out_sib = to_sibling(layer, OUT)
        done(later)
        ready(GATE)
        in_rows(0, G)
        gate_sib = to_sibling(layer, GATE)
        out_z = to_shards(layer, OUT, out_sib)
        gate_z = to_shards(layer, GATE, gate_sib)
        if layer == 0:
            arrived[1, OUT][0].forward()
            arrived[1, GATE][0].forward()
            arrived[1, REST] = to_plane(1, REST, rest_z)

        def serve():
            for copy in waiting:
                copy.start()

        scan_backward(
            G, r.proj, r.dy, r.yp, r.st, conv, head, wide, r.sel, g_wide, g_conv, g_head,
            r.pad, r.xc, r.dts, r.dstate, serve,
        )
        waiting.clear()
        relay(layer, OUT, out_z)
        relay(layer, GATE, gate_z)
        if layer == 0:
            small_sib = put(r.sm.at[sibling], r.sm_sib, SECTION, sibling)
        if layer == 0:
            arrived[1, REST][0].forward()
            small_sib.wait_recv()
            r.sm_own[...] = r.sm[core] + r.sm_sib[...]
            small_z = [
                put(r.sm_own, r.sm_z.at[k - 1], WT, lax.rem(shard + k, w)) for k in range(1, w)
            ]
        if layer == 1:
            first = load(0, (r.of_i, r.of), (r.mixed_i, r.mixed))
            later = load(0, (r.yp_i, r.yp), (r.st_i, r.st))

        def in_product(block):
            at = aligned(block * rows, rows)

            def tile(lanes):
                r.part[block, :, lanes] = dot(r.proj[at, :], r.wf[:, lanes], 1, 0).astype(BF)

            column_tiles(0, D, tile)

        summing = []
        for k in range(1, n):
            peer = lax.rem(here + k, n)
            in_product(peer)
            summing.append(wire.put(r.part.at[peer], arrivals.at[k - 1], SEQ, peer))
        in_product(here)
        if layer == 1:
            later += load(0, (r.wf_i, r.wf))
        ready(REST)
        in_rows(G, NC)
        if layer == 1:
            first += load(0, (r.proj_i, r.proj))
            later += load(0, (r.n_i, r.n))
        rest_sib = to_sibling(layer, REST)
        rest_z = to_shards(layer, REST, rest_sib)
        done(summing)
        while waiting:
            waiting.pop(0).start()
        if arrivals is not r.got:
            done(
                [
                    mover.put(arrivals.at[k - 1], r.part.at[lax.rem(here + k, n)])
                    for k in range(1, n)
                ]
            )

        def finish(at):
            if arrivals is r.got:
                d_in = total_of(n, r.part, r.got, at)
            else:
                d_in = r.part[0, at, :].astype(F32)
                for k in range(1, n):
                    d_in = d_in + r.part[k, at, :].astype(F32)
            h = r.h1[at, :] if layer == 1 else r.h0[at, :]
            above = r.cot[at, :] if layer == 1 else r.grads[1, at, :]
            inv = lax.rsqrt(jnp.mean(h * h, axis=1, keepdims=True) + EPSILON)
            normed = h * inv
            g_gain[0:1, :] += jnp.sum(d_in * normed, axis=0, keepdims=True)
            d_s = d_in * r.packs[layer, 0:1, gain_at:]
            d_h = above + inv * (d_s - normed * jnp.mean(d_s * normed, axis=1, keepdims=True))
            r.grads[layer, at, :] = d_h
            if layer == 1:
                out = d_h.astype(BF)
                whole = pl.ds(pl.multiple_of(here * rows + at.start, TILE), TILE)
                r.gb[whole, :] = out
                dots = jnp.sum(out.astype(F32) * r.pout[at, :], axis=1, keepdims=True)
                r.mdots[at, :] = jnp.broadcast_to(dots * (1.0 / INNER), (TILE, 128))

        rows_loop(rows, finish)
        if layer == 1:
            r.stats[here] = r.own_stat[...]
            r.stats[here, 1:2, :] = r.mdots[...].T[0:1, :]
            own = aligned(here * rows, rows)
            gathering = []

            def rows_of_group(group, half):
                size = rows if half is None else rows // 2
                return r.gb.at[aligned(group * rows + (half or 0) * size, size)]

            grad_rows = PlaneGather(put, n, here, r.gb.at[own], rows_of_group)
            for k in range(1, n):
                peer = lax.rem(here + k, n)
                gathering.append(put(r.stats.at[here], r.stats.at[here], SEQ, peer))
            relay(1, REST, rest_z)
            grad_rows.forward()
            arrived[1, OUT] = to_plane(1, OUT, out_z)
            arrived[1, GATE] = to_plane(1, GATE, gate_z)
            grad_rows.wait_recv()
            for copy in gathering:
                copy.wait_recv()
    gains = []
    ends = [put(r.grads.at[sibling], r.ig.at[core], SECTION, sibling)]
    for k in range(1, n):
        gains.append(put(r.gain.at[here], r.gain.at[here], SEQ, lax.rem(here + k, n)))
    local_grad = mover.put(r.grads.at[core], r.ig.at[core])
    relay(0, REST, rest_z)
    arrived[0, OUT] = to_plane(0, OUT, out_z)
    arrived[0, GATE] = to_plane(0, GATE, gate_z)
    arrived[0, OUT][0].forward()
    arrived[0, GATE][0].forward()
    for copy in small_z:
        copy.wait_recv()
    total = r.sm_own[...]
    for k in range(w - 1):
        total = total + r.sm_z[k]
    r.small[here] = total
    sums = [
        put(r.small.at[here], r.small.at[here], SEQ, lax.rem(here + k, n)) for k in range(1, n)
    ]
    for copy in gains:
        copy.wait_recv()
    total = r.gain[0]
    for k in range(1, n):
        total = total + r.gain[k]
    r.gain_z[shard] = total
    gains = [
        put(r.gain_z.at[shard], r.gain_z.at[shard], WT, lax.rem(shard + k, w)) for k in range(1, w)
    ]
    arrived[0, REST] = to_plane(0, REST, rest_z)
    ends.append(landed(OUT, arrived[1, OUT], arrived[0, OUT]))
    ends.append(landed(GATE, arrived[1, GATE], arrived[0, GATE]))
    arrived[0, REST][0].forward()
    ends.append(landed(REST, arrived[1, REST], arrived[0, REST]))
    for copy in gains:
        copy.wait_recv()
    total = r.gain_z[0]
    for k in range(1, w):
        total = total + r.gain_z[k]
    r.gain_sum[core] = total
    ends.append(put(r.gain_sum.at[core], r.gain_sum.at[core], SECTION, sibling))
    for copy in ends + sums:
        copy.wait_recv()
    r.late[...] = r.gain_sum[0] + r.gain_sum[1]
    local_grad.wait()
    for kind in KINDS:
        ready(kind)
    for copy in open_sends:
        copy.wait_send()


def backward_call(g, n, w, fwd, tokens, cotangent):
    rows = tokens.shape[2]
    L, G, NC, CX = rows * n, g.G, g.NC, g.CX
    PK = CX + 128 + G + D
    S = jax.ShapeDtypeStruct
    o_half, lanes_of = G // (2 * w), D // w
    spill = n > 8
    outs = BackwardOuts(
        ig=S((2, rows, D), F32),
        gi=S((2, n, g.half, lanes_of), BF),
        go=S((2, n, o_half, D), BF),
        gi_sib=S((n, g.half, lanes_of), BF),
        go_sib=S((n, o_half, D), BF),
        small=S((n, 8, PK), F32),
        far=S((n - 1, rows, D) if spill else (8, 128), BF),
        late=S((8, D), F32),
    )
    scratch = [
        S((2, 8, PK), F32), S((NC, D), BF), S((G, D), BF), S((L, D), BF), S((L, NC), BF), S((L, G), BF),
        S((L, G), F32), S((L // Q, STATE, G), F32), S((L, D), BF), S((n, 8, 128), F32), S((rows, D), F32),
        S((rows, D), F32), S((rows, D), F32), S((rows, D), F32),
        S((L, G), BF), S((8 + L, 128), F32), S((L, CX), F32), S((L, 128), F32), S((STATE, G), F32),
        S((n, rows, D), BF), S((1 if spill else n - 1, rows, D), BF), S((8, 128), F32), S((rows, 128), F32), S((2, rows, D), F32),
        S((NC, D), BF), S((G, D), BF), S((g.half, D), BF), S((G // 2, D), BF),
        S((2, w - 1, g.half, lanes_of), BF),
        S((2, w - 1, o_half, D), BF), S((2, g.half, lanes_of), BF), S((2, o_half, D), BF), S((2, 8, PK), F32), S((8, PK), F32), S((w - 1, 8, PK), F32), S((8, PK), F32),
        S((128, 128), BF), S((n, 8, D), F32), S((w, 8, D), F32), S((2, 8, D), F32),
    ]
    remote = 2 * (3 * (w + w + n - 1) + n - 1) + 2 * (n - 1) + 6 + 2 * (w - 1) + 2 * (n - 1)
    args = [
        fwd.packs_o, fwd.wf_o, fwd.of_o, fwd.n_o, fwd.proj_o, fwd.mixed_o, fwd.yp_o, fwd.st_o,
        fwd.gb_o, fwd.stats, fwd.stat0, fwd.pout, fwd.h1, tokens, cotangent,
    ]
    results = pl.pallas_call(
        functools.partial(backward_kernel, g, n, w, rows),
        out_shape=list(outs),
        in_specs=[ANY] * len(args),
        out_specs=[VM, ANY, ANY, ANY, ANY, VM, ANY, VM],
        scratch_shapes=[pltpu.VMEM(s.shape, s.dtype) for s in scratch]
        + [
            pltpu.SemaphoreType.DMA((remote,)),
            pltpu.SemaphoreType.DMA((remote,)),
            pltpu.SemaphoreType.DMA((36 + 2 * n,)),
            pltpu.SemaphoreType.REGULAR((3,)),
        ],
        compiler_params=pltpu.CompilerParams(
            collective_id=1, has_side_effects=True, vmem_limit_bytes=BACKWARD_VMEM
        ),
        name="backward",
    )(*args)
    return BackwardOuts(*results)


def pack_small(g, here, conv_ref, bias_ref, dtb_ref, a_ref, skip_ref, gate_ref, norm_ref, pack_ref):
    G, width = g.G, g.run_heads * HEAD_DIM
    win = -(-(width + 64) // 128) * 128
    start = here * width
    base = pl.multiple_of(start // 128 * 128, 128)
    from_ids = lax.broadcasted_iota(jnp.int32, (win, G), 0)
    to_ids = lax.broadcasted_iota(jnp.int32, (win, G), 1)
    exact = lax.Precision.HIGHEST

    def take(ref, rows):
        total = jnp.zeros((rows, G), F32)
        for run in range(g.runs):
            window = ref[0:rows, pl.ds(pl.multiple_of(base + run * (INNER // g.runs), 128), win)]
            inside = (to_ids >= run * width) & (to_ids < (run + 1) * width)
            pick = one_hot(inside & (from_ids == to_ids - run * width + (start - base)))
            total = total + dot(window, pick, 1, 0, exact)
        return total

    head_from = lax.broadcasted_iota(jnp.int32, (HEADS, 128), 0)
    head_to = lax.broadcasted_iota(jnp.int32, (HEADS, 128), 1)
    head_pick = one_hot((head_from == head_of(g, here, head_to)) & (head_to < g.heads))
    wide_from = lax.broadcasted_iota(jnp.int32, (HEADS, G), 0)
    wide_to = lax.broadcasted_iota(jnp.int32, (HEADS, G), 1)
    wide_pick = (wide_from == head_of(g, here, wide_to // HEAD_DIM)) & (wide_to < g.chans)
    head_at, wide_at, gain_at = g.CX, g.CX + 128, g.CX + 128 + G
    pack_ref[...] = jnp.zeros_like(pack_ref)
    pack_ref[0:KERNEL, 0:G] = take(conv_ref, KERNEL)
    pack_ref[4:5, 0:G] = take(bias_ref, 1)
    pack_ref[0:KERNEL, G:head_at] = conv_ref[:, INNER:]
    pack_ref[4:5, G:head_at] = bias_ref[:, INNER:]
    pack_ref[0:1, head_at:wide_at] = dot(dtb_ref[...], head_pick, 1, 0, exact)
    pack_ref[1:2, head_at:wide_at] = dot(-jnp.exp(a_ref[...]), head_pick, 1, 0, exact)
    pack_ref[0:1, wide_at:gain_at] = take(gate_ref, 1)
    pack_ref[1:2, wide_at:gain_at] = dot(skip_ref[...], one_hot(wide_pick), 1, 0, exact)
    pack_ref[0:1, gain_at:] = norm_ref[...]


def halves_of_heads(g, ref_of, column_at, head):
    parts = []
    for h in (head, head + 1):
        stride = HEADS // g.runs
        group = h % stride // g.run_heads
        local_head = h // stride * g.run_heads + h % g.run_heads
        value = ref_of(group, slice(column_at + local_head // 2 * 128, column_at + local_head // 2 * 128 + 128))
        parts.append(value if local_head % 2 == h % 2 else pltpu.roll(value, HEAD_DIM, 1))
    lanes = lax.broadcasted_iota(jnp.int32, parts[0].shape, 1)
    return jnp.where(lanes < HEAD_DIM, parts[0], parts[1])


def layout_kernel(g, own_ref, sib_ref, own_out_ref, sib_out_ref, small_ref, late_ref, g_in_ref, g_out_ref, norm_ref, conv_ref, bias_ref, dtb_ref, a_ref, skip_ref, gate_ref):
    n, G = g.n_seq, g.G
    first_core = lax.axis_index(SECTION) == 0

    def copy(groups, kind_at, half_at, half_rows, source, target, size):
        done = 0
        while done < size:
            half, offset = divmod(source + done, half_rows)
            count = min(size - done, half_rows - offset)
            at = slice(half_at + offset, half_at + offset + count)
            total = None
            for group in groups:
                own, sib = own_ref[0, group, at, :], sib_ref[group, at, :]
                value = (jnp.where(first_core, own, sib) if half == 0 else jnp.where(first_core, sib, own)).astype(F32)
                total = value if total is None else total + value
            g_in_ref[target + done : target + done + count, :] = total
            done += count

    own, sib = own_out_ref[0].astype(F32), sib_out_ref[...].astype(F32)
    g_out_ref[:, 0] = jnp.where(first_core, own, sib)
    g_out_ref[:, 1] = jnp.where(first_core, sib, own)
    width = g.run_heads * HEAD_DIM
    rest = (G, G // 2, g.rest // 2)
    everyone = range(n)
    for run in range(g.runs):
        for group in range(n):
            target = run * (INNER // g.runs) + group * width
            copy([group], 0, 0, G // 2, run * width, target, width)
            copy([group], *rest, run * width, INNER + target, width)
    copy(everyone, *rest, G, 2 * INNER, 2 * STATE)
    copy(everyone, *rest, G + 2 * STATE, 2 * INNER + 2 * STATE, HEADS)

    @pl.when(pl.program_id(0) == 0)
    def _():
        from_ids = lax.broadcasted_iota(jnp.int32, (128, HEADS), 0)
        to_ids = lax.broadcasted_iota(jnp.int32, (128, HEADS), 1)
        picks = [one_hot((to_ids == head_of(g, group, from_ids)) & (from_ids < g.heads)) for group in range(n)]
        exact = lax.Precision.HIGHEST
        head_at, wide_at, gain_at = g.CX, g.CX + 128, g.CX + 128 + G

        def small(group, columns):
            return small_ref[group, :, columns]

        for head in range(0, HEADS, 2):
            at = slice(head * HEAD_DIM, head * HEAD_DIM + 128)
            conv = halves_of_heads(g, small, 0, head)
            conv_ref[:, at] = conv[0:KERNEL]
            bias_ref[:, at] = conv[KERNEL : KERNEL + 1]
            gate_ref[:, at] = halves_of_heads(g, small, wide_at, head)[0:1]
        conv = small(0, slice(G, head_at))
        norm = small(0, slice(gain_at, gain_at + D))
        for group in range(1, n):
            conv = conv + small(group, slice(G, head_at))
            norm = norm + small(group, slice(gain_at, gain_at + D))
        conv_ref[:, INNER:] = conv[0:KERNEL]
        bias_ref[:, INNER:] = conv[KERNEL : KERNEL + 1]
        norm_ref[...] = jnp.where(first_core, late_ref[0:1, :], norm[0:1])
        heads = jnp.zeros((8, HEADS), F32)
        skips = jnp.zeros((8, HEADS), F32)
        wide_from = lax.broadcasted_iota(jnp.int32, (G, HEADS), 0)
        wide_to = lax.broadcasted_iota(jnp.int32, (G, HEADS), 1)
        for group in range(n):
            heads = heads + dot(small(group, slice(head_at, wide_at)), picks[group], 1, 0, exact)
            pick = (wide_to == head_of(g, group, wide_from // HEAD_DIM)) & (wide_from < g.chans)
            skips = skips + dot(small(group, slice(wide_at, gain_at)), one_hot(pick), 1, 0, exact)
        dtb_ref[...] = heads[0:1]
        a_ref[...] = heads[1:2]
        skip_ref[...] = skips[1:2]


def layout_call(g, core, gi, gi_sib, go, go_sib, small, late):
    _, n, half, lanes = gi.shape
    out_half = go.shape[2]
    steps = lanes // 128
    out_lanes = D // steps
    PK = small.shape[2]
    columns = 2 * INNER + 2 * STATE + HEADS
    S = jax.ShapeDtypeStruct
    shapes = (
        S((columns, lanes), F32), S((n, 2, out_half, D), F32), S((1, D), F32), S((KERNEL, CONV), F32),
        S((1, CONV), F32), S((1, HEADS), F32), S((1, HEADS), F32), S((1, HEADS), F32), S((1, INNER), F32),
    )
    return pl.pallas_call(
        lambda core_ref, *refs: layout_kernel(g, *refs),
        grid_spec=pltpu.PrefetchScalarGridSpec(
            num_scalar_prefetch=1,
            grid=(steps,),
            in_specs=[
                pl.BlockSpec((1, n, half, 128), lambda t, c: (c[0], 0, 0, t)),
                pl.BlockSpec((n, half, 128), lambda t, c: (0, 0, t)),
                pl.BlockSpec((1, n, out_half, out_lanes), lambda t, c: (c[0], 0, 0, t)),
                pl.BlockSpec((n, out_half, out_lanes), lambda t, c: (0, 0, t)),
                pl.BlockSpec((n, 8, PK), lambda t, c: (0, 0, 0)),
                pl.BlockSpec((8, D), lambda t, c: (0, 0)),
            ],
            out_specs=[
                pl.BlockSpec((columns, 128), lambda t, c: (0, t)),
                pl.BlockSpec((n, 2, out_half, out_lanes), lambda t, c: (0, 0, 0, t)),
            ]
            + [pl.BlockSpec(s.shape, lambda t, c: (0, 0)) for s in shapes[2:]],
        ),
        out_shape=shapes,
        compiler_params=pltpu.CompilerParams(vmem_limit_bytes=SMALL_VMEM),
        name="layout",
    )(core, gi, gi_sib, go, go_sib, small, late)


def local(
    tokens, cotangent, norm_gain, w_in, conv_w, conv_b, dt_bias, a_log, skip_d, gate_gain, w_out
):
    n_seq, n_wt = lax.axis_size(SEQ), lax.axis_size(WT)
    here = lax.axis_index(SEQ)
    group = Group(n_seq, n_wt)
    core = lax.axis_index(SECTION).reshape(1)
    G = group.G

    small = (conv_w[0], conv_b, dt_bias, a_log, skip_d, gate_gain, norm_gain)
    w_src = jnp.swapaxes(w_in[0], 0, 1)
    if group.runs == n_wt:
        o_src = w_out[0]
    else:
        o_src = lax.all_gather(w_out[0], WT, axis=0, tiled=True)
        o_src = lax.dynamic_slice_in_dim(o_src, here * group.chans, group.chans, 0)
        o_src = jnp.pad(o_src, ((0, G - group.chans), (0, 0)))
    fwd = forward_call(group, n_seq, n_wt, tokens, cotangent, small, w_src, o_src)
    bwd = backward_call(group, n_seq, n_wt, fwd, tokens, cotangent)
    g_in, g_out, g_norm, g_conv, g_bias, g_dtb, g_a, g_skip, g_gate = layout_call(
        group, core, bwd.gi, bwd.gi_sib, bwd.go, bwd.go_sib, bwd.small, bwd.late
    )
    if group.runs == n_wt:
        g_out = g_out.reshape(INNER // n_wt, D)
    else:
        g_out = g_out.astype(BF).reshape(n_seq, G // n_wt, D)
        g_out = lax.all_gather(g_out, WT, axis=1, tiled=True)[:, : group.chans].reshape(INNER, D)
        mine = INNER // n_wt
        g_out = lax.dynamic_slice_in_dim(g_out, lax.axis_index(WT) * mine, mine, 0).astype(F32)
    return (
        fwd.sec[None, :, None],
        bwd.ig[None, :, None],
        g_norm,
        jnp.swapaxes(g_in, 0, 1)[None],
        g_conv[None],
        g_bias,
        g_dtb,
        g_a,
        g_skip,
        g_gate,
        g_out[None],
    )


def solution(mesh):
    placed = (
        P(None, WT, SEQ, None),
        P(None, WT, SEQ, None),
        P(SECTION, None),
        P(SECTION, WT, None),
        P(SECTION, None, None),
        P(SECTION, None),
        P(SECTION, None),
        P(SECTION, None),
        P(SECTION, None),
        P(SECTION, None),
        P(SECTION, WT, None),
    )
    return jax.shard_map(
        local,
        mesh=mesh,
        in_specs=placed,
        out_specs=(
            P(SECTION, None, WT, SEQ, None),
            P(SECTION, None, WT, SEQ, None),
            P(SECTION, None),
            P(SECTION, WT, None),
            P(SECTION, None, None),
            P(SECTION, None),
            P(SECTION, None),
            P(SECTION, None),
            P(SECTION, None),
            P(SECTION, None),
            P(SECTION, WT, None),
        ),
        check_vma=False,
    )
```

```python
import functools
from typing import Any, NamedTuple

import jax
import jax.numpy as jnp
from jax import lax
from jax.experimental import pallas as pl
from jax.experimental.pallas import tpu as pltpu
from jax.sharding import PartitionSpec as P

D = 1536
HEADS = 48
HEAD_DIM = 64
STATE = 128
KERNEL = 4
INNER = 3072
CONV = 3328
EPSILON = 1e-05

Q = 128
F32 = jnp.float32
BF = jnp.bfloat16
SEQ, WT, SECTION = "seq", "wt", "section"
FORWARD_VMEM = 56 * 2**20
BACKWARD_VMEM = 62 * 2**20
SMALL_VMEM = 60 * 2**20
MESH = pl.DeviceIdType.MESH
VM = pl.BlockSpec(memory_space=pltpu.VMEM)
ANY = pl.BlockSpec(memory_space=pl.ANY)
TILE = 16


def dot(a, b, ca, cb, precision=None):
    return lax.dot_general(a, b, (((ca,), (cb,)), ((), ())), precision=precision, preferred_element_type=F32)

def sigmoid(x):
    return 1.0 / (1.0 + jnp.exp(-x))

def softplus(x):
    return jnp.maximum(x, 0.0) + jnp.log1p(jnp.exp(-jnp.abs(x)))

def lane_mask(rows):
    return lax.broadcasted_iota(jnp.int32, (rows, 128), 1) < HEAD_DIM

def spread(cols, pair, mask):
    a = jnp.broadcast_to(cols[:, 2 * pair : 2 * pair + 1], mask.shape)
    b = jnp.broadcast_to(cols[:, 2 * pair + 1 : 2 * pair + 2], mask.shape)
    return jnp.where(mask, a, b)

def split_pair(u, mask):
    zero = jnp.zeros_like(u)
    return jnp.concatenate([jnp.where(mask, u, zero), jnp.where(mask, zero, u)], axis=0)

def conv_tile(proj_ref, cw_ref, pad, proj_at, conv_at, rows):
    pad[0:8, :] = jnp.zeros((8, 128), F32)
    pad[8 : 8 + rows, :] = proj_ref[:, pl.ds(proj_at, 128)].astype(F32)
    pre = jnp.broadcast_to(cw_ref[4:5, pl.ds(conv_at, 128)], (rows, 128))
    for k in range(KERNEL):
        pre = pre + cw_ref[k : k + 1, pl.ds(conv_at, 128)] * pad[5 + k : 5 + k + rows, :]
    return pre

def step_inputs(proj_ref, at, hp_ref, sel_ref, dt_at):
    return dot(proj_ref[at, dt_at : dt_at + 128], sel_ref[...], 1, 0) + hp_ref[0:1, :]

def chunk_factors(dt, hp_ref):
    rate = dt * hp_ref[1:2, :]
    rows = lax.broadcasted_iota(jnp.int32, (Q, Q), 0)
    cols = lax.broadcasted_iota(jnp.int32, (Q, Q), 1)
    tri = (rows >= cols).astype(F32)
    cum = dot(tri, rate, 1, 0, lax.Precision.HIGHEST)
    return rate, cum, rows >= cols

def decay_pair(cum, cum_t, causal, pair):
    parts = []
    for h in (2 * pair, 2 * pair + 1):
        diff = jnp.broadcast_to(cum[:, h : h + 1], (Q, Q)) - jnp.broadcast_to(cum_t[h : h + 1, :], (Q, Q))
        parts.append(jnp.exp(jnp.where(causal, diff, -1e30)))
    return jnp.concatenate(parts, axis=1)

def scan_forward(G, proj_ref, cw_ref, hp_ref, gw_ref, sel_ref, mixed_ref, yp_ref, st_ref, pad, xc, dts, state):
    L = proj_ref.shape[0]

    def conv(tile, carry):
        lanes = pl.ds(pl.multiple_of(tile * 128, 128), 128)
        pre = conv_tile(proj_ref, cw_ref, pad, pl.multiple_of(G + tile * 128, 128), lanes.start, L)
        xc[:, lanes] = pre * sigmoid(pre)
        return carry

    lax.fori_loop(0, (G + 2 * STATE) // 128, conv, 0)
    dt_at = 2 * G + 2 * STATE
    dts[...] = softplus(step_inputs(proj_ref, slice(0, L), hp_ref, sel_ref, dt_at))
    state[...] = jnp.zeros_like(state)
    mask = lane_mask(Q)

    def chunk(c, _):
        at = pl.ds(pl.multiple_of(c * Q, Q), Q)
        dt = dts[at, :]
        rate, cum, causal = chunk_factors(dt, hp_ref)
        cum_t = cum.T
        last = cum[Q - 1 : Q, :]
        e_cum = jnp.exp(cum)
        tail = jnp.exp(last - cum) * dt
        e_last = jnp.broadcast_to(jnp.exp(last), (8, 128))
        b = xc[at, G : G + STATE].astype(BF)
        cc = xc[at, G + STATE : G + 2 * STATE].astype(BF)
        scores = dot(cc, b, 1, 1)
        scores2 = jnp.concatenate([scores, scores], axis=1)
        for p in range(G // 128):
            lanes = slice(p * 128, p * 128 + 128)
            x = xc[at, lanes]
            u = (x * spread(dt, p, mask)).astype(BF)
            m = (scores2 * decay_pair(cum, cum_t, causal, p)).astype(BF)
            before = state[:, lanes]
            st_ref[c, :, lanes] = before
            y = dot(m, split_pair(u, mask), 1, 0)
            y = y + dot(cc, before.astype(BF), 1, 0) * spread(e_cum, p, mask)
            yp_ref[at, lanes] = y
            after = dot(b, (x * spread(tail, p, mask)).astype(BF), 0, 0)
            state[:, lanes] = before * spread(e_last, p, mask[0:8])[0:1, :] + after
            mixed_ref[at, lanes] = (y + gw_ref[1:2, lanes] * x).astype(BF)
        return 0

    lax.fori_loop(0, L // Q, chunk, 0)


def gate_forward(G, proj_ref, gw_ref, mixed_ref, vg_ref, ssq_ref):
    def chunk(c, _):
        at = pl.ds(pl.multiple_of(c * Q, Q), Q)
        ssq = jnp.zeros((Q, 1), F32)
        for p in range(G // 128):
            lanes = slice(p * 128, p * 128 + 128)
            gate = proj_ref[at, lanes].astype(F32)
            v = mixed_ref[at, lanes].astype(F32) * (gate * sigmoid(gate))
            vg_ref[at, lanes] = (v * gw_ref[0:1, lanes]).astype(BF)
            ssq = ssq + jnp.sum(v * v, axis=1, keepdims=True)
        ssq_ref[c] = jnp.broadcast_to(ssq, (Q, 128)).T[0:8, :]
        return 0

    lax.fori_loop(0, proj_ref.shape[0] // Q, chunk, 0)


def lane_sums(values, pick):
    high = values.astype(BF)
    low = (values - high.astype(F32)).astype(BF)
    return dot(high, pick, 1, 0) + dot(low, pick, 1, 0)


def gate_backward(G, proj_ref, mixed_ref, dn_ref, sc_ref, gw_ref, dy_ref, gg_ref):
    gg_ref[...] = jnp.zeros_like(gg_ref)

    def chunk(c, _):
        at = pl.ds(pl.multiple_of(c * Q, Q), Q)
        sc = jnp.concatenate([sc_ref[c], jnp.zeros((Q - 8, 128), F32)], axis=0).T
        inv2 = jnp.broadcast_to(sc[:, 0:1], (Q, 128))
        mdot = jnp.broadcast_to(sc[:, 1:2], (Q, 128))
        for p in range(G // 128):
            lanes = slice(p * 128, p * 128 + 128)
            gate = proj_ref[at, lanes].astype(F32)
            sig = sigmoid(gate)
            act = gate * sig
            mixed = mixed_ref[at, lanes].astype(F32)
            n2 = mixed * act * inv2
            mixed_ref[at, lanes] = (n2 * gw_ref[0:1, lanes]).astype(BF)
            dn = dn_ref[at, lanes]
            gg_ref[0:1, lanes] += jnp.sum(dn * n2, axis=0, keepdims=True)
            d_v = inv2 * (dn * gw_ref[0:1, lanes] - n2 * mdot)
            dy_ref[at, lanes] = (d_v * act).astype(BF)
            proj_ref[at, lanes] = (d_v * mixed * (sig * (1.0 + gate * (1.0 - sig)))).astype(BF)
        return 0

    lax.fori_loop(0, proj_ref.shape[0] // Q, chunk, 0)


def scan_backward(G, proj_ref, dy_ref, yp_ref, st_ref, cw_ref, hp_ref, gw_ref, sel_ref, gg_ref, gc_ref, gh_ref,
                  pad, xc, dts, dstate, serve):
    L = proj_ref.shape[0]
    nb = L // Q
    mask = lane_mask(Q)

    def conv(tile, carry):
        lanes = pl.ds(pl.multiple_of(tile * 128, 128), 128)
        pre = conv_tile(proj_ref, cw_ref, pad, pl.multiple_of(G + tile * 128, 128), lanes.start, L)
        xc[:, lanes] = pre * sigmoid(pre)
        return carry

    lax.fori_loop(0, (G + 2 * STATE) // 128, conv, 0)
    dt_at = 2 * G + 2 * STATE
    dts[...] = softplus(step_inputs(proj_ref, slice(0, L), hp_ref, sel_ref, dt_at))
    dstate[...] = jnp.zeros_like(dstate)
    gh_ref[...] = jnp.zeros_like(gh_ref)

    def chunk(step, _):
        c = nb - 1 - step
        pl.when(step == nb // 4)(serve)
        at = pl.ds(pl.multiple_of(c * Q, Q), Q)
        dt = dts[at, :]
        rate, cum, causal = chunk_factors(dt, hp_ref)
        cum_t = cum.T
        last = cum[Q - 1 : Q, :]
        e_cum = jnp.exp(cum)
        tail = jnp.exp(last - cum)
        e_last = jnp.broadcast_to(jnp.exp(last), (8, 128))
        b = xc[at, G : G + STATE].astype(BF)
        cc = xc[at, G + STATE : G + 2 * STATE].astype(BF)
        scores = dot(cc, b, 1, 1)
        scores2 = jnp.concatenate([scores, scores], axis=1)
        d_scores = jnp.zeros((Q, Q), F32)
        d_b = jnp.zeros((Q, STATE), F32)
        d_c = jnp.zeros((Q, STATE), F32)
        d_cum = jnp.zeros((Q, 128), F32)
        d_dt = jnp.zeros((Q, 128), F32)
        d_last = jnp.zeros((8, 128), F32)
        lane_ids = lax.broadcasted_iota(jnp.int32, (Q, 128), 1)
        row_ids = lax.broadcasted_iota(jnp.int32, (Q, 128), 0)
        for p in range(G // 128):
            lanes = slice(p * 128, p * 128 + 128)
            dyb = dy_ref[at, lanes]
            d_y = dyb.astype(F32)
            x = xc[at, lanes]
            dt_x = spread(dt, p, mask)
            u = (x * dt_x).astype(BF)
            u2 = split_pair(u, mask)
            uf = u.astype(F32)
            dec = decay_pair(cum, cum_t, causal, p)
            m = (scores2 * dec).astype(BF)
            dm = dot(dyb, u2, 1, 1) * dec
            d_scores = d_scores + dm[:, :Q] + dm[:, Q:]
            both = dot(m, dyb, 0, 0)
            du = jnp.where(mask, both[:Q], both[Q:])
            tail_x = spread(tail, p, mask)
            before = st_ref[c, :, lanes]
            after = dstate[:, lanes]
            afterb = after.astype(BF)
            du_out = tail_x * dot(b, afterb, 1, 0)
            du = du + du_out
            dye = (d_y * spread(e_cum, p, mask)).astype(BF)
            d_c = d_c + dot(dye, before.astype(BF), 1, 1)
            d_b = d_b + dot((uf * tail_x).astype(BF), afterb, 1, 1)
            e_last_x = spread(e_last, p, mask[0:8])
            dstate[:, lanes] = after * e_last_x[0:1, :] + dot(cc, dye, 0, 0)
            z3 = jnp.sum(uf * du_out, axis=0, keepdims=True) + e_last_x[0:1, :] * jnp.sum(before * after, axis=0, keepdims=True)
            z1 = d_y * yp_ref[at, lanes] - uf * du
            z2 = x * du
            pick = jnp.where(lane_ids == 2 * p + jnp.where(row_ids < HEAD_DIM, 0, 1), 1.0, 0.0).astype(BF)
            d_cum = d_cum + lane_sums(z1, pick)
            d_dt = d_dt + lane_sums(z2, pick)
            d_last = d_last + lane_sums(jnp.broadcast_to(z3, (8, 128)), pick)
            xc[at, lanes] = dt_x * du + gw_ref[1:2, lanes] * d_y
            gg_ref[1:2, lanes] += jnp.sum(d_y * x, axis=0, keepdims=True)
        dsb = d_scores.astype(BF)
        xc[at, G : G + STATE] = d_b + dot(dsb, cc, 0, 0)
        xc[at, G + STATE : G + 2 * STATE] = d_c + dot(dsb, b, 1, 0)
        rows = lax.broadcasted_iota(jnp.int32, (Q, Q), 0)
        cols = lax.broadcasted_iota(jnp.int32, (Q, Q), 1)
        upper = (rows <= cols).astype(F32)
        d_rate = dot(upper, d_cum, 1, 0, lax.Precision.HIGHEST) + d_last[0:1, :]
        d_step = d_dt + d_rate * hp_ref[1:2, :]
        d_raw = d_step * sigmoid(step_inputs(proj_ref, at, hp_ref, sel_ref, dt_at))
        proj_ref[at, dt_at : dt_at + 128] = dot(d_raw.astype(BF), sel_ref[...], 1, 1).astype(BF)
        gh_ref[0:1, :] += jnp.sum(d_raw, axis=0, keepdims=True)
        gh_ref[1:2, :] += jnp.sum(d_rate * rate, axis=0, keepdims=True)
        return 0

    lax.fori_loop(0, nb, chunk, 0)

    gc_ref[...] = jnp.zeros_like(gc_ref)

    def conv_back(tile, carry):
        lanes = pl.ds(pl.multiple_of(tile * 128, 128), 128)
        proj_at = pl.multiple_of(G + tile * 128, 128)
        pre = conv_tile(proj_ref, cw_ref, pad, proj_at, lanes.start, L)
        sig = sigmoid(pre)
        d_pre = xc[:, lanes] * (sig * (1.0 + pre * (1.0 - sig)))
        for k in range(KERNEL):
            gc_ref[k : k + 1, lanes] = jnp.sum(d_pre * pad[5 + k : 5 + k + L, :], axis=0, keepdims=True)
        gc_ref[4:5, lanes] = jnp.sum(d_pre, axis=0, keepdims=True)
        pad[0:L, :] = d_pre
        pad[L : L + 8, :] = jnp.zeros((8, 128), F32)
        d_in = cw_ref[3:4, lanes] * d_pre
        for k in range(KERNEL - 1):
            d_in = d_in + cw_ref[k : k + 1, lanes] * pad[3 - k : 3 - k + L, :]
        proj_ref[:, pl.ds(proj_at, 128)] = d_in.astype(BF)
        return carry

    lax.fori_loop(0, (G + 2 * STATE) // 128, conv_back, 0)


def column(row):
    return jnp.broadcast_to(row, (128, 128)).T


def rows_loop(rows, body):
    def step(r, carry):
        body(pl.ds(pl.multiple_of(r * TILE, TILE), TILE))
        return carry

    lax.fori_loop(0, rows // TILE, step, 0)


def total_of(n, part_ref, got, at):
    total = part_ref[lax.axis_index(SEQ), at, :].astype(F32)
    for k in range(n - 1):
        total = total + got[k, at, :].astype(F32)
    return total


class Group:
    def __init__(self, n_seq, n_wt):
        self.n_seq = n_seq
        self.heads = HEADS // n_seq
        self.runs = n_wt if HEADS % (n_seq * n_wt) == 0 else 1
        self.run_heads = self.heads // self.runs
        self.chans = self.heads * HEAD_DIM
        self.G = -(-self.chans // 128) * 128
        self.CX = self.G + 2 * STATE
        self.NC = 2 * self.G + 2 * STATE + 128
        self.rest = self.G + 2 * STATE + 64
        self.half = (self.G + self.rest) // 2


def head_of(g, here, local_head):
    stride = HEADS // g.runs
    run = local_head // g.run_heads
    return run * stride + here * g.run_heads + (local_head - run * g.run_heads)


def one_hot(found):
    return jnp.where(found, 1.0, 0.0)


def step_select(g, here):
    from_ids = lax.broadcasted_iota(jnp.int32, (128, 128), 0)
    to_ids = lax.broadcasted_iota(jnp.int32, (128, 128), 1)
    return one_hot((from_ids == head_of(g, here, to_ids)) & (to_ids < g.heads))


OUT, GATE, REST = KINDS = range(3)


class Wire:
    def __init__(self, send_sems, recv_sems):
        self.send_sems, self.recv_sems, self.used = send_sems, recv_sems, 0

    def reserve(self):
        self.used += 1
        return self.used - 1

    def make(self, src, dst, axis, peer, at_send, at_recv):
        return pltpu.make_async_remote_copy(
            src, dst, self.send_sems.at[at_send], self.recv_sems.at[at_recv],
            device_id={axis: peer}, device_id_type=MESH,
        )

    def put(self, src, dst, axis, peer):
        at = self.reserve()
        copy = self.make(src, dst, axis, peer, at, at)
        copy.start()
        return copy


class Maybe:
    def __init__(self, condition, copy):
        self.condition, self.copy = condition, copy

    def start(self):
        pl.when(self.condition)(self.copy.start)
        return self

    def wait_send(self):
        pl.when(self.condition)(self.copy.wait_send)


class PlaneGather:
    def __init__(self, put, n, here, source, block):
        self.put, self.block, self.plane = put, block, n == 4
        mine = block(here, None)
        if not self.plane:
            self.copies = [put(source, mine, SEQ, lax.rem(here + k, n)) for k in range(1, n)]
            return
        self.x = here + 1 - 2 * lax.rem(here, 2)
        self.y = lax.rem(here + 2, 4)
        self.copies = [put(source, mine, SEQ, self.x), put(source, mine, SEQ, self.y)]

    def forward(self):
        if self.plane:
            for copy, group, half, peer in (
                (self.copies[0], self.x, 0, self.y),
                (self.copies[1], self.y, 1, self.x),
            ):
                copy.wait_recv()
                part = self.block(group, half)
                self.copies.append(self.put(part, part, SEQ, peer))

    def wait_recv(self):
        for copy in self.copies[2:] if self.plane else self.copies:
            copy.wait_recv()

    def wait_send(self):
        for copy in self.copies:
            copy.wait_send()


class Mover:
    def __init__(self, sems):
        self.sems, self.used = sems, 0

    def put(self, src, dst):
        copy = pltpu.make_async_copy(src, dst, self.sems.at[self.used])
        copy.start()
        self.used += 1
        return copy


def meet_all(axes):
    barrier = pltpu.get_barrier_semaphore()
    count = 0
    for axis, n in axes:
        me = lax.axis_index(axis)
        for k in range(1, n):
            pl.semaphore_signal(
                barrier, inc=1, device_id={axis: lax.rem(me + k, n)}, device_id_type=MESH
            )
        count += n - 1
    pl.semaphore_wait(barrier, count)


def column_tiles(first, last, body):
    whole = (last - first) // 256

    def step(t, carry):
        body(pl.ds(pl.multiple_of(first + t * 256, 128), 256))
        return carry

    lax.fori_loop(0, whole, step, 0)
    if first + whole * 256 < last:
        body(slice(first + whole * 256, last))


class ForwardOuts(NamedTuple):
    sec: Any
    pout: Any
    stat0: Any
    h1: Any
    gb_o: Any
    stats: Any
    packs_o: Any
    wf_o: Any
    of_o: Any
    n_o: Any
    proj_o: Any
    mixed_o: Any
    yp_o: Any
    st_o: Any


class ForwardRefs(NamedTuple):
    tokens: Any
    cotangent: Any
    conv_w: Any
    conv_b: Any
    dt_bias: Any
    a_log: Any
    skip_d: Any
    gate_gain: Any
    norm_gain: Any
    w_src: Any
    o_src: Any
    sec: Any
    pout: Any
    stat0: Any
    h1: Any
    gb_o: Any
    stats: Any
    packs_o: Any
    wf_o: Any
    of_o: Any
    n_o: Any
    proj_o: Any
    mixed_o: Any
    yp_o: Any
    st_o: Any
    h0: Any
    cot: Any
    packs: Any
    wf: Any
    of: Any
    normed: Any
    proj: Any
    mixed: Any
    yp: Any
    st: Any
    pad: Any
    xc: Any
    dts: Any
    state: Any
    vg: Any
    ssq: Any
    part: Any
    got: Any
    got_stat: Any
    hbuf: Any
    own_stat: Any
    cols: Any
    mdots: Any
    sel: Any
    pack: Any
    ss: Any
    rs: Any
    ls: Any


def forward_kernel(g, n, w, rows, *refs):
    r = ForwardRefs(*refs)
    G, NC = g.G, g.NC
    core, here, shard = lax.axis_index(SECTION), lax.axis_index(SEQ), lax.axis_index(WT)
    sibling = 1 - core
    wire, mover = Wire(r.ss, r.rs), Mover(r.ls)
    wf, of, packs = r.wf, r.of, r.packs
    sends, saves = [], []

    def aligned(at, size):
        return pl.ds(pl.multiple_of(at, 16), size)

    def put(src, dst, axis, peer):
        copy = wire.put(src, dst, axis, peer)
        sends.append(copy)
        return copy

    for layer in range(2):
        for first, last in ((g.chans, G), (G + g.chans, 2 * G), (2 * G + 2 * STATE + HEADS, NC)):
            if first < last:
                wf[layer, first:last, :] = jnp.zeros((last - first, D), BF)
    meet_all(((SEQ, n), (WT, w), (SECTION, 2)))
    o_rows = G // w
    lanes_of = D // w
    mine_o = aligned(shard * o_rows, o_rows)
    piece = here if g.runs == w else shard
    o_own = r.o_src.at[aligned(piece * o_rows, o_rows)]
    mine_lanes = pl.ds(pl.multiple_of(shard * lanes_of, 128), lanes_of)
    width = g.run_heads * HEAD_DIM
    runs = []
    for kind_at, source_at in ((0, 0), (G, INNER)):
        for run in range(g.runs):
            source = source_at + run * (INNER // g.runs) + here * width
            runs.append((source, kind_at + run * width, width))
    runs.append((2 * INNER, 2 * G, 2 * STATE))
    runs.append((2 * INNER + 2 * STATE, 2 * G + 2 * STATE, HEADS))
    siblings, locals_ = [], []
    for source, target, size in runs:
        taken = r.w_src.at[aligned(source, size)]
        siblings.append(put(taken, wf.at[core, target : target + size, mine_lanes], SECTION, sibling))
        locals_.append(mover.put(taken, wf.at[core, target : target + size, mine_lanes]))
    others = [put(o_own, of.at[core, mine_o], SECTION, sibling)]
    locals_later = [
        mover.put(o_own, of.at[core, mine_o]),
        mover.put(r.tokens.at[core, 0], r.h0),
        mover.put(r.cotangent.at[core, 0], r.cot),
    ]

    def part_of(layer, kind, at_shard, at_core):
        if kind == OUT:
            return of.at[layer, aligned(at_shard * o_rows + at_core * (o_rows // 2), o_rows // 2)]
        size = (G if kind == GATE else g.rest) // 2
        first = (0 if kind == GATE else G) + at_core * size
        lanes = pl.ds(pl.multiple_of(at_shard * lanes_of, 128), lanes_of)
        return wf.at[layer, aligned(first, size), lanes]

    line = w == 4

    def fetch(layer, kind):
        mine = part_of(layer, kind, shard, core)
        at = [wire.reserve() for _ in range(w)]
        copies = [
            wire.make(mine, mine, WT, lax.rem(shard + k, w), at[k], at[k]) for k in range(1, w)
        ]
        if line:
            copies[1].start()
            sends.append(copies[1])
            sends.append(Maybe(shard != w - 1, copies[0]).start())
            sends.append(Maybe(shard != 0, copies[2]).start())
        else:
            for copy in copies:
                copy.start()
            sends.extend(copies)
        return copies, at

    def far_part(fetched, layer, kind):
        if not line:
            return []
        at = fetched[1]
        fetched[0][1].wait_recv()
        block = part_of(layer, kind, lax.rem(shard + 2, w), core)
        up = wire.make(block, block, WT, lax.rem(shard + 1, w), at[0], at[3])
        down = wire.make(block, block, WT, lax.rem(shard + w - 1, w), at[0], at[1])
        sends.append(Maybe(shard == 2, up).start())
        sends.append(Maybe(shard == 1, down).start())
        return [put(block, block, SECTION, sibling)]

    def near_parts(fetched, layer, kind):
        found = []
        for k in (1, 3) if line else range(1, w):
            fetched[0][k - 1].wait_recv()
            block = part_of(layer, kind, lax.rem(shard + w - k, w), core)
            found.append(put(block, block, SECTION, sibling))
        return found

    def received(copies):
        for copy in copies:
            copy.wait_recv()

    own_rows = aligned(here * rows, rows)

    def gather(whole):
        def block(group, half):
            size = rows if half is None else rows // 2
            return whole.at[aligned(group * rows + (half or 0) * size, size)]

        return PlaneGather(wire.put, n, here, block(here, None), block)

    def save(source, target):
        saves.append(mover.put(source, target))

    def saved():
        while saves:
            saves.pop().wait()

    for copy in locals_:
        copy.wait()
    received(siblings)
    pending = fetch(0, REST)
    gain_at = g.CX + 128 + G
    r.sel[...] = step_select(g, here).astype(BF)
    pack_small(g, here, r.conv_w, r.conv_b, r.dt_bias, r.a_log, r.skip_d, r.gate_gain, r.norm_gain, r.pack)
    others.append(put(r.pack, packs.at[core], SECTION, sibling))
    locals_later.append(mover.put(r.pack, packs.at[core]))
    for copy in locals_later:
        copy.wait()
    received(others)

    def norm(at):
        h = r.h0[at, :]
        inv = lax.rsqrt(jnp.mean(h * h, axis=1, keepdims=True) + EPSILON)
        r.normed[pl.ds(pl.multiple_of(here * rows + at.start, TILE), TILE), :] = (
            h * inv * packs[0, 0:1, gain_at:]
        ).astype(BF)

    rows_loop(rows, norm)
    arriving = gather(r.normed)
    handed = far_part(pending, 0, REST)
    coming = [fetch(0, GATE), fetch(0, OUT)]
    arriving.forward()
    handed += near_parts(pending, 0, REST)

    for layer in range(2):
        proj, mixed, normed = r.proj, r.mixed, r.normed
        conv = packs.at[layer, :, 0 : g.CX]
        head = packs.at[layer, :, g.CX : g.CX + 128]
        wide = packs.at[layer, :, g.CX + 128 : gain_at]

        def project(lanes):
            proj[:, lanes] = dot(normed[...], wf[layer, lanes, :], 1, 1).astype(BF)

        arriving.wait_recv()
        received(handed)
        gathered = arriving
        column_tiles(G, NC, project)
        scan_forward(
            G, proj, conv, head, wide, r.sel, mixed, r.yp, r.st,
            r.pad, r.xc, r.dts, r.state,
        )
        save(mixed, r.mixed_o.at[layer])
        save(r.yp, r.yp_o.at[layer])
        save(r.st, r.st_o.at[layer])
        save(normed, r.n_o.at[layer])
        handed = far_part(coming[0], layer, GATE) + far_part(coming[1], layer, OUT)
        handed += near_parts(coming[0], layer, GATE) + near_parts(coming[1], layer, OUT)
        if layer == 0:
            pending = fetch(1, REST)
        received(handed)
        column_tiles(0, G, project)
        save(proj, r.proj_o.at[layer])
        gate_forward(G, proj, wide, mixed, r.vg, r.ssq)

        def out_product(block):
            at = aligned(block * rows, rows)

            def tile(lanes):
                r.part[block, :, lanes] = dot(r.vg[at, :], of[layer, :, lanes], 1, 0).astype(BF)

            column_tiles(0, D, tile)

        saved()
        gathered.wait_send()
        summing = []
        for k in range(1, n):
            peer = lax.rem(here + k, n)
            out_product(peer)
            summing.append(wire.put(r.part.at[peer], r.got.at[k - 1], SEQ, peer))
            summing.append(wire.put(r.ssq.at[peer], r.got_stat.at[k - 1], SEQ, peer))
        out_product(here)
        for copy in summing:
            copy.wait()
        if layer == 0:
            handed = far_part(pending, 1, REST)
            coming = [fetch(1, GATE), fetch(1, OUT)]
        ssq = r.ssq[here]
        for k in range(n - 1):
            ssq = ssq + r.got_stat[k]
        inv2 = lax.rsqrt(ssq * (1.0 / INNER) + EPSILON)
        r.own_stat[...] = inv2
        r.cols[...] = column(inv2[0:1, :])
        if layer == 0:
            r.stat0[...] = inv2

        def finish(at):
            pout = total_of(n, r.part, r.got, at) * r.cols[at, 0:1]
            whole = pl.ds(pl.multiple_of(here * rows + at.start, TILE), TILE)
            h_in = r.h0[at, :] if layer == 0 else r.hbuf[0, at, :]
            h = h_in + pout
            r.hbuf[layer, at, :] = h
            if layer == 0:
                r.pout[at, :] = pout
                r.h1[at, :] = h
                inv = lax.rsqrt(jnp.mean(h * h, axis=1, keepdims=True) + EPSILON)
                r.normed[whole, :] = (h * inv * packs[1, 0:1, gain_at:]).astype(BF)
            else:
                out = r.cot[at, :].astype(BF)
                dots = jnp.sum(out.astype(F32) * pout, axis=1, keepdims=True)
                r.mdots[at, :] = jnp.broadcast_to(dots * (1.0 / INNER), (TILE, 128))
                r.normed[whole, :] = out

        rows_loop(rows, finish)
        if layer == 0:
            arriving = gather(r.normed)
            arriving.forward()
            handed += near_parts(pending, 1, REST)
    r.stats[here] = r.own_stat[...]
    r.stats[here, 1:2, :] = r.mdots[...].T[0:1, :]
    last_rows = gather(r.normed)
    arriving = []
    for k in range(1, n):
        block = r.stats.at[here]
        arriving.append(put(block, block, SEQ, lax.rem(here + k, n)))
    arriving.append(put(r.hbuf.at[1 - core], r.sec.at[core], SECTION, sibling))
    save(r.hbuf.at[core], r.sec.at[core])
    save(packs, r.packs_o)
    save(wf, r.wf_o)
    save(of, r.of_o)
    last_rows.forward()
    last_rows.wait_recv()
    received(arriving)
    save(r.normed, r.gb_o)
    last_rows.wait_send()
    for copy in sends:
        copy.wait_send()
    saved()


def forward_call(g, n, w, tokens, cotangent, small, w_src, o_src):
    rows = tokens.shape[2]
    L, G, NC, CX, PK = rows * n, g.G, g.NC, g.CX, g.CX + 128 + g.G + D
    S = jax.ShapeDtypeStruct
    shapes = ForwardOuts(
        sec=S((2, rows, D), F32),
        pout=S((rows, D), F32),
        stat0=S((8, 128), F32),
        h1=S((rows, D), F32),
        gb_o=S((L, D), BF),
        stats=S((n, 8, 128), F32),
        packs_o=S((2, 8, PK), F32),
        wf_o=S((2, NC, D), BF),
        of_o=S((2, G, D), BF),
        n_o=S((2, L, D), BF),
        proj_o=S((2, L, NC), BF),
        mixed_o=S((2, L, G), BF),
        yp_o=S((2, L, G), F32),
        st_o=S((2, L // Q, STATE, G), F32),
    )
    scratch = [
        S((rows, D), F32), S((rows, D), F32), shapes.packs_o, shapes.wf_o, shapes.of_o, S((L, D), BF), S((L, NC), BF), S((L, G), BF),
        S((L, G), F32), S((L // Q, STATE, G), F32), S((8 + L, 128), F32), S((L, CX), F32), S((L, 128), F32), S((STATE, G), F32),
        S((L, G), BF), S((n, 8, 128), F32), S((n, rows, D), BF), S((n - 1, rows, D), BF), S((n - 1, 8, 128), F32),
        S((2, rows, D), F32), S((8, 128), F32), S((rows, 128), F32), S((rows, 128), F32),
        S((128, 128), BF), S((8, PK), F32),
    ]
    remote = 4 + 2 * g.runs + 6 * w + 6 * (w - 1) + 3 + 8 * (n - 1) + 2
    outs = pl.pallas_call(
        functools.partial(forward_kernel, g, n, w, rows),
        out_shape=list(shapes),
        in_specs=[ANY, ANY] + [VM] * len(small) + [ANY, ANY],
        out_specs=[VM] * 4 + [ANY, VM] + [ANY] * 8,
        scratch_shapes=[pltpu.VMEM(s.shape, s.dtype) for s in scratch]
        + [
            pltpu.SemaphoreType.DMA((remote,)),
            pltpu.SemaphoreType.DMA((remote,)),
            pltpu.SemaphoreType.DMA((22 + 2 * g.runs,)),
        ],
        compiler_params=pltpu.CompilerParams(
            collective_id=0, has_side_effects=True, vmem_limit_bytes=FORWARD_VMEM
        ),
        name="forward",
    )(tokens, cotangent, *small, w_src, o_src)
    return ForwardOuts(*outs)


class BackwardOuts(NamedTuple):
    ig: Any
    gi: Any
    go: Any
    gi_sib: Any
    go_sib: Any
    small: Any
    far: Any
    late: Any


class BackwardRefs(NamedTuple):
    packs_i: Any
    wf_i: Any
    of_i: Any
    n_i: Any
    proj_i: Any
    mixed_i: Any
    yp_i: Any
    st_i: Any
    gb_i: Any
    stats1_i: Any
    stat0_i: Any
    pout_i: Any
    h1_i: Any
    tokens_i: Any
    cotangent_i: Any
    ig: Any
    gi: Any
    go: Any
    gi_sib: Any
    go_sib: Any
    small: Any
    far: Any
    late: Any
    packs: Any
    wf: Any
    of: Any
    n: Any
    proj: Any
    mixed: Any
    yp: Any
    st: Any
    gb: Any
    stats: Any
    pout: Any
    h1: Any
    h0: Any
    cot: Any
    dy: Any
    pad: Any
    xc: Any
    dts: Any
    dstate: Any
    part: Any
    got: Any
    own_stat: Any
    mdots: Any
    grads: Any
    gw: Any
    gout: Any
    sib_w: Any
    sib_o: Any
    z_w: Any
    z_o: Any
    relay_w: Any
    relay_o: Any
    sm: Any
    sm_sib: Any
    sm_z: Any
    sm_own: Any
    sel: Any
    gain: Any
    gain_z: Any
    gain_sum: Any
    ss: Any
    rs: Any
    ls: Any
    free: Any


def backward_kernel(g, n, w, rows, *refs):
    r = BackwardRefs(*refs)
    G, NC, CX = g.G, g.NC, g.CX
    core, here, shard = lax.axis_index(SECTION), lax.axis_index(SEQ), lax.axis_index(WT)
    sibling = 1 - core
    wire, mover = Wire(r.ss, r.rs), Mover(r.ls)
    o_half, lanes_of = G // (2 * w), D // w
    gain_at = CX + 128 + G

    def aligned(at, size):
        return pl.ds(pl.multiple_of(at, 16), size)

    def load(layer, *pairs):
        return [mover.put(source.at[layer], target) for source, target in pairs]

    first = load(1, (r.of_i, r.of), (r.proj_i, r.proj), (r.mixed_i, r.mixed))
    first += [mover.put(r.packs_i, r.packs), mover.put(r.gb_i, r.gb), mover.put(r.stats1_i, r.stats)]
    later = load(1, (r.n_i, r.n), (r.yp_i, r.yp), (r.st_i, r.st), (r.wf_i, r.wf))
    later += [mover.put(r.pout_i, r.pout), mover.put(r.h1_i, r.h1), mover.put(r.stat0_i, r.own_stat)]
    later += [mover.put(r.tokens_i.at[core, 0], r.h0), mover.put(r.cotangent_i.at[core, 0], r.cot)]
    meet_all(((SEQ, n), (WT, w), (SECTION, 2)))
    r.sm[...] = jnp.zeros_like(r.sm)
    r.sel[...] = step_select(g, here).astype(BF)
    r.gain[here] = jnp.zeros((8, D), F32)
    open_sends, record = [], {}
    line = w == 4
    arrivals = r.got if r.got.shape[0] == n - 1 else r.far

    def put(src, dst, axis, peer):
        copy = wire.put(src, dst, axis, peer)
        open_sends.append(copy)
        return copy

    def rows_of(kind):
        return ((0, G), (0, G), (G, g.rest))[kind]

    def kept(kind):
        return (slice(0, G // (2 * w)), slice(0, G // 2), slice(G // 2, g.half))[kind]

    def buffers(kind):
        if kind == OUT:
            return r.gout, r.sib_o, r.z_o, r.go, r.go_sib
        return r.gw, r.sib_w, r.z_w, r.gi, r.gi_sib

    def block_of(kind, at_shard, at_core):
        if kind == OUT:
            return aligned((2 * at_shard + at_core) * o_half, o_half), slice(0, D)
        first, size = rows_of(kind)
        return (
            aligned(first + at_core * (size // 2), size // 2),
            pl.ds(pl.multiple_of(at_shard * lanes_of, 128), lanes_of),
        )

    def ready(kind):
        for copy in record.pop(kind, ()):
            copy.wait_send()

    def to_sibling(layer, kind):
        grad, sib, _, _, _ = buffers(kind)
        if layer == 0:
            pl.semaphore_wait(r.free.at[kind], 1)
        if kind == OUT:
            pairs = [
                (grad.at[block_of(kind, q, sibling)], sib.at[aligned(q * o_half, o_half)])
                for q in range(w)
            ]
        else:
            first, size = rows_of(kind)
            rows_there = aligned(first + sibling * (size // 2), size // 2)
            pairs = [(grad.at[rows_there], sib.at[kept(kind)])]
        copies = [wire.put(source, target, SECTION, sibling) for source, target in pairs]
        record[kind] = list(copies)
        return copies

    def to_shards(layer, kind, copies):
        grad, sib, z, _, _ = buffers(kind)
        for copy in copies:
            copy.wait_recv()
        if kind == OUT:
            per = o_half // TILE

            def places(t):
                q = t // per
                return (2 * q + core) * o_half + (t - q * per) * TILE, t * TILE

            steps = w * per
        else:
            first, size = rows_of(kind)
            steps = size // 2 // TILE

            def places(t):
                return first + core * (size // 2) + t * TILE, kept(kind).start + t * TILE

        def add(t, carry):
            mine, theirs = (pl.ds(pl.multiple_of(at, TILE), TILE) for at in places(t))
            grad[mine, :] = (grad[mine, :].astype(F32) + sib[theirs, :].astype(F32)).astype(BF)
            return carry

        lax.fori_loop(0, steps, add, 0)
        if layer == 1:
            pl.semaphore_signal(
                r.free.at[kind], inc=1, device_id={SECTION: sibling}, device_id_type=MESH
            )
        at = [wire.reserve() for _ in range(w)]
        found = []
        for k in range(1, w):
            peer = lax.rem(shard + k, w)
            source = grad.at[block_of(kind, peer, core)]
            found.append(wire.make(source, z.at[layer, k - 1, kept(kind)], WT, peer, at[k], at[k]))
        if not line:
            for copy in found:
                copy.start()
            record[kind] += found
            return found, None
        buffer = (r.relay_o if kind == OUT else r.relay_w).at[layer, kept(kind)]
        up = wire.make(grad.at[block_of(kind, w - 1, core)], buffer, WT, 1, at[0], at[0])
        down = wire.make(grad.at[block_of(kind, 0, core)], buffer, WT, w - 2, at[0], at[0])
        inner = (shard == 1) | (shard == 2)
        first = [
            Maybe(shard == 0, up),
            Maybe(shard == w - 1, down),
            Maybe(inner, found[0]),
            Maybe(inner, found[2]),
        ]
        others = [
            Maybe(jnp.logical_not(inner), found[1]),
            Maybe(shard == 0, found[0]),
            Maybe(shard == w - 1, found[2]),
        ]
        record[kind] += [*first, *others, Maybe(inner, found[1])]
        for copy in first:
            copy.start()
        waiting.extend(others)
        arriving = wire.make(buffer, buffer, WT, lax.rem(shard + 1, w), at[0], at[0])
        return found, arriving

    def relay(layer, kind, moving):
        found, arriving = moving
        if not line:
            return
        grad, buffer = (r.gout, r.relay_o) if kind == OUT else (r.gw, r.relay_w)
        rows_here = kept(kind)

        @pl.when((shard == 1) | (shard == 2))
        def _():
            arriving.wait_recv()
            at_rows, at_lanes = block_of(kind, lax.rem(shard + 2, w), core)

            def add(at):
                mine = pl.ds(pl.multiple_of(at_rows.start + at.start, TILE), TILE)
                there = pl.ds(pl.multiple_of(rows_here.start + at.start, TILE), TILE)
                total = grad[mine, at_lanes].astype(F32) + buffer[layer, there, :].astype(F32)
                grad[mine, at_lanes] = total.astype(BF)

            rows_loop(rows_here.stop - rows_here.start, add)
            found[1].start()

    def to_plane(layer, kind, moving):
        grad, _, z, result, _ = buffers(kind)
        copies, _ = moving
        if line:
            pl.when(shard != 0)(copies[0].wait_recv)
            copies[1].wait_recv()
            pl.when(shard != w - 1)(copies[2].wait_recv)
        else:
            for copy in copies:
                copy.wait_recv()
        at_rows, at_lanes = block_of(kind, shard, core)
        here_rows = kept(kind)

        def add(at):
            mine = pl.ds(pl.multiple_of(at_rows.start + at.start, TILE), TILE)
            there = pl.ds(pl.multiple_of(here_rows.start + at.start, TILE), TILE)
            total = grad[mine, at_lanes].astype(F32)
            for k in range(w - 1):
                total = total + z[layer, k, there, :].astype(F32)
            z[layer, 1, there, :] = total.astype(BF)

        def add_end(at, near):
            mine = pl.ds(pl.multiple_of(at_rows.start + at.start, TILE), TILE)
            there = pl.ds(pl.multiple_of(here_rows.start + at.start, TILE), TILE)
            total = grad[mine, at_lanes].astype(F32)
            total = total + z[layer, 1, there, :].astype(F32) + z[layer, near, there, :].astype(F32)
            z[layer, 1, there, :] = total.astype(BF)

        count = here_rows.stop - here_rows.start
        if line:

            @pl.when(shard == 0)
            def _():
                rows_loop(count, lambda at: add_end(at, 2))

            @pl.when(shard == w - 1)
            def _():
                rows_loop(count, lambda at: add_end(at, 0))

            @pl.when((shard == 1) | (shard == 2))
            def _():
                rows_loop(count, add)
        else:
            rows_loop(count, add)
        def target(group, half):
            size = here_rows.stop - here_rows.start
            if half is None:
                return result.at[layer, group, here_rows]
            first = here_rows.start + half * (size // 2)
            return result.at[layer, group, first : first + size // 2]

        block = z.at[layer, 1, here_rows]
        return PlaneGather(put, n, here, block, target), mover.put(block, target(here, None))

    def landed(kind, *arrivals):
        _, _, _, result, target = buffers(kind)
        for found, own in arrivals:
            found.wait_recv()
            own.wait()
        return put(result.at[sibling, :, kept(kind)], target.at[:, kept(kind)], SECTION, sibling)

    def done(copies):
        for copy in copies:
            copy.wait()

    arrived, waiting = {}, []
    for layer in (1, 0):
        conv = r.packs.at[layer, :, 0:CX]
        head = r.packs.at[layer, :, CX : CX + 128]
        wide = r.packs.at[layer, :, CX + 128 : gain_at]
        g_conv = r.sm.at[layer, :, 0:CX]
        g_head = r.sm.at[layer, :, CX : CX + 128]
        g_wide = r.sm.at[layer, :, CX + 128 : gain_at]
        g_gain = r.sm.at[layer, :, gain_at : gain_at + D] if layer == 1 else r.gain.at[here]
        done(first)

        def d_normed(lanes):
            r.xc[:, lanes] = dot(r.gb[...], r.of[lanes, :], 1, 1)

        column_tiles(0, G, d_normed)
        gate_backward(
            G, r.proj, r.mixed, r.xc, r.stats, wide, r.dy, g_wide
        )

        def out_rows(t, carry):
            at = pl.ds(pl.multiple_of(t * 128, 128), 128)
            r.gout[at, :] = dot(r.mixed[:, at], r.gb[...], 0, 0).astype(BF)
            return carry

        def in_rows(first, last):
            def step(t, carry):
                at = pl.ds(pl.multiple_of(t * 128, 128), 128)
                r.gw[at, :] = dot(r.proj[:, at], r.n[...], 0, 0).astype(BF)
                return carry

            lax.fori_loop(first // 128, last // 128, step, 0)

        ready(OUT)
        lax.fori_loop(0, G // 128, out_rows, 0)
        out_sib = to_sibling(layer, OUT)
        done(later)
        ready(GATE)
        in_rows(0, G)
        gate_sib = to_sibling(layer, GATE)
        out_z = to_shards(layer, OUT, out_sib)
        gate_z = to_shards(layer, GATE, gate_sib)
        if layer == 0:
            arrived[1, OUT][0].forward()
            arrived[1, GATE][0].forward()
            arrived[1, REST] = to_plane(1, REST, rest_z)

        def serve():
            for copy in waiting:
                copy.start()

        scan_backward(
            G, r.proj, r.dy, r.yp, r.st, conv, head, wide, r.sel, g_wide, g_conv, g_head,
            r.pad, r.xc, r.dts, r.dstate, serve,
        )
        waiting.clear()
        relay(layer, OUT, out_z)
        relay(layer, GATE, gate_z)
        if layer == 0:
            small_sib = put(r.sm.at[sibling], r.sm_sib, SECTION, sibling)
        if layer == 0:
            arrived[1, REST][0].forward()
            small_sib.wait_recv()
            r.sm_own[...] = r.sm[core] + r.sm_sib[...]
            small_z = [
                put(r.sm_own, r.sm_z.at[k - 1], WT, lax.rem(shard + k, w)) for k in range(1, w)
            ]
        if layer == 1:
            first = load(0, (r.of_i, r.of), (r.mixed_i, r.mixed))
            later = load(0, (r.yp_i, r.yp), (r.st_i, r.st))

        def in_product(block):
            at = aligned(block * rows, rows)

            def tile(lanes):
                r.part[block, :, lanes] = dot(r.proj[at, :], r.wf[:, lanes], 1, 0).astype(BF)

            column_tiles(0, D, tile)

        summing = []
        for k in range(1, n):
            peer = lax.rem(here + k, n)
            in_product(peer)
            summing.append(wire.put(r.part.at[peer], arrivals.at[k - 1], SEQ, peer))
        in_product(here)
        if layer == 1:
            later += load(0, (r.wf_i, r.wf))
        ready(REST)
        in_rows(G, NC)
        if layer == 1:
            first += load(0, (r.proj_i, r.proj))
            later += load(0, (r.n_i, r.n))
        rest_sib = to_sibling(layer, REST)
        rest_z = to_shards(layer, REST, rest_sib)
        done(summing)
        while waiting:
            waiting.pop(0).start()
        if arrivals is not r.got:
            done(
                [
                    mover.put(arrivals.at[k - 1], r.part.at[lax.rem(here + k, n)])
                    for k in range(1, n)
                ]
            )

        def finish(at):
            if arrivals is r.got:
                d_in = total_of(n, r.part, r.got, at)
            else:
                d_in = r.part[0, at, :].astype(F32)
                for k in range(1, n):
                    d_in = d_in + r.part[k, at, :].astype(F32)
            h = r.h1[at, :] if layer == 1 else r.h0[at, :]
            above = r.cot[at, :] if layer == 1 else r.grads[1, at, :]
            inv = lax.rsqrt(jnp.mean(h * h, axis=1, keepdims=True) + EPSILON)
            normed = h * inv
            g_gain[0:1, :] += jnp.sum(d_in * normed, axis=0, keepdims=True)
            d_s = d_in * r.packs[layer, 0:1, gain_at:]
            d_h = above + inv * (d_s - normed * jnp.mean(d_s * normed, axis=1, keepdims=True))
            r.grads[layer, at, :] = d_h
            if layer == 1:
                out = d_h.astype(BF)
                whole = pl.ds(pl.multiple_of(here * rows + at.start, TILE), TILE)
                r.gb[whole, :] = out
                dots = jnp.sum(out.astype(F32) * r.pout[at, :], axis=1, keepdims=True)
                r.mdots[at, :] = jnp.broadcast_to(dots * (1.0 / INNER), (TILE, 128))

        rows_loop(rows, finish)
        if layer == 1:
            r.stats[here] = r.own_stat[...]
            r.stats[here, 1:2, :] = r.mdots[...].T[0:1, :]
            own = aligned(here * rows, rows)
            gathering = []

            def rows_of_group(group, half):
                size = rows if half is None else rows // 2
                return r.gb.at[aligned(group * rows + (half or 0) * size, size)]

            grad_rows = PlaneGather(put, n, here, r.gb.at[own], rows_of_group)
            for k in range(1, n):
                peer = lax.rem(here + k, n)
                gathering.append(put(r.stats.at[here], r.stats.at[here], SEQ, peer))
            relay(1, REST, rest_z)
            grad_rows.forward()
            arrived[1, OUT] = to_plane(1, OUT, out_z)
            arrived[1, GATE] = to_plane(1, GATE, gate_z)
            grad_rows.wait_recv()
            for copy in gathering:
                copy.wait_recv()
    gains = []
    ends = [put(r.grads.at[sibling], r.ig.at[core], SECTION, sibling)]
    for k in range(1, n):
        gains.append(put(r.gain.at[here], r.gain.at[here], SEQ, lax.rem(here + k, n)))
    local_grad = mover.put(r.grads.at[core], r.ig.at[core])
    relay(0, REST, rest_z)
    arrived[0, OUT] = to_plane(0, OUT, out_z)
    arrived[0, GATE] = to_plane(0, GATE, gate_z)
    arrived[0, OUT][0].forward()
    arrived[0, GATE][0].forward()
    for copy in small_z:
        copy.wait_recv()
    total = r.sm_own[...]
    for k in range(w - 1):
        total = total + r.sm_z[k]
    r.small[here] = total
    sums = [
        put(r.small.at[here], r.small.at[here], SEQ, lax.rem(here + k, n)) for k in range(1, n)
    ]
    for copy in gains:
        copy.wait_recv()
    total = r.gain[0]
    for k in range(1, n):
        total = total + r.gain[k]
    r.gain_z[shard] = total
    gains = [
        put(r.gain_z.at[shard], r.gain_z.at[shard], WT, lax.rem(shard + k, w)) for k in range(1, w)
    ]
    arrived[0, REST] = to_plane(0, REST, rest_z)
    ends.append(landed(OUT, arrived[1, OUT], arrived[0, OUT]))
    ends.append(landed(GATE, arrived[1, GATE], arrived[0, GATE]))
    arrived[0, REST][0].forward()
    ends.append(landed(REST, arrived[1, REST], arrived[0, REST]))
    for copy in gains:
        copy.wait_recv()
    total = r.gain_z[0]
    for k in range(1, w):
        total = total + r.gain_z[k]
    r.gain_sum[core] = total
    ends.append(put(r.gain_sum.at[core], r.gain_sum.at[core], SECTION, sibling))
    for copy in ends + sums:
        copy.wait_recv()
    r.late[...] = r.gain_sum[0] + r.gain_sum[1]
    local_grad.wait()
    for kind in KINDS:
        ready(kind)
    for copy in open_sends:
        copy.wait_send()


def backward_call(g, n, w, fwd, tokens, cotangent):
    rows = tokens.shape[2]
    L, G, NC, CX = rows * n, g.G, g.NC, g.CX
    PK = CX + 128 + G + D
    S = jax.ShapeDtypeStruct
    o_half, lanes_of = G // (2 * w), D // w
    spill = n > 8
    outs = BackwardOuts(
        ig=S((2, rows, D), F32),
        gi=S((2, n, g.half, lanes_of), BF),
        go=S((2, n, o_half, D), BF),
        gi_sib=S((n, g.half, lanes_of), BF),
        go_sib=S((n, o_half, D), BF),
        small=S((n, 8, PK), F32),
        far=S((n - 1, rows, D) if spill else (8, 128), BF),
        late=S((8, D), F32),
    )
    scratch = [
        S((2, 8, PK), F32), S((NC, D), BF), S((G, D), BF), S((L, D), BF), S((L, NC), BF), S((L, G), BF),
        S((L, G), F32), S((L // Q, STATE, G), F32), S((L, D), BF), S((n, 8, 128), F32), S((rows, D), F32),
        S((rows, D), F32), S((rows, D), F32), S((rows, D), F32),
        S((L, G), BF), S((8 + L, 128), F32), S((L, CX), F32), S((L, 128), F32), S((STATE, G), F32),
        S((n, rows, D), BF), S((1 if spill else n - 1, rows, D), BF), S((8, 128), F32), S((rows, 128), F32), S((2, rows, D), F32),
        S((NC, D), BF), S((G, D), BF), S((g.half, D), BF), S((G // 2, D), BF),
        S((2, w - 1, g.half, lanes_of), BF),
        S((2, w - 1, o_half, D), BF), S((2, g.half, lanes_of), BF), S((2, o_half, D), BF), S((2, 8, PK), F32), S((8, PK), F32), S((w - 1, 8, PK), F32), S((8, PK), F32),
        S((128, 128), BF), S((n, 8, D), F32), S((w, 8, D), F32), S((2, 8, D), F32),
    ]
    remote = 2 * (3 * (w + w + n - 1) + n - 1) + 2 * (n - 1) + 6 + 2 * (w - 1) + 2 * (n - 1)
    args = [
        fwd.packs_o, fwd.wf_o, fwd.of_o, fwd.n_o, fwd.proj_o, fwd.mixed_o, fwd.yp_o, fwd.st_o,
        fwd.gb_o, fwd.stats, fwd.stat0, fwd.pout, fwd.h1, tokens, cotangent,
    ]
    results = pl.pallas_call(
        functools.partial(backward_kernel, g, n, w, rows),
        out_shape=list(outs),
        in_specs=[ANY] * len(args),
        out_specs=[VM, ANY, ANY, ANY, ANY, VM, ANY, VM],
        scratch_shapes=[pltpu.VMEM(s.shape, s.dtype) for s in scratch]
        + [
            pltpu.SemaphoreType.DMA((remote,)),
            pltpu.SemaphoreType.DMA((remote,)),
            pltpu.SemaphoreType.DMA((36 + 2 * n,)),
            pltpu.SemaphoreType.REGULAR((3,)),
        ],
        compiler_params=pltpu.CompilerParams(
            collective_id=1, has_side_effects=True, vmem_limit_bytes=BACKWARD_VMEM
        ),
        name="backward",
    )(*args)
    return BackwardOuts(*results)


def pack_small(g, here, conv_ref, bias_ref, dtb_ref, a_ref, skip_ref, gate_ref, norm_ref, pack_ref):
    G, width = g.G, g.run_heads * HEAD_DIM
    win = -(-(width + 64) // 128) * 128
    start = here * width
    base = pl.multiple_of(start // 128 * 128, 128)
    from_ids = lax.broadcasted_iota(jnp.int32, (win, G), 0)
    to_ids = lax.broadcasted_iota(jnp.int32, (win, G), 1)
    exact = lax.Precision.HIGHEST

    def take(ref, rows):
        total = jnp.zeros((rows, G), F32)
        for run in range(g.runs):
            window = ref[0:rows, pl.ds(pl.multiple_of(base + run * (INNER // g.runs), 128), win)]
            inside = (to_ids >= run * width) & (to_ids < (run + 1) * width)
            pick = one_hot(inside & (from_ids == to_ids - run * width + (start - base)))
            total = total + dot(window, pick, 1, 0, exact)
        return total

    head_from = lax.broadcasted_iota(jnp.int32, (HEADS, 128), 0)
    head_to = lax.broadcasted_iota(jnp.int32, (HEADS, 128), 1)
    head_pick = one_hot((head_from == head_of(g, here, head_to)) & (head_to < g.heads))
    wide_from = lax.broadcasted_iota(jnp.int32, (HEADS, G), 0)
    wide_to = lax.broadcasted_iota(jnp.int32, (HEADS, G), 1)
    wide_pick = (wide_from == head_of(g, here, wide_to // HEAD_DIM)) & (wide_to < g.chans)
    head_at, wide_at, gain_at = g.CX, g.CX + 128, g.CX + 128 + G
    pack_ref[...] = jnp.zeros_like(pack_ref)
    pack_ref[0:KERNEL, 0:G] = take(conv_ref, KERNEL)
    pack_ref[4:5, 0:G] = take(bias_ref, 1)
    pack_ref[0:KERNEL, G:head_at] = conv_ref[:, INNER:]
    pack_ref[4:5, G:head_at] = bias_ref[:, INNER:]
    pack_ref[0:1, head_at:wide_at] = dot(dtb_ref[...], head_pick, 1, 0, exact)
    pack_ref[1:2, head_at:wide_at] = dot(-jnp.exp(a_ref[...]), head_pick, 1, 0, exact)
    pack_ref[0:1, wide_at:gain_at] = take(gate_ref, 1)
    pack_ref[1:2, wide_at:gain_at] = dot(skip_ref[...], one_hot(wide_pick), 1, 0, exact)
    pack_ref[0:1, gain_at:] = norm_ref[...]


def halves_of_heads(g, ref_of, column_at, head):
    parts = []
    for h in (head, head + 1):
        stride = HEADS // g.runs
        group = h % stride // g.run_heads
        local_head = h // stride * g.run_heads + h % g.run_heads
        value = ref_of(group, slice(column_at + local_head // 2 * 128, column_at + local_head // 2 * 128 + 128))
        parts.append(value if local_head % 2 == h % 2 else pltpu.roll(value, HEAD_DIM, 1))
    lanes = lax.broadcasted_iota(jnp.int32, parts[0].shape, 1)
    return jnp.where(lanes < HEAD_DIM, parts[0], parts[1])


def layout_kernel(g, own_ref, sib_ref, own_out_ref, sib_out_ref, small_ref, late_ref, sec_ref, ig_ref, g_in_ref, g_out_ref, sec_out, ig_out, norm_ref, conv_ref, bias_ref, dtb_ref, a_ref, skip_ref, gate_ref):
    n, G = g.n_seq, g.G
    first_core = lax.axis_index(SECTION) == 0

    def all_rows(halves, outs):
        def copy(groups, kind_at, half_at, half_rows, source, target, size):
            done = 0
            while done < size:
                half, offset = divmod(source + done, half_rows)
                count = min(size - done, half_rows - offset)
                at = slice(half_at + offset, half_at + offset + count)
                total = None
                for group in groups:
                    value = halves[half][group, at, :].astype(F32)
                    total = value if total is None else total + value
                g_in_ref[target + done : target + done + count, :] = total
                done += count

        for half in range(2):
            g_out_ref[:, half] = outs[half][...].astype(F32)
        width = g.run_heads * HEAD_DIM
        rest = (G, G // 2, g.rest // 2)
        everyone = range(n)
        for run in range(g.runs):
            for group in range(n):
                target = run * (INNER // g.runs) + group * width
                copy([group], 0, 0, G // 2, run * width, target, width)
                copy([group], *rest, run * width, INNER + target, width)
        copy(everyone, *rest, G, 2 * INNER, 2 * STATE)
        copy(everyone, *rest, G + 2 * STATE, 2 * INNER + 2 * STATE, HEADS)

    sec_out[...] = sec_ref[...]
    ig_out[...] = ig_ref[...]
    own, own_out = own_ref.at[0], own_out_ref.at[0]

    @pl.when(first_core)
    def _():
        all_rows((own, sib_ref), (own_out, sib_out_ref))

    @pl.when(jnp.logical_not(first_core))
    def _():
        all_rows((sib_ref, own), (sib_out_ref, own_out))

    @pl.when(pl.program_id(0) == 0)
    def _():
        from_ids = lax.broadcasted_iota(jnp.int32, (128, HEADS), 0)
        to_ids = lax.broadcasted_iota(jnp.int32, (128, HEADS), 1)
        picks = [one_hot((to_ids == head_of(g, group, from_ids)) & (from_ids < g.heads)) for group in range(n)]
        exact = lax.Precision.HIGHEST
        head_at, wide_at, gain_at = g.CX, g.CX + 128, g.CX + 128 + G

        def small(group, columns):
            return small_ref[group, :, columns]

        for head in range(0, HEADS, 2):
            at = slice(head * HEAD_DIM, head * HEAD_DIM + 128)
            conv = halves_of_heads(g, small, 0, head)
            conv_ref[:, at] = conv[0:KERNEL]
            bias_ref[:, at] = conv[KERNEL : KERNEL + 1]
            gate_ref[:, at] = halves_of_heads(g, small, wide_at, head)[0:1]
        conv = small(0, slice(G, head_at))
        norm = small(0, slice(gain_at, gain_at + D))
        for group in range(1, n):
            conv = conv + small(group, slice(G, head_at))
            norm = norm + small(group, slice(gain_at, gain_at + D))
        conv_ref[:, INNER:] = conv[0:KERNEL]
        bias_ref[:, INNER:] = conv[KERNEL : KERNEL + 1]
        norm_ref[...] = jnp.where(first_core, late_ref[0:1, :], norm[0:1])
        heads = jnp.zeros((8, HEADS), F32)
        skips = jnp.zeros((8, HEADS), F32)
        wide_from = lax.broadcasted_iota(jnp.int32, (G, HEADS), 0)
        wide_to = lax.broadcasted_iota(jnp.int32, (G, HEADS), 1)
        for group in range(n):
            heads = heads + dot(small(group, slice(head_at, wide_at)), picks[group], 1, 0, exact)
            pick = (wide_to == head_of(g, group, wide_from // HEAD_DIM)) & (wide_from < g.chans)
            skips = skips + dot(small(group, slice(wide_at, gain_at)), one_hot(pick), 1, 0, exact)
        dtb_ref[...] = heads[0:1]
        a_ref[...] = heads[1:2]
        skip_ref[...] = skips[1:2]


def layout_call(g, core, gi, gi_sib, go, go_sib, small, late, sec, ig):
    _, n, half, lanes = gi.shape
    out_half = go.shape[2]
    steps = lanes // 128
    out_lanes = D // steps
    rows_spec = pl.BlockSpec(sec.shape[:2] + (out_lanes,), lambda t, c: (0, 0, t))
    PK = small.shape[2]
    columns = 2 * INNER + 2 * STATE + HEADS
    S = jax.ShapeDtypeStruct
    shapes = (
        S((columns, lanes), F32), S((n, 2, out_half, D), F32), S(sec.shape, F32), S(ig.shape, F32), S((1, D), F32), S((KERNEL, CONV), F32),
        S((1, CONV), F32), S((1, HEADS), F32), S((1, HEADS), F32), S((1, HEADS), F32), S((1, INNER), F32),
    )
    return pl.pallas_call(
        lambda core_ref, *refs: layout_kernel(g, *refs),
        grid_spec=pltpu.PrefetchScalarGridSpec(
            num_scalar_prefetch=1,
            grid=(steps,),
            in_specs=[
                pl.BlockSpec((1, n, half, 128), lambda t, c: (c[0], 0, 0, t)),
                pl.BlockSpec((n, half, 128), lambda t, c: (0, 0, t)),
                pl.BlockSpec((1, n, out_half, out_lanes), lambda t, c: (c[0], 0, 0, t)),
                pl.BlockSpec((n, out_half, out_lanes), lambda t, c: (0, 0, t)),
                pl.BlockSpec((n, 8, PK), lambda t, c: (0, 0, 0)),
                pl.BlockSpec((8, D), lambda t, c: (0, 0)),
                rows_spec,
                rows_spec,
            ],
            out_specs=[
                pl.BlockSpec((columns, 128), lambda t, c: (0, t)),
                pl.BlockSpec((n, 2, out_half, out_lanes), lambda t, c: (0, 0, 0, t)),
                rows_spec,
                rows_spec,
            ]
            + [pl.BlockSpec(s.shape, lambda t, c: (0, 0)) for s in shapes[4:]],
        ),
        out_shape=shapes,
        compiler_params=pltpu.CompilerParams(vmem_limit_bytes=SMALL_VMEM),
        name="layout",
    )(core, gi, gi_sib, go, go_sib, small, late, sec, ig)


def local(
    tokens, cotangent, norm_gain, w_in, conv_w, conv_b, dt_bias, a_log, skip_d, gate_gain, w_out
):
    n_seq, n_wt = lax.axis_size(SEQ), lax.axis_size(WT)
    here = lax.axis_index(SEQ)
    group = Group(n_seq, n_wt)
    core = lax.axis_index(SECTION).reshape(1)
    G = group.G

    small = (conv_w[0], conv_b, dt_bias, a_log, skip_d, gate_gain, norm_gain)
    w_src = jnp.swapaxes(w_in[0], 0, 1)
    if group.runs == n_wt:
        o_src = w_out[0]
    else:
        o_src = lax.all_gather(w_out[0], WT, axis=0, tiled=True)
        o_src = lax.dynamic_slice_in_dim(o_src, here * group.chans, group.chans, 0)
        o_src = jnp.pad(o_src, ((0, G - group.chans), (0, 0)))
    fwd = forward_call(group, n_seq, n_wt, tokens, cotangent, small, w_src, o_src)
    bwd = backward_call(group, n_seq, n_wt, fwd, tokens, cotangent)
    g_in, g_out, section_out, input_grad, g_norm, g_conv, g_bias, g_dtb, g_a, g_skip, g_gate = layout_call(
        group, core, bwd.gi, bwd.gi_sib, bwd.go, bwd.go_sib, bwd.small, bwd.late, fwd.sec, bwd.ig
    )
    if group.runs == n_wt:
        g_out = g_out.reshape(INNER // n_wt, D)
    else:
        g_out = g_out.astype(BF).reshape(n_seq, G // n_wt, D)
        g_out = lax.all_gather(g_out, WT, axis=1, tiled=True)[:, : group.chans].reshape(INNER, D)
        mine = INNER // n_wt
        g_out = lax.dynamic_slice_in_dim(g_out, lax.axis_index(WT) * mine, mine, 0).astype(F32)
    return (
        section_out[None, :, None],
        input_grad[None, :, None],
        g_norm,
        jnp.swapaxes(g_in, 0, 1)[None],
        g_conv[None],
        g_bias,
        g_dtb,
        g_a,
        g_skip,
        g_gate,
        g_out[None],
    )


def solution(mesh):
    placed = (
        P(None, WT, SEQ, None),
        P(None, WT, SEQ, None),
        P(SECTION, None),
        P(SECTION, WT, None),
        P(SECTION, None, None),
        P(SECTION, None),
        P(SECTION, None),
        P(SECTION, None),
        P(SECTION, None),
        P(SECTION, None),
        P(SECTION, WT, None),
    )
    return jax.shard_map(
        local,
        mesh=mesh,
        in_specs=placed,
        out_specs=(
            P(SECTION, None, WT, SEQ, None),
            P(SECTION, None, WT, SEQ, None),
            P(SECTION, None),
            P(SECTION, WT, None),
            P(SECTION, None, None),
            P(SECTION, None),
            P(SECTION, None),
            P(SECTION, None),
            P(SECTION, None),
            P(SECTION, None),
            P(SECTION, WT, None),
        ),
        check_vma=False,
    )
```

```python
import functools
from typing import Any, NamedTuple

import jax
import jax.numpy as jnp
from jax import lax
from jax.experimental import pallas as pl
from jax.experimental.pallas import tpu as pltpu
from jax.sharding import PartitionSpec as P

D = 1536
HEADS = 48
HEAD_DIM = 64
STATE = 128
KERNEL = 4
INNER = 3072
CONV = 3328
EPSILON = 1e-05

Q = 128
F32 = jnp.float32
BF = jnp.bfloat16
SEQ, WT, SECTION = "seq", "wt", "section"
FORWARD_VMEM = 56 * 2**20
BACKWARD_VMEM = 62 * 2**20
SMALL_VMEM = 60 * 2**20
MESH = pl.DeviceIdType.MESH
VM = pl.BlockSpec(memory_space=pltpu.VMEM)
ANY = pl.BlockSpec(memory_space=pl.ANY)
TILE = 16


def dot(a, b, ca, cb, precision=None):
    return lax.dot_general(a, b, (((ca,), (cb,)), ((), ())), precision=precision, preferred_element_type=F32)

def sigmoid(x):
    return 1.0 / (1.0 + jnp.exp(-x))

def softplus(x):
    return jnp.maximum(x, 0.0) + jnp.log1p(jnp.exp(-jnp.abs(x)))

def lane_mask(rows):
    return lax.broadcasted_iota(jnp.int32, (rows, 128), 1) < HEAD_DIM

def spread(cols, pair, mask):
    a = jnp.broadcast_to(cols[:, 2 * pair : 2 * pair + 1], mask.shape)
    b = jnp.broadcast_to(cols[:, 2 * pair + 1 : 2 * pair + 2], mask.shape)
    return jnp.where(mask, a, b)

def split_pair(u, mask):
    zero = jnp.zeros_like(u)
    return jnp.concatenate([jnp.where(mask, u, zero), jnp.where(mask, zero, u)], axis=0)

def conv_tile(proj_ref, cw_ref, pad, proj_at, conv_at, rows):
    pad[0:8, :] = jnp.zeros((8, 128), F32)
    pad[8 : 8 + rows, :] = proj_ref[:, pl.ds(proj_at, 128)].astype(F32)
    pre = jnp.broadcast_to(cw_ref[4:5, pl.ds(conv_at, 128)], (rows, 128))
    for k in range(KERNEL):
        pre = pre + cw_ref[k : k + 1, pl.ds(conv_at, 128)] * pad[5 + k : 5 + k + rows, :]
    return pre

def step_inputs(proj_ref, at, hp_ref, sel_ref, dt_at):
    return dot(proj_ref[at, dt_at : dt_at + 128], sel_ref[...], 1, 0) + hp_ref[0:1, :]

def chunk_factors(dt, hp_ref):
    rate = dt * hp_ref[1:2, :]
    rows = lax.broadcasted_iota(jnp.int32, (Q, Q), 0)
    cols = lax.broadcasted_iota(jnp.int32, (Q, Q), 1)
    tri = (rows >= cols).astype(F32)
    cum = dot(tri, rate, 1, 0, lax.Precision.HIGHEST)
    return rate, cum, rows >= cols

def decay_pair(cum, cum_t, causal, pair):
    parts = []
    for h in (2 * pair, 2 * pair + 1):
        diff = jnp.broadcast_to(cum[:, h : h + 1], (Q, Q)) - jnp.broadcast_to(cum_t[h : h + 1, :], (Q, Q))
        parts.append(jnp.exp(jnp.where(causal, diff, -1e30)))
    return jnp.concatenate(parts, axis=1)

def scan_forward(G, proj_ref, cw_ref, hp_ref, gw_ref, sel_ref, mixed_ref, yp_ref, st_ref, pad, xc, dts, state):
    L = proj_ref.shape[0]

    def conv(tile, carry):
        lanes = pl.ds(pl.multiple_of(tile * 128, 128), 128)
        pre = conv_tile(proj_ref, cw_ref, pad, pl.multiple_of(G + tile * 128, 128), lanes.start, L)
        xc[:, lanes] = pre * sigmoid(pre)
        return carry

    lax.fori_loop(0, (G + 2 * STATE) // 128, conv, 0)
    dt_at = 2 * G + 2 * STATE
    dts[...] = softplus(step_inputs(proj_ref, slice(0, L), hp_ref, sel_ref, dt_at))
    state[...] = jnp.zeros_like(state)
    mask = lane_mask(Q)

    def chunk(c, _):
        at = pl.ds(pl.multiple_of(c * Q, Q), Q)
        dt = dts[at, :]
        rate, cum, causal = chunk_factors(dt, hp_ref)
        cum_t = cum.T
        last = cum[Q - 1 : Q, :]
        e_cum = jnp.exp(cum)
        tail = jnp.exp(last - cum) * dt
        e_last = jnp.broadcast_to(jnp.exp(last), (8, 128))
        b = xc[at, G : G + STATE].astype(BF)
        cc = xc[at, G + STATE : G + 2 * STATE].astype(BF)
        scores = dot(cc, b, 1, 1)
        scores2 = jnp.concatenate([scores, scores], axis=1)
        for p in range(G // 128):
            lanes = slice(p * 128, p * 128 + 128)
            x = xc[at, lanes]
            u = (x * spread(dt, p, mask)).astype(BF)
            m = (scores2 * decay_pair(cum, cum_t, causal, p)).astype(BF)
            before = state[:, lanes]
            st_ref[c, :, lanes] = before
            y = dot(m, split_pair(u, mask), 1, 0)
            y = y + dot(cc, before.astype(BF), 1, 0) * spread(e_cum, p, mask)
            yp_ref[at, lanes] = y
            after = dot(b, (x * spread(tail, p, mask)).astype(BF), 0, 0)
            state[:, lanes] = before * spread(e_last, p, mask[0:8])[0:1, :] + after
            mixed_ref[at, lanes] = (y + gw_ref[1:2, lanes] * x).astype(BF)
        return 0

    lax.fori_loop(0, L // Q, chunk, 0)


def gate_forward(G, proj_ref, gw_ref, mixed_ref, vg_ref, ssq_ref):
    def chunk(c, _):
        at = pl.ds(pl.multiple_of(c * Q, Q), Q)
        ssq = jnp.zeros((Q, 1), F32)
        for p in range(G // 128):
            lanes = slice(p * 128, p * 128 + 128)
            gate = proj_ref[at, lanes].astype(F32)
            v = mixed_ref[at, lanes].astype(F32) * (gate * sigmoid(gate))
            vg_ref[at, lanes] = (v * gw_ref[0:1, lanes]).astype(BF)
            ssq = ssq + jnp.sum(v * v, axis=1, keepdims=True)
        ssq_ref[c] = jnp.broadcast_to(ssq, (Q, 128)).T[0:8, :]
        return 0

    lax.fori_loop(0, proj_ref.shape[0] // Q, chunk, 0)


def lane_sums(values, pick):
    high = values.astype(BF)
    low = (values - high.astype(F32)).astype(BF)
    return dot(high, pick, 1, 0) + dot(low, pick, 1, 0)


def gate_backward(G, proj_ref, mixed_ref, dn_ref, sc_ref, gw_ref, dy_ref, gg_ref):
    gg_ref[...] = jnp.zeros_like(gg_ref)

    def chunk(c, _):
        at = pl.ds(pl.multiple_of(c * Q, Q), Q)
        sc = jnp.concatenate([sc_ref[c], jnp.zeros((Q - 8, 128), F32)], axis=0).T
        inv2 = jnp.broadcast_to(sc[:, 0:1], (Q, 128))
        mdot = jnp.broadcast_to(sc[:, 1:2], (Q, 128))
        for p in range(G // 128):
            lanes = slice(p * 128, p * 128 + 128)
            gate = proj_ref[at, lanes].astype(F32)
            sig = sigmoid(gate)
            act = gate * sig
            mixed = mixed_ref[at, lanes].astype(F32)
            n2 = mixed * act * inv2
            mixed_ref[at, lanes] = (n2 * gw_ref[0:1, lanes]).astype(BF)
            dn = dn_ref[at, lanes]
            gg_ref[0:1, lanes] += jnp.sum(dn * n2, axis=0, keepdims=True)
            d_v = inv2 * (dn * gw_ref[0:1, lanes] - n2 * mdot)
            dy_ref[at, lanes] = (d_v * act).astype(BF)
            proj_ref[at, lanes] = (d_v * mixed * (sig * (1.0 + gate * (1.0 - sig)))).astype(BF)
        return 0

    lax.fori_loop(0, proj_ref.shape[0] // Q, chunk, 0)


def scan_backward(G, proj_ref, dy_ref, yp_ref, st_ref, cw_ref, hp_ref, gw_ref, sel_ref, gg_ref, gc_ref, gh_ref,
                  pad, xc, dts, dstate, serve):
    L = proj_ref.shape[0]
    nb = L // Q
    mask = lane_mask(Q)

    def conv(tile, carry):
        lanes = pl.ds(pl.multiple_of(tile * 128, 128), 128)
        pre = conv_tile(proj_ref, cw_ref, pad, pl.multiple_of(G + tile * 128, 128), lanes.start, L)
        xc[:, lanes] = pre * sigmoid(pre)
        return carry

    lax.fori_loop(0, (G + 2 * STATE) // 128, conv, 0)
    dt_at = 2 * G + 2 * STATE
    dts[...] = softplus(step_inputs(proj_ref, slice(0, L), hp_ref, sel_ref, dt_at))
    dstate[...] = jnp.zeros_like(dstate)
    gh_ref[...] = jnp.zeros_like(gh_ref)

    def chunk(step, _):
        c = nb - 1 - step
        pl.when(step == nb // 4)(serve)
        at = pl.ds(pl.multiple_of(c * Q, Q), Q)
        dt = dts[at, :]
        rate, cum, causal = chunk_factors(dt, hp_ref)
        cum_t = cum.T
        last = cum[Q - 1 : Q, :]
        e_cum = jnp.exp(cum)
        tail = jnp.exp(last - cum)
        e_last = jnp.broadcast_to(jnp.exp(last), (8, 128))
        b = xc[at, G : G + STATE].astype(BF)
        cc = xc[at, G + STATE : G + 2 * STATE].astype(BF)
        scores = dot(cc, b, 1, 1)
        scores2 = jnp.concatenate([scores, scores], axis=1)
        d_scores = jnp.zeros((Q, Q), F32)
        d_b = jnp.zeros((Q, STATE), F32)
        d_c = jnp.zeros((Q, STATE), F32)
        d_cum = jnp.zeros((Q, 128), F32)
        d_dt = jnp.zeros((Q, 128), F32)
        d_last = jnp.zeros((8, 128), F32)
        lane_ids = lax.broadcasted_iota(jnp.int32, (Q, 128), 1)
        row_ids = lax.broadcasted_iota(jnp.int32, (Q, 128), 0)
        for p in range(G // 128):
            lanes = slice(p * 128, p * 128 + 128)
            dyb = dy_ref[at, lanes]
            d_y = dyb.astype(F32)
            x = xc[at, lanes]
            dt_x = spread(dt, p, mask)
            u = (x * dt_x).astype(BF)
            u2 = split_pair(u, mask)
            uf = u.astype(F32)
            dec = decay_pair(cum, cum_t, causal, p)
            m = (scores2 * dec).astype(BF)
            dm = dot(dyb, u2, 1, 1) * dec
            d_scores = d_scores + dm[:, :Q] + dm[:, Q:]
            both = dot(m, dyb, 0, 0)
            du = jnp.where(mask, both[:Q], both[Q:])
            tail_x = spread(tail, p, mask)
            before = st_ref[c, :, lanes]
            after = dstate[:, lanes]
            afterb = after.astype(BF)
            du_out = tail_x * dot(b, afterb, 1, 0)
            du = du + du_out
            dye = (d_y * spread(e_cum, p, mask)).astype(BF)
            d_c = d_c + dot(dye, before.astype(BF), 1, 1)
            d_b = d_b + dot((uf * tail_x).astype(BF), afterb, 1, 1)
            e_last_x = spread(e_last, p, mask[0:8])
            dstate[:, lanes] = after * e_last_x[0:1, :] + dot(cc, dye, 0, 0)
            z3 = jnp.sum(uf * du_out, axis=0, keepdims=True) + e_last_x[0:1, :] * jnp.sum(before * after, axis=0, keepdims=True)
            z1 = d_y * yp_ref[at, lanes] - uf * du
            z2 = x * du
            pick = jnp.where(lane_ids == 2 * p + jnp.where(row_ids < HEAD_DIM, 0, 1), 1.0, 0.0).astype(BF)
            d_cum = d_cum + lane_sums(z1, pick)
            d_dt = d_dt + lane_sums(z2, pick)
            d_last = d_last + lane_sums(jnp.broadcast_to(z3, (8, 128)), pick)
            xc[at, lanes] = dt_x * du + gw_ref[1:2, lanes] * d_y
            gg_ref[1:2, lanes] += jnp.sum(d_y * x, axis=0, keepdims=True)
        dsb = d_scores.astype(BF)
        xc[at, G : G + STATE] = d_b + dot(dsb, cc, 0, 0)
        xc[at, G + STATE : G + 2 * STATE] = d_c + dot(dsb, b, 1, 0)
        rows = lax.broadcasted_iota(jnp.int32, (Q, Q), 0)
        cols = lax.broadcasted_iota(jnp.int32, (Q, Q), 1)
        upper = (rows <= cols).astype(F32)
        d_rate = dot(upper, d_cum, 1, 0, lax.Precision.HIGHEST) + d_last[0:1, :]
        d_step = d_dt + d_rate * hp_ref[1:2, :]
        d_raw = d_step * sigmoid(step_inputs(proj_ref, at, hp_ref, sel_ref, dt_at))
        proj_ref[at, dt_at : dt_at + 128] = dot(d_raw.astype(BF), sel_ref[...], 1, 1).astype(BF)
        gh_ref[0:1, :] += jnp.sum(d_raw, axis=0, keepdims=True)
        gh_ref[1:2, :] += jnp.sum(d_rate * rate, axis=0, keepdims=True)
        return 0

    lax.fori_loop(0, nb, chunk, 0)

    gc_ref[...] = jnp.zeros_like(gc_ref)

    def conv_back(tile, carry):
        lanes = pl.ds(pl.multiple_of(tile * 128, 128), 128)
        proj_at = pl.multiple_of(G + tile * 128, 128)
        pre = conv_tile(proj_ref, cw_ref, pad, proj_at, lanes.start, L)
        sig = sigmoid(pre)
        d_pre = xc[:, lanes] * (sig * (1.0 + pre * (1.0 - sig)))
        for k in range(KERNEL):
            gc_ref[k : k + 1, lanes] = jnp.sum(d_pre * pad[5 + k : 5 + k + L, :], axis=0, keepdims=True)
        gc_ref[4:5, lanes] = jnp.sum(d_pre, axis=0, keepdims=True)
        pad[0:L, :] = d_pre
        pad[L : L + 8, :] = jnp.zeros((8, 128), F32)
        d_in = cw_ref[3:4, lanes] * d_pre
        for k in range(KERNEL - 1):
            d_in = d_in + cw_ref[k : k + 1, lanes] * pad[3 - k : 3 - k + L, :]
        proj_ref[:, pl.ds(proj_at, 128)] = d_in.astype(BF)
        return carry

    lax.fori_loop(0, (G + 2 * STATE) // 128, conv_back, 0)


def column(row):
    return jnp.broadcast_to(row, (128, 128)).T


def rows_loop(rows, body):
    def step(r, carry):
        body(pl.ds(pl.multiple_of(r * TILE, TILE), TILE))
        return carry

    lax.fori_loop(0, rows // TILE, step, 0)


class Group:
    def __init__(self, n_seq, n_wt):
        self.n_seq = n_seq
        self.heads = HEADS // n_seq
        self.runs = n_wt if HEADS % (n_seq * n_wt) == 0 else 1
        self.run_heads = self.heads // self.runs
        self.chans = self.heads * HEAD_DIM
        self.G = -(-self.chans // 128) * 128
        self.CX = self.G + 2 * STATE
        self.NC = 2 * self.G + 2 * STATE + 128
        self.rest = self.G + 2 * STATE + 64
        self.half = (self.G + self.rest) // 2


def head_of(g, here, local_head):
    stride = HEADS // g.runs
    run = local_head // g.run_heads
    return run * stride + here * g.run_heads + (local_head - run * g.run_heads)


def one_hot(found):
    return jnp.where(found, 1.0, 0.0)


def step_select(g, here):
    from_ids = lax.broadcasted_iota(jnp.int32, (128, 128), 0)
    to_ids = lax.broadcasted_iota(jnp.int32, (128, 128), 1)
    return one_hot((from_ids == head_of(g, here, to_ids)) & (to_ids < g.heads))


OUT, GATE, REST = KINDS = range(3)


class Wire:
    def __init__(self, send_sems, recv_sems):
        self.send_sems, self.recv_sems, self.used = send_sems, recv_sems, 0

    def reserve(self):
        self.used += 1
        return self.used - 1

    def make(self, src, dst, axis, peer, at_send, at_recv):
        return pltpu.make_async_remote_copy(
            src, dst, self.send_sems.at[at_send], self.recv_sems.at[at_recv],
            device_id={axis: peer}, device_id_type=MESH,
        )

    def put(self, src, dst, axis, peer):
        at = self.reserve()
        copy = self.make(src, dst, axis, peer, at, at)
        copy.start()
        return copy


class Maybe:
    def __init__(self, condition, copy):
        self.condition, self.copy = condition, copy

    def start(self):
        pl.when(self.condition)(self.copy.start)
        return self

    def wait_send(self):
        pl.when(self.condition)(self.copy.wait_send)


class PlaneGather:
    def __init__(self, put, n, here, source, block):
        self.put, self.block, self.plane = put, block, n == 4
        mine = block(here, None)
        if not self.plane:
            self.copies = [put(source, mine, SEQ, lax.rem(here + k, n)) for k in range(1, n)]
            return
        self.x = here + 1 - 2 * lax.rem(here, 2)
        self.y = lax.rem(here + 2, 4)
        self.copies = [put(source, mine, SEQ, self.x), put(source, mine, SEQ, self.y)]

    def forward(self, landed=None):
        if self.plane:
            for copy, group, half, peer in (
                (self.copies[0], self.x, 0, self.y),
                (self.copies[1], self.y, 1, self.x),
            ):
                copy.wait_recv()
                part = self.block(group, half)
                self.copies.append(self.put(part, part, SEQ, peer))
                if landed is not None:
                    landed(group)

    def wait_recv(self):
        for copy in self.copies[2:] if self.plane else self.copies:
            copy.wait_recv()

    def wait_send(self):
        for copy in self.copies:
            copy.wait_send()


class PlaneSum:
    def __init__(self, put, n, here, part, got, mid):
        self.put, self.n, self.here, self.part, self.got, self.mid = put, n, here, part, got, mid
        self.plane = n == 4
        self.half = part.shape[1] // 2
        self.peers = [lax.rem(here + k, n) for k in range(1, n)]
        if self.plane:
            self.x = here + 1 - 2 * lax.rem(here, 2)
            self.y = lax.rem(here + 2, 4)
            self.peers = [lax.rem(self.x + 2, 4), self.y, self.x]

    def start(self, product, stat=None, got_stat=None):
        half, part, got = self.half, self.part, self.got
        self.copies = []
        for k, peer in enumerate(self.peers):
            product(peer)
            if not self.plane:
                self.copies.append(self.put(part.at[peer], got.at[k], SEQ, peer))
            elif k == 0:
                self.mids = [
                    self.put(part.at[peer, 0:half], self.mid.at[0], SEQ, self.x),
                    self.put(part.at[peer, half:], self.mid.at[1], SEQ, self.y),
                ]
            elif k == 1:
                self.copies.append(self.put(part.at[peer, half:], got.at[1, half:], SEQ, peer))
            else:
                self.copies.append(self.put(part.at[peer, 0:half], got.at[0, 0:half], SEQ, peer))
            if stat is not None:
                self.copies.append(self.put(stat.at[peer], got_stat.at[k], SEQ, peer))
        product(self.here)

    def middle(self):
        if not self.plane:
            return
        half, part = self.half, self.part
        for copy in self.mids:
            copy.wait()

        def add(at):
            late = pl.ds(pl.multiple_of(at.start + half, TILE), TILE)
            for peer, rows, slot in ((self.y, at, 0), (self.x, late, 1)):
                total = part[peer, rows, :].astype(F32) + self.mid[slot, at, :].astype(F32)
                part[peer, rows, :] = total.astype(BF)

        rows_loop(half, add)
        self.copies += [
            self.put(part.at[self.y, 0:half], self.got.at[1, 0:half], SEQ, self.y),
            self.put(part.at[self.x, half:], self.got.at[0, half:], SEQ, self.x),
        ]

    def end(self):
        for copy in self.copies:
            copy.wait()

    def total(self, at):
        total = self.part[self.here, at, :].astype(F32)
        for k in range(2 if self.plane else self.n - 1):
            total = total + self.got[k, at, :].astype(F32)
        return total


class Mover:
    def __init__(self, sems):
        self.sems, self.used = sems, 0

    def put(self, src, dst):
        copy = pltpu.make_async_copy(src, dst, self.sems.at[self.used])
        copy.start()
        self.used += 1
        return copy


def meet_all(axes):
    barrier = pltpu.get_barrier_semaphore()
    count = 0
    for axis, n in axes:
        me = lax.axis_index(axis)
        for k in range(1, n):
            pl.semaphore_signal(
                barrier, inc=1, device_id={axis: lax.rem(me + k, n)}, device_id_type=MESH
            )
        count += n - 1
    pl.semaphore_wait(barrier, count)


def column_tiles(first, last, body):
    whole = (last - first) // 256

    def step(t, carry):
        body(pl.ds(pl.multiple_of(first + t * 256, 128), 256))
        return carry

    lax.fori_loop(0, whole, step, 0)
    if first + whole * 256 < last:
        body(slice(first + whole * 256, last))


class ForwardOuts(NamedTuple):
    sec: Any
    pout: Any
    stat0: Any
    h1: Any
    gb_o: Any
    stats: Any
    packs_o: Any
    wf_o: Any
    of_o: Any
    n_o: Any
    proj_o: Any
    mixed_o: Any
    yp_o: Any
    st_o: Any


class ForwardRefs(NamedTuple):
    tokens: Any
    cotangent: Any
    conv_w: Any
    conv_b: Any
    dt_bias: Any
    a_log: Any
    skip_d: Any
    gate_gain: Any
    norm_gain: Any
    w_src: Any
    o_src: Any
    sec: Any
    pout: Any
    stat0: Any
    h1: Any
    gb_o: Any
    stats: Any
    packs_o: Any
    wf_o: Any
    of_o: Any
    n_o: Any
    proj_o: Any
    mixed_o: Any
    yp_o: Any
    st_o: Any
    h0: Any
    cot: Any
    packs: Any
    wf: Any
    of: Any
    normed: Any
    proj: Any
    mixed: Any
    yp: Any
    st: Any
    pad: Any
    xc: Any
    dts: Any
    state: Any
    vg: Any
    ssq: Any
    part: Any
    got: Any
    got_stat: Any
    hbuf: Any
    own_stat: Any
    cols: Any
    mdots: Any
    sel: Any
    pack: Any
    mid: Any
    ss: Any
    rs: Any
    ls: Any


def forward_kernel(g, n, w, rows, *refs):
    r = ForwardRefs(*refs)
    G, NC = g.G, g.NC
    core, here, shard = lax.axis_index(SECTION), lax.axis_index(SEQ), lax.axis_index(WT)
    sibling = 1 - core
    wire, mover = Wire(r.ss, r.rs), Mover(r.ls)
    wf, of, packs = r.wf, r.of, r.packs
    sends, saves = [], []

    def aligned(at, size):
        return pl.ds(pl.multiple_of(at, 16), size)

    def put(src, dst, axis, peer):
        copy = wire.put(src, dst, axis, peer)
        sends.append(copy)
        return copy

    for layer in range(2):
        for first, last in ((g.chans, G), (G + g.chans, 2 * G), (2 * G + 2 * STATE + HEADS, NC)):
            if first < last:
                wf[layer, first:last, :] = jnp.zeros((last - first, D), BF)
    meet_all(((SEQ, n), (WT, w), (SECTION, 2)))
    o_rows = G // w
    lanes_of = D // w
    mine_o = aligned(shard * o_rows, o_rows)
    piece = here if g.runs == w else shard
    o_own = r.o_src.at[aligned(piece * o_rows, o_rows)]
    mine_lanes = pl.ds(pl.multiple_of(shard * lanes_of, 128), lanes_of)
    width = g.run_heads * HEAD_DIM
    runs = []
    for kind_at, source_at in ((0, 0), (G, INNER)):
        for run in range(g.runs):
            source = source_at + run * (INNER // g.runs) + here * width
            runs.append((source, kind_at + run * width, width))
    runs.append((2 * INNER, 2 * G, 2 * STATE))
    runs.append((2 * INNER + 2 * STATE, 2 * G + 2 * STATE, HEADS))
    siblings, locals_ = [], []
    for source, target, size in runs:
        taken = r.w_src.at[aligned(source, size)]
        siblings.append(put(taken, wf.at[core, target : target + size, mine_lanes], SECTION, sibling))
        locals_.append(mover.put(taken, wf.at[core, target : target + size, mine_lanes]))
    others = [put(o_own, of.at[core, mine_o], SECTION, sibling)]
    locals_later = [
        mover.put(o_own, of.at[core, mine_o]),
        mover.put(r.tokens.at[core, 0], r.h0),
        mover.put(r.cotangent.at[core, 0], r.cot),
    ]

    def part_of(layer, kind, at_shard, at_core):
        if kind == OUT:
            return of.at[layer, aligned(at_shard * o_rows + at_core * (o_rows // 2), o_rows // 2)]
        size = (G if kind == GATE else g.rest) // 2
        first = (0 if kind == GATE else G) + at_core * size
        lanes = pl.ds(pl.multiple_of(at_shard * lanes_of, 128), lanes_of)
        return wf.at[layer, aligned(first, size), lanes]

    line = w == 4

    def fetch(layer, kind):
        mine = part_of(layer, kind, shard, core)
        at = [wire.reserve() for _ in range(w)]
        copies = [
            wire.make(mine, mine, WT, lax.rem(shard + k, w), at[k], at[k]) for k in range(1, w)
        ]
        if line:
            copies[1].start()
            sends.append(copies[1])
            sends.append(Maybe(shard != w - 1, copies[0]).start())
            sends.append(Maybe(shard != 0, copies[2]).start())
        else:
            for copy in copies:
                copy.start()
            sends.extend(copies)
        return copies, at

    def far_part(fetched, layer, kind):
        if not line:
            return []
        at = fetched[1]
        fetched[0][1].wait_recv()
        block = part_of(layer, kind, lax.rem(shard + 2, w), core)
        up = wire.make(block, block, WT, lax.rem(shard + 1, w), at[0], at[3])
        down = wire.make(block, block, WT, lax.rem(shard + w - 1, w), at[0], at[1])
        sends.append(Maybe(shard == 2, up).start())
        sends.append(Maybe(shard == 1, down).start())
        return [put(block, block, SECTION, sibling)]

    def near_parts(fetched, layer, kind):
        found = []
        for k in (1, 3) if line else range(1, w):
            fetched[0][k - 1].wait_recv()
            block = part_of(layer, kind, lax.rem(shard + w - k, w), core)
            found.append(put(block, block, SECTION, sibling))
        return found

    def received(copies):
        for copy in copies:
            copy.wait_recv()

    own_rows = aligned(here * rows, rows)

    def gather(whole):
        def block(group, half):
            size = rows if half is None else rows // 2
            return whole.at[aligned(group * rows + (half or 0) * size, size)]

        return PlaneGather(wire.put, n, here, block(here, None), block)

    def save(source, target):
        saves.append(mover.put(source, target))

    def saved():
        while saves:
            saves.pop().wait()

    for copy in locals_:
        copy.wait()
    received(siblings)
    pending = fetch(0, REST)
    gain_at = g.CX + 128 + G
    r.sel[...] = step_select(g, here).astype(BF)
    pack_small(g, here, r.conv_w, r.conv_b, r.dt_bias, r.a_log, r.skip_d, r.gate_gain, r.norm_gain, r.pack)
    others.append(put(r.pack, packs.at[core], SECTION, sibling))
    locals_later.append(mover.put(r.pack, packs.at[core]))
    for copy in locals_later:
        copy.wait()
    received(others)

    def norm(at):
        h = r.h0[at, :]
        inv = lax.rsqrt(jnp.mean(h * h, axis=1, keepdims=True) + EPSILON)
        r.normed[pl.ds(pl.multiple_of(here * rows + at.start, TILE), TILE), :] = (
            h * inv * packs[0, 0:1, gain_at:]
        ).astype(BF)

    rows_loop(rows, norm)
    arriving = gather(r.normed)
    handed = far_part(pending, 0, REST)
    coming = [fetch(0, GATE), fetch(0, OUT)]
    arriving.forward()
    handed += near_parts(pending, 0, REST)

    for layer in range(2):
        proj, mixed, normed = r.proj, r.mixed, r.normed
        conv = packs.at[layer, :, 0 : g.CX]
        head = packs.at[layer, :, g.CX : g.CX + 128]
        wide = packs.at[layer, :, g.CX + 128 : gain_at]

        def project(lanes):
            proj[:, lanes] = dot(normed[...], wf[layer, lanes, :], 1, 1).astype(BF)

        arriving.wait_recv()
        received(handed)
        gathered = arriving
        column_tiles(G, NC, project)
        scan_forward(
            G, proj, conv, head, wide, r.sel, mixed, r.yp, r.st,
            r.pad, r.xc, r.dts, r.state,
        )
        save(mixed, r.mixed_o.at[layer])
        save(r.yp, r.yp_o.at[layer])
        save(r.st, r.st_o.at[layer])
        save(normed, r.n_o.at[layer])
        handed = far_part(coming[0], layer, GATE) + far_part(coming[1], layer, OUT)
        handed += near_parts(coming[0], layer, GATE) + near_parts(coming[1], layer, OUT)
        if layer == 0:
            pending = fetch(1, REST)
        received(handed)
        column_tiles(0, G, project)
        save(proj, r.proj_o.at[layer])
        gate_forward(G, proj, wide, mixed, r.vg, r.ssq)

        def out_product(block):
            at = aligned(block * rows, rows)

            def tile(lanes):
                r.part[block, :, lanes] = dot(r.vg[at, :], of[layer, :, lanes], 1, 0).astype(BF)

            column_tiles(0, D, tile)

        saved()
        gathered.wait_send()
        summing = PlaneSum(wire.put, n, here, r.part, r.got, r.mid)
        summing.start(out_product, r.ssq, r.got_stat)
        summing.middle()
        summing.end()
        if layer == 0:
            handed = far_part(pending, 1, REST)
            coming = [fetch(1, GATE), fetch(1, OUT)]
        ssq = r.ssq[here]
        for k in range(n - 1):
            ssq = ssq + r.got_stat[k]
        inv2 = lax.rsqrt(ssq * (1.0 / INNER) + EPSILON)
        r.own_stat[...] = inv2
        r.cols[...] = column(inv2[0:1, :])
        if layer == 0:
            r.stat0[...] = inv2

        def finish(at):
            pout = summing.total(at) * r.cols[at, 0:1]
            whole = pl.ds(pl.multiple_of(here * rows + at.start, TILE), TILE)
            h_in = r.h0[at, :] if layer == 0 else r.hbuf[0, at, :]
            h = h_in + pout
            r.hbuf[layer, at, :] = h
            if layer == 0:
                r.pout[at, :] = pout
                r.h1[at, :] = h
                inv = lax.rsqrt(jnp.mean(h * h, axis=1, keepdims=True) + EPSILON)
                r.normed[whole, :] = (h * inv * packs[1, 0:1, gain_at:]).astype(BF)
            else:
                out = r.cot[at, :].astype(BF)
                dots = jnp.sum(out.astype(F32) * pout, axis=1, keepdims=True)
                r.mdots[at, :] = jnp.broadcast_to(dots * (1.0 / INNER), (TILE, 128))
                r.normed[whole, :] = out

        rows_loop(rows, finish)
        if layer == 0:
            arriving = gather(r.normed)
            arriving.forward()
            handed += near_parts(pending, 1, REST)
    r.stats[here] = r.own_stat[...]
    r.stats[here, 1:2, :] = r.mdots[...].T[0:1, :]
    last_rows = gather(r.normed)
    arriving = []
    for k in range(1, n):
        block = r.stats.at[here]
        arriving.append(put(block, block, SEQ, lax.rem(here + k, n)))
    arriving.append(put(r.hbuf.at[1 - core], r.sec.at[core], SECTION, sibling))
    save(r.hbuf.at[core], r.sec.at[core])
    save(packs, r.packs_o)
    save(wf, r.wf_o)
    save(of, r.of_o)
    last_rows.forward()
    last_rows.wait_recv()
    received(arriving)
    save(r.normed, r.gb_o)
    last_rows.wait_send()
    assert wire.used <= r.ss.shape[0] and mover.used <= r.ls.shape[0]
    for copy in sends:
        copy.wait_send()
    saved()


def forward_call(g, n, w, tokens, cotangent, small, w_src, o_src):
    rows = tokens.shape[2]
    L, G, NC, CX, PK = rows * n, g.G, g.NC, g.CX, g.CX + 128 + g.G + D
    S = jax.ShapeDtypeStruct
    shapes = ForwardOuts(
        sec=S((2, rows, D), F32),
        pout=S((rows, D), F32),
        stat0=S((8, 128), F32),
        h1=S((rows, D), F32),
        gb_o=S((L, D), BF),
        stats=S((n, 8, 128), F32),
        packs_o=S((2, 8, PK), F32),
        wf_o=S((2, NC, D), BF),
        of_o=S((2, G, D), BF),
        n_o=S((2, L, D), BF),
        proj_o=S((2, L, NC), BF),
        mixed_o=S((2, L, G), BF),
        yp_o=S((2, L, G), F32),
        st_o=S((2, L // Q, STATE, G), F32),
    )
    scratch = [
        S((rows, D), F32), S((rows, D), F32), shapes.packs_o, shapes.wf_o, shapes.of_o, S((L, D), BF), S((L, NC), BF), S((L, G), BF),
        S((L, G), F32), S((L // Q, STATE, G), F32), S((8 + L, 128), F32), S((L, CX), F32), S((L, 128), F32), S((STATE, G), F32),
        S((L, G), BF), S((n, 8, 128), F32), S((n, rows, D), BF), S((n - 1, rows, D), BF), S((n - 1, 8, 128), F32),
        S((2, rows, D), F32), S((8, 128), F32), S((rows, 128), F32), S((rows, 128), F32),
        S((128, 128), BF), S((8, PK), F32), S((2, rows // 2, D), BF),
    ]
    remote = 4 + 2 * g.runs + 6 * w + 6 * (w - 1) + 24 + 8 * (n - 1)
    outs = pl.pallas_call(
        functools.partial(forward_kernel, g, n, w, rows),
        out_shape=list(shapes),
        in_specs=[ANY, ANY] + [VM] * len(small) + [ANY, ANY],
        out_specs=[VM] * 4 + [ANY, VM] + [ANY] * 8,
        scratch_shapes=[pltpu.VMEM(s.shape, s.dtype) for s in scratch]
        + [
            pltpu.SemaphoreType.DMA((remote,)),
            pltpu.SemaphoreType.DMA((remote,)),
            pltpu.SemaphoreType.DMA((22 + 2 * g.runs,)),
        ],
        compiler_params=pltpu.CompilerParams(
            collective_id=0, has_side_effects=True, vmem_limit_bytes=FORWARD_VMEM
        ),
        name="forward",
    )(tokens, cotangent, *small, w_src, o_src)
    return ForwardOuts(*outs)


class BackwardOuts(NamedTuple):
    ig: Any
    gi: Any
    go: Any
    gi_sib: Any
    go_sib: Any
    small: Any
    far: Any
    late: Any


class BackwardRefs(NamedTuple):
    packs_i: Any
    wf_i: Any
    of_i: Any
    n_i: Any
    proj_i: Any
    mixed_i: Any
    yp_i: Any
    st_i: Any
    gb_i: Any
    stats1_i: Any
    stat0_i: Any
    pout_i: Any
    h1_i: Any
    tokens_i: Any
    cotangent_i: Any
    ig: Any
    gi: Any
    go: Any
    gi_sib: Any
    go_sib: Any
    small: Any
    far: Any
    late: Any
    packs: Any
    wf: Any
    of: Any
    n: Any
    proj: Any
    mixed: Any
    yp: Any
    st: Any
    gb: Any
    stats: Any
    pout: Any
    h1: Any
    h0: Any
    cot: Any
    dy: Any
    pad: Any
    xc: Any
    dts: Any
    dstate: Any
    part: Any
    got: Any
    own_stat: Any
    mdots: Any
    grads: Any
    gw: Any
    gout: Any
    sib_w: Any
    sib_o: Any
    z_w: Any
    z_o: Any
    relay_w: Any
    relay_o: Any
    sm: Any
    sm_sib: Any
    sm_z: Any
    sm_own: Any
    sel: Any
    gain: Any
    gain_z: Any
    gain_sum: Any
    mid: Any
    ss: Any
    rs: Any
    ls: Any
    free: Any


def backward_kernel(g, n, w, rows, *refs):
    r = BackwardRefs(*refs)
    G, NC, CX = g.G, g.NC, g.CX
    core, here, shard = lax.axis_index(SECTION), lax.axis_index(SEQ), lax.axis_index(WT)
    sibling = 1 - core
    wire, mover = Wire(r.ss, r.rs), Mover(r.ls)
    o_half, lanes_of = G // (2 * w), D // w
    gain_at = CX + 128 + G

    def aligned(at, size):
        return pl.ds(pl.multiple_of(at, 16), size)

    def load(layer, *pairs):
        return [mover.put(source.at[layer], target) for source, target in pairs]

    first = load(1, (r.of_i, r.of), (r.proj_i, r.proj), (r.mixed_i, r.mixed))
    first += [mover.put(r.packs_i, r.packs), mover.put(r.gb_i, r.gb), mover.put(r.stats1_i, r.stats)]
    later = load(1, (r.n_i, r.n), (r.yp_i, r.yp), (r.st_i, r.st), (r.wf_i, r.wf))
    later += [mover.put(r.pout_i, r.pout), mover.put(r.h1_i, r.h1), mover.put(r.stat0_i, r.own_stat)]
    later += [mover.put(r.tokens_i.at[core, 0], r.h0), mover.put(r.cotangent_i.at[core, 0], r.cot)]
    meet_all(((SEQ, n), (WT, w), (SECTION, 2)))
    r.sm[...] = jnp.zeros_like(r.sm)
    r.sel[...] = step_select(g, here).astype(BF)
    r.gain[here] = jnp.zeros((8, D), F32)
    open_sends, record = [], {}
    line = w == 4
    arrivals = r.got if r.got.shape[0] == n - 1 else r.far

    def put(src, dst, axis, peer):
        copy = wire.put(src, dst, axis, peer)
        open_sends.append(copy)
        return copy

    def rows_of(kind):
        return ((0, G), (0, G), (G, g.rest))[kind]

    def kept(kind):
        return (slice(0, G // (2 * w)), slice(0, G // 2), slice(G // 2, g.half))[kind]

    def buffers(kind):
        if kind == OUT:
            return r.gout, r.sib_o, r.z_o, r.go, r.go_sib
        return r.gw, r.sib_w, r.z_w, r.gi, r.gi_sib

    def block_of(kind, at_shard, at_core):
        if kind == OUT:
            return aligned((2 * at_shard + at_core) * o_half, o_half), slice(0, D)
        first, size = rows_of(kind)
        return (
            aligned(first + at_core * (size // 2), size // 2),
            pl.ds(pl.multiple_of(at_shard * lanes_of, 128), lanes_of),
        )

    def ready(kind):
        for copy in record.pop(kind, ()):
            copy.wait_send()

    def to_sibling(layer, kind):
        grad, sib, _, _, _ = buffers(kind)
        if layer == 0:
            pl.semaphore_wait(r.free.at[kind], 1)
        if kind == OUT:
            pairs = [
                (grad.at[block_of(kind, q, sibling)], sib.at[aligned(q * o_half, o_half)])
                for q in range(w)
            ]
        else:
            first, size = rows_of(kind)
            rows_there = aligned(first + sibling * (size // 2), size // 2)
            pairs = [(grad.at[rows_there], sib.at[kept(kind)])]
        copies = [wire.put(source, target, SECTION, sibling) for source, target in pairs]
        record[kind] = list(copies)
        return copies

    def to_shards(layer, kind, copies):
        grad, sib, z, _, _ = buffers(kind)
        for copy in copies:
            copy.wait_recv()
        if kind == OUT:
            per = o_half // TILE

            def places(t):
                q = t // per
                return (2 * q + core) * o_half + (t - q * per) * TILE, t * TILE

            steps = w * per
        else:
            first, size = rows_of(kind)
            steps = size // 2 // TILE

            def places(t):
                return first + core * (size // 2) + t * TILE, kept(kind).start + t * TILE

        def add(t, carry):
            mine, theirs = (pl.ds(pl.multiple_of(at, TILE), TILE) for at in places(t))
            grad[mine, :] = (grad[mine, :].astype(F32) + sib[theirs, :].astype(F32)).astype(BF)
            return carry

        lax.fori_loop(0, steps, add, 0)
        if layer == 1:
            pl.semaphore_signal(
                r.free.at[kind], inc=1, device_id={SECTION: sibling}, device_id_type=MESH
            )
        at = [wire.reserve() for _ in range(w)]
        found = []
        for k in range(1, w):
            peer = lax.rem(shard + k, w)
            source = grad.at[block_of(kind, peer, core)]
            found.append(wire.make(source, z.at[layer, k - 1, kept(kind)], WT, peer, at[k], at[k]))
        if not line:
            for copy in found:
                copy.start()
            record[kind] += found
            return found, None
        buffer = (r.relay_o if kind == OUT else r.relay_w).at[layer, kept(kind)]
        up = wire.make(grad.at[block_of(kind, w - 1, core)], buffer, WT, 1, at[0], at[0])
        down = wire.make(grad.at[block_of(kind, 0, core)], buffer, WT, w - 2, at[0], at[0])
        inner = (shard == 1) | (shard == 2)
        first = [
            Maybe(shard == 0, up),
            Maybe(shard == w - 1, down),
            Maybe(inner, found[0]),
            Maybe(inner, found[2]),
        ]
        others = [
            Maybe(jnp.logical_not(inner), found[1]),
            Maybe(shard == 0, found[0]),
            Maybe(shard == w - 1, found[2]),
        ]
        record[kind] += [*first, *others, Maybe(inner, found[1])]
        for copy in first:
            copy.start()
        waiting.extend(others)
        arriving = wire.make(buffer, buffer, WT, lax.rem(shard + 1, w), at[0], at[0])
        return found, arriving

    def relay(layer, kind, moving):
        found, arriving = moving
        if not line:
            return
        grad, buffer = (r.gout, r.relay_o) if kind == OUT else (r.gw, r.relay_w)
        rows_here = kept(kind)

        @pl.when((shard == 1) | (shard == 2))
        def _():
            arriving.wait_recv()
            at_rows, at_lanes = block_of(kind, lax.rem(shard + 2, w), core)

            def add(at):
                mine = pl.ds(pl.multiple_of(at_rows.start + at.start, TILE), TILE)
                there = pl.ds(pl.multiple_of(rows_here.start + at.start, TILE), TILE)
                total = grad[mine, at_lanes].astype(F32) + buffer[layer, there, :].astype(F32)
                grad[mine, at_lanes] = total.astype(BF)

            rows_loop(rows_here.stop - rows_here.start, add)
            found[1].start()

    def to_plane(layer, kind, moving):
        grad, _, z, result, _ = buffers(kind)
        copies, _ = moving
        if line:
            pl.when(shard != 0)(copies[0].wait_recv)
            copies[1].wait_recv()
            pl.when(shard != w - 1)(copies[2].wait_recv)
        else:
            for copy in copies:
                copy.wait_recv()
        at_rows, at_lanes = block_of(kind, shard, core)
        here_rows = kept(kind)

        def add(at):
            mine = pl.ds(pl.multiple_of(at_rows.start + at.start, TILE), TILE)
            there = pl.ds(pl.multiple_of(here_rows.start + at.start, TILE), TILE)
            total = grad[mine, at_lanes].astype(F32)
            for k in range(w - 1):
                total = total + z[layer, k, there, :].astype(F32)
            z[layer, 1, there, :] = total.astype(BF)

        def add_end(at, near):
            mine = pl.ds(pl.multiple_of(at_rows.start + at.start, TILE), TILE)
            there = pl.ds(pl.multiple_of(here_rows.start + at.start, TILE), TILE)
            total = grad[mine, at_lanes].astype(F32)
            total = total + z[layer, 1, there, :].astype(F32) + z[layer, near, there, :].astype(F32)
            z[layer, 1, there, :] = total.astype(BF)

        count = here_rows.stop - here_rows.start
        if line:

            @pl.when(shard == 0)
            def _():
                rows_loop(count, lambda at: add_end(at, 2))

            @pl.when(shard == w - 1)
            def _():
                rows_loop(count, lambda at: add_end(at, 0))

            @pl.when((shard == 1) | (shard == 2))
            def _():
                rows_loop(count, add)
        else:
            rows_loop(count, add)
        def target(group, half):
            size = here_rows.stop - here_rows.start
            if half is None:
                return result.at[layer, group, here_rows]
            first = here_rows.start + half * (size // 2)
            return result.at[layer, group, first : first + size // 2]

        block = z.at[layer, 1, here_rows]
        return PlaneGather(put, n, here, block, target), mover.put(block, target(here, None))

    def landed(kind, *arrivals):
        _, _, _, result, target = buffers(kind)
        for found, own in arrivals:
            found.wait_recv()
            own.wait()
        return put(result.at[sibling, :, kept(kind)], target.at[:, kept(kind)], SECTION, sibling)

    def done(copies):
        for copy in copies:
            copy.wait()

    arrived, waiting = {}, []
    for layer in (1, 0):
        conv = r.packs.at[layer, :, 0:CX]
        head = r.packs.at[layer, :, CX : CX + 128]
        wide = r.packs.at[layer, :, CX + 128 : gain_at]
        g_conv = r.sm.at[layer, :, 0:CX]
        g_head = r.sm.at[layer, :, CX : CX + 128]
        g_wide = r.sm.at[layer, :, CX + 128 : gain_at]
        g_gain = r.sm.at[layer, :, gain_at : gain_at + D] if layer == 1 else r.gain.at[here]
        done(first)

        def d_normed(lanes):
            r.xc[:, lanes] = dot(r.gb[...], r.of[lanes, :], 1, 1)

        column_tiles(0, G, d_normed)
        gate_backward(
            G, r.proj, r.mixed, r.xc, r.stats, wide, r.dy, g_wide
        )

        def out_rows(t, carry):
            at = pl.ds(pl.multiple_of(t * 128, 128), 128)
            r.gout[at, :] = dot(r.mixed[:, at], r.gb[...], 0, 0).astype(BF)
            return carry

        def in_rows(first, last):
            def step(t, carry):
                at = pl.ds(pl.multiple_of(t * 128, 128), 128)
                r.gw[at, :] = dot(r.proj[:, at], r.n[...], 0, 0).astype(BF)
                return carry

            lax.fori_loop(first // 128, last // 128, step, 0)

        ready(OUT)
        lax.fori_loop(0, G // 128, out_rows, 0)
        out_sib = to_sibling(layer, OUT)
        done(later)
        ready(GATE)
        in_rows(0, G)
        gate_sib = to_sibling(layer, GATE)
        out_z = to_shards(layer, OUT, out_sib)
        gate_z = to_shards(layer, GATE, gate_sib)
        if layer == 0:
            arrived[1, OUT][0].forward()
            arrived[1, GATE][0].forward()
            arrived[1, REST] = to_plane(1, REST, rest_z)

        def serve():
            for copy in waiting:
                copy.start()

        scan_backward(
            G, r.proj, r.dy, r.yp, r.st, conv, head, wide, r.sel, g_wide, g_conv, g_head,
            r.pad, r.xc, r.dts, r.dstate, serve,
        )
        waiting.clear()
        relay(layer, OUT, out_z)
        relay(layer, GATE, gate_z)
        if layer == 0:
            small_sib = put(r.sm.at[sibling], r.sm_sib, SECTION, sibling)
        if layer == 0:
            arrived[1, REST][0].forward()
            small_sib.wait_recv()
            r.sm_own[...] = r.sm[core] + r.sm_sib[...]
            small_z = [
                put(r.sm_own, r.sm_z.at[k - 1], WT, lax.rem(shard + k, w)) for k in range(1, w)
            ]
        if layer == 1:
            first = load(0, (r.of_i, r.of), (r.mixed_i, r.mixed))
            later = load(0, (r.yp_i, r.yp), (r.st_i, r.st))

        def in_product(block):
            at = aligned(block * rows, rows)

            def tile(lanes):
                r.part[block, :, lanes] = dot(r.proj[at, :], r.wf[:, lanes], 1, 0).astype(BF)

            column_tiles(0, D, tile)

        summing = PlaneSum(wire.put, n, here, r.part, arrivals, r.mid)

        def rest_gradient():
            ready(REST)
            in_rows(G, NC)
            return to_sibling(layer, REST)

        if layer == 0:
            rest_sib = rest_gradient()
            rest_z = to_shards(layer, REST, rest_sib)
        summing.start(in_product)
        if layer == 1:
            later += load(0, (r.wf_i, r.wf))
        summing.middle()
        if layer == 1:
            rest_sib = rest_gradient()
            first += load(0, (r.proj_i, r.proj))
            later += load(0, (r.n_i, r.n))
            rest_z = to_shards(layer, REST, rest_sib)
        summing.end()
        while waiting:
            waiting.pop(0).start()
        if arrivals is not r.got:
            done(
                [
                    mover.put(arrivals.at[k - 1], r.part.at[lax.rem(here + k, n)])
                    for k in range(1, n)
                ]
            )

        def finish(at):
            if arrivals is r.got:
                d_in = summing.total(at)
            else:
                d_in = r.part[0, at, :].astype(F32)
                for k in range(1, n):
                    d_in = d_in + r.part[k, at, :].astype(F32)
            h = r.h1[at, :] if layer == 1 else r.h0[at, :]
            above = r.cot[at, :] if layer == 1 else r.grads[1, at, :]
            inv = lax.rsqrt(jnp.mean(h * h, axis=1, keepdims=True) + EPSILON)
            normed = h * inv
            g_gain[0:1, :] += jnp.sum(d_in * normed, axis=0, keepdims=True)
            d_s = d_in * r.packs[layer, 0:1, gain_at:]
            d_h = above + inv * (d_s - normed * jnp.mean(d_s * normed, axis=1, keepdims=True))
            r.grads[layer, at, :] = d_h
            if layer == 1:
                out = d_h.astype(BF)
                whole = pl.ds(pl.multiple_of(here * rows + at.start, TILE), TILE)
                r.gb[whole, :] = out
                dots = jnp.sum(out.astype(F32) * r.pout[at, :], axis=1, keepdims=True)
                r.mdots[at, :] = jnp.broadcast_to(dots * (1.0 / INNER), (TILE, 128))

        rows_loop(rows, finish)
        if layer == 1:
            r.stats[here] = r.own_stat[...]
            r.stats[here, 1:2, :] = r.mdots[...].T[0:1, :]
            own = aligned(here * rows, rows)
            gathering = []

            def rows_of_group(group, half):
                size = rows if half is None else rows // 2
                return r.gb.at[aligned(group * rows + (half or 0) * size, size)]

            grad_rows = PlaneGather(put, n, here, r.gb.at[own], rows_of_group)
            for k in range(1, n):
                peer = lax.rem(here + k, n)
                gathering.append(put(r.stats.at[here], r.stats.at[here], SEQ, peer))
            relay(1, REST, rest_z)
            grad_rows.forward()
            arrived[1, OUT] = to_plane(1, OUT, out_z)
            arrived[1, GATE] = to_plane(1, GATE, gate_z)
            grad_rows.wait_recv()
            for copy in gathering:
                copy.wait_recv()
    gains = []
    ends = [put(r.grads.at[sibling], r.ig.at[core], SECTION, sibling)]
    for k in range(1, n):
        gains.append(put(r.gain.at[here], r.gain.at[here], SEQ, lax.rem(here + k, n)))
    local_grad = mover.put(r.grads.at[core], r.ig.at[core])
    relay(0, REST, rest_z)
    arrived[0, OUT] = to_plane(0, OUT, out_z)
    arrived[0, GATE] = to_plane(0, GATE, gate_z)
    arrived[0, OUT][0].forward()
    arrived[0, GATE][0].forward()
    for copy in small_z:
        copy.wait_recv()
    total = r.sm_own[...]
    for k in range(w - 1):
        total = total + r.sm_z[k]
    r.small[here] = total
    sums = [
        put(r.small.at[here], r.small.at[here], SEQ, lax.rem(here + k, n)) for k in range(1, n)
    ]
    for copy in gains:
        copy.wait_recv()
    total = r.gain[0]
    for k in range(1, n):
        total = total + r.gain[k]
    r.gain_z[shard] = total
    gains = [
        put(r.gain_z.at[shard], r.gain_z.at[shard], WT, lax.rem(shard + k, w)) for k in range(1, w)
    ]
    arrived[0, REST] = to_plane(0, REST, rest_z)
    ends.append(landed(OUT, arrived[1, OUT], arrived[0, OUT]))
    ends.append(landed(GATE, arrived[1, GATE], arrived[0, GATE]))
    arrived[1, REST][0].wait_recv()
    arrived[1, REST][1].wait()
    last, last_own = arrived[0, REST]

    def hand_over(group):
        source, target = r.gi.at[sibling, group, kept(REST)], r.gi_sib.at[group, kept(REST)]
        ends.append(put(source, target, SECTION, sibling))

    last_own.wait()
    hand_over(here)
    if last.plane:
        last.forward(hand_over)
        last.wait_recv()
        hand_over(lax.rem(last.x + 2, 4))
    else:
        last.wait_recv()
        for k in range(1, n):
            hand_over(lax.rem(here + k, n))
    for copy in gains:
        copy.wait_recv()
    total = r.gain_z[0]
    for k in range(1, w):
        total = total + r.gain_z[k]
    r.gain_sum[core] = total
    ends.append(put(r.gain_sum.at[core], r.gain_sum.at[core], SECTION, sibling))
    for copy in ends + sums:
        copy.wait_recv()
    r.late[...] = r.gain_sum[0] + r.gain_sum[1]
    local_grad.wait()
    assert wire.used <= r.ss.shape[0] and mover.used <= r.ls.shape[0]
    for kind in KINDS:
        ready(kind)
    for copy in open_sends:
        copy.wait_send()


def backward_call(g, n, w, fwd, tokens, cotangent):
    rows = tokens.shape[2]
    L, G, NC, CX = rows * n, g.G, g.NC, g.CX
    PK = CX + 128 + G + D
    S = jax.ShapeDtypeStruct
    o_half, lanes_of = G // (2 * w), D // w
    spill = n > 8
    outs = BackwardOuts(
        ig=S((2, rows, D), F32),
        gi=S((2, n, g.half, lanes_of), BF),
        go=S((2, n, o_half, D), BF),
        gi_sib=S((n, g.half, lanes_of), BF),
        go_sib=S((n, o_half, D), BF),
        small=S((n, 8, PK), F32),
        far=S((n - 1, rows, D) if spill else (8, 128), BF),
        late=S((8, D), F32),
    )
    scratch = [
        S((2, 8, PK), F32), S((NC, D), BF), S((G, D), BF), S((L, D), BF), S((L, NC), BF), S((L, G), BF),
        S((L, G), F32), S((L // Q, STATE, G), F32), S((L, D), BF), S((n, 8, 128), F32), S((rows, D), F32),
        S((rows, D), F32), S((rows, D), F32), S((rows, D), F32),
        S((L, G), BF), S((8 + L, 128), F32), S((L, CX), F32), S((L, 128), F32), S((STATE, G), F32),
        S((n, rows, D), BF), S((1 if spill else n - 1, rows, D), BF), S((8, 128), F32), S((rows, 128), F32), S((2, rows, D), F32),
        S((NC, D), BF), S((G, D), BF), S((g.half, D), BF), S((G // 2, D), BF),
        S((2, w - 1, g.half, lanes_of), BF),
        S((2, w - 1, o_half, D), BF), S((2, g.half, lanes_of), BF), S((2, o_half, D), BF), S((2, 8, PK), F32), S((8, PK), F32), S((w - 1, 8, PK), F32), S((8, PK), F32),
        S((128, 128), BF), S((n, 8, D), F32), S((w, 8, D), F32), S((2, 8, D), F32),
        S((2, rows // 2, D), BF),
    ]
    remote = 2 * (3 * (w + w + n - 1) + n - 1) + 2 * (n - 1) + 40 + 2 * (w - 1) + 2 * (n - 1) + n
    args = [
        fwd.packs_o, fwd.wf_o, fwd.of_o, fwd.n_o, fwd.proj_o, fwd.mixed_o, fwd.yp_o, fwd.st_o,
        fwd.gb_o, fwd.stats, fwd.stat0, fwd.pout, fwd.h1, tokens, cotangent,
    ]
    results = pl.pallas_call(
        functools.partial(backward_kernel, g, n, w, rows),
        out_shape=list(outs),
        in_specs=[ANY] * len(args),
        out_specs=[VM, ANY, ANY, ANY, ANY, VM, ANY, VM],
        scratch_shapes=[pltpu.VMEM(s.shape, s.dtype) for s in scratch]
        + [
            pltpu.SemaphoreType.DMA((remote,)),
            pltpu.SemaphoreType.DMA((remote,)),
            pltpu.SemaphoreType.DMA((36 + 2 * n,)),
            pltpu.SemaphoreType.REGULAR((3,)),
        ],
        compiler_params=pltpu.CompilerParams(
            collective_id=1, has_side_effects=True, vmem_limit_bytes=BACKWARD_VMEM
        ),
        name="backward",
    )(*args)
    return BackwardOuts(*results)


def pack_small(g, here, conv_ref, bias_ref, dtb_ref, a_ref, skip_ref, gate_ref, norm_ref, pack_ref):
    G, width = g.G, g.run_heads * HEAD_DIM
    win = -(-(width + 64) // 128) * 128
    start = here * width
    base = pl.multiple_of(start // 128 * 128, 128)
    from_ids = lax.broadcasted_iota(jnp.int32, (win, G), 0)
    to_ids = lax.broadcasted_iota(jnp.int32, (win, G), 1)
    exact = lax.Precision.HIGHEST

    def take(ref, rows):
        total = jnp.zeros((rows, G), F32)
        for run in range(g.runs):
            window = ref[0:rows, pl.ds(pl.multiple_of(base + run * (INNER // g.runs), 128), win)]
            inside = (to_ids >= run * width) & (to_ids < (run + 1) * width)
            pick = one_hot(inside & (from_ids == to_ids - run * width + (start - base)))
            total = total + dot(window, pick, 1, 0, exact)
        return total

    head_from = lax.broadcasted_iota(jnp.int32, (HEADS, 128), 0)
    head_to = lax.broadcasted_iota(jnp.int32, (HEADS, 128), 1)
    head_pick = one_hot((head_from == head_of(g, here, head_to)) & (head_to < g.heads))
    wide_from = lax.broadcasted_iota(jnp.int32, (HEADS, G), 0)
    wide_to = lax.broadcasted_iota(jnp.int32, (HEADS, G), 1)
    wide_pick = (wide_from == head_of(g, here, wide_to // HEAD_DIM)) & (wide_to < g.chans)
    head_at, wide_at, gain_at = g.CX, g.CX + 128, g.CX + 128 + G
    pack_ref[...] = jnp.zeros_like(pack_ref)
    pack_ref[0:KERNEL, 0:G] = take(conv_ref, KERNEL)
    pack_ref[4:5, 0:G] = take(bias_ref, 1)
    pack_ref[0:KERNEL, G:head_at] = conv_ref[:, INNER:]
    pack_ref[4:5, G:head_at] = bias_ref[:, INNER:]
    pack_ref[0:1, head_at:wide_at] = dot(dtb_ref[...], head_pick, 1, 0, exact)
    pack_ref[1:2, head_at:wide_at] = dot(-jnp.exp(a_ref[...]), head_pick, 1, 0, exact)
    pack_ref[0:1, wide_at:gain_at] = take(gate_ref, 1)
    pack_ref[1:2, wide_at:gain_at] = dot(skip_ref[...], one_hot(wide_pick), 1, 0, exact)
    pack_ref[0:1, gain_at:] = norm_ref[...]


def halves_of_heads(g, ref_of, column_at, head):
    parts = []
    for h in (head, head + 1):
        stride = HEADS // g.runs
        group = h % stride // g.run_heads
        local_head = h // stride * g.run_heads + h % g.run_heads
        value = ref_of(group, slice(column_at + local_head // 2 * 128, column_at + local_head // 2 * 128 + 128))
        parts.append(value if local_head % 2 == h % 2 else pltpu.roll(value, HEAD_DIM, 1))
    lanes = lax.broadcasted_iota(jnp.int32, parts[0].shape, 1)
    return jnp.where(lanes < HEAD_DIM, parts[0], parts[1])


def layout_kernel(g, own_ref, sib_ref, own_out_ref, sib_out_ref, small_ref, late_ref, sec_ref, ig_ref, g_in_ref, g_out_ref, sec_out, ig_out, norm_ref, conv_ref, bias_ref, dtb_ref, a_ref, skip_ref, gate_ref):
    n, G = g.n_seq, g.G
    first_core = lax.axis_index(SECTION) == 0

    def all_rows(halves, outs):
        def copy(groups, kind_at, half_at, half_rows, source, target, size):
            done = 0
            while done < size:
                half, offset = divmod(source + done, half_rows)
                count = min(size - done, half_rows - offset)
                at = slice(half_at + offset, half_at + offset + count)
                total = None
                for group in groups:
                    value = halves[half][group, at, :].astype(F32)
                    total = value if total is None else total + value
                g_in_ref[target + done : target + done + count, :] = total
                done += count

        for half in range(2):
            g_out_ref[:, half] = outs[half][...].astype(F32)
        width = g.run_heads * HEAD_DIM
        rest = (G, G // 2, g.rest // 2)
        everyone = range(n)
        for run in range(g.runs):
            for group in range(n):
                target = run * (INNER // g.runs) + group * width
                copy([group], 0, 0, G // 2, run * width, target, width)
                copy([group], *rest, run * width, INNER + target, width)
        copy(everyone, *rest, G, 2 * INNER, 2 * STATE)
        copy(everyone, *rest, G + 2 * STATE, 2 * INNER + 2 * STATE, HEADS)

    sec_out[...] = sec_ref[...]
    ig_out[...] = ig_ref[...]
    own, own_out = own_ref.at[0], own_out_ref.at[0]

    @pl.when(first_core)
    def _():
        all_rows((own, sib_ref), (own_out, sib_out_ref))

    @pl.when(jnp.logical_not(first_core))
    def _():
        all_rows((sib_ref, own), (sib_out_ref, own_out))

    @pl.when(pl.program_id(0) == 0)
    def _():
        from_ids = lax.broadcasted_iota(jnp.int32, (128, HEADS), 0)
        to_ids = lax.broadcasted_iota(jnp.int32, (128, HEADS), 1)
        picks = [one_hot((to_ids == head_of(g, group, from_ids)) & (from_ids < g.heads)) for group in range(n)]
        exact = lax.Precision.HIGHEST
        head_at, wide_at, gain_at = g.CX, g.CX + 128, g.CX + 128 + G

        def small(group, columns):
            return small_ref[group, :, columns]

        for head in range(0, HEADS, 2):
            at = slice(head * HEAD_DIM, head * HEAD_DIM + 128)
            conv = halves_of_heads(g, small, 0, head)
            conv_ref[:, at] = conv[0:KERNEL]
            bias_ref[:, at] = conv[KERNEL : KERNEL + 1]
            gate_ref[:, at] = halves_of_heads(g, small, wide_at, head)[0:1]
        conv = small(0, slice(G, head_at))
        norm = small(0, slice(gain_at, gain_at + D))
        for group in range(1, n):
            conv = conv + small(group, slice(G, head_at))
            norm = norm + small(group, slice(gain_at, gain_at + D))
        conv_ref[:, INNER:] = conv[0:KERNEL]
        bias_ref[:, INNER:] = conv[KERNEL : KERNEL + 1]
        norm_ref[...] = jnp.where(first_core, late_ref[0:1, :], norm[0:1])
        heads = jnp.zeros((8, HEADS), F32)
        skips = jnp.zeros((8, HEADS), F32)
        wide_from = lax.broadcasted_iota(jnp.int32, (G, HEADS), 0)
        wide_to = lax.broadcasted_iota(jnp.int32, (G, HEADS), 1)
        for group in range(n):
            heads = heads + dot(small(group, slice(head_at, wide_at)), picks[group], 1, 0, exact)
            pick = (wide_to == head_of(g, group, wide_from // HEAD_DIM)) & (wide_from < g.chans)
            skips = skips + dot(small(group, slice(wide_at, gain_at)), one_hot(pick), 1, 0, exact)
        dtb_ref[...] = heads[0:1]
        a_ref[...] = heads[1:2]
        skip_ref[...] = skips[1:2]


def layout_call(g, core, gi, gi_sib, go, go_sib, small, late, sec, ig):
    _, n, half, lanes = gi.shape
    out_half = go.shape[2]
    steps = lanes // 128
    out_lanes = D // steps
    rows_spec = pl.BlockSpec(sec.shape[:2] + (out_lanes,), lambda t, c: (0, 0, t))
    PK = small.shape[2]
    columns = 2 * INNER + 2 * STATE + HEADS
    S = jax.ShapeDtypeStruct
    shapes = (
        S((columns, lanes), F32), S((n, 2, out_half, D), F32), S(sec.shape, F32), S(ig.shape, F32), S((1, D), F32), S((KERNEL, CONV), F32),
        S((1, CONV), F32), S((1, HEADS), F32), S((1, HEADS), F32), S((1, HEADS), F32), S((1, INNER), F32),
    )
    return pl.pallas_call(
        lambda core_ref, *refs: layout_kernel(g, *refs),
        grid_spec=pltpu.PrefetchScalarGridSpec(
            num_scalar_prefetch=1,
            grid=(steps,),
            in_specs=[
                pl.BlockSpec((1, n, half, 128), lambda t, c: (c[0], 0, 0, t)),
                pl.BlockSpec((n, half, 128), lambda t, c: (0, 0, t)),
                pl.BlockSpec((1, n, out_half, out_lanes), lambda t, c: (c[0], 0, 0, t)),
                pl.BlockSpec((n, out_half, out_lanes), lambda t, c: (0, 0, t)),
                pl.BlockSpec((n, 8, PK), lambda t, c: (0, 0, 0)),
                pl.BlockSpec((8, D), lambda t, c: (0, 0)),
                rows_spec,
                rows_spec,
            ],
            out_specs=[
                pl.BlockSpec((columns, 128), lambda t, c: (0, t)),
                pl.BlockSpec((n, 2, out_half, out_lanes), lambda t, c: (0, 0, 0, t)),
                rows_spec,
                rows_spec,
            ]
            + [pl.BlockSpec(s.shape, lambda t, c: (0, 0)) for s in shapes[4:]],
        ),
        out_shape=shapes,
        compiler_params=pltpu.CompilerParams(vmem_limit_bytes=SMALL_VMEM),
        name="layout",
    )(core, gi, gi_sib, go, go_sib, small, late, sec, ig)


def local(
    tokens, cotangent, norm_gain, w_in, conv_w, conv_b, dt_bias, a_log, skip_d, gate_gain, w_out
):
    n_seq, n_wt = lax.axis_size(SEQ), lax.axis_size(WT)
    here = lax.axis_index(SEQ)
    group = Group(n_seq, n_wt)
    core = lax.axis_index(SECTION).reshape(1)
    G = group.G

    small = (conv_w[0], conv_b, dt_bias, a_log, skip_d, gate_gain, norm_gain)
    w_src = jnp.swapaxes(w_in[0], 0, 1)
    if group.runs == n_wt:
        o_src = w_out[0]
    else:
        o_src = lax.all_gather(w_out[0], WT, axis=0, tiled=True)
        o_src = lax.dynamic_slice_in_dim(o_src, here * group.chans, group.chans, 0)
        o_src = jnp.pad(o_src, ((0, G - group.chans), (0, 0)))
    fwd = forward_call(group, n_seq, n_wt, tokens, cotangent, small, w_src, o_src)
    bwd = backward_call(group, n_seq, n_wt, fwd, tokens, cotangent)
    g_in, g_out, section_out, input_grad, g_norm, g_conv, g_bias, g_dtb, g_a, g_skip, g_gate = layout_call(
        group, core, bwd.gi, bwd.gi_sib, bwd.go, bwd.go_sib, bwd.small, bwd.late, fwd.sec, bwd.ig
    )
    if group.runs == n_wt:
        g_out = g_out.reshape(INNER // n_wt, D)
    else:
        g_out = g_out.astype(BF).reshape(n_seq, G // n_wt, D)
        g_out = lax.all_gather(g_out, WT, axis=1, tiled=True)[:, : group.chans].reshape(INNER, D)
        mine = INNER // n_wt
        g_out = lax.dynamic_slice_in_dim(g_out, lax.axis_index(WT) * mine, mine, 0).astype(F32)
    return (
        section_out[None, :, None],
        input_grad[None, :, None],
        g_norm,
        jnp.swapaxes(g_in, 0, 1)[None],
        g_conv[None],
        g_bias,
        g_dtb,
        g_a,
        g_skip,
        g_gate,
        g_out[None],
    )


def solution(mesh):
    placed = (
        P(None, WT, SEQ, None),
        P(None, WT, SEQ, None),
        P(SECTION, None),
        P(SECTION, WT, None),
        P(SECTION, None, None),
        P(SECTION, None),
        P(SECTION, None),
        P(SECTION, None),
        P(SECTION, None),
        P(SECTION, None),
        P(SECTION, WT, None),
    )
    return jax.shard_map(
        local,
        mesh=mesh,
        in_specs=placed,
        out_specs=(
            P(SECTION, None, WT, SEQ, None),
            P(SECTION, None, WT, SEQ, None),
            P(SECTION, None),
            P(SECTION, WT, None),
            P(SECTION, None, None),
            P(SECTION, None),
            P(SECTION, None),
            P(SECTION, None),
            P(SECTION, None),
            P(SECTION, None),
            P(SECTION, WT, None),
        ),
        check_vma=False,
    )
```

```python
import functools
from typing import Any, NamedTuple

import jax
import jax.numpy as jnp
from jax import lax
from jax.experimental import pallas as pl
from jax.experimental.pallas import tpu as pltpu
from jax.sharding import PartitionSpec as P

D = 1536
HEADS = 48
HEAD_DIM = 64
STATE = 128
KERNEL = 4
INNER = 3072
CONV = 3328
EPSILON = 1e-05

Q = 128
F32 = jnp.float32
BF = jnp.bfloat16
SEQ, WT, SECTION = "seq", "wt", "section"
FORWARD_VMEM = 56 * 2**20
BACKWARD_VMEM = 62 * 2**20
SMALL_VMEM = 60 * 2**20
MESH = pl.DeviceIdType.MESH
VM = pl.BlockSpec(memory_space=pltpu.VMEM)
ANY = pl.BlockSpec(memory_space=pl.ANY)
TILE = 16


def dot(a, b, ca, cb, precision=None):
    return lax.dot_general(a, b, (((ca,), (cb,)), ((), ())), precision=precision, preferred_element_type=F32)

def sigmoid(x):
    return 1.0 / (1.0 + jnp.exp(-x))

def softplus(x):
    return jnp.maximum(x, 0.0) + jnp.log1p(jnp.exp(-jnp.abs(x)))

def lane_mask(rows):
    return lax.broadcasted_iota(jnp.int32, (rows, 128), 1) < HEAD_DIM

def spread(cols, pair, mask):
    a = jnp.broadcast_to(cols[:, 2 * pair : 2 * pair + 1], mask.shape)
    b = jnp.broadcast_to(cols[:, 2 * pair + 1 : 2 * pair + 2], mask.shape)
    return jnp.where(mask, a, b)

def split_pair(u, mask):
    zero = jnp.zeros_like(u)
    return jnp.concatenate([jnp.where(mask, u, zero), jnp.where(mask, zero, u)], axis=0)

def conv_tile(proj_ref, cw_ref, pad, proj_at, conv_at, rows):
    pad[0:8, :] = jnp.zeros((8, 128), F32)
    pad[8 : 8 + rows, :] = proj_ref[:, pl.ds(proj_at, 128)].astype(F32)
    pre = jnp.broadcast_to(cw_ref[4:5, pl.ds(conv_at, 128)], (rows, 128))
    for k in range(KERNEL):
        pre = pre + cw_ref[k : k + 1, pl.ds(conv_at, 128)] * pad[5 + k : 5 + k + rows, :]
    return pre

def step_inputs(proj_ref, at, hp_ref, sel_ref, dt_at):
    return dot(proj_ref[at, dt_at : dt_at + 128], sel_ref[...], 1, 0) + hp_ref[0:1, :]

def chunk_factors(dt, hp_ref):
    rate = dt * hp_ref[1:2, :]
    rows = lax.broadcasted_iota(jnp.int32, (Q, Q), 0)
    cols = lax.broadcasted_iota(jnp.int32, (Q, Q), 1)
    tri = (rows >= cols).astype(F32)
    cum = dot(tri, rate, 1, 0, lax.Precision.HIGHEST)
    return rate, cum, rows >= cols

def decay_pair(cum, cum_t, causal, pair):
    parts = []
    for h in (2 * pair, 2 * pair + 1):
        diff = jnp.broadcast_to(cum[:, h : h + 1], (Q, Q)) - jnp.broadcast_to(cum_t[h : h + 1, :], (Q, Q))
        parts.append(jnp.exp(jnp.where(causal, diff, -1e30)))
    return jnp.concatenate(parts, axis=1)

def scan_forward(G, proj_ref, cw_ref, hp_ref, gw_ref, sel_ref, mixed_ref, yp_ref, st_ref, pad, xc, dts, state):
    L = proj_ref.shape[0]

    def conv(tile, carry):
        lanes = pl.ds(pl.multiple_of(tile * 128, 128), 128)
        pre = conv_tile(proj_ref, cw_ref, pad, pl.multiple_of(G + tile * 128, 128), lanes.start, L)
        xc[:, lanes] = pre * sigmoid(pre)
        return carry

    lax.fori_loop(0, (G + 2 * STATE) // 128, conv, 0)
    dt_at = 2 * G + 2 * STATE
    dts[...] = softplus(step_inputs(proj_ref, slice(0, L), hp_ref, sel_ref, dt_at))
    state[...] = jnp.zeros_like(state)
    mask = lane_mask(Q)

    def chunk(c, _):
        at = pl.ds(pl.multiple_of(c * Q, Q), Q)
        dt = dts[at, :]
        rate, cum, causal = chunk_factors(dt, hp_ref)
        cum_t = cum.T
        last = cum[Q - 1 : Q, :]
        e_cum = jnp.exp(cum)
        tail = jnp.exp(last - cum) * dt
        e_last = jnp.broadcast_to(jnp.exp(last), (8, 128))
        b = xc[at, G : G + STATE].astype(BF)
        cc = xc[at, G + STATE : G + 2 * STATE].astype(BF)
        scores = dot(cc, b, 1, 1)
        scores2 = jnp.concatenate([scores, scores], axis=1)
        for p in range(G // 128):
            lanes = slice(p * 128, p * 128 + 128)
            x = xc[at, lanes]
            u = (x * spread(dt, p, mask)).astype(BF)
            m = (scores2 * decay_pair(cum, cum_t, causal, p)).astype(BF)
            before = state[:, lanes]
            st_ref[c, :, lanes] = before
            y = dot(m, split_pair(u, mask), 1, 0)
            y = y + dot(cc, before.astype(BF), 1, 0) * spread(e_cum, p, mask)
            yp_ref[at, lanes] = y
            after = dot(b, (x * spread(tail, p, mask)).astype(BF), 0, 0)
            state[:, lanes] = before * spread(e_last, p, mask[0:8])[0:1, :] + after
            mixed_ref[at, lanes] = (y + gw_ref[1:2, lanes] * x).astype(BF)
        return 0

    lax.fori_loop(0, L // Q, chunk, 0)


def gate_forward(G, proj_ref, gw_ref, mixed_ref, vg_ref, ssq_ref):
    def chunk(c, _):
        at = pl.ds(pl.multiple_of(c * Q, Q), Q)
        ssq = jnp.zeros((Q, 1), F32)
        for p in range(G // 128):
            lanes = slice(p * 128, p * 128 + 128)
            gate = proj_ref[at, lanes].astype(F32)
            v = mixed_ref[at, lanes].astype(F32) * (gate * sigmoid(gate))
            vg_ref[at, lanes] = (v * gw_ref[0:1, lanes]).astype(BF)
            ssq = ssq + jnp.sum(v * v, axis=1, keepdims=True)
        ssq_ref[c] = jnp.broadcast_to(ssq, (Q, 128)).T[0:8, :]
        return 0

    lax.fori_loop(0, proj_ref.shape[0] // Q, chunk, 0)


def lane_sums(values, pick):
    high = values.astype(BF)
    low = (values - high.astype(F32)).astype(BF)
    return dot(high, pick, 1, 0) + dot(low, pick, 1, 0)


def gate_backward(G, proj_ref, mixed_ref, dn_ref, sc_ref, gw_ref, dy_ref, gg_ref):
    gg_ref[...] = jnp.zeros_like(gg_ref)

    def chunk(c, _):
        at = pl.ds(pl.multiple_of(c * Q, Q), Q)
        sc = jnp.concatenate([sc_ref[c], jnp.zeros((Q - 8, 128), F32)], axis=0).T
        inv2 = jnp.broadcast_to(sc[:, 0:1], (Q, 128))
        mdot = jnp.broadcast_to(sc[:, 1:2], (Q, 128))
        for p in range(G // 128):
            lanes = slice(p * 128, p * 128 + 128)
            gate = proj_ref[at, lanes].astype(F32)
            sig = sigmoid(gate)
            act = gate * sig
            mixed = mixed_ref[at, lanes].astype(F32)
            n2 = mixed * act * inv2
            mixed_ref[at, lanes] = (n2 * gw_ref[0:1, lanes]).astype(BF)
            dn = dn_ref[at, lanes]
            gg_ref[0:1, lanes] += jnp.sum(dn * n2, axis=0, keepdims=True)
            d_v = inv2 * (dn * gw_ref[0:1, lanes] - n2 * mdot)
            dy_ref[at, lanes] = (d_v * act).astype(BF)
            proj_ref[at, lanes] = (d_v * mixed * (sig * (1.0 + gate * (1.0 - sig)))).astype(BF)
        return 0

    lax.fori_loop(0, proj_ref.shape[0] // Q, chunk, 0)


def scan_backward(G, proj_ref, dy_ref, yp_ref, st_ref, cw_ref, hp_ref, gw_ref, sel_ref, gg_ref, gc_ref, gh_ref,
                  pad, xc, dts, dstate, serve):
    L = proj_ref.shape[0]
    nb = L // Q
    mask = lane_mask(Q)

    def conv(tile, carry):
        lanes = pl.ds(pl.multiple_of(tile * 128, 128), 128)
        pre = conv_tile(proj_ref, cw_ref, pad, pl.multiple_of(G + tile * 128, 128), lanes.start, L)
        xc[:, lanes] = pre * sigmoid(pre)
        return carry

    lax.fori_loop(0, (G + 2 * STATE) // 128, conv, 0)
    dt_at = 2 * G + 2 * STATE
    dts[...] = softplus(step_inputs(proj_ref, slice(0, L), hp_ref, sel_ref, dt_at))
    dstate[...] = jnp.zeros_like(dstate)
    gh_ref[...] = jnp.zeros_like(gh_ref)

    def chunk(step, _):
        c = nb - 1 - step
        pl.when(step == nb // 4)(serve)
        at = pl.ds(pl.multiple_of(c * Q, Q), Q)
        dt = dts[at, :]
        rate, cum, causal = chunk_factors(dt, hp_ref)
        cum_t = cum.T
        last = cum[Q - 1 : Q, :]
        e_cum = jnp.exp(cum)
        tail = jnp.exp(last - cum)
        e_last = jnp.broadcast_to(jnp.exp(last), (8, 128))
        b = xc[at, G : G + STATE].astype(BF)
        cc = xc[at, G + STATE : G + 2 * STATE].astype(BF)
        scores = dot(cc, b, 1, 1)
        scores2 = jnp.concatenate([scores, scores], axis=1)
        d_scores = jnp.zeros((Q, Q), F32)
        d_b = jnp.zeros((Q, STATE), F32)
        d_c = jnp.zeros((Q, STATE), F32)
        d_cum = jnp.zeros((Q, 128), F32)
        d_dt = jnp.zeros((Q, 128), F32)
        d_last = jnp.zeros((8, 128), F32)
        lane_ids = lax.broadcasted_iota(jnp.int32, (Q, 128), 1)
        row_ids = lax.broadcasted_iota(jnp.int32, (Q, 128), 0)
        for p in range(G // 128):
            lanes = slice(p * 128, p * 128 + 128)
            dyb = dy_ref[at, lanes]
            d_y = dyb.astype(F32)
            x = xc[at, lanes]
            dt_x = spread(dt, p, mask)
            u = (x * dt_x).astype(BF)
            u2 = split_pair(u, mask)
            uf = u.astype(F32)
            dec = decay_pair(cum, cum_t, causal, p)
            m = (scores2 * dec).astype(BF)
            dm = dot(dyb, u2, 1, 1) * dec
            d_scores = d_scores + dm[:, :Q] + dm[:, Q:]
            both = dot(m, dyb, 0, 0)
            du = jnp.where(mask, both[:Q], both[Q:])
            tail_x = spread(tail, p, mask)
            before = st_ref[c, :, lanes]
            after = dstate[:, lanes]
            afterb = after.astype(BF)
            du_out = tail_x * dot(b, afterb, 1, 0)
            du = du + du_out
            dye = (d_y * spread(e_cum, p, mask)).astype(BF)
            d_c = d_c + dot(dye, before.astype(BF), 1, 1)
            d_b = d_b + dot((uf * tail_x).astype(BF), afterb, 1, 1)
            e_last_x = spread(e_last, p, mask[0:8])
            dstate[:, lanes] = after * e_last_x[0:1, :] + dot(cc, dye, 0, 0)
            z3 = jnp.sum(uf * du_out, axis=0, keepdims=True) + e_last_x[0:1, :] * jnp.sum(before * after, axis=0, keepdims=True)
            z1 = d_y * yp_ref[at, lanes] - uf * du
            z2 = x * du
            pick = jnp.where(lane_ids == 2 * p + jnp.where(row_ids < HEAD_DIM, 0, 1), 1.0, 0.0).astype(BF)
            d_cum = d_cum + lane_sums(z1, pick)
            d_dt = d_dt + lane_sums(z2, pick)
            d_last = d_last + lane_sums(jnp.broadcast_to(z3, (8, 128)), pick)
            xc[at, lanes] = dt_x * du + gw_ref[1:2, lanes] * d_y
            gg_ref[1:2, lanes] += jnp.sum(d_y * x, axis=0, keepdims=True)
        dsb = d_scores.astype(BF)
        xc[at, G : G + STATE] = d_b + dot(dsb, cc, 0, 0)
        xc[at, G + STATE : G + 2 * STATE] = d_c + dot(dsb, b, 1, 0)
        rows = lax.broadcasted_iota(jnp.int32, (Q, Q), 0)
        cols = lax.broadcasted_iota(jnp.int32, (Q, Q), 1)
        upper = (rows <= cols).astype(F32)
        d_rate = dot(upper, d_cum, 1, 0, lax.Precision.HIGHEST) + d_last[0:1, :]
        d_step = d_dt + d_rate * hp_ref[1:2, :]
        d_raw = d_step * sigmoid(step_inputs(proj_ref, at, hp_ref, sel_ref, dt_at))
        proj_ref[at, dt_at : dt_at + 128] = dot(d_raw.astype(BF), sel_ref[...], 1, 1).astype(BF)
        gh_ref[0:1, :] += jnp.sum(d_raw, axis=0, keepdims=True)
        gh_ref[1:2, :] += jnp.sum(d_rate * rate, axis=0, keepdims=True)
        return 0

    lax.fori_loop(0, nb, chunk, 0)

    gc_ref[...] = jnp.zeros_like(gc_ref)

    def conv_back(tile, carry):
        lanes = pl.ds(pl.multiple_of(tile * 128, 128), 128)
        proj_at = pl.multiple_of(G + tile * 128, 128)
        pre = conv_tile(proj_ref, cw_ref, pad, proj_at, lanes.start, L)
        sig = sigmoid(pre)
        d_pre = xc[:, lanes] * (sig * (1.0 + pre * (1.0 - sig)))
        for k in range(KERNEL):
            gc_ref[k : k + 1, lanes] = jnp.sum(d_pre * pad[5 + k : 5 + k + L, :], axis=0, keepdims=True)
        gc_ref[4:5, lanes] = jnp.sum(d_pre, axis=0, keepdims=True)
        pad[0:L, :] = d_pre
        pad[L : L + 8, :] = jnp.zeros((8, 128), F32)
        d_in = cw_ref[3:4, lanes] * d_pre
        for k in range(KERNEL - 1):
            d_in = d_in + cw_ref[k : k + 1, lanes] * pad[3 - k : 3 - k + L, :]
        proj_ref[:, pl.ds(proj_at, 128)] = d_in.astype(BF)
        return carry

    lax.fori_loop(0, (G + 2 * STATE) // 128, conv_back, 0)


def column(row):
    return jnp.broadcast_to(row, (128, 128)).T


def rows_loop(rows, body):
    def step(r, carry):
        body(pl.ds(pl.multiple_of(r * TILE, TILE), TILE))
        return carry

    lax.fori_loop(0, rows // TILE, step, 0)


class Group:
    def __init__(self, n_seq, n_wt):
        self.n_seq = n_seq
        self.heads = HEADS // n_seq
        self.runs = n_wt if HEADS % (n_seq * n_wt) == 0 else 1
        self.run_heads = self.heads // self.runs
        self.chans = self.heads * HEAD_DIM
        self.G = -(-self.chans // 128) * 128
        self.CX = self.G + 2 * STATE
        self.NC = 2 * self.G + 2 * STATE + 128
        self.rest = self.G + 2 * STATE + 64
        self.half = (self.G + self.rest) // 2


def head_of(g, here, local_head):
    stride = HEADS // g.runs
    run = local_head // g.run_heads
    return run * stride + here * g.run_heads + (local_head - run * g.run_heads)


def one_hot(found):
    return jnp.where(found, 1.0, 0.0)


def step_select(g, here):
    from_ids = lax.broadcasted_iota(jnp.int32, (128, 128), 0)
    to_ids = lax.broadcasted_iota(jnp.int32, (128, 128), 1)
    return one_hot((from_ids == head_of(g, here, to_ids)) & (to_ids < g.heads))


OUT, GATE, REST = KINDS = range(3)


class Wire:
    def __init__(self, send_sems, recv_sems):
        self.send_sems, self.recv_sems, self.used = send_sems, recv_sems, 0

    def reserve(self):
        self.used += 1
        return self.used - 1

    def make(self, src, dst, axis, peer, at_send, at_recv):
        return pltpu.make_async_remote_copy(
            src, dst, self.send_sems.at[at_send], self.recv_sems.at[at_recv],
            device_id={axis: peer}, device_id_type=MESH,
        )

    def put(self, src, dst, axis, peer):
        at = self.reserve()
        copy = self.make(src, dst, axis, peer, at, at)
        copy.start()
        return copy


class Maybe:
    def __init__(self, condition, copy):
        self.condition, self.copy = condition, copy

    def start(self):
        pl.when(self.condition)(self.copy.start)
        return self

    def wait_send(self):
        pl.when(self.condition)(self.copy.wait_send)


class PlaneGather:
    def __init__(self, put, n, here, source, block):
        self.put, self.block, self.plane = put, block, n == 4
        mine = block(here, None)
        if not self.plane:
            self.copies = [put(source, mine, SEQ, lax.rem(here + k, n)) for k in range(1, n)]
            return
        self.x = here + 1 - 2 * lax.rem(here, 2)
        self.y = lax.rem(here + 2, 4)
        self.copies = [put(source, mine, SEQ, self.x), put(source, mine, SEQ, self.y)]

    def forward(self, landed=None):
        if self.plane:
            for copy, group, half, peer in (
                (self.copies[0], self.x, 0, self.y),
                (self.copies[1], self.y, 1, self.x),
            ):
                copy.wait_recv()
                part = self.block(group, half)
                self.copies.append(self.put(part, part, SEQ, peer))
                if landed is not None:
                    landed(group)

    def wait_recv(self):
        for copy in self.copies[2:] if self.plane else self.copies:
            copy.wait_recv()

    def wait_send(self):
        for copy in self.copies:
            copy.wait_send()


class PlaneSum:
    def __init__(self, put, n, here, part, got, mid):
        self.put, self.n, self.here, self.part, self.got, self.mid = put, n, here, part, got, mid
        self.plane = n == 4
        self.half = part.shape[1] // 2
        self.peers = [lax.rem(here + k, n) for k in range(1, n)]
        if self.plane:
            self.x = here + 1 - 2 * lax.rem(here, 2)
            self.y = lax.rem(here + 2, 4)
            self.peers = [lax.rem(self.x + 2, 4), self.y, self.x]

    def start(self, product, stat=None, got_stat=None):
        half, part, got = self.half, self.part, self.got
        self.copies = []
        product()
        for k, peer in enumerate(self.peers):
            if not self.plane:
                self.copies.append(self.put(part.at[peer], got.at[k], SEQ, peer))
            elif k == 0:
                self.mids = [
                    self.put(part.at[peer, 0:half], self.mid.at[0], SEQ, self.x),
                    self.put(part.at[peer, half:], self.mid.at[1], SEQ, self.y),
                ]
            elif k == 1:
                self.copies.append(self.put(part.at[peer, half:], got.at[1, half:], SEQ, peer))
            else:
                self.copies.append(self.put(part.at[peer, 0:half], got.at[0, 0:half], SEQ, peer))
            if stat is not None:
                self.copies.append(self.put(stat.at[peer], got_stat.at[k], SEQ, peer))

    def middle(self):
        if not self.plane:
            return
        half, part = self.half, self.part
        for copy in self.mids:
            copy.wait()

        def add(at):
            late = pl.ds(pl.multiple_of(at.start + half, TILE), TILE)
            for peer, rows, slot in ((self.y, at, 0), (self.x, late, 1)):
                total = part[peer, rows, :].astype(F32) + self.mid[slot, at, :].astype(F32)
                part[peer, rows, :] = total.astype(BF)

        rows_loop(half, add)
        self.copies += [
            self.put(part.at[self.y, 0:half], self.got.at[1, 0:half], SEQ, self.y),
            self.put(part.at[self.x, half:], self.got.at[0, half:], SEQ, self.x),
        ]

    def end(self):
        for copy in self.copies:
            copy.wait()

    def total(self, at):
        total = self.part[self.here, at, :].astype(F32)
        for k in range(2 if self.plane else self.n - 1):
            total = total + self.got[k, at, :].astype(F32)
        return total


class Mover:
    def __init__(self, sems):
        self.sems, self.used = sems, 0

    def put(self, src, dst):
        copy = pltpu.make_async_copy(src, dst, self.sems.at[self.used])
        copy.start()
        self.used += 1
        return copy


def meet_all(axes):
    barrier = pltpu.get_barrier_semaphore()
    count = 0
    for axis, n in axes:
        me = lax.axis_index(axis)
        for k in range(1, n):
            pl.semaphore_signal(
                barrier, inc=1, device_id={axis: lax.rem(me + k, n)}, device_id_type=MESH
            )
        count += n - 1
    pl.semaphore_wait(barrier, count)


def column_tiles(first, last, body):
    whole = (last - first) // 256

    def step(t, carry):
        body(pl.ds(pl.multiple_of(first + t * 256, 128), 256))
        return carry

    lax.fori_loop(0, whole, step, 0)
    if first + whole * 256 < last:
        body(slice(first + whole * 256, last))


def four_blocks(part, product):
    count, rows, columns = part.shape

    def step(q, carry):
        at = pl.ds(pl.multiple_of(q * 4 * rows, TILE), 4 * rows)

        def tile(lanes):
            value = product(at, lanes).astype(BF)
            for b in range(4):
                part[q * 4 + b, :, lanes] = value[b * rows : (b + 1) * rows]

        column_tiles(0, columns, tile)
        return carry

    lax.fori_loop(0, count // 4, step, 0)


class ForwardOuts(NamedTuple):
    sec: Any
    pout: Any
    stat0: Any
    h1: Any
    gb_o: Any
    stats: Any
    packs_o: Any
    wf_o: Any
    of_o: Any
    n_o: Any
    proj_o: Any
    mixed_o: Any
    yp_o: Any
    st_o: Any


class ForwardRefs(NamedTuple):
    tokens: Any
    cotangent: Any
    conv_w: Any
    conv_b: Any
    dt_bias: Any
    a_log: Any
    skip_d: Any
    gate_gain: Any
    norm_gain: Any
    w_src: Any
    o_src: Any
    sec: Any
    pout: Any
    stat0: Any
    h1: Any
    gb_o: Any
    stats: Any
    packs_o: Any
    wf_o: Any
    of_o: Any
    n_o: Any
    proj_o: Any
    mixed_o: Any
    yp_o: Any
    st_o: Any
    h0: Any
    cot: Any
    packs: Any
    wf: Any
    of: Any
    normed: Any
    proj: Any
    mixed: Any
    yp: Any
    st: Any
    pad: Any
    xc: Any
    dts: Any
    state: Any
    vg: Any
    ssq: Any
    part: Any
    got: Any
    got_stat: Any
    hbuf: Any
    own_stat: Any
    cols: Any
    mdots: Any
    sel: Any
    pack: Any
    mid: Any
    ss: Any
    rs: Any
    ls: Any


def forward_kernel(g, n, w, rows, *refs):
    r = ForwardRefs(*refs)
    G, NC = g.G, g.NC
    core, here, shard = lax.axis_index(SECTION), lax.axis_index(SEQ), lax.axis_index(WT)
    sibling = 1 - core
    wire, mover = Wire(r.ss, r.rs), Mover(r.ls)
    wf, of, packs = r.wf, r.of, r.packs
    sends, saves = [], []

    def aligned(at, size):
        return pl.ds(pl.multiple_of(at, 16), size)

    def put(src, dst, axis, peer):
        copy = wire.put(src, dst, axis, peer)
        sends.append(copy)
        return copy

    for layer in range(2):
        for first, last in ((g.chans, G), (G + g.chans, 2 * G), (2 * G + 2 * STATE + HEADS, NC)):
            if first < last:
                wf[layer, first:last, :] = jnp.zeros((last - first, D), BF)
    meet_all(((SEQ, n), (WT, w), (SECTION, 2)))
    o_rows = G // w
    lanes_of = D // w
    mine_o = aligned(shard * o_rows, o_rows)
    piece = here if g.runs == w else shard
    o_own = r.o_src.at[aligned(piece * o_rows, o_rows)]
    mine_lanes = pl.ds(pl.multiple_of(shard * lanes_of, 128), lanes_of)
    width = g.run_heads * HEAD_DIM
    runs = []
    for kind_at, source_at in ((0, 0), (G, INNER)):
        for run in range(g.runs):
            source = source_at + run * (INNER // g.runs) + here * width
            runs.append((source, kind_at + run * width, width))
    runs.append((2 * INNER, 2 * G, 2 * STATE))
    runs.append((2 * INNER + 2 * STATE, 2 * G + 2 * STATE, HEADS))
    siblings, locals_ = [], []
    for source, target, size in runs:
        taken = r.w_src.at[aligned(source, size)]
        siblings.append(put(taken, wf.at[core, target : target + size, mine_lanes], SECTION, sibling))
        locals_.append(mover.put(taken, wf.at[core, target : target + size, mine_lanes]))
    others = [put(o_own, of.at[core, mine_o], SECTION, sibling)]
    locals_later = [
        mover.put(o_own, of.at[core, mine_o]),
        mover.put(r.tokens.at[core, 0], r.h0),
        mover.put(r.cotangent.at[core, 0], r.cot),
    ]

    def part_of(layer, kind, at_shard, at_core):
        if kind == OUT:
            return of.at[layer, aligned(at_shard * o_rows + at_core * (o_rows // 2), o_rows // 2)]
        size = (G if kind == GATE else g.rest) // 2
        first = (0 if kind == GATE else G) + at_core * size
        lanes = pl.ds(pl.multiple_of(at_shard * lanes_of, 128), lanes_of)
        return wf.at[layer, aligned(first, size), lanes]

    line = w == 4

    def fetch(layer, kind):
        mine = part_of(layer, kind, shard, core)
        at = [wire.reserve() for _ in range(w)]
        copies = [
            wire.make(mine, mine, WT, lax.rem(shard + k, w), at[k], at[k]) for k in range(1, w)
        ]
        if line:
            copies[1].start()
            sends.append(copies[1])
            sends.append(Maybe(shard != w - 1, copies[0]).start())
            sends.append(Maybe(shard != 0, copies[2]).start())
        else:
            for copy in copies:
                copy.start()
            sends.extend(copies)
        return copies, at

    def far_part(fetched, layer, kind):
        if not line:
            return []
        at = fetched[1]
        fetched[0][1].wait_recv()
        block = part_of(layer, kind, lax.rem(shard + 2, w), core)
        up = wire.make(block, block, WT, lax.rem(shard + 1, w), at[0], at[3])
        down = wire.make(block, block, WT, lax.rem(shard + w - 1, w), at[0], at[1])
        sends.append(Maybe(shard == 2, up).start())
        sends.append(Maybe(shard == 1, down).start())
        return [put(block, block, SECTION, sibling)]

    def near_parts(fetched, layer, kind):
        found = []
        for k in (1, 3) if line else range(1, w):
            fetched[0][k - 1].wait_recv()
            block = part_of(layer, kind, lax.rem(shard + w - k, w), core)
            found.append(put(block, block, SECTION, sibling))
        return found

    def received(copies):
        for copy in copies:
            copy.wait_recv()

    own_rows = aligned(here * rows, rows)

    def gather(whole):
        def block(group, half):
            size = rows if half is None else rows // 2
            return whole.at[aligned(group * rows + (half or 0) * size, size)]

        return PlaneGather(wire.put, n, here, block(here, None), block)

    def save(source, target):
        saves.append(mover.put(source, target))

    def saved():
        while saves:
            saves.pop().wait()

    for copy in locals_:
        copy.wait()
    received(siblings)
    pending = fetch(0, REST)
    gain_at = g.CX + 128 + G
    r.sel[...] = step_select(g, here).astype(BF)
    pack_small(g, here, r.conv_w, r.conv_b, r.dt_bias, r.a_log, r.skip_d, r.gate_gain, r.norm_gain, r.pack)
    others.append(put(r.pack, packs.at[core], SECTION, sibling))
    locals_later.append(mover.put(r.pack, packs.at[core]))
    for copy in locals_later:
        copy.wait()
    received(others)

    def norm(at):
        h = r.h0[at, :]
        inv = lax.rsqrt(jnp.mean(h * h, axis=1, keepdims=True) + EPSILON)
        r.normed[pl.ds(pl.multiple_of(here * rows + at.start, TILE), TILE), :] = (
            h * inv * packs[0, 0:1, gain_at:]
        ).astype(BF)

    rows_loop(rows, norm)
    arriving = gather(r.normed)
    handed = far_part(pending, 0, REST)
    coming = [fetch(0, GATE), fetch(0, OUT)]
    arriving.forward()
    handed += near_parts(pending, 0, REST)

    for layer in range(2):
        proj, mixed, normed = r.proj, r.mixed, r.normed
        conv = packs.at[layer, :, 0 : g.CX]
        head = packs.at[layer, :, g.CX : g.CX + 128]
        wide = packs.at[layer, :, g.CX + 128 : gain_at]

        def project(lanes):
            proj[:, lanes] = dot(normed[...], wf[layer, lanes, :], 1, 1).astype(BF)

        arriving.wait_recv()
        received(handed)
        gathered = arriving
        column_tiles(G, NC, project)
        scan_forward(
            G, proj, conv, head, wide, r.sel, mixed, r.yp, r.st,
            r.pad, r.xc, r.dts, r.state,
        )
        save(mixed, r.mixed_o.at[layer])
        save(r.yp, r.yp_o.at[layer])
        save(r.st, r.st_o.at[layer])
        save(normed, r.n_o.at[layer])
        handed = far_part(coming[0], layer, GATE) + far_part(coming[1], layer, OUT)
        handed += near_parts(coming[0], layer, GATE) + near_parts(coming[1], layer, OUT)
        if layer == 0:
            pending = fetch(1, REST)
        received(handed)
        column_tiles(0, G, project)
        save(proj, r.proj_o.at[layer])
        gate_forward(G, proj, wide, mixed, r.vg, r.ssq)

        def out_product():
            four_blocks(r.part, lambda at, lanes: dot(r.vg[at, :], of[layer, :, lanes], 1, 0))

        saved()
        gathered.wait_send()
        summing = PlaneSum(wire.put, n, here, r.part, r.got, r.mid)
        summing.start(out_product, r.ssq, r.got_stat)
        summing.middle()
        summing.end()
        if layer == 0:
            handed = far_part(pending, 1, REST)
            coming = [fetch(1, GATE), fetch(1, OUT)]
        ssq = r.ssq[here]
        for k in range(n - 1):
            ssq = ssq + r.got_stat[k]
        inv2 = lax.rsqrt(ssq * (1.0 / INNER) + EPSILON)
        r.own_stat[...] = inv2
        r.cols[...] = column(inv2[0:1, :])
        if layer == 0:
            r.stat0[...] = inv2

        def finish(at):
            pout = summing.total(at) * r.cols[at, 0:1]
            whole = pl.ds(pl.multiple_of(here * rows + at.start, TILE), TILE)
            h_in = r.h0[at, :] if layer == 0 else r.hbuf[0, at, :]
            h = h_in + pout
            r.hbuf[layer, at, :] = h
            if layer == 0:
                r.pout[at, :] = pout
                r.h1[at, :] = h
                inv = lax.rsqrt(jnp.mean(h * h, axis=1, keepdims=True) + EPSILON)
                r.normed[whole, :] = (h * inv * packs[1, 0:1, gain_at:]).astype(BF)
            else:
                out = r.cot[at, :].astype(BF)
                dots = jnp.sum(out.astype(F32) * pout, axis=1, keepdims=True)
                r.mdots[at, :] = jnp.broadcast_to(dots * (1.0 / INNER), (TILE, 128))
                r.normed[whole, :] = out

        rows_loop(rows, finish)
        if layer == 0:
            arriving = gather(r.normed)
            arriving.forward()
            handed += near_parts(pending, 1, REST)
    r.stats[here] = r.own_stat[...]
    r.stats[here, 1:2, :] = r.mdots[...].T[0:1, :]
    last_rows = gather(r.normed)
    arriving = []
    for k in range(1, n):
        block = r.stats.at[here]
        arriving.append(put(block, block, SEQ, lax.rem(here + k, n)))
    arriving.append(put(r.hbuf.at[1 - core], r.sec.at[core], SECTION, sibling))
    save(r.hbuf.at[core], r.sec.at[core])
    save(packs, r.packs_o)
    save(wf, r.wf_o)
    save(of, r.of_o)
    last_rows.forward()
    last_rows.wait_recv()
    received(arriving)
    save(r.normed, r.gb_o)
    last_rows.wait_send()
    assert wire.used <= r.ss.shape[0] and mover.used <= r.ls.shape[0]
    for copy in sends:
        copy.wait_send()
    saved()


def forward_call(g, n, w, tokens, cotangent, small, w_src, o_src):
    rows = tokens.shape[2]
    L, G, NC, CX, PK = rows * n, g.G, g.NC, g.CX, g.CX + 128 + g.G + D
    S = jax.ShapeDtypeStruct
    shapes = ForwardOuts(
        sec=S((2, rows, D), F32),
        pout=S((rows, D), F32),
        stat0=S((8, 128), F32),
        h1=S((rows, D), F32),
        gb_o=S((L, D), BF),
        stats=S((n, 8, 128), F32),
        packs_o=S((2, 8, PK), F32),
        wf_o=S((2, NC, D), BF),
        of_o=S((2, G, D), BF),
        n_o=S((2, L, D), BF),
        proj_o=S((2, L, NC), BF),
        mixed_o=S((2, L, G), BF),
        yp_o=S((2, L, G), F32),
        st_o=S((2, L // Q, STATE, G), F32),
    )
    scratch = [
        S((rows, D), F32), S((rows, D), F32), shapes.packs_o, shapes.wf_o, shapes.of_o, S((L, D), BF), S((L, NC), BF), S((L, G), BF),
        S((L, G), F32), S((L // Q, STATE, G), F32), S((8 + L, 128), F32), S((L, CX), F32), S((L, 128), F32), S((STATE, G), F32),
        S((L, G), BF), S((n, 8, 128), F32), S((n, rows, D), BF), S((n - 1, rows, D), BF), S((n - 1, 8, 128), F32),
        S((2, rows, D), F32), S((8, 128), F32), S((rows, 128), F32), S((rows, 128), F32),
        S((128, 128), BF), S((8, PK), F32), S((2, rows // 2, D), BF),
    ]
    remote = 4 + 2 * g.runs + 6 * w + 6 * (w - 1) + 24 + 8 * (n - 1)
    outs = pl.pallas_call(
        functools.partial(forward_kernel, g, n, w, rows),
        out_shape=list(shapes),
        in_specs=[ANY, ANY] + [VM] * len(small) + [ANY, ANY],
        out_specs=[VM] * 4 + [ANY, VM] + [ANY] * 8,
        scratch_shapes=[pltpu.VMEM(s.shape, s.dtype) for s in scratch]
        + [
            pltpu.SemaphoreType.DMA((remote,)),
            pltpu.SemaphoreType.DMA((remote,)),
            pltpu.SemaphoreType.DMA((22 + 2 * g.runs,)),
        ],
        compiler_params=pltpu.CompilerParams(
            collective_id=0, has_side_effects=True, vmem_limit_bytes=FORWARD_VMEM
        ),
        name="forward",
    )(tokens, cotangent, *small, w_src, o_src)
    return ForwardOuts(*outs)


class BackwardOuts(NamedTuple):
    ig: Any
    gi: Any
    go: Any
    gi_sib: Any
    go_sib: Any
    small: Any
    far: Any
    late: Any


class BackwardRefs(NamedTuple):
    packs_i: Any
    wf_i: Any
    of_i: Any
    n_i: Any
    proj_i: Any
    mixed_i: Any
    yp_i: Any
    st_i: Any
    gb_i: Any
    stats1_i: Any
    stat0_i: Any
    pout_i: Any
    h1_i: Any
    tokens_i: Any
    cotangent_i: Any
    ig: Any
    gi: Any
    go: Any
    gi_sib: Any
    go_sib: Any
    small: Any
    far: Any
    late: Any
    packs: Any
    wf: Any
    of: Any
    n: Any
    proj: Any
    mixed: Any
    yp: Any
    st: Any
    gb: Any
    stats: Any
    pout: Any
    h1: Any
    h0: Any
    cot: Any
    dy: Any
    pad: Any
    xc: Any
    dts: Any
    dstate: Any
    part: Any
    got: Any
    own_stat: Any
    mdots: Any
    grads: Any
    gw: Any
    gout: Any
    sib_w: Any
    sib_o: Any
    z_w: Any
    z_o: Any
    relay_w: Any
    relay_o: Any
    sm: Any
    sm_sib: Any
    sm_z: Any
    sm_own: Any
    sel: Any
    gain: Any
    gain_z: Any
    gain_sum: Any
    mid: Any
    ss: Any
    rs: Any
    ls: Any
    free: Any


def backward_kernel(g, n, w, rows, *refs):
    r = BackwardRefs(*refs)
    G, NC, CX = g.G, g.NC, g.CX
    core, here, shard = lax.axis_index(SECTION), lax.axis_index(SEQ), lax.axis_index(WT)
    sibling = 1 - core
    wire, mover = Wire(r.ss, r.rs), Mover(r.ls)
    o_half, lanes_of = G // (2 * w), D // w
    gain_at = CX + 128 + G

    def aligned(at, size):
        return pl.ds(pl.multiple_of(at, 16), size)

    def load(layer, *pairs):
        return [mover.put(source.at[layer], target) for source, target in pairs]

    first = load(1, (r.of_i, r.of), (r.proj_i, r.proj), (r.mixed_i, r.mixed))
    first += [mover.put(r.packs_i, r.packs), mover.put(r.gb_i, r.gb), mover.put(r.stats1_i, r.stats)]
    later = load(1, (r.n_i, r.n), (r.yp_i, r.yp), (r.st_i, r.st), (r.wf_i, r.wf))
    later += [mover.put(r.pout_i, r.pout), mover.put(r.h1_i, r.h1), mover.put(r.stat0_i, r.own_stat)]
    later += [mover.put(r.tokens_i.at[core, 0], r.h0), mover.put(r.cotangent_i.at[core, 0], r.cot)]
    meet_all(((SEQ, n), (WT, w), (SECTION, 2)))
    r.sm[...] = jnp.zeros_like(r.sm)
    r.sel[...] = step_select(g, here).astype(BF)
    r.gain[here] = jnp.zeros((8, D), F32)
    open_sends, record = [], {}
    line = w == 4
    arrivals = r.got if r.got.shape[0] == n - 1 else r.far

    def put(src, dst, axis, peer):
        copy = wire.put(src, dst, axis, peer)
        open_sends.append(copy)
        return copy

    def rows_of(kind):
        return ((0, G), (0, G), (G, g.rest))[kind]

    def kept(kind):
        return (slice(0, G // (2 * w)), slice(0, G // 2), slice(G // 2, g.half))[kind]

    def buffers(kind):
        if kind == OUT:
            return r.gout, r.sib_o, r.z_o, r.go, r.go_sib
        return r.gw, r.sib_w, r.z_w, r.gi, r.gi_sib

    def block_of(kind, at_shard, at_core):
        if kind == OUT:
            return aligned((2 * at_shard + at_core) * o_half, o_half), slice(0, D)
        first, size = rows_of(kind)
        return (
            aligned(first + at_core * (size // 2), size // 2),
            pl.ds(pl.multiple_of(at_shard * lanes_of, 128), lanes_of),
        )

    def ready(kind):
        for copy in record.pop(kind, ()):
            copy.wait_send()

    def to_sibling(layer, kind):
        grad, sib, _, _, _ = buffers(kind)
        if layer == 0:
            pl.semaphore_wait(r.free.at[kind], 1)
        if kind == OUT:
            pairs = [
                (grad.at[block_of(kind, q, sibling)], sib.at[aligned(q * o_half, o_half)])
                for q in range(w)
            ]
        else:
            first, size = rows_of(kind)
            rows_there = aligned(first + sibling * (size // 2), size // 2)
            pairs = [(grad.at[rows_there], sib.at[kept(kind)])]
        copies = [wire.put(source, target, SECTION, sibling) for source, target in pairs]
        record[kind] = list(copies)
        return copies

    def to_shards(layer, kind, copies):
        grad, sib, z, _, _ = buffers(kind)
        for copy in copies:
            copy.wait_recv()
        if kind == OUT:
            per = o_half // TILE

            def places(t):
                q = t // per
                return (2 * q + core) * o_half + (t - q * per) * TILE, t * TILE

            steps = w * per
        else:
            first, size = rows_of(kind)
            steps = size // 2 // TILE

            def places(t):
                return first + core * (size // 2) + t * TILE, kept(kind).start + t * TILE

        def add(t, carry):
            mine, theirs = (pl.ds(pl.multiple_of(at, TILE), TILE) for at in places(t))
            grad[mine, :] = (grad[mine, :].astype(F32) + sib[theirs, :].astype(F32)).astype(BF)
            return carry

        lax.fori_loop(0, steps, add, 0)
        if layer == 1:
            pl.semaphore_signal(
                r.free.at[kind], inc=1, device_id={SECTION: sibling}, device_id_type=MESH
            )
        at = [wire.reserve() for _ in range(w)]
        found = []
        for k in range(1, w):
            peer = lax.rem(shard + k, w)
            source = grad.at[block_of(kind, peer, core)]
            found.append(wire.make(source, z.at[layer, k - 1, kept(kind)], WT, peer, at[k], at[k]))
        if not line:
            for copy in found:
                copy.start()
            record[kind] += found
            return found, None
        buffer = (r.relay_o if kind == OUT else r.relay_w).at[layer, kept(kind)]
        up = wire.make(grad.at[block_of(kind, w - 1, core)], buffer, WT, 1, at[0], at[0])
        down = wire.make(grad.at[block_of(kind, 0, core)], buffer, WT, w - 2, at[0], at[0])
        inner = (shard == 1) | (shard == 2)
        first = [
            Maybe(shard == 0, up),
            Maybe(shard == w - 1, down),
            Maybe(inner, found[0]),
            Maybe(inner, found[2]),
        ]
        others = [
            Maybe(jnp.logical_not(inner), found[1]),
            Maybe(shard == 0, found[0]),
            Maybe(shard == w - 1, found[2]),
        ]
        record[kind] += [*first, *others, Maybe(inner, found[1])]
        for copy in first:
            copy.start()
        waiting.extend(others)
        arriving = wire.make(buffer, buffer, WT, lax.rem(shard + 1, w), at[0], at[0])
        return found, arriving

    def relay(layer, kind, moving):
        found, arriving = moving
        if not line:
            return
        grad, buffer = (r.gout, r.relay_o) if kind == OUT else (r.gw, r.relay_w)
        rows_here = kept(kind)

        @pl.when((shard == 1) | (shard == 2))
        def _():
            arriving.wait_recv()
            at_rows, at_lanes = block_of(kind, lax.rem(shard + 2, w), core)

            def add(at):
                mine = pl.ds(pl.multiple_of(at_rows.start + at.start, TILE), TILE)
                there = pl.ds(pl.multiple_of(rows_here.start + at.start, TILE), TILE)
                total = grad[mine, at_lanes].astype(F32) + buffer[layer, there, :].astype(F32)
                grad[mine, at_lanes] = total.astype(BF)

            rows_loop(rows_here.stop - rows_here.start, add)
            found[1].start()

    def to_plane(layer, kind, moving):
        grad, _, z, result, _ = buffers(kind)
        copies, _ = moving
        if line:
            pl.when(shard != 0)(copies[0].wait_recv)
            copies[1].wait_recv()
            pl.when(shard != w - 1)(copies[2].wait_recv)
        else:
            for copy in copies:
                copy.wait_recv()
        at_rows, at_lanes = block_of(kind, shard, core)
        here_rows = kept(kind)

        def add(at):
            mine = pl.ds(pl.multiple_of(at_rows.start + at.start, TILE), TILE)
            there = pl.ds(pl.multiple_of(here_rows.start + at.start, TILE), TILE)
            total = grad[mine, at_lanes].astype(F32)
            for k in range(w - 1):
                total = total + z[layer, k, there, :].astype(F32)
            z[layer, 1, there, :] = total.astype(BF)

        def add_end(at, near):
            mine = pl.ds(pl.multiple_of(at_rows.start + at.start, TILE), TILE)
            there = pl.ds(pl.multiple_of(here_rows.start + at.start, TILE), TILE)
            total = grad[mine, at_lanes].astype(F32)
            total = total + z[layer, 1, there, :].astype(F32) + z[layer, near, there, :].astype(F32)
            z[layer, 1, there, :] = total.astype(BF)

        count = here_rows.stop - here_rows.start
        if line:

            @pl.when(shard == 0)
            def _():
                rows_loop(count, lambda at: add_end(at, 2))

            @pl.when(shard == w - 1)
            def _():
                rows_loop(count, lambda at: add_end(at, 0))

            @pl.when((shard == 1) | (shard == 2))
            def _():
                rows_loop(count, add)
        else:
            rows_loop(count, add)
        def target(group, half):
            size = here_rows.stop - here_rows.start
            if half is None:
                return result.at[layer, group, here_rows]
            first = here_rows.start + half * (size // 2)
            return result.at[layer, group, first : first + size // 2]

        block = z.at[layer, 1, here_rows]
        return PlaneGather(put, n, here, block, target), mover.put(block, target(here, None))

    def landed(kind, *arrivals):
        _, _, _, result, target = buffers(kind)
        for found, own in arrivals:
            found.wait_recv()
            own.wait()
        return put(result.at[sibling, :, kept(kind)], target.at[:, kept(kind)], SECTION, sibling)

    def done(copies):
        for copy in copies:
            copy.wait()

    arrived, waiting = {}, []
    for layer in (1, 0):
        conv = r.packs.at[layer, :, 0:CX]
        head = r.packs.at[layer, :, CX : CX + 128]
        wide = r.packs.at[layer, :, CX + 128 : gain_at]
        g_conv = r.sm.at[layer, :, 0:CX]
        g_head = r.sm.at[layer, :, CX : CX + 128]
        g_wide = r.sm.at[layer, :, CX + 128 : gain_at]
        done(first)

        def d_normed(lanes):
            r.xc[:, lanes] = dot(r.gb[...], r.of[lanes, :], 1, 1)

        column_tiles(0, G, d_normed)
        gate_backward(
            G, r.proj, r.mixed, r.xc, r.stats, wide, r.dy, g_wide
        )

        def out_rows(at):
            r.gout[at, :] = dot(r.mixed[:, at], r.gb[...], 0, 0).astype(BF)

        def in_rows(at):
            r.gw[at, :] = dot(r.proj[:, at], r.n[...], 0, 0).astype(BF)

        ready(OUT)
        column_tiles(0, G, out_rows)
        out_sib = to_sibling(layer, OUT)
        done(later)
        ready(GATE)
        column_tiles(0, G, in_rows)
        gate_sib = to_sibling(layer, GATE)
        out_z = to_shards(layer, OUT, out_sib)
        gate_z = to_shards(layer, GATE, gate_sib)
        if layer == 0:
            arrived[1, OUT][0].forward()
            arrived[1, GATE][0].forward()
            arrived[1, REST] = to_plane(1, REST, rest_z)

        def serve():
            for copy in waiting:
                copy.start()

        scan_backward(
            G, r.proj, r.dy, r.yp, r.st, conv, head, wide, r.sel, g_wide, g_conv, g_head,
            r.pad, r.xc, r.dts, r.dstate, serve,
        )
        waiting.clear()
        relay(layer, OUT, out_z)
        relay(layer, GATE, gate_z)
        if layer == 0:
            small_sib = put(r.sm.at[sibling], r.sm_sib, SECTION, sibling)
        if layer == 0:
            arrived[1, REST][0].forward()
            small_sib.wait_recv()
            r.sm_own[...] = r.sm[core] + r.sm_sib[...]
            small_z = [
                put(r.sm_own, r.sm_z.at[k - 1], WT, lax.rem(shard + k, w)) for k in range(1, w)
            ]
        if layer == 1:
            first = load(0, (r.of_i, r.of), (r.mixed_i, r.mixed))
            later = load(0, (r.yp_i, r.yp), (r.st_i, r.st))

        def in_product():
            four_blocks(r.part, lambda at, lanes: dot(r.proj[at, :], r.wf[:, lanes], 1, 0))

        summing = PlaneSum(wire.put, n, here, r.part, arrivals, r.mid)

        def rest_gradient():
            ready(REST)
            column_tiles(G, NC, in_rows)
            return to_sibling(layer, REST)

        if layer == 0:
            rest_sib = rest_gradient()
            summing.start(in_product)
            rest_z = to_shards(layer, REST, rest_sib)
            summing.middle()
        else:
            summing.start(in_product)
            later += load(0, (r.wf_i, r.wf))
            rest_sib = rest_gradient()
            first += load(0, (r.proj_i, r.proj))
            later += load(0, (r.n_i, r.n))
            summing.middle()
            rest_z = to_shards(layer, REST, rest_sib)
        summing.end()
        while waiting:
            waiting.pop(0).start()
        if arrivals is not r.got:
            done(
                [
                    mover.put(arrivals.at[k - 1], r.part.at[lax.rem(here + k, n)])
                    for k in range(1, n)
                ]
            )

        def finish(at):
            if arrivals is r.got:
                d_in = summing.total(at)
            else:
                d_in = r.part[0, at, :].astype(F32)
                for k in range(1, n):
                    d_in = d_in + r.part[k, at, :].astype(F32)
            h = r.h1[at, :] if layer == 1 else r.h0[at, :]
            above = r.cot[at, :] if layer == 1 else r.grads[1, at, :]
            inv = lax.rsqrt(jnp.mean(h * h, axis=1, keepdims=True) + EPSILON)
            normed = h * inv
            r.gain[here, layer : layer + 1, :] += jnp.sum(d_in * normed, axis=0, keepdims=True)
            d_s = d_in * r.packs[layer, 0:1, gain_at:]
            d_h = above + inv * (d_s - normed * jnp.mean(d_s * normed, axis=1, keepdims=True))
            r.grads[layer, at, :] = d_h
            if layer == 1:
                out = d_h.astype(BF)
                whole = pl.ds(pl.multiple_of(here * rows + at.start, TILE), TILE)
                r.gb[whole, :] = out
                dots = jnp.sum(out.astype(F32) * r.pout[at, :], axis=1, keepdims=True)
                r.mdots[at, :] = jnp.broadcast_to(dots * (1.0 / INNER), (TILE, 128))

        rows_loop(rows, finish)
        if layer == 1:
            r.stats[here] = r.own_stat[...]
            r.stats[here, 1:2, :] = r.mdots[...].T[0:1, :]
            own = aligned(here * rows, rows)
            gathering = []

            def rows_of_group(group, half):
                size = rows if half is None else rows // 2
                return r.gb.at[aligned(group * rows + (half or 0) * size, size)]

            grad_rows = PlaneGather(put, n, here, r.gb.at[own], rows_of_group)
            for k in range(1, n):
                peer = lax.rem(here + k, n)
                gathering.append(put(r.stats.at[here], r.stats.at[here], SEQ, peer))
            grad_rows.forward()
            relay(1, REST, rest_z)
            arrived[1, OUT] = to_plane(1, OUT, out_z)
            arrived[1, GATE] = to_plane(1, GATE, gate_z)
            grad_rows.wait_recv()
            for copy in gathering:
                copy.wait_recv()
    gains = []
    ends = [put(r.grads.at[sibling], r.ig.at[core], SECTION, sibling)]
    for k in range(1, n):
        gains.append(put(r.gain.at[here], r.gain.at[here], SEQ, lax.rem(here + k, n)))
    local_grad = mover.put(r.grads.at[core], r.ig.at[core])
    relay(0, REST, rest_z)
    arrived[0, OUT] = to_plane(0, OUT, out_z)
    arrived[0, GATE] = to_plane(0, GATE, gate_z)
    arrived[0, OUT][0].forward()
    arrived[0, GATE][0].forward()
    for copy in small_z:
        copy.wait_recv()
    total = r.sm_own[...]
    for k in range(w - 1):
        total = total + r.sm_z[k]
    r.small[here] = total
    sums = [
        put(r.small.at[here], r.small.at[here], SEQ, lax.rem(here + k, n)) for k in range(1, n)
    ]
    for copy in gains:
        copy.wait_recv()
    total = r.gain[0]
    for k in range(1, n):
        total = total + r.gain[k]
    r.gain_z[shard] = total
    gains = [
        put(r.gain_z.at[shard], r.gain_z.at[shard], WT, lax.rem(shard + k, w)) for k in range(1, w)
    ]
    arrived[0, REST] = to_plane(0, REST, rest_z)
    ends.append(landed(OUT, arrived[1, OUT], arrived[0, OUT]))
    ends.append(landed(GATE, arrived[1, GATE], arrived[0, GATE]))
    arrived[1, REST][0].wait_recv()
    arrived[1, REST][1].wait()
    last, last_own = arrived[0, REST]

    def hand_over(group):
        source, target = r.gi.at[sibling, group, kept(REST)], r.gi_sib.at[group, kept(REST)]
        ends.append(put(source, target, SECTION, sibling))

    last_own.wait()
    hand_over(here)
    if last.plane:
        last.forward(hand_over)
        last.wait_recv()
        hand_over(lax.rem(last.x + 2, 4))
    else:
        last.wait_recv()
        for k in range(1, n):
            hand_over(lax.rem(here + k, n))
    for copy in gains:
        copy.wait_recv()
    total = r.gain_z[0]
    for k in range(1, w):
        total = total + r.gain_z[k]
    r.gain_sum[core] = total
    ends.append(put(r.gain_sum.at[core], r.gain_sum.at[core], SECTION, sibling))
    for copy in ends + sums:
        copy.wait_recv()
    r.late[...] = r.gain_sum[0] + r.gain_sum[1]
    local_grad.wait()
    assert wire.used <= r.ss.shape[0] and mover.used <= r.ls.shape[0]
    for kind in KINDS:
        ready(kind)
    for copy in open_sends:
        copy.wait_send()


def backward_call(g, n, w, fwd, tokens, cotangent):
    rows = tokens.shape[2]
    L, G, NC, CX = rows * n, g.G, g.NC, g.CX
    PK = CX + 128 + G + D
    S = jax.ShapeDtypeStruct
    o_half, lanes_of = G // (2 * w), D // w
    spill = n > 8
    outs = BackwardOuts(
        ig=S((2, rows, D), F32),
        gi=S((2, n, g.half, lanes_of), BF),
        go=S((2, n, o_half, D), BF),
        gi_sib=S((n, g.half, lanes_of), BF),
        go_sib=S((n, o_half, D), BF),
        small=S((n, 8, PK - D), F32),
        far=S((n - 1, rows, D) if spill else (8, 128), BF),
        late=S((8, D), F32),
    )
    scratch = [
        S((2, 8, PK), F32), S((NC, D), BF), S((G, D), BF), S((L, D), BF), S((L, NC), BF), S((L, G), BF),
        S((L, G), F32), S((L // Q, STATE, G), F32), S((L, D), BF), S((n, 8, 128), F32), S((rows, D), F32),
        S((rows, D), F32), S((rows, D), F32), S((rows, D), F32),
        S((L, G), BF), S((8 + L, 128), F32), S((L, CX), F32), S((L, 128), F32), S((STATE, G), F32),
        S((n, rows, D), BF), S((1 if spill else n - 1, rows, D), BF), S((8, 128), F32), S((rows, 128), F32), S((2, rows, D), F32),
        S((NC, D), BF), S((G, D), BF), S((g.half, D), BF), S((G // 2, D), BF),
        S((2, w - 1, g.half, lanes_of), BF),
        S((2, w - 1, o_half, D), BF), S((2, g.half, lanes_of), BF), S((2, o_half, D), BF), S((2, 8, PK - D), F32), S((8, PK - D), F32), S((w - 1, 8, PK - D), F32), S((8, PK - D), F32),
        S((128, 128), BF), S((n, 8, D), F32), S((w, 8, D), F32), S((2, 8, D), F32),
        S((2, rows // 2, D), BF),
    ]
    remote = 2 * (3 * (w + w + n - 1) + n - 1) + 2 * (n - 1) + 40 + 2 * (w - 1) + 2 * (n - 1) + n
    args = [
        fwd.packs_o, fwd.wf_o, fwd.of_o, fwd.n_o, fwd.proj_o, fwd.mixed_o, fwd.yp_o, fwd.st_o,
        fwd.gb_o, fwd.stats, fwd.stat0, fwd.pout, fwd.h1, tokens, cotangent,
    ]
    results = pl.pallas_call(
        functools.partial(backward_kernel, g, n, w, rows),
        out_shape=list(outs),
        in_specs=[ANY] * len(args),
        out_specs=[VM, ANY, ANY, ANY, ANY, VM, ANY, VM],
        scratch_shapes=[pltpu.VMEM(s.shape, s.dtype) for s in scratch]
        + [
            pltpu.SemaphoreType.DMA((remote,)),
            pltpu.SemaphoreType.DMA((remote,)),
            pltpu.SemaphoreType.DMA((36 + 2 * n,)),
            pltpu.SemaphoreType.REGULAR((3,)),
        ],
        compiler_params=pltpu.CompilerParams(
            collective_id=1, has_side_effects=True, vmem_limit_bytes=BACKWARD_VMEM
        ),
        name="backward",
    )(*args)
    return BackwardOuts(*results)


def pack_small(g, here, conv_ref, bias_ref, dtb_ref, a_ref, skip_ref, gate_ref, norm_ref, pack_ref):
    G, width = g.G, g.run_heads * HEAD_DIM
    win = -(-(width + 64) // 128) * 128
    start = here * width
    base = pl.multiple_of(start // 128 * 128, 128)
    from_ids = lax.broadcasted_iota(jnp.int32, (win, G), 0)
    to_ids = lax.broadcasted_iota(jnp.int32, (win, G), 1)
    exact = lax.Precision.HIGHEST

    def take(ref, rows):
        total = jnp.zeros((rows, G), F32)
        for run in range(g.runs):
            window = ref[0:rows, pl.ds(pl.multiple_of(base + run * (INNER // g.runs), 128), win)]
            inside = (to_ids >= run * width) & (to_ids < (run + 1) * width)
            pick = one_hot(inside & (from_ids == to_ids - run * width + (start - base)))
            total = total + dot(window, pick, 1, 0, exact)
        return total

    head_from = lax.broadcasted_iota(jnp.int32, (HEADS, 128), 0)
    head_to = lax.broadcasted_iota(jnp.int32, (HEADS, 128), 1)
    head_pick = one_hot((head_from == head_of(g, here, head_to)) & (head_to < g.heads))
    wide_from = lax.broadcasted_iota(jnp.int32, (HEADS, G), 0)
    wide_to = lax.broadcasted_iota(jnp.int32, (HEADS, G), 1)
    wide_pick = (wide_from == head_of(g, here, wide_to // HEAD_DIM)) & (wide_to < g.chans)
    head_at, wide_at, gain_at = g.CX, g.CX + 128, g.CX + 128 + G
    pack_ref[...] = jnp.zeros_like(pack_ref)
    pack_ref[0:KERNEL, 0:G] = take(conv_ref, KERNEL)
    pack_ref[4:5, 0:G] = take(bias_ref, 1)
    pack_ref[0:KERNEL, G:head_at] = conv_ref[:, INNER:]
    pack_ref[4:5, G:head_at] = bias_ref[:, INNER:]
    pack_ref[0:1, head_at:wide_at] = dot(dtb_ref[...], head_pick, 1, 0, exact)
    pack_ref[1:2, head_at:wide_at] = dot(-jnp.exp(a_ref[...]), head_pick, 1, 0, exact)
    pack_ref[0:1, wide_at:gain_at] = take(gate_ref, 1)
    pack_ref[1:2, wide_at:gain_at] = dot(skip_ref[...], one_hot(wide_pick), 1, 0, exact)
    pack_ref[0:1, gain_at:] = norm_ref[...]


def halves_of_heads(g, ref_of, column_at, head):
    parts = []
    for h in (head, head + 1):
        stride = HEADS // g.runs
        group = h % stride // g.run_heads
        local_head = h // stride * g.run_heads + h % g.run_heads
        value = ref_of(group, slice(column_at + local_head // 2 * 128, column_at + local_head // 2 * 128 + 128))
        parts.append(value if local_head % 2 == h % 2 else pltpu.roll(value, HEAD_DIM, 1))
    lanes = lax.broadcasted_iota(jnp.int32, parts[0].shape, 1)
    return jnp.where(lanes < HEAD_DIM, parts[0], parts[1])


def layout_kernel(g, own_ref, sib_ref, own_out_ref, sib_out_ref, small_ref, late_ref, sec_ref, ig_ref, g_in_ref, g_out_ref, sec_out, ig_out, norm_ref, conv_ref, bias_ref, dtb_ref, a_ref, skip_ref, gate_ref):
    n, G = g.n_seq, g.G
    first_core = lax.axis_index(SECTION) == 0

    def all_rows(halves, outs):
        def copy(groups, kind_at, half_at, half_rows, source, target, size):
            done = 0
            while done < size:
                half, offset = divmod(source + done, half_rows)
                count = min(size - done, half_rows - offset)
                at = slice(half_at + offset, half_at + offset + count)
                total = None
                for group in groups:
                    value = halves[half][group, at, :].astype(F32)
                    total = value if total is None else total + value
                g_in_ref[target + done : target + done + count, :] = total
                done += count

        for half in range(2):
            g_out_ref[:, half] = outs[half][...].astype(F32)
        width = g.run_heads * HEAD_DIM
        rest = (G, G // 2, g.rest // 2)
        everyone = range(n)
        for run in range(g.runs):
            for group in range(n):
                target = run * (INNER // g.runs) + group * width
                copy([group], 0, 0, G // 2, run * width, target, width)
                copy([group], *rest, run * width, INNER + target, width)
        copy(everyone, *rest, G, 2 * INNER, 2 * STATE)
        copy(everyone, *rest, G + 2 * STATE, 2 * INNER + 2 * STATE, HEADS)

    sec_out[...] = sec_ref[...]
    ig_out[...] = ig_ref[...]
    own, own_out = own_ref.at[0], own_out_ref.at[0]

    @pl.when(first_core)
    def _():
        all_rows((own, sib_ref), (own_out, sib_out_ref))

    @pl.when(jnp.logical_not(first_core))
    def _():
        all_rows((sib_ref, own), (sib_out_ref, own_out))

    @pl.when(pl.program_id(0) == 0)
    def _():
        from_ids = lax.broadcasted_iota(jnp.int32, (128, HEADS), 0)
        to_ids = lax.broadcasted_iota(jnp.int32, (128, HEADS), 1)
        picks = [one_hot((to_ids == head_of(g, group, from_ids)) & (from_ids < g.heads)) for group in range(n)]
        exact = lax.Precision.HIGHEST
        head_at, wide_at, gain_at = g.CX, g.CX + 128, g.CX + 128 + G

        def small(group, columns):
            return small_ref[group, :, columns]

        for head in range(0, HEADS, 2):
            at = slice(head * HEAD_DIM, head * HEAD_DIM + 128)
            conv = halves_of_heads(g, small, 0, head)
            conv_ref[:, at] = conv[0:KERNEL]
            bias_ref[:, at] = conv[KERNEL : KERNEL + 1]
            gate_ref[:, at] = halves_of_heads(g, small, wide_at, head)[0:1]
        conv = small(0, slice(G, head_at))
        for group in range(1, n):
            conv = conv + small(group, slice(G, head_at))
        conv_ref[:, INNER:] = conv[0:KERNEL]
        bias_ref[:, INNER:] = conv[KERNEL : KERNEL + 1]
        norm_ref[...] = jnp.where(first_core, late_ref[0:1, :], late_ref[1:2, :])
        heads = jnp.zeros((8, HEADS), F32)
        skips = jnp.zeros((8, HEADS), F32)
        wide_from = lax.broadcasted_iota(jnp.int32, (G, HEADS), 0)
        wide_to = lax.broadcasted_iota(jnp.int32, (G, HEADS), 1)
        for group in range(n):
            heads = heads + dot(small(group, slice(head_at, wide_at)), picks[group], 1, 0, exact)
            pick = (wide_to == head_of(g, group, wide_from // HEAD_DIM)) & (wide_from < g.chans)
            skips = skips + dot(small(group, slice(wide_at, gain_at)), one_hot(pick), 1, 0, exact)
        dtb_ref[...] = heads[0:1]
        a_ref[...] = heads[1:2]
        skip_ref[...] = skips[1:2]


def layout_call(g, core, gi, gi_sib, go, go_sib, small, late, sec, ig):
    _, n, half, lanes = gi.shape
    out_half = go.shape[2]
    steps = lanes // 128
    out_lanes = D // steps
    rows_spec = pl.BlockSpec(sec.shape[:2] + (out_lanes,), lambda t, c: (0, 0, t))
    PK = small.shape[2]
    columns = 2 * INNER + 2 * STATE + HEADS
    S = jax.ShapeDtypeStruct
    shapes = (
        S((columns, lanes), F32), S((n, 2, out_half, D), F32), S(sec.shape, F32), S(ig.shape, F32), S((1, D), F32), S((KERNEL, CONV), F32),
        S((1, CONV), F32), S((1, HEADS), F32), S((1, HEADS), F32), S((1, HEADS), F32), S((1, INNER), F32),
    )
    return pl.pallas_call(
        lambda core_ref, *refs: layout_kernel(g, *refs),
        grid_spec=pltpu.PrefetchScalarGridSpec(
            num_scalar_prefetch=1,
            grid=(steps,),
            in_specs=[
                pl.BlockSpec((1, n, half, 128), lambda t, c: (c[0], 0, 0, t)),
                pl.BlockSpec((n, half, 128), lambda t, c: (0, 0, t)),
                pl.BlockSpec((1, n, out_half, out_lanes), lambda t, c: (c[0], 0, 0, t)),
                pl.BlockSpec((n, out_half, out_lanes), lambda t, c: (0, 0, t)),
                pl.BlockSpec((n, 8, PK), lambda t, c: (0, 0, 0)),
                pl.BlockSpec((8, D), lambda t, c: (0, 0)),
                rows_spec,
                rows_spec,
            ],
            out_specs=[
                pl.BlockSpec((columns, 128), lambda t, c: (0, t)),
                pl.BlockSpec((n, 2, out_half, out_lanes), lambda t, c: (0, 0, 0, t)),
                rows_spec,
                rows_spec,
            ]
            + [pl.BlockSpec(s.shape, lambda t, c: (0, 0)) for s in shapes[4:]],
        ),
        out_shape=shapes,
        compiler_params=pltpu.CompilerParams(vmem_limit_bytes=SMALL_VMEM),
        name="layout",
    )(core, gi, gi_sib, go, go_sib, small, late, sec, ig)


def local(
    tokens, cotangent, norm_gain, w_in, conv_w, conv_b, dt_bias, a_log, skip_d, gate_gain, w_out
):
    n_seq, n_wt = lax.axis_size(SEQ), lax.axis_size(WT)
    here = lax.axis_index(SEQ)
    group = Group(n_seq, n_wt)
    core = lax.axis_index(SECTION).reshape(1)
    G = group.G

    small = (conv_w[0], conv_b, dt_bias, a_log, skip_d, gate_gain, norm_gain)
    w_src = jnp.swapaxes(w_in[0], 0, 1)
    if group.runs == n_wt:
        o_src = w_out[0]
    else:
        o_src = lax.all_gather(w_out[0], WT, axis=0, tiled=True)
        o_src = lax.dynamic_slice_in_dim(o_src, here * group.chans, group.chans, 0)
        o_src = jnp.pad(o_src, ((0, G - group.chans), (0, 0)))
    fwd = forward_call(group, n_seq, n_wt, tokens, cotangent, small, w_src, o_src)
    bwd = backward_call(group, n_seq, n_wt, fwd, tokens, cotangent)
    g_in, g_out, section_out, input_grad, g_norm, g_conv, g_bias, g_dtb, g_a, g_skip, g_gate = layout_call(
        group, core, bwd.gi, bwd.gi_sib, bwd.go, bwd.go_sib, bwd.small, bwd.late, fwd.sec, bwd.ig
    )
    if group.runs == n_wt:
        g_out = g_out.reshape(INNER // n_wt, D)
    else:
        g_out = g_out.astype(BF).reshape(n_seq, G // n_wt, D)
        g_out = lax.all_gather(g_out, WT, axis=1, tiled=True)[:, : group.chans].reshape(INNER, D)
        mine = INNER // n_wt
        g_out = lax.dynamic_slice_in_dim(g_out, lax.axis_index(WT) * mine, mine, 0).astype(F32)
    return (
        section_out[None, :, None],
        input_grad[None, :, None],
        g_norm,
        jnp.swapaxes(g_in, 0, 1)[None],
        g_conv[None],
        g_bias,
        g_dtb,
        g_a,
        g_skip,
        g_gate,
        g_out[None],
    )


def solution(mesh):
    placed = (
        P(None, WT, SEQ, None),
        P(None, WT, SEQ, None),
        P(SECTION, None),
        P(SECTION, WT, None),
        P(SECTION, None, None),
        P(SECTION, None),
        P(SECTION, None),
        P(SECTION, None),
        P(SECTION, None),
        P(SECTION, None),
        P(SECTION, WT, None),
    )
    return jax.shard_map(
        local,
        mesh=mesh,
        in_specs=placed,
        out_specs=(
            P(SECTION, None, WT, SEQ, None),
            P(SECTION, None, WT, SEQ, None),
            P(SECTION, None),
            P(SECTION, WT, None),
            P(SECTION, None, None),
            P(SECTION, None),
            P(SECTION, None),
            P(SECTION, None),
            P(SECTION, None),
            P(SECTION, None),
            P(SECTION, WT, None),
        ),
        check_vma=False,
    )
```

```python
import functools
from typing import Any, NamedTuple

import jax
import jax.numpy as jnp
from jax import lax
from jax.experimental import pallas as pl
from jax.experimental.pallas import tpu as pltpu
from jax.sharding import PartitionSpec as P

D = 1536
HEADS = 48
HEAD_DIM = 64
STATE = 128
KERNEL = 4
INNER = 3072
CONV = 3328
EPSILON = 1e-05

Q = 128
F32 = jnp.float32
BF = jnp.bfloat16
SEQ, WT, SECTION = "seq", "wt", "section"
FORWARD_VMEM = 56 * 2**20
BACKWARD_VMEM = 62 * 2**20
SMALL_VMEM = 60 * 2**20
MESH = pl.DeviceIdType.MESH
VM = pl.BlockSpec(memory_space=pltpu.VMEM)
ANY = pl.BlockSpec(memory_space=pl.ANY)
TILE = 16


def dot(a, b, ca, cb, precision=None):
    return lax.dot_general(a, b, (((ca,), (cb,)), ((), ())), precision=precision, preferred_element_type=F32)

def sigmoid(x):
    return 1.0 / (1.0 + jnp.exp(-x))

def softplus(x):
    return jnp.maximum(x, 0.0) + jnp.log1p(jnp.exp(-jnp.abs(x)))

def lane_mask(rows):
    return lax.broadcasted_iota(jnp.int32, (rows, 128), 1) < HEAD_DIM

def spread(cols, pair, mask):
    a = jnp.broadcast_to(cols[:, 2 * pair : 2 * pair + 1], mask.shape)
    b = jnp.broadcast_to(cols[:, 2 * pair + 1 : 2 * pair + 2], mask.shape)
    return jnp.where(mask, a, b)

def split_pair(u, mask):
    zero = jnp.zeros_like(u)
    return jnp.concatenate([jnp.where(mask, u, zero), jnp.where(mask, zero, u)], axis=0)

def conv_tile(proj_ref, cw_ref, pad, proj_at, conv_at, rows):
    pad[0:8, :] = jnp.zeros((8, 128), F32)
    pad[8 : 8 + rows, :] = proj_ref[:, pl.ds(proj_at, 128)].astype(F32)
    pre = jnp.broadcast_to(cw_ref[4:5, pl.ds(conv_at, 128)], (rows, 128))
    for k in range(KERNEL):
        pre = pre + cw_ref[k : k + 1, pl.ds(conv_at, 128)] * pad[5 + k : 5 + k + rows, :]
    return pre

def step_inputs(proj_ref, at, hp_ref, sel_ref, dt_at):
    return dot(proj_ref[at, dt_at : dt_at + 128], sel_ref[...], 1, 0) + hp_ref[0:1, :]

def chunk_factors(dt, hp_ref):
    rate = dt * hp_ref[1:2, :]
    rows = lax.broadcasted_iota(jnp.int32, (Q, Q), 0)
    cols = lax.broadcasted_iota(jnp.int32, (Q, Q), 1)
    tri = (rows >= cols).astype(F32)
    cum = dot(tri, rate, 1, 0, lax.Precision.HIGHEST)
    return rate, cum, rows >= cols

def decay_pair(cum, cum_t, causal, pair):
    parts = []
    for h in (2 * pair, 2 * pair + 1):
        diff = jnp.broadcast_to(cum[:, h : h + 1], (Q, Q)) - jnp.broadcast_to(cum_t[h : h + 1, :], (Q, Q))
        parts.append(jnp.exp(jnp.where(causal, diff, -1e30)))
    return jnp.concatenate(parts, axis=1)

def scan_forward(G, proj_ref, cw_ref, hp_ref, gw_ref, sel_ref, mixed_ref, yp_ref, st_ref, pad, xc, dts, state):
    L = proj_ref.shape[0]

    def conv(tile, carry):
        lanes = pl.ds(pl.multiple_of(tile * 128, 128), 128)
        pre = conv_tile(proj_ref, cw_ref, pad, pl.multiple_of(G + tile * 128, 128), lanes.start, L)
        xc[:, lanes] = pre * sigmoid(pre)
        return carry

    lax.fori_loop(0, (G + 2 * STATE) // 128, conv, 0)
    dt_at = 2 * G + 2 * STATE
    dts[...] = softplus(step_inputs(proj_ref, slice(0, L), hp_ref, sel_ref, dt_at))
    state[...] = jnp.zeros_like(state)
    mask = lane_mask(Q)

    def chunk(c, _):
        at = pl.ds(pl.multiple_of(c * Q, Q), Q)
        dt = dts[at, :]
        rate, cum, causal = chunk_factors(dt, hp_ref)
        cum_t = cum.T
        last = cum[Q - 1 : Q, :]
        e_cum = jnp.exp(cum)
        tail = jnp.exp(last - cum) * dt
        e_last = jnp.broadcast_to(jnp.exp(last), (8, 128))
        b = xc[at, G : G + STATE].astype(BF)
        cc = xc[at, G + STATE : G + 2 * STATE].astype(BF)
        scores = dot(cc, b, 1, 1)
        scores2 = jnp.concatenate([scores, scores], axis=1)
        for p in range(G // 128):
            lanes = slice(p * 128, p * 128 + 128)
            x = xc[at, lanes]
            u = (x * spread(dt, p, mask)).astype(BF)
            m = (scores2 * decay_pair(cum, cum_t, causal, p)).astype(BF)
            before = state[:, lanes]
            st_ref[c, :, lanes] = before
            y = dot(m, split_pair(u, mask), 1, 0)
            y = y + dot(cc, before.astype(BF), 1, 0) * spread(e_cum, p, mask)
            yp_ref[at, lanes] = y
            after = dot(b, (x * spread(tail, p, mask)).astype(BF), 0, 0)
            state[:, lanes] = before * spread(e_last, p, mask[0:8])[0:1, :] + after
            mixed_ref[at, lanes] = (y + gw_ref[1:2, lanes] * x).astype(BF)
        return 0

    lax.fori_loop(0, L // Q, chunk, 0)


def gate_forward(G, proj_ref, gw_ref, mixed_ref, vg_ref, ssq_ref):
    def chunk(c, _):
        at = pl.ds(pl.multiple_of(c * Q, Q), Q)
        ssq = jnp.zeros((Q, 1), F32)
        for p in range(G // 128):
            lanes = slice(p * 128, p * 128 + 128)
            gate = proj_ref[at, lanes].astype(F32)
            v = mixed_ref[at, lanes].astype(F32) * (gate * sigmoid(gate))
            vg_ref[at, lanes] = (v * gw_ref[0:1, lanes]).astype(BF)
            ssq = ssq + jnp.sum(v * v, axis=1, keepdims=True)
        ssq_ref[c] = jnp.broadcast_to(ssq, (Q, 128)).T[0:8, :]
        return 0

    lax.fori_loop(0, proj_ref.shape[0] // Q, chunk, 0)


def lane_sums(values, pick):
    high = values.astype(BF)
    low = (values - high.astype(F32)).astype(BF)
    return dot(high, pick, 1, 0) + dot(low, pick, 1, 0)


def gate_backward(G, proj_ref, mixed_ref, dn_ref, sc_ref, gw_ref, dy_ref, gg_ref):
    gg_ref[...] = jnp.zeros_like(gg_ref)

    def chunk(c, _):
        at = pl.ds(pl.multiple_of(c * Q, Q), Q)
        sc = jnp.concatenate([sc_ref[c], jnp.zeros((Q - 8, 128), F32)], axis=0).T
        inv2 = jnp.broadcast_to(sc[:, 0:1], (Q, 128))
        mdot = jnp.broadcast_to(sc[:, 1:2], (Q, 128))
        for p in range(G // 128):
            lanes = slice(p * 128, p * 128 + 128)
            gate = proj_ref[at, lanes].astype(F32)
            sig = sigmoid(gate)
            act = gate * sig
            mixed = mixed_ref[at, lanes].astype(F32)
            n2 = mixed * act * inv2
            mixed_ref[at, lanes] = (n2 * gw_ref[0:1, lanes]).astype(BF)
            dn = dn_ref[at, lanes]
            gg_ref[0:1, lanes] += jnp.sum(dn * n2, axis=0, keepdims=True)
            d_v = inv2 * (dn * gw_ref[0:1, lanes] - n2 * mdot)
            dy_ref[at, lanes] = (d_v * act).astype(BF)
            proj_ref[at, lanes] = (d_v * mixed * (sig * (1.0 + gate * (1.0 - sig)))).astype(BF)
        return 0

    lax.fori_loop(0, proj_ref.shape[0] // Q, chunk, 0)


def scan_backward(G, proj_ref, dy_ref, yp_ref, st_ref, cw_ref, hp_ref, gw_ref, sel_ref, gg_ref, gc_ref, gh_ref,
                  pad, xc, dts, dstate, serve):
    L = proj_ref.shape[0]
    nb = L // Q
    mask = lane_mask(Q)

    def conv(tile, carry):
        lanes = pl.ds(pl.multiple_of(tile * 128, 128), 128)
        pre = conv_tile(proj_ref, cw_ref, pad, pl.multiple_of(G + tile * 128, 128), lanes.start, L)
        xc[:, lanes] = pre * sigmoid(pre)
        return carry

    lax.fori_loop(0, (G + 2 * STATE) // 128, conv, 0)
    dt_at = 2 * G + 2 * STATE
    dts[...] = softplus(step_inputs(proj_ref, slice(0, L), hp_ref, sel_ref, dt_at))
    dstate[...] = jnp.zeros_like(dstate)
    gh_ref[...] = jnp.zeros_like(gh_ref)

    def chunk(step, _):
        c = nb - 1 - step
        pl.when(step == nb // 4)(serve)
        at = pl.ds(pl.multiple_of(c * Q, Q), Q)
        dt = dts[at, :]
        rate, cum, causal = chunk_factors(dt, hp_ref)
        cum_t = cum.T
        last = cum[Q - 1 : Q, :]
        e_cum = jnp.exp(cum)
        tail = jnp.exp(last - cum)
        e_last = jnp.broadcast_to(jnp.exp(last), (8, 128))
        b = xc[at, G : G + STATE].astype(BF)
        cc = xc[at, G + STATE : G + 2 * STATE].astype(BF)
        scores = dot(cc, b, 1, 1)
        scores2 = jnp.concatenate([scores, scores], axis=1)
        d_scores = jnp.zeros((Q, Q), F32)
        d_b = jnp.zeros((Q, STATE), F32)
        d_c = jnp.zeros((Q, STATE), F32)
        d_cum = jnp.zeros((Q, 128), F32)
        d_dt = jnp.zeros((Q, 128), F32)
        d_last = jnp.zeros((8, 128), F32)
        lane_ids = lax.broadcasted_iota(jnp.int32, (Q, 128), 1)
        row_ids = lax.broadcasted_iota(jnp.int32, (Q, 128), 0)
        for p in range(G // 128):
            lanes = slice(p * 128, p * 128 + 128)
            dyb = dy_ref[at, lanes]
            d_y = dyb.astype(F32)
            x = xc[at, lanes]
            dt_x = spread(dt, p, mask)
            u = (x * dt_x).astype(BF)
            u2 = split_pair(u, mask)
            uf = u.astype(F32)
            dec = decay_pair(cum, cum_t, causal, p)
            m = (scores2 * dec).astype(BF)
            dm = dot(dyb, u2, 1, 1) * dec
            d_scores = d_scores + dm[:, :Q] + dm[:, Q:]
            both = dot(m, dyb, 0, 0)
            du = jnp.where(mask, both[:Q], both[Q:])
            tail_x = spread(tail, p, mask)
            before = st_ref[c, :, lanes]
            after = dstate[:, lanes]
            afterb = after.astype(BF)
            du_out = tail_x * dot(b, afterb, 1, 0)
            du = du + du_out
            dye = (d_y * spread(e_cum, p, mask)).astype(BF)
            d_c = d_c + dot(dye, before.astype(BF), 1, 1)
            d_b = d_b + dot((uf * tail_x).astype(BF), afterb, 1, 1)
            e_last_x = spread(e_last, p, mask[0:8])
            dstate[:, lanes] = after * e_last_x[0:1, :] + dot(cc, dye, 0, 0)
            z3 = jnp.sum(uf * du_out, axis=0, keepdims=True) + e_last_x[0:1, :] * jnp.sum(before * after, axis=0, keepdims=True)
            z1 = d_y * yp_ref[at, lanes] - uf * du
            z2 = x * du
            pick = jnp.where(lane_ids == 2 * p + jnp.where(row_ids < HEAD_DIM, 0, 1), 1.0, 0.0).astype(BF)
            d_cum = d_cum + lane_sums(z1, pick)
            d_dt = d_dt + lane_sums(z2, pick)
            d_last = d_last + lane_sums(jnp.broadcast_to(z3, (8, 128)), pick)
            xc[at, lanes] = dt_x * du + gw_ref[1:2, lanes] * d_y
            gg_ref[1:2, lanes] += jnp.sum(d_y * x, axis=0, keepdims=True)
        dsb = d_scores.astype(BF)
        xc[at, G : G + STATE] = d_b + dot(dsb, cc, 0, 0)
        xc[at, G + STATE : G + 2 * STATE] = d_c + dot(dsb, b, 1, 0)
        rows = lax.broadcasted_iota(jnp.int32, (Q, Q), 0)
        cols = lax.broadcasted_iota(jnp.int32, (Q, Q), 1)
        upper = (rows <= cols).astype(F32)
        d_rate = dot(upper, d_cum, 1, 0, lax.Precision.HIGHEST) + d_last[0:1, :]
        d_step = d_dt + d_rate * hp_ref[1:2, :]
        d_raw = d_step * sigmoid(step_inputs(proj_ref, at, hp_ref, sel_ref, dt_at))
        proj_ref[at, dt_at : dt_at + 128] = dot(d_raw.astype(BF), sel_ref[...], 1, 1).astype(BF)
        gh_ref[0:1, :] += jnp.sum(d_raw, axis=0, keepdims=True)
        gh_ref[1:2, :] += jnp.sum(d_rate * rate, axis=0, keepdims=True)
        return 0

    lax.fori_loop(0, nb, chunk, 0)

    gc_ref[...] = jnp.zeros_like(gc_ref)

    def conv_back(tile, carry):
        lanes = pl.ds(pl.multiple_of(tile * 128, 128), 128)
        proj_at = pl.multiple_of(G + tile * 128, 128)
        pre = conv_tile(proj_ref, cw_ref, pad, proj_at, lanes.start, L)
        sig = sigmoid(pre)
        d_pre = xc[:, lanes] * (sig * (1.0 + pre * (1.0 - sig)))
        for k in range(KERNEL):
            gc_ref[k : k + 1, lanes] = jnp.sum(d_pre * pad[5 + k : 5 + k + L, :], axis=0, keepdims=True)
        gc_ref[4:5, lanes] = jnp.sum(d_pre, axis=0, keepdims=True)
        pad[0:L, :] = d_pre
        pad[L : L + 8, :] = jnp.zeros((8, 128), F32)
        d_in = cw_ref[3:4, lanes] * d_pre
        for k in range(KERNEL - 1):
            d_in = d_in + cw_ref[k : k + 1, lanes] * pad[3 - k : 3 - k + L, :]
        proj_ref[:, pl.ds(proj_at, 128)] = d_in.astype(BF)
        return carry

    lax.fori_loop(0, (G + 2 * STATE) // 128, conv_back, 0)


def column(row):
    return jnp.broadcast_to(row, (128, 128)).T


def rows_loop(rows, body):
    def step(r, carry):
        body(pl.ds(pl.multiple_of(r * TILE, TILE), TILE))
        return carry

    lax.fori_loop(0, rows // TILE, step, 0)


class Group:
    def __init__(self, n_seq, n_wt):
        self.n_seq = n_seq
        self.heads = HEADS // n_seq
        self.runs = n_wt if HEADS % (n_seq * n_wt) == 0 else 1
        self.run_heads = self.heads // self.runs
        self.chans = self.heads * HEAD_DIM
        self.G = -(-self.chans // 128) * 128
        self.CX = self.G + 2 * STATE
        self.NC = 2 * self.G + 2 * STATE + 128
        self.rest = self.G + 2 * STATE + 64
        self.half = (self.G + self.rest) // 2
        self.cut = self.rest // 128 * 64


def head_of(g, here, local_head):
    stride = HEADS // g.runs
    run = local_head // g.run_heads
    return run * stride + here * g.run_heads + (local_head - run * g.run_heads)


def one_hot(found):
    return jnp.where(found, 1.0, 0.0)


def step_select(g, here):
    from_ids = lax.broadcasted_iota(jnp.int32, (128, 128), 0)
    to_ids = lax.broadcasted_iota(jnp.int32, (128, 128), 1)
    return one_hot((from_ids == head_of(g, here, to_ids)) & (to_ids < g.heads))


OUT, GATE, REST, LAST = KINDS = range(4)


class Wire:
    def __init__(self, send_sems, recv_sems):
        self.send_sems, self.recv_sems, self.used = send_sems, recv_sems, 0

    def reserve(self):
        self.used += 1
        return self.used - 1

    def make(self, src, dst, axis, peer, at_send, at_recv):
        return pltpu.make_async_remote_copy(
            src, dst, self.send_sems.at[at_send], self.recv_sems.at[at_recv],
            device_id={axis: peer}, device_id_type=MESH,
        )

    def put(self, src, dst, axis, peer):
        at = self.reserve()
        copy = self.make(src, dst, axis, peer, at, at)
        copy.start()
        return copy


class Maybe:
    def __init__(self, condition, copy):
        self.condition, self.copy = condition, copy

    def start(self):
        pl.when(self.condition)(self.copy.start)
        return self

    def wait_send(self):
        pl.when(self.condition)(self.copy.wait_send)


class PlaneGather:
    def __init__(self, put, n, here, source, block):
        self.put, self.block, self.plane = put, block, n == 4
        mine = block(here, None)
        if not self.plane:
            self.copies = [put(source, mine, SEQ, lax.rem(here + k, n)) for k in range(1, n)]
            return
        self.x = here + 1 - 2 * lax.rem(here, 2)
        self.y = lax.rem(here + 2, 4)
        self.copies = [put(source, mine, SEQ, self.x), put(source, mine, SEQ, self.y)]

    def forward(self, landed=None):
        if self.plane:
            for copy, group, half, peer in (
                (self.copies[0], self.x, 0, self.y),
                (self.copies[1], self.y, 1, self.x),
            ):
                copy.wait_recv()
                part = self.block(group, half)
                self.copies.append(self.put(part, part, SEQ, peer))
                if landed is not None:
                    landed(group)

    def wait_recv(self):
        for copy in self.copies[2:] if self.plane else self.copies:
            copy.wait_recv()

    def wait_send(self):
        for copy in self.copies:
            copy.wait_send()


class PlaneSum:
    def __init__(self, put, n, here, part, got, mid):
        self.put, self.n, self.here, self.part, self.got, self.mid = put, n, here, part, got, mid
        self.plane = n == 4
        self.half = part.shape[1] // 2
        self.peers = [lax.rem(here + k, n) for k in range(1, n)]
        if self.plane:
            self.x = here + 1 - 2 * lax.rem(here, 2)
            self.y = lax.rem(here + 2, 4)
            self.peers = [lax.rem(self.x + 2, 4), self.y, self.x]

    def start(self, product, stat=None, got_stat=None):
        half, part, got = self.half, self.part, self.got
        self.copies = []
        product()
        for k, peer in enumerate(self.peers):
            if not self.plane:
                self.copies.append(self.put(part.at[peer], got.at[k], SEQ, peer))
            elif k == 0:
                self.mids = [
                    self.put(part.at[peer, 0:half], self.mid.at[0], SEQ, self.x),
                    self.put(part.at[peer, half:], self.mid.at[1], SEQ, self.y),
                ]
            elif k == 1:
                self.copies.append(self.put(part.at[peer, half:], got.at[1, half:], SEQ, peer))
            else:
                self.copies.append(self.put(part.at[peer, 0:half], got.at[0, 0:half], SEQ, peer))
            if stat is not None:
                self.copies.append(self.put(stat.at[peer], got_stat.at[k], SEQ, peer))

    def middle(self):
        if not self.plane:
            return
        half, part = self.half, self.part
        for copy in self.mids:
            copy.wait()

        def add(at):
            late = pl.ds(pl.multiple_of(at.start + half, TILE), TILE)
            for peer, rows, slot in ((self.y, at, 0), (self.x, late, 1)):
                total = part[peer, rows, :].astype(F32) + self.mid[slot, at, :].astype(F32)
                part[peer, rows, :] = total.astype(BF)

        rows_loop(half, add)
        self.copies += [
            self.put(part.at[self.y, 0:half], self.got.at[1, 0:half], SEQ, self.y),
            self.put(part.at[self.x, half:], self.got.at[0, half:], SEQ, self.x),
        ]

    def end(self):
        for copy in self.copies:
            copy.wait()

    def total(self, at):
        total = self.part[self.here, at, :].astype(F32)
        for k in range(2 if self.plane else self.n - 1):
            total = total + self.got[k, at, :].astype(F32)
        return total


class Mover:
    def __init__(self, sems):
        self.sems, self.used = sems, 0

    def put(self, src, dst):
        copy = pltpu.make_async_copy(src, dst, self.sems.at[self.used])
        copy.start()
        self.used += 1
        return copy


def meet_all(axes):
    barrier = pltpu.get_barrier_semaphore()
    count = 0
    for axis, n in axes:
        me = lax.axis_index(axis)
        for k in range(1, n):
            pl.semaphore_signal(
                barrier, inc=1, device_id={axis: lax.rem(me + k, n)}, device_id_type=MESH
            )
        count += n - 1
    pl.semaphore_wait(barrier, count)


def column_tiles(first, last, body):
    whole = (last - first) // 256

    def step(t, carry):
        body(pl.ds(pl.multiple_of(first + t * 256, 128), 256))
        return carry

    lax.fori_loop(0, whole, step, 0)
    if first + whole * 256 < last:
        body(slice(first + whole * 256, last))


def four_blocks(part, product):
    count, rows, columns = part.shape

    def step(q, carry):
        at = pl.ds(pl.multiple_of(q * 4 * rows, TILE), 4 * rows)

        def tile(lanes):
            value = product(at, lanes).astype(BF)
            for b in range(4):
                part[q * 4 + b, :, lanes] = value[b * rows : (b + 1) * rows]

        column_tiles(0, columns, tile)
        return carry

    lax.fori_loop(0, count // 4, step, 0)


class ForwardOuts(NamedTuple):
    sec: Any
    pout: Any
    stat0: Any
    h1: Any
    gb_o: Any
    stats: Any
    packs_o: Any
    wf_o: Any
    of_o: Any
    n_o: Any
    proj_o: Any
    mixed_o: Any
    yp_o: Any
    st_o: Any


class ForwardRefs(NamedTuple):
    tokens: Any
    cotangent: Any
    conv_w: Any
    conv_b: Any
    dt_bias: Any
    a_log: Any
    skip_d: Any
    gate_gain: Any
    norm_gain: Any
    w_src: Any
    o_src: Any
    sec: Any
    pout: Any
    stat0: Any
    h1: Any
    gb_o: Any
    stats: Any
    packs_o: Any
    wf_o: Any
    of_o: Any
    n_o: Any
    proj_o: Any
    mixed_o: Any
    yp_o: Any
    st_o: Any
    h0: Any
    cot: Any
    packs: Any
    wf: Any
    of: Any
    normed: Any
    proj: Any
    mixed: Any
    yp: Any
    st: Any
    pad: Any
    xc: Any
    dts: Any
    state: Any
    vg: Any
    ssq: Any
    part: Any
    got: Any
    got_stat: Any
    hbuf: Any
    own_stat: Any
    cols: Any
    mdots: Any
    sel: Any
    pack: Any
    mid: Any
    ss: Any
    rs: Any
    ls: Any


def forward_kernel(g, n, w, rows, *refs):
    r = ForwardRefs(*refs)
    G, NC = g.G, g.NC
    core, here, shard = lax.axis_index(SECTION), lax.axis_index(SEQ), lax.axis_index(WT)
    sibling = 1 - core
    wire, mover = Wire(r.ss, r.rs), Mover(r.ls)
    wf, of, packs = r.wf, r.of, r.packs
    sends, saves = [], []

    def aligned(at, size):
        return pl.ds(pl.multiple_of(at, 16), size)

    def put(src, dst, axis, peer):
        copy = wire.put(src, dst, axis, peer)
        sends.append(copy)
        return copy

    for layer in range(2):
        for first, last in ((g.chans, G), (G + g.chans, 2 * G), (2 * G + 2 * STATE + HEADS, NC)):
            if first < last:
                wf[layer, first:last, :] = jnp.zeros((last - first, D), BF)
    meet_all(((SEQ, n), (WT, w), (SECTION, 2)))
    o_rows = G // w
    lanes_of = D // w
    mine_o = aligned(shard * o_rows, o_rows)
    piece = here if g.runs == w else shard
    o_own = r.o_src.at[aligned(piece * o_rows, o_rows)]
    mine_lanes = pl.ds(pl.multiple_of(shard * lanes_of, 128), lanes_of)
    width = g.run_heads * HEAD_DIM
    runs = []
    for kind_at, source_at in ((0, 0), (G, INNER)):
        for run in range(g.runs):
            source = source_at + run * (INNER // g.runs) + here * width
            runs.append((source, kind_at + run * width, width))
    runs.append((2 * INNER, 2 * G, 2 * STATE))
    runs.append((2 * INNER + 2 * STATE, 2 * G + 2 * STATE, HEADS))
    siblings, locals_ = [], []
    for source, target, size in runs:
        taken = r.w_src.at[aligned(source, size)]
        siblings.append(put(taken, wf.at[core, target : target + size, mine_lanes], SECTION, sibling))
        locals_.append(mover.put(taken, wf.at[core, target : target + size, mine_lanes]))
    others = [put(o_own, of.at[core, mine_o], SECTION, sibling)]
    locals_later = [
        mover.put(o_own, of.at[core, mine_o]),
        mover.put(r.tokens.at[core, 0], r.h0),
        mover.put(r.cotangent.at[core, 0], r.cot),
    ]

    def part_of(layer, kind, at_shard, at_core):
        if kind == OUT:
            return of.at[layer, aligned(at_shard * o_rows + at_core * (o_rows // 2), o_rows // 2)]
        size = (G if kind == GATE else g.rest) // 2
        first = (0 if kind == GATE else G) + at_core * size
        lanes = pl.ds(pl.multiple_of(at_shard * lanes_of, 128), lanes_of)
        return wf.at[layer, aligned(first, size), lanes]

    line = w == 4

    def fetch(layer, kind):
        mine = part_of(layer, kind, shard, core)
        at = [wire.reserve() for _ in range(w)]
        copies = [
            wire.make(mine, mine, WT, lax.rem(shard + k, w), at[k], at[k]) for k in range(1, w)
        ]
        if line:
            copies[1].start()
            sends.append(copies[1])
            sends.append(Maybe(shard != w - 1, copies[0]).start())
            sends.append(Maybe(shard != 0, copies[2]).start())
        else:
            for copy in copies:
                copy.start()
            sends.extend(copies)
        return copies, at

    def far_part(fetched, layer, kind):
        if not line:
            return []
        at = fetched[1]
        fetched[0][1].wait_recv()
        block = part_of(layer, kind, lax.rem(shard + 2, w), core)
        up = wire.make(block, block, WT, lax.rem(shard + 1, w), at[0], at[3])
        down = wire.make(block, block, WT, lax.rem(shard + w - 1, w), at[0], at[1])
        sends.append(Maybe(shard == 2, up).start())
        sends.append(Maybe(shard == 1, down).start())
        return [put(block, block, SECTION, sibling)]

    def near_parts(fetched, layer, kind):
        found = []
        for k in (1, 3) if line else range(1, w):
            fetched[0][k - 1].wait_recv()
            block = part_of(layer, kind, lax.rem(shard + w - k, w), core)
            found.append(put(block, block, SECTION, sibling))
        return found

    def received(copies):
        for copy in copies:
            copy.wait_recv()

    own_rows = aligned(here * rows, rows)

    def gather(whole):
        def block(group, half):
            size = rows if half is None else rows // 2
            return whole.at[aligned(group * rows + (half or 0) * size, size)]

        return PlaneGather(wire.put, n, here, block(here, None), block)

    def save(source, target):
        saves.append(mover.put(source, target))

    def saved():
        while saves:
            saves.pop().wait()

    for copy in locals_:
        copy.wait()
    received(siblings)
    pending = fetch(0, REST)
    gain_at = g.CX + 128 + G
    r.sel[...] = step_select(g, here).astype(BF)
    pack_small(g, here, r.conv_w, r.conv_b, r.dt_bias, r.a_log, r.skip_d, r.gate_gain, r.norm_gain, r.pack)
    others.append(put(r.pack, packs.at[core], SECTION, sibling))
    locals_later.append(mover.put(r.pack, packs.at[core]))
    for copy in locals_later:
        copy.wait()
    received(others)

    def norm(at):
        h = r.h0[at, :]
        inv = lax.rsqrt(jnp.mean(h * h, axis=1, keepdims=True) + EPSILON)
        r.normed[pl.ds(pl.multiple_of(here * rows + at.start, TILE), TILE), :] = (
            h * inv * packs[0, 0:1, gain_at:]
        ).astype(BF)

    rows_loop(rows, norm)
    arriving = gather(r.normed)
    handed = far_part(pending, 0, REST)
    coming = [fetch(0, GATE), fetch(0, OUT)]
    arriving.forward()
    handed += near_parts(pending, 0, REST)

    for layer in range(2):
        proj, mixed, normed = r.proj, r.mixed, r.normed
        conv = packs.at[layer, :, 0 : g.CX]
        head = packs.at[layer, :, g.CX : g.CX + 128]
        wide = packs.at[layer, :, g.CX + 128 : gain_at]

        def project(lanes):
            proj[:, lanes] = dot(normed[...], wf[layer, lanes, :], 1, 1).astype(BF)

        arriving.wait_recv()
        received(handed)
        gathered = arriving
        column_tiles(G, NC, project)
        scan_forward(
            G, proj, conv, head, wide, r.sel, mixed, r.yp, r.st,
            r.pad, r.xc, r.dts, r.state,
        )
        save(mixed, r.mixed_o.at[layer])
        save(r.yp, r.yp_o.at[layer])
        save(r.st, r.st_o.at[layer])
        save(normed, r.n_o.at[layer])
        handed = far_part(coming[0], layer, GATE) + far_part(coming[1], layer, OUT)
        handed += near_parts(coming[0], layer, GATE) + near_parts(coming[1], layer, OUT)
        if layer == 0:
            pending = fetch(1, REST)
        received(handed)
        column_tiles(0, G, project)
        save(proj, r.proj_o.at[layer])
        gate_forward(G, proj, wide, mixed, r.vg, r.ssq)

        def out_product():
            four_blocks(r.part, lambda at, lanes: dot(r.vg[at, :], of[layer, :, lanes], 1, 0))

        saved()
        gathered.wait_send()
        summing = PlaneSum(wire.put, n, here, r.part, r.got, r.mid)
        summing.start(out_product, r.ssq, r.got_stat)
        summing.middle()
        summing.end()
        if layer == 0:
            handed = far_part(pending, 1, REST)
            coming = [fetch(1, GATE), fetch(1, OUT)]
        ssq = r.ssq[here]
        for k in range(n - 1):
            ssq = ssq + r.got_stat[k]
        inv2 = lax.rsqrt(ssq * (1.0 / INNER) + EPSILON)
        r.own_stat[...] = inv2
        r.cols[...] = column(inv2[0:1, :])
        if layer == 0:
            r.stat0[...] = inv2

        def finish(at):
            pout = summing.total(at) * r.cols[at, 0:1]
            whole = pl.ds(pl.multiple_of(here * rows + at.start, TILE), TILE)
            h_in = r.h0[at, :] if layer == 0 else r.hbuf[0, at, :]
            h = h_in + pout
            r.hbuf[layer, at, :] = h
            if layer == 0:
                r.pout[at, :] = pout
                r.h1[at, :] = h
                inv = lax.rsqrt(jnp.mean(h * h, axis=1, keepdims=True) + EPSILON)
                r.normed[whole, :] = (h * inv * packs[1, 0:1, gain_at:]).astype(BF)
            else:
                out = r.cot[at, :].astype(BF)
                dots = jnp.sum(out.astype(F32) * pout, axis=1, keepdims=True)
                r.mdots[at, :] = jnp.broadcast_to(dots * (1.0 / INNER), (TILE, 128))
                r.normed[whole, :] = out

        rows_loop(rows, finish)
        if layer == 0:
            arriving = gather(r.normed)
            arriving.forward()
            handed += near_parts(pending, 1, REST)
    r.stats[here] = r.own_stat[...]
    r.stats[here, 1:2, :] = r.mdots[...].T[0:1, :]
    last_rows = gather(r.normed)
    arriving = []
    for k in range(1, n):
        block = r.stats.at[here]
        arriving.append(put(block, block, SEQ, lax.rem(here + k, n)))
    arriving.append(put(r.hbuf.at[1 - core], r.sec.at[core], SECTION, sibling))
    save(r.hbuf.at[core], r.sec.at[core])
    save(packs, r.packs_o)
    save(wf, r.wf_o)
    save(of, r.of_o)
    last_rows.forward()
    last_rows.wait_recv()
    received(arriving)
    save(r.normed, r.gb_o)
    last_rows.wait_send()
    assert wire.used <= r.ss.shape[0] and mover.used <= r.ls.shape[0]
    for copy in sends:
        copy.wait_send()
    saved()


def forward_call(g, n, w, tokens, cotangent, small, w_src, o_src):
    rows = tokens.shape[2]
    L, G, NC, CX, PK = rows * n, g.G, g.NC, g.CX, g.CX + 128 + g.G + D
    S = jax.ShapeDtypeStruct
    shapes = ForwardOuts(
        sec=S((2, rows, D), F32),
        pout=S((rows, D), F32),
        stat0=S((8, 128), F32),
        h1=S((rows, D), F32),
        gb_o=S((L, D), BF),
        stats=S((n, 8, 128), F32),
        packs_o=S((2, 8, PK), F32),
        wf_o=S((2, NC, D), BF),
        of_o=S((2, G, D), BF),
        n_o=S((2, L, D), BF),
        proj_o=S((2, L, NC), BF),
        mixed_o=S((2, L, G), BF),
        yp_o=S((2, L, G), F32),
        st_o=S((2, L // Q, STATE, G), F32),
    )
    scratch = [
        S((rows, D), F32), S((rows, D), F32), shapes.packs_o, shapes.wf_o, shapes.of_o, S((L, D), BF), S((L, NC), BF), S((L, G), BF),
        S((L, G), F32), S((L // Q, STATE, G), F32), S((8 + L, 128), F32), S((L, CX), F32), S((L, 128), F32), S((STATE, G), F32),
        S((L, G), BF), S((n, 8, 128), F32), S((n, rows, D), BF), S((n - 1, rows, D), BF), S((n - 1, 8, 128), F32),
        S((2, rows, D), F32), S((8, 128), F32), S((rows, 128), F32), S((rows, 128), F32),
        S((128, 128), BF), S((8, PK), F32), S((2, rows // 2, D), BF),
    ]
    remote = 4 + 2 * g.runs + 6 * w + 6 * (w - 1) + 24 + 8 * (n - 1)
    outs = pl.pallas_call(
        functools.partial(forward_kernel, g, n, w, rows),
        out_shape=list(shapes),
        in_specs=[ANY, ANY] + [VM] * len(small) + [ANY, ANY],
        out_specs=[VM] * 4 + [ANY, VM] + [ANY] * 8,
        scratch_shapes=[pltpu.VMEM(s.shape, s.dtype) for s in scratch]
        + [
            pltpu.SemaphoreType.DMA((remote,)),
            pltpu.SemaphoreType.DMA((remote,)),
            pltpu.SemaphoreType.DMA((22 + 2 * g.runs,)),
        ],
        compiler_params=pltpu.CompilerParams(
            collective_id=0, has_side_effects=True, vmem_limit_bytes=FORWARD_VMEM
        ),
        name="forward",
    )(tokens, cotangent, *small, w_src, o_src)
    return ForwardOuts(*outs)


class BackwardOuts(NamedTuple):
    ig: Any
    gi: Any
    go: Any
    gi_sib: Any
    go_sib: Any
    small: Any
    far: Any
    late: Any


class BackwardRefs(NamedTuple):
    packs_i: Any
    wf_i: Any
    of_i: Any
    n_i: Any
    proj_i: Any
    mixed_i: Any
    yp_i: Any
    st_i: Any
    gb_i: Any
    stats1_i: Any
    stat0_i: Any
    pout_i: Any
    h1_i: Any
    tokens_i: Any
    cotangent_i: Any
    ig: Any
    gi: Any
    go: Any
    gi_sib: Any
    go_sib: Any
    small: Any
    far: Any
    late: Any
    packs: Any
    wf: Any
    of: Any
    n: Any
    proj: Any
    mixed: Any
    yp: Any
    st: Any
    gb: Any
    stats: Any
    pout: Any
    h1: Any
    h0: Any
    cot: Any
    dy: Any
    pad: Any
    xc: Any
    dts: Any
    dstate: Any
    part: Any
    got: Any
    own_stat: Any
    mdots: Any
    grads: Any
    gw: Any
    gout: Any
    sib_w: Any
    sib_o: Any
    z_w: Any
    z_o: Any
    relay_w: Any
    relay_o: Any
    sm: Any
    sm_sib: Any
    sm_z: Any
    sm_own: Any
    sel: Any
    gain: Any
    gain_z: Any
    gain_sum: Any
    mid: Any
    ss: Any
    rs: Any
    ls: Any
    free: Any


def backward_kernel(g, n, w, rows, *refs):
    r = BackwardRefs(*refs)
    G, NC, CX = g.G, g.NC, g.CX
    core, here, shard = lax.axis_index(SECTION), lax.axis_index(SEQ), lax.axis_index(WT)
    sibling = 1 - core
    wire, mover = Wire(r.ss, r.rs), Mover(r.ls)
    o_half, lanes_of = G // (2 * w), D // w
    gain_at = CX + 128 + G

    def aligned(at, size):
        return pl.ds(pl.multiple_of(at, 16), size)

    def load(layer, *pairs):
        return [mover.put(source.at[layer], target) for source, target in pairs]

    first = load(1, (r.of_i, r.of), (r.proj_i, r.proj), (r.mixed_i, r.mixed))
    first += [mover.put(r.packs_i, r.packs), mover.put(r.gb_i, r.gb), mover.put(r.stats1_i, r.stats)]
    later = load(1, (r.n_i, r.n), (r.yp_i, r.yp), (r.st_i, r.st), (r.wf_i, r.wf))
    later += [mover.put(r.pout_i, r.pout), mover.put(r.h1_i, r.h1), mover.put(r.stat0_i, r.own_stat)]
    later += [mover.put(r.tokens_i.at[core, 0], r.h0), mover.put(r.cotangent_i.at[core, 0], r.cot)]
    meet_all(((SEQ, n), (WT, w), (SECTION, 2)))
    r.sm[...] = jnp.zeros_like(r.sm)
    r.sel[...] = step_select(g, here).astype(BF)
    r.gain[here] = jnp.zeros((8, D), F32)
    open_sends, record = [], {}
    line = w == 4
    arrivals = r.got if r.got.shape[0] == n - 1 else r.far

    def put(src, dst, axis, peer):
        copy = wire.put(src, dst, axis, peer)
        open_sends.append(copy)
        return copy

    def rows_of(kind):
        return ((0, G), (0, G), (G, g.cut), (G + g.cut, g.rest - g.cut))[kind]

    def kept(kind):
        middle = (G + g.cut) // 2
        return (slice(0, G // (2 * w)), slice(0, G // 2), slice(G // 2, middle), slice(middle, g.half))[kind]

    def buffers(kind):
        if kind == OUT:
            return r.gout, r.sib_o, r.z_o, r.go, r.go_sib
        return r.gw, r.sib_w, r.z_w, r.gi, r.gi_sib

    def block_of(kind, at_shard, at_core):
        if kind == OUT:
            return aligned((2 * at_shard + at_core) * o_half, o_half), slice(0, D)
        first, size = rows_of(kind)
        return (
            aligned(first + at_core * (size // 2), size // 2),
            pl.ds(pl.multiple_of(at_shard * lanes_of, 128), lanes_of),
        )

    def ready(kind):
        for copy in record.pop(kind, ()):
            copy.wait_send()

    def to_sibling(layer, kind):
        grad, sib, _, _, _ = buffers(kind)
        if layer == 0:
            pl.semaphore_wait(r.free.at[kind], 1)
        if kind == OUT:
            pairs = [
                (grad.at[block_of(kind, q, sibling)], sib.at[aligned(q * o_half, o_half)])
                for q in range(w)
            ]
        else:
            first, size = rows_of(kind)
            rows_there = aligned(first + sibling * (size // 2), size // 2)
            pairs = [(grad.at[rows_there], sib.at[kept(kind)])]
        copies = [wire.put(source, target, SECTION, sibling) for source, target in pairs]
        record[kind] = list(copies)
        return copies

    def to_shards(layer, kind, copies):
        grad, sib, z, _, _ = buffers(kind)
        for copy in copies:
            copy.wait_recv()
        if kind == OUT:
            per = o_half // TILE

            def places(t):
                q = t // per
                return (2 * q + core) * o_half + (t - q * per) * TILE, t * TILE

            steps = w * per
        else:
            first, size = rows_of(kind)
            steps = size // 2 // TILE

            def places(t):
                return first + core * (size // 2) + t * TILE, kept(kind).start + t * TILE

        def add(t, carry):
            mine, theirs = (pl.ds(pl.multiple_of(at, TILE), TILE) for at in places(t))
            grad[mine, :] = (grad[mine, :].astype(F32) + sib[theirs, :].astype(F32)).astype(BF)
            return carry

        lax.fori_loop(0, steps, add, 0)
        if layer == 1:
            pl.semaphore_signal(
                r.free.at[kind], inc=1, device_id={SECTION: sibling}, device_id_type=MESH
            )
        at = [wire.reserve() for _ in range(w)]
        found = []
        for k in range(1, w):
            peer = lax.rem(shard + k, w)
            source = grad.at[block_of(kind, peer, core)]
            found.append(wire.make(source, z.at[layer, k - 1, kept(kind)], WT, peer, at[k], at[k]))
        if not line:
            for copy in found:
                copy.start()
            record[kind] += found
            return found, None
        buffer = (r.relay_o if kind == OUT else r.relay_w).at[layer, kept(kind)]
        up = wire.make(grad.at[block_of(kind, w - 1, core)], buffer, WT, 1, at[0], at[0])
        down = wire.make(grad.at[block_of(kind, 0, core)], buffer, WT, w - 2, at[0], at[0])
        inner = (shard == 1) | (shard == 2)
        first = [
            Maybe(shard == 0, up),
            Maybe(shard == w - 1, down),
            Maybe(inner, found[0]),
            Maybe(inner, found[2]),
        ]
        others = [
            Maybe(jnp.logical_not(inner), found[1]),
            Maybe(shard == 0, found[0]),
            Maybe(shard == w - 1, found[2]),
        ]
        record[kind] += [*first, *others, Maybe(inner, found[1])]
        for copy in first:
            copy.start()
        waiting.extend(others)
        arriving = wire.make(buffer, buffer, WT, lax.rem(shard + 1, w), at[0], at[0])
        return found, arriving

    def relay(layer, kind, moving):
        found, arriving = moving
        if not line:
            return
        grad, buffer = (r.gout, r.relay_o) if kind == OUT else (r.gw, r.relay_w)
        rows_here = kept(kind)

        @pl.when((shard == 1) | (shard == 2))
        def _():
            arriving.wait_recv()
            at_rows, at_lanes = block_of(kind, lax.rem(shard + 2, w), core)

            def add(at):
                mine = pl.ds(pl.multiple_of(at_rows.start + at.start, TILE), TILE)
                there = pl.ds(pl.multiple_of(rows_here.start + at.start, TILE), TILE)
                total = grad[mine, at_lanes].astype(F32) + buffer[layer, there, :].astype(F32)
                grad[mine, at_lanes] = total.astype(BF)

            rows_loop(rows_here.stop - rows_here.start, add)
            found[1].start()

    def to_plane(layer, kind, moving):
        grad, _, z, result, _ = buffers(kind)
        copies, _ = moving
        if line:
            pl.when(shard != 0)(copies[0].wait_recv)
            copies[1].wait_recv()
            pl.when(shard != w - 1)(copies[2].wait_recv)
        else:
            for copy in copies:
                copy.wait_recv()
        at_rows, at_lanes = block_of(kind, shard, core)
        here_rows = kept(kind)

        def add(at):
            mine = pl.ds(pl.multiple_of(at_rows.start + at.start, TILE), TILE)
            there = pl.ds(pl.multiple_of(here_rows.start + at.start, TILE), TILE)
            total = grad[mine, at_lanes].astype(F32)
            for k in range(w - 1):
                total = total + z[layer, k, there, :].astype(F32)
            z[layer, 1, there, :] = total.astype(BF)

        def add_end(at, near):
            mine = pl.ds(pl.multiple_of(at_rows.start + at.start, TILE), TILE)
            there = pl.ds(pl.multiple_of(here_rows.start + at.start, TILE), TILE)
            total = grad[mine, at_lanes].astype(F32)
            total = total + z[layer, 1, there, :].astype(F32) + z[layer, near, there, :].astype(F32)
            z[layer, 1, there, :] = total.astype(BF)

        count = here_rows.stop - here_rows.start
        if line:

            @pl.when(shard == 0)
            def _():
                rows_loop(count, lambda at: add_end(at, 2))

            @pl.when(shard == w - 1)
            def _():
                rows_loop(count, lambda at: add_end(at, 0))

            @pl.when((shard == 1) | (shard == 2))
            def _():
                rows_loop(count, add)
        else:
            rows_loop(count, add)
        def target(group, half):
            size = here_rows.stop - here_rows.start
            if half is None:
                return result.at[layer, group, here_rows]
            first = here_rows.start + half * (size // 2)
            return result.at[layer, group, first : first + size // 2]

        block = z.at[layer, 1, here_rows]
        return PlaneGather(put, n, here, block, target), mover.put(block, target(here, None))

    def landed(kind, *arrivals):
        _, _, _, result, target = buffers(kind)
        for found, own in arrivals:
            found.wait_recv()
            own.wait()
        return put(result.at[sibling, :, kept(kind)], target.at[:, kept(kind)], SECTION, sibling)

    def done(copies):
        for copy in copies:
            copy.wait()

    arrived, waiting = {}, []
    for layer in (1, 0):
        conv = r.packs.at[layer, :, 0:CX]
        head = r.packs.at[layer, :, CX : CX + 128]
        wide = r.packs.at[layer, :, CX + 128 : gain_at]
        g_conv = r.sm.at[layer, :, 0:CX]
        g_head = r.sm.at[layer, :, CX : CX + 128]
        g_wide = r.sm.at[layer, :, CX + 128 : gain_at]
        done(first)

        def d_normed(lanes):
            r.xc[:, lanes] = dot(r.gb[...], r.of[lanes, :], 1, 1)

        column_tiles(0, G, d_normed)
        gate_backward(
            G, r.proj, r.mixed, r.xc, r.stats, wide, r.dy, g_wide
        )

        def out_rows(at):
            r.gout[at, :] = dot(r.mixed[:, at], r.gb[...], 0, 0).astype(BF)

        def in_rows(at):
            r.gw[at, :] = dot(r.proj[:, at], r.n[...], 0, 0).astype(BF)

        ready(OUT)
        column_tiles(0, G, out_rows)
        out_sib = to_sibling(layer, OUT)
        done(later)
        ready(GATE)
        column_tiles(0, G, in_rows)
        gate_sib = to_sibling(layer, GATE)
        out_z = to_shards(layer, OUT, out_sib)
        gate_z = to_shards(layer, GATE, gate_sib)
        if layer == 0:
            arrived[1, OUT][0].forward()
            arrived[1, GATE][0].forward()
            arrived[1, REST] = to_plane(1, REST, rest_z[0])
            arrived[1, LAST] = to_plane(1, LAST, rest_z[1])

        def serve():
            for copy in waiting:
                copy.start()

        scan_backward(
            G, r.proj, r.dy, r.yp, r.st, conv, head, wide, r.sel, g_wide, g_conv, g_head,
            r.pad, r.xc, r.dts, r.dstate, serve,
        )
        waiting.clear()
        relay(layer, OUT, out_z)
        relay(layer, GATE, gate_z)
        if layer == 0:
            small_sib = put(r.sm.at[sibling], r.sm_sib, SECTION, sibling)
        if layer == 0:
            arrived[1, REST][0].forward()
            arrived[1, LAST][0].forward()
            small_sib.wait_recv()
            r.sm_own[...] = r.sm[core] + r.sm_sib[...]
            small_z = [
                put(r.sm_own, r.sm_z.at[k - 1], WT, lax.rem(shard + k, w)) for k in range(1, w)
            ]
        if layer == 1:
            first = load(0, (r.of_i, r.of), (r.mixed_i, r.mixed))
            later = load(0, (r.yp_i, r.yp), (r.st_i, r.st))

        def in_product():
            four_blocks(r.part, lambda at, lanes: dot(r.proj[at, :], r.wf[:, lanes], 1, 0))

        summing = PlaneSum(wire.put, n, here, r.part, arrivals, r.mid)

        def rest_gradient():
            ready(REST)
            ready(LAST)
            column_tiles(G, NC, in_rows)
            return to_sibling(layer, REST), to_sibling(layer, LAST)

        def rest_to_shards(copies):
            return to_shards(layer, REST, copies[0]), to_shards(layer, LAST, copies[1])

        if layer == 0:
            rest_sib = rest_gradient()
            summing.start(in_product)
            rest_z = rest_to_shards(rest_sib)
            summing.middle()
        else:
            summing.start(in_product)
            later += load(0, (r.wf_i, r.wf))
            rest_sib = rest_gradient()
            first += load(0, (r.proj_i, r.proj))
            later += load(0, (r.n_i, r.n))
            summing.middle()
            rest_z = rest_to_shards(rest_sib)
        summing.end()
        while waiting:
            waiting.pop(0).start()
        if arrivals is not r.got:
            done(
                [
                    mover.put(arrivals.at[k - 1], r.part.at[lax.rem(here + k, n)])
                    for k in range(1, n)
                ]
            )

        def finish(at):
            if arrivals is r.got:
                d_in = summing.total(at)
            else:
                d_in = r.part[0, at, :].astype(F32)
                for k in range(1, n):
                    d_in = d_in + r.part[k, at, :].astype(F32)
            h = r.h1[at, :] if layer == 1 else r.h0[at, :]
            above = r.cot[at, :] if layer == 1 else r.grads[1, at, :]
            inv = lax.rsqrt(jnp.mean(h * h, axis=1, keepdims=True) + EPSILON)
            normed = h * inv
            r.gain[here, layer : layer + 1, :] += jnp.sum(d_in * normed, axis=0, keepdims=True)
            d_s = d_in * r.packs[layer, 0:1, gain_at:]
            d_h = above + inv * (d_s - normed * jnp.mean(d_s * normed, axis=1, keepdims=True))
            r.grads[layer, at, :] = d_h
            if layer == 1:
                out = d_h.astype(BF)
                whole = pl.ds(pl.multiple_of(here * rows + at.start, TILE), TILE)
                r.gb[whole, :] = out
                dots = jnp.sum(out.astype(F32) * r.pout[at, :], axis=1, keepdims=True)
                r.mdots[at, :] = jnp.broadcast_to(dots * (1.0 / INNER), (TILE, 128))

        rows_loop(rows, finish)
        if layer == 1:
            r.stats[here] = r.own_stat[...]
            r.stats[here, 1:2, :] = r.mdots[...].T[0:1, :]
            own = aligned(here * rows, rows)
            gathering = []

            def rows_of_group(group, half):
                size = rows if half is None else rows // 2
                return r.gb.at[aligned(group * rows + (half or 0) * size, size)]

            grad_rows = PlaneGather(put, n, here, r.gb.at[own], rows_of_group)
            for k in range(1, n):
                peer = lax.rem(here + k, n)
                gathering.append(put(r.stats.at[here], r.stats.at[here], SEQ, peer))
            grad_rows.forward()
            relay(1, REST, rest_z[0])
            relay(1, LAST, rest_z[1])
            arrived[1, OUT] = to_plane(1, OUT, out_z)
            arrived[1, GATE] = to_plane(1, GATE, gate_z)
            grad_rows.wait_recv()
            for copy in gathering:
                copy.wait_recv()
    gains = []
    ends = [put(r.grads.at[sibling], r.ig.at[core], SECTION, sibling)]
    for k in range(1, n):
        gains.append(put(r.gain.at[here], r.gain.at[here], SEQ, lax.rem(here + k, n)))
    local_grad = mover.put(r.grads.at[core], r.ig.at[core])
    relay(0, REST, rest_z[0])
    arrived[0, OUT] = to_plane(0, OUT, out_z)
    arrived[0, GATE] = to_plane(0, GATE, gate_z)
    relay(0, LAST, rest_z[1])
    arrived[0, OUT][0].forward()
    arrived[0, GATE][0].forward()
    for copy in small_z:
        copy.wait_recv()
    total = r.sm_own[...]
    for k in range(w - 1):
        total = total + r.sm_z[k]
    r.small[here] = total
    sums = [
        put(r.small.at[here], r.small.at[here], SEQ, lax.rem(here + k, n)) for k in range(1, n)
    ]
    for copy in gains:
        copy.wait_recv()
    total = r.gain[0]
    for k in range(1, n):
        total = total + r.gain[k]
    r.gain_z[shard] = total
    gains = [
        put(r.gain_z.at[shard], r.gain_z.at[shard], WT, lax.rem(shard + k, w)) for k in range(1, w)
    ]
    arrived[0, REST] = to_plane(0, REST, rest_z[0])
    ends.append(landed(OUT, arrived[1, OUT], arrived[0, OUT]))
    ends.append(landed(GATE, arrived[1, GATE], arrived[0, GATE]))
    arrived[0, LAST] = to_plane(0, LAST, rest_z[1])
    arrived[0, REST][0].forward()
    ends.append(landed(REST, arrived[1, REST], arrived[0, REST]))
    arrived[1, LAST][0].wait_recv()
    arrived[1, LAST][1].wait()
    last, last_own = arrived[0, LAST]

    def hand_over(group):
        source, target = r.gi.at[sibling, group, kept(LAST)], r.gi_sib.at[group, kept(LAST)]
        ends.append(put(source, target, SECTION, sibling))

    last_own.wait()
    hand_over(here)
    if last.plane:
        last.forward(hand_over)
        last.wait_recv()
        hand_over(lax.rem(last.x + 2, 4))
    else:
        last.wait_recv()
        for k in range(1, n):
            hand_over(lax.rem(here + k, n))
    for copy in gains:
        copy.wait_recv()
    total = r.gain_z[0]
    for k in range(1, w):
        total = total + r.gain_z[k]
    r.gain_sum[core] = total
    ends.append(put(r.gain_sum.at[core], r.gain_sum.at[core], SECTION, sibling))
    for copy in ends + sums:
        copy.wait_recv()
    r.late[...] = r.gain_sum[0] + r.gain_sum[1]
    local_grad.wait()
    assert wire.used <= r.ss.shape[0] and mover.used <= r.ls.shape[0]
    for kind in KINDS:
        ready(kind)
    for copy in open_sends:
        copy.wait_send()


def backward_call(g, n, w, fwd, tokens, cotangent):
    rows = tokens.shape[2]
    L, G, NC, CX = rows * n, g.G, g.NC, g.CX
    PK = CX + 128 + G + D
    S = jax.ShapeDtypeStruct
    o_half, lanes_of = G // (2 * w), D // w
    spill = n > 8
    outs = BackwardOuts(
        ig=S((2, rows, D), F32),
        gi=S((2, n, g.half, lanes_of), BF),
        go=S((2, n, o_half, D), BF),
        gi_sib=S((n, g.half, lanes_of), BF),
        go_sib=S((n, o_half, D), BF),
        small=S((n, 8, PK - D), F32),
        far=S((n - 1, rows, D) if spill else (8, 128), BF),
        late=S((8, D), F32),
    )
    scratch = [
        S((2, 8, PK), F32), S((NC, D), BF), S((G, D), BF), S((L, D), BF), S((L, NC), BF), S((L, G), BF),
        S((L, G), F32), S((L // Q, STATE, G), F32), S((L, D), BF), S((n, 8, 128), F32), S((rows, D), F32),
        S((rows, D), F32), S((rows, D), F32), S((rows, D), F32),
        S((L, G), BF), S((8 + L, 128), F32), S((L, CX), F32), S((L, 128), F32), S((STATE, G), F32),
        S((n, rows, D), BF), S((1 if spill else n - 1, rows, D), BF), S((8, 128), F32), S((rows, 128), F32), S((2, rows, D), F32),
        S((NC, D), BF), S((G, D), BF), S((g.half, D), BF), S((G // 2, D), BF),
        S((2, w - 1, g.half, lanes_of), BF),
        S((2, w - 1, o_half, D), BF), S((2, g.half, lanes_of), BF), S((2, o_half, D), BF), S((2, 8, PK - D), F32), S((8, PK - D), F32), S((w - 1, 8, PK - D), F32), S((8, PK - D), F32),
        S((128, 128), BF), S((n, 8, D), F32), S((w, 8, D), F32), S((2, 8, D), F32),
        S((2, rows // 2, D), BF),
    ]
    remote = 2 * (4 * (w + w + n) + n - 1) + 2 * (n - 1) + 40 + 2 * (w - 1) + 2 * (n - 1) + n
    args = [
        fwd.packs_o, fwd.wf_o, fwd.of_o, fwd.n_o, fwd.proj_o, fwd.mixed_o, fwd.yp_o, fwd.st_o,
        fwd.gb_o, fwd.stats, fwd.stat0, fwd.pout, fwd.h1, tokens, cotangent,
    ]
    results = pl.pallas_call(
        functools.partial(backward_kernel, g, n, w, rows),
        out_shape=list(outs),
        in_specs=[ANY] * len(args),
        out_specs=[VM, ANY, ANY, ANY, ANY, VM, ANY, VM],
        scratch_shapes=[pltpu.VMEM(s.shape, s.dtype) for s in scratch]
        + [
            pltpu.SemaphoreType.DMA((remote,)),
            pltpu.SemaphoreType.DMA((remote,)),
            pltpu.SemaphoreType.DMA((40 + 2 * n,)),
            pltpu.SemaphoreType.REGULAR((4,)),
        ],
        compiler_params=pltpu.CompilerParams(
            collective_id=1, has_side_effects=True, vmem_limit_bytes=BACKWARD_VMEM
        ),
        name="backward",
    )(*args)
    return BackwardOuts(*results)


def pack_small(g, here, conv_ref, bias_ref, dtb_ref, a_ref, skip_ref, gate_ref, norm_ref, pack_ref):
    G, width = g.G, g.run_heads * HEAD_DIM
    win = -(-(width + 64) // 128) * 128
    start = here * width
    base = pl.multiple_of(start // 128 * 128, 128)
    from_ids = lax.broadcasted_iota(jnp.int32, (win, G), 0)
    to_ids = lax.broadcasted_iota(jnp.int32, (win, G), 1)
    exact = lax.Precision.HIGHEST

    def take(ref, rows):
        total = jnp.zeros((rows, G), F32)
        for run in range(g.runs):
            window = ref[0:rows, pl.ds(pl.multiple_of(base + run * (INNER // g.runs), 128), win)]
            inside = (to_ids >= run * width) & (to_ids < (run + 1) * width)
            pick = one_hot(inside & (from_ids == to_ids - run * width + (start - base)))
            total = total + dot(window, pick, 1, 0, exact)
        return total

    head_from = lax.broadcasted_iota(jnp.int32, (HEADS, 128), 0)
    head_to = lax.broadcasted_iota(jnp.int32, (HEADS, 128), 1)
    head_pick = one_hot((head_from == head_of(g, here, head_to)) & (head_to < g.heads))
    wide_from = lax.broadcasted_iota(jnp.int32, (HEADS, G), 0)
    wide_to = lax.broadcasted_iota(jnp.int32, (HEADS, G), 1)
    wide_pick = (wide_from == head_of(g, here, wide_to // HEAD_DIM)) & (wide_to < g.chans)
    head_at, wide_at, gain_at = g.CX, g.CX + 128, g.CX + 128 + G
    pack_ref[...] = jnp.zeros_like(pack_ref)
    pack_ref[0:KERNEL, 0:G] = take(conv_ref, KERNEL)
    pack_ref[4:5, 0:G] = take(bias_ref, 1)
    pack_ref[0:KERNEL, G:head_at] = conv_ref[:, INNER:]
    pack_ref[4:5, G:head_at] = bias_ref[:, INNER:]
    pack_ref[0:1, head_at:wide_at] = dot(dtb_ref[...], head_pick, 1, 0, exact)
    pack_ref[1:2, head_at:wide_at] = dot(-jnp.exp(a_ref[...]), head_pick, 1, 0, exact)
    pack_ref[0:1, wide_at:gain_at] = take(gate_ref, 1)
    pack_ref[1:2, wide_at:gain_at] = dot(skip_ref[...], one_hot(wide_pick), 1, 0, exact)
    pack_ref[0:1, gain_at:] = norm_ref[...]


def halves_of_heads(g, ref_of, column_at, head):
    parts = []
    for h in (head, head + 1):
        stride = HEADS // g.runs
        group = h % stride // g.run_heads
        local_head = h // stride * g.run_heads + h % g.run_heads
        value = ref_of(group, slice(column_at + local_head // 2 * 128, column_at + local_head // 2 * 128 + 128))
        parts.append(value if local_head % 2 == h % 2 else pltpu.roll(value, HEAD_DIM, 1))
    lanes = lax.broadcasted_iota(jnp.int32, parts[0].shape, 1)
    return jnp.where(lanes < HEAD_DIM, parts[0], parts[1])


def layout_kernel(g, own_ref, sib_ref, own_out_ref, sib_out_ref, small_ref, late_ref, sec_ref, ig_ref, g_in_ref, g_out_ref, sec_out, ig_out, norm_ref, conv_ref, bias_ref, dtb_ref, a_ref, skip_ref, gate_ref):
    n, G = g.n_seq, g.G
    first_core = lax.axis_index(SECTION) == 0

    def all_rows(halves, outs):
        def copy(groups, parts, source, target, size):
            done = 0
            while done < size:
                row = source + done
                first, part_rows, half_at = next(x for x in parts if x[0] <= row < x[0] + x[1])
                half, offset = divmod(row - first, part_rows // 2)
                count = min(size - done, part_rows // 2 - offset)
                at = slice(half_at + offset, half_at + offset + count)
                total = None
                for group in groups:
                    value = halves[half][group, at, :].astype(F32)
                    total = value if total is None else total + value
                g_in_ref[target + done : target + done + count, :] = total
                done += count

        for half in range(2):
            g_out_ref[:, half] = outs[half][...].astype(F32)
        width = g.run_heads * HEAD_DIM
        gate = ((0, G, 0),)
        rest = ((0, g.cut, G // 2), (g.cut, g.rest - g.cut, (G + g.cut) // 2))
        everyone = range(n)
        for run in range(g.runs):
            for group in range(n):
                target = run * (INNER // g.runs) + group * width
                copy([group], gate, run * width, target, width)
                copy([group], rest, run * width, INNER + target, width)
        copy(everyone, rest, G, 2 * INNER, 2 * STATE)
        copy(everyone, rest, G + 2 * STATE, 2 * INNER + 2 * STATE, HEADS)

    sec_out[...] = sec_ref[...]
    ig_out[...] = ig_ref[...]
    own, own_out = own_ref.at[0], own_out_ref.at[0]

    @pl.when(first_core)
    def _():
        all_rows((own, sib_ref), (own_out, sib_out_ref))

    @pl.when(jnp.logical_not(first_core))
    def _():
        all_rows((sib_ref, own), (sib_out_ref, own_out))

    @pl.when(pl.program_id(0) == 0)
    def _():
        from_ids = lax.broadcasted_iota(jnp.int32, (128, HEADS), 0)
        to_ids = lax.broadcasted_iota(jnp.int32, (128, HEADS), 1)
        picks = [one_hot((to_ids == head_of(g, group, from_ids)) & (from_ids < g.heads)) for group in range(n)]
        exact = lax.Precision.HIGHEST
        head_at, wide_at, gain_at = g.CX, g.CX + 128, g.CX + 128 + G

        def small(group, columns):
            return small_ref[group, :, columns]

        for head in range(0, HEADS, 2):
            at = slice(head * HEAD_DIM, head * HEAD_DIM + 128)
            conv = halves_of_heads(g, small, 0, head)
            conv_ref[:, at] = conv[0:KERNEL]
            bias_ref[:, at] = conv[KERNEL : KERNEL + 1]
            gate_ref[:, at] = halves_of_heads(g, small, wide_at, head)[0:1]
        conv = small(0, slice(G, head_at))
        for group in range(1, n):
            conv = conv + small(group, slice(G, head_at))
        conv_ref[:, INNER:] = conv[0:KERNEL]
        bias_ref[:, INNER:] = conv[KERNEL : KERNEL + 1]
        norm_ref[...] = jnp.where(first_core, late_ref[0:1, :], late_ref[1:2, :])
        heads = jnp.zeros((8, HEADS), F32)
        skips = jnp.zeros((8, HEADS), F32)
        wide_from = lax.broadcasted_iota(jnp.int32, (G, HEADS), 0)
        wide_to = lax.broadcasted_iota(jnp.int32, (G, HEADS), 1)
        for group in range(n):
            heads = heads + dot(small(group, slice(head_at, wide_at)), picks[group], 1, 0, exact)
            pick = (wide_to == head_of(g, group, wide_from // HEAD_DIM)) & (wide_from < g.chans)
            skips = skips + dot(small(group, slice(wide_at, gain_at)), one_hot(pick), 1, 0, exact)
        dtb_ref[...] = heads[0:1]
        a_ref[...] = heads[1:2]
        skip_ref[...] = skips[1:2]


def layout_call(g, core, gi, gi_sib, go, go_sib, small, late, sec, ig):
    _, n, half, lanes = gi.shape
    out_half = go.shape[2]
    steps = lanes // 128
    out_lanes = D // steps
    rows_spec = pl.BlockSpec(sec.shape[:2] + (out_lanes,), lambda t, c: (0, 0, t))
    PK = small.shape[2]
    columns = 2 * INNER + 2 * STATE + HEADS
    S = jax.ShapeDtypeStruct
    shapes = (
        S((columns, lanes), F32), S((n, 2, out_half, D), F32), S(sec.shape, F32), S(ig.shape, F32), S((1, D), F32), S((KERNEL, CONV), F32),
        S((1, CONV), F32), S((1, HEADS), F32), S((1, HEADS), F32), S((1, HEADS), F32), S((1, INNER), F32),
    )
    return pl.pallas_call(
        lambda core_ref, *refs: layout_kernel(g, *refs),
        grid_spec=pltpu.PrefetchScalarGridSpec(
            num_scalar_prefetch=1,
            grid=(steps,),
            in_specs=[
                pl.BlockSpec((1, n, half, 128), lambda t, c: (c[0], 0, 0, t)),
                pl.BlockSpec((n, half, 128), lambda t, c: (0, 0, t)),
                pl.BlockSpec((1, n, out_half, out_lanes), lambda t, c: (c[0], 0, 0, t)),
                pl.BlockSpec((n, out_half, out_lanes), lambda t, c: (0, 0, t)),
                pl.BlockSpec((n, 8, PK), lambda t, c: (0, 0, 0)),
                pl.BlockSpec((8, D), lambda t, c: (0, 0)),
                rows_spec,
                rows_spec,
            ],
            out_specs=[
                pl.BlockSpec((columns, 128), lambda t, c: (0, t)),
                pl.BlockSpec((n, 2, out_half, out_lanes), lambda t, c: (0, 0, 0, t)),
                rows_spec,
                rows_spec,
            ]
            + [pl.BlockSpec(s.shape, lambda t, c: (0, 0)) for s in shapes[4:]],
        ),
        out_shape=shapes,
        compiler_params=pltpu.CompilerParams(vmem_limit_bytes=SMALL_VMEM),
        name="layout",
    )(core, gi, gi_sib, go, go_sib, small, late, sec, ig)


def local(
    tokens, cotangent, norm_gain, w_in, conv_w, conv_b, dt_bias, a_log, skip_d, gate_gain, w_out
):
    n_seq, n_wt = lax.axis_size(SEQ), lax.axis_size(WT)
    here = lax.axis_index(SEQ)
    group = Group(n_seq, n_wt)
    core = lax.axis_index(SECTION).reshape(1)
    G = group.G

    small = (conv_w[0], conv_b, dt_bias, a_log, skip_d, gate_gain, norm_gain)
    w_src = jnp.swapaxes(w_in[0], 0, 1)
    if group.runs == n_wt:
        o_src = w_out[0]
    else:
        o_src = lax.all_gather(w_out[0], WT, axis=0, tiled=True)
        o_src = lax.dynamic_slice_in_dim(o_src, here * group.chans, group.chans, 0)
        o_src = jnp.pad(o_src, ((0, G - group.chans), (0, 0)))
    fwd = forward_call(group, n_seq, n_wt, tokens, cotangent, small, w_src, o_src)
    bwd = backward_call(group, n_seq, n_wt, fwd, tokens, cotangent)
    g_in, g_out, section_out, input_grad, g_norm, g_conv, g_bias, g_dtb, g_a, g_skip, g_gate = layout_call(
        group, core, bwd.gi, bwd.gi_sib, bwd.go, bwd.go_sib, bwd.small, bwd.late, fwd.sec, bwd.ig
    )
    if group.runs == n_wt:
        g_out = g_out.reshape(INNER // n_wt, D)
    else:
        g_out = g_out.astype(BF).reshape(n_seq, G // n_wt, D)
        g_out = lax.all_gather(g_out, WT, axis=1, tiled=True)[:, : group.chans].reshape(INNER, D)
        mine = INNER // n_wt
        g_out = lax.dynamic_slice_in_dim(g_out, lax.axis_index(WT) * mine, mine, 0).astype(F32)
    return (
        section_out[None, :, None],
        input_grad[None, :, None],
        g_norm,
        jnp.swapaxes(g_in, 0, 1)[None],
        g_conv[None],
        g_bias,
        g_dtb,
        g_a,
        g_skip,
        g_gate,
        g_out[None],
    )


def solution(mesh):
    placed = (
        P(None, WT, SEQ, None),
        P(None, WT, SEQ, None),
        P(SECTION, None),
        P(SECTION, WT, None),
        P(SECTION, None, None),
        P(SECTION, None),
        P(SECTION, None),
        P(SECTION, None),
        P(SECTION, None),
        P(SECTION, None),
        P(SECTION, WT, None),
    )
    return jax.shard_map(
        local,
        mesh=mesh,
        in_specs=placed,
        out_specs=(
            P(SECTION, None, WT, SEQ, None),
            P(SECTION, None, WT, SEQ, None),
            P(SECTION, None),
            P(SECTION, WT, None),
            P(SECTION, None, None),
            P(SECTION, None),
            P(SECTION, None),
            P(SECTION, None),
            P(SECTION, None),
            P(SECTION, None),
            P(SECTION, WT, None),
        ),
        check_vma=False,
    )
```

```python
import functools
from typing import Any, NamedTuple

import jax
import jax.numpy as jnp
from jax import lax
from jax.experimental import pallas as pl
from jax.experimental.pallas import tpu as pltpu
from jax.sharding import PartitionSpec as P

D = 1536
HEADS = 48
HEAD_DIM = 64
STATE = 128
KERNEL = 4
INNER = 3072
CONV = 3328
EPSILON = 1e-05

Q = 128
F32 = jnp.float32
BF = jnp.bfloat16
SEQ, WT, SECTION = "seq", "wt", "section"
FORWARD_VMEM = 56 * 2**20
BACKWARD_VMEM = 62 * 2**20
SMALL_VMEM = 60 * 2**20
MESH = pl.DeviceIdType.MESH
VM = pl.BlockSpec(memory_space=pltpu.VMEM)
ANY = pl.BlockSpec(memory_space=pl.ANY)
TILE = 16


def dot(a, b, ca, cb, precision=None):
    return lax.dot_general(a, b, (((ca,), (cb,)), ((), ())), precision=precision, preferred_element_type=F32)

def sigmoid(x):
    return 1.0 / (1.0 + jnp.exp(-x))

def softplus(x):
    return jnp.maximum(x, 0.0) + jnp.log1p(jnp.exp(-jnp.abs(x)))

def lane_mask(rows):
    return lax.broadcasted_iota(jnp.int32, (rows, 128), 1) < HEAD_DIM

def spread(cols, pair, mask):
    a = jnp.broadcast_to(cols[:, 2 * pair : 2 * pair + 1], mask.shape)
    b = jnp.broadcast_to(cols[:, 2 * pair + 1 : 2 * pair + 2], mask.shape)
    return jnp.where(mask, a, b)

def split_pair(u, mask):
    zero = jnp.zeros_like(u)
    return jnp.concatenate([jnp.where(mask, u, zero), jnp.where(mask, zero, u)], axis=0)

def conv_tile(proj_ref, cw_ref, pad, proj_at, conv_at, rows):
    pad[0:8, :] = jnp.zeros((8, 128), F32)
    pad[8 : 8 + rows, :] = proj_ref[:, pl.ds(proj_at, 128)].astype(F32)
    pre = jnp.broadcast_to(cw_ref[4:5, pl.ds(conv_at, 128)], (rows, 128))
    for k in range(KERNEL):
        pre = pre + cw_ref[k : k + 1, pl.ds(conv_at, 128)] * pad[5 + k : 5 + k + rows, :]
    return pre

def step_inputs(proj_ref, at, hp_ref, sel_ref, dt_at):
    return dot(proj_ref[at, dt_at : dt_at + 128], sel_ref[...], 1, 0) + hp_ref[0:1, :]

def chunk_factors(dt, hp_ref):
    rate = dt * hp_ref[1:2, :]
    rows = lax.broadcasted_iota(jnp.int32, (Q, Q), 0)
    cols = lax.broadcasted_iota(jnp.int32, (Q, Q), 1)
    tri = (rows >= cols).astype(F32)
    cum = dot(tri, rate, 1, 0, lax.Precision.HIGHEST)
    return rate, cum, rows >= cols

def decay_pair(cum, cum_t, causal, pair):
    parts = []
    for h in (2 * pair, 2 * pair + 1):
        diff = jnp.broadcast_to(cum[:, h : h + 1], (Q, Q)) - jnp.broadcast_to(cum_t[h : h + 1, :], (Q, Q))
        parts.append(jnp.exp(jnp.where(causal, diff, -1e30)))
    return jnp.concatenate(parts, axis=1)

def scan_forward(G, proj_ref, cw_ref, hp_ref, gw_ref, sel_ref, mixed_ref, yp_ref, st_ref, pad, xc, dts, state):
    L = proj_ref.shape[0]

    def conv(tile, carry):
        lanes = pl.ds(pl.multiple_of(tile * 128, 128), 128)
        pre = conv_tile(proj_ref, cw_ref, pad, pl.multiple_of(G + tile * 128, 128), lanes.start, L)
        xc[:, lanes] = pre * sigmoid(pre)
        return carry

    lax.fori_loop(0, (G + 2 * STATE) // 128, conv, 0)
    dt_at = 2 * G + 2 * STATE
    dts[...] = softplus(step_inputs(proj_ref, slice(0, L), hp_ref, sel_ref, dt_at))
    state[...] = jnp.zeros_like(state)
    mask = lane_mask(Q)

    def chunk(c, _):
        at = pl.ds(pl.multiple_of(c * Q, Q), Q)
        dt = dts[at, :]
        rate, cum, causal = chunk_factors(dt, hp_ref)
        cum_t = cum.T
        last = cum[Q - 1 : Q, :]
        e_cum = jnp.exp(cum)
        tail = jnp.exp(last - cum) * dt
        e_last = jnp.broadcast_to(jnp.exp(last), (8, 128))
        b = xc[at, G : G + STATE].astype(BF)
        cc = xc[at, G + STATE : G + 2 * STATE].astype(BF)
        scores = dot(cc, b, 1, 1)
        scores2 = jnp.concatenate([scores, scores], axis=1)
        for p in range(G // 128):
            lanes = slice(p * 128, p * 128 + 128)
            x = xc[at, lanes]
            u = (x * spread(dt, p, mask)).astype(BF)
            m = (scores2 * decay_pair(cum, cum_t, causal, p)).astype(BF)
            before = state[:, lanes]
            st_ref[c, :, lanes] = before
            y = dot(m, split_pair(u, mask), 1, 0)
            y = y + dot(cc, before.astype(BF), 1, 0) * spread(e_cum, p, mask)
            yp_ref[at, lanes] = y
            after = dot(b, (x * spread(tail, p, mask)).astype(BF), 0, 0)
            state[:, lanes] = before * spread(e_last, p, mask[0:8])[0:1, :] + after
            mixed_ref[at, lanes] = (y + gw_ref[1:2, lanes] * x).astype(BF)
        return 0

    lax.fori_loop(0, L // Q, chunk, 0)


def gate_forward(G, proj_ref, gw_ref, mixed_ref, vg_ref, ssq_ref):
    def chunk(c, _):
        at = pl.ds(pl.multiple_of(c * Q, Q), Q)
        ssq = jnp.zeros((Q, 1), F32)
        for p in range(G // 128):
            lanes = slice(p * 128, p * 128 + 128)
            gate = proj_ref[at, lanes].astype(F32)
            v = mixed_ref[at, lanes].astype(F32) * (gate * sigmoid(gate))
            vg_ref[at, lanes] = (v * gw_ref[0:1, lanes]).astype(BF)
            ssq = ssq + jnp.sum(v * v, axis=1, keepdims=True)
        ssq_ref[c] = jnp.broadcast_to(ssq, (Q, 128)).T[0:8, :]
        return 0

    lax.fori_loop(0, proj_ref.shape[0] // Q, chunk, 0)


def lane_sums(values, pick):
    high = values.astype(BF)
    low = (values - high.astype(F32)).astype(BF)
    return dot(high, pick, 1, 0) + dot(low, pick, 1, 0)


def gate_backward(G, proj_ref, mixed_ref, dn_ref, sc_ref, gw_ref, dy_ref, gg_ref):
    gg_ref[...] = jnp.zeros_like(gg_ref)

    def chunk(c, _):
        at = pl.ds(pl.multiple_of(c * Q, Q), Q)
        sc = jnp.concatenate([sc_ref[c], jnp.zeros((Q - 8, 128), F32)], axis=0).T
        inv2 = jnp.broadcast_to(sc[:, 0:1], (Q, 128))
        mdot = jnp.broadcast_to(sc[:, 1:2], (Q, 128))
        for p in range(G // 128):
            lanes = slice(p * 128, p * 128 + 128)
            gate = proj_ref[at, lanes].astype(F32)
            sig = sigmoid(gate)
            act = gate * sig
            mixed = mixed_ref[at, lanes].astype(F32)
            n2 = mixed * act * inv2
            mixed_ref[at, lanes] = (n2 * gw_ref[0:1, lanes]).astype(BF)
            dn = dn_ref[at, lanes]
            gg_ref[0:1, lanes] += jnp.sum(dn * n2, axis=0, keepdims=True)
            d_v = inv2 * (dn * gw_ref[0:1, lanes] - n2 * mdot)
            dy_ref[at, lanes] = (d_v * act).astype(BF)
            proj_ref[at, lanes] = (d_v * mixed * (sig * (1.0 + gate * (1.0 - sig)))).astype(BF)
        return 0

    lax.fori_loop(0, proj_ref.shape[0] // Q, chunk, 0)


def scan_backward(G, proj_ref, dy_ref, yp_ref, st_ref, cw_ref, hp_ref, gw_ref, sel_ref, gg_ref, gc_ref, gh_ref,
                  pad, xc, dts, dstate, serve):
    L = proj_ref.shape[0]
    nb = L // Q
    mask = lane_mask(Q)

    def conv(tile, carry):
        lanes = pl.ds(pl.multiple_of(tile * 128, 128), 128)
        pre = conv_tile(proj_ref, cw_ref, pad, pl.multiple_of(G + tile * 128, 128), lanes.start, L)
        xc[:, lanes] = pre * sigmoid(pre)
        return carry

    lax.fori_loop(0, (G + 2 * STATE) // 128, conv, 0)
    dt_at = 2 * G + 2 * STATE
    dts[...] = softplus(step_inputs(proj_ref, slice(0, L), hp_ref, sel_ref, dt_at))
    dstate[...] = jnp.zeros_like(dstate)
    gh_ref[...] = jnp.zeros_like(gh_ref)

    def chunk(step, _):
        c = nb - 1 - step
        pl.when(step == nb // 4)(serve)
        at = pl.ds(pl.multiple_of(c * Q, Q), Q)
        dt = dts[at, :]
        rate, cum, causal = chunk_factors(dt, hp_ref)
        cum_t = cum.T
        last = cum[Q - 1 : Q, :]
        e_cum = jnp.exp(cum)
        tail = jnp.exp(last - cum)
        e_last = jnp.broadcast_to(jnp.exp(last), (8, 128))
        b = xc[at, G : G + STATE].astype(BF)
        cc = xc[at, G + STATE : G + 2 * STATE].astype(BF)
        scores = dot(cc, b, 1, 1)
        scores2 = jnp.concatenate([scores, scores], axis=1)
        d_scores = jnp.zeros((Q, Q), F32)
        d_b = jnp.zeros((Q, STATE), F32)
        d_c = jnp.zeros((Q, STATE), F32)
        d_cum = jnp.zeros((Q, 128), F32)
        d_dt = jnp.zeros((Q, 128), F32)
        d_last = jnp.zeros((8, 128), F32)
        lane_ids = lax.broadcasted_iota(jnp.int32, (Q, 128), 1)
        row_ids = lax.broadcasted_iota(jnp.int32, (Q, 128), 0)
        for p in range(G // 128):
            lanes = slice(p * 128, p * 128 + 128)
            dyb = dy_ref[at, lanes]
            d_y = dyb.astype(F32)
            x = xc[at, lanes]
            dt_x = spread(dt, p, mask)
            u = (x * dt_x).astype(BF)
            u2 = split_pair(u, mask)
            uf = u.astype(F32)
            dec = decay_pair(cum, cum_t, causal, p)
            m = (scores2 * dec).astype(BF)
            dm = dot(dyb, u2, 1, 1) * dec
            d_scores = d_scores + dm[:, :Q] + dm[:, Q:]
            both = dot(m, dyb, 0, 0)
            du = jnp.where(mask, both[:Q], both[Q:])
            tail_x = spread(tail, p, mask)
            before = st_ref[c, :, lanes]
            after = dstate[:, lanes]
            afterb = after.astype(BF)
            du_out = tail_x * dot(b, afterb, 1, 0)
            du = du + du_out
            dye = (d_y * spread(e_cum, p, mask)).astype(BF)
            d_c = d_c + dot(dye, before.astype(BF), 1, 1)
            d_b = d_b + dot((uf * tail_x).astype(BF), afterb, 1, 1)
            e_last_x = spread(e_last, p, mask[0:8])
            dstate[:, lanes] = after * e_last_x[0:1, :] + dot(cc, dye, 0, 0)
            z3 = jnp.sum(uf * du_out, axis=0, keepdims=True) + e_last_x[0:1, :] * jnp.sum(before * after, axis=0, keepdims=True)
            z1 = d_y * yp_ref[at, lanes] - uf * du
            z2 = x * du
            pick = jnp.where(lane_ids == 2 * p + jnp.where(row_ids < HEAD_DIM, 0, 1), 1.0, 0.0).astype(BF)
            d_cum = d_cum + lane_sums(z1, pick)
            d_dt = d_dt + lane_sums(z2, pick)
            d_last = d_last + lane_sums(jnp.broadcast_to(z3, (8, 128)), pick)
            xc[at, lanes] = dt_x * du + gw_ref[1:2, lanes] * d_y
            gg_ref[1:2, lanes] += jnp.sum(d_y * x, axis=0, keepdims=True)
        dsb = d_scores.astype(BF)
        xc[at, G : G + STATE] = d_b + dot(dsb, cc, 0, 0)
        xc[at, G + STATE : G + 2 * STATE] = d_c + dot(dsb, b, 1, 0)
        rows = lax.broadcasted_iota(jnp.int32, (Q, Q), 0)
        cols = lax.broadcasted_iota(jnp.int32, (Q, Q), 1)
        upper = (rows <= cols).astype(F32)
        d_rate = dot(upper, d_cum, 1, 0, lax.Precision.HIGHEST) + d_last[0:1, :]
        d_step = d_dt + d_rate * hp_ref[1:2, :]
        d_raw = d_step * sigmoid(step_inputs(proj_ref, at, hp_ref, sel_ref, dt_at))
        proj_ref[at, dt_at : dt_at + 128] = dot(d_raw.astype(BF), sel_ref[...], 1, 1).astype(BF)
        gh_ref[:, 0:128] += jnp.sum(d_raw, axis=0, keepdims=True)
        gh_ref[:, 128:256] += jnp.sum(d_rate * rate, axis=0, keepdims=True)
        return 0

    lax.fori_loop(0, nb, chunk, 0)

    gc_ref[...] = jnp.zeros_like(gc_ref)

    def conv_back(tile, carry):
        lanes = pl.ds(pl.multiple_of(tile * 128, 128), 128)
        proj_at = pl.multiple_of(G + tile * 128, 128)
        pre = conv_tile(proj_ref, cw_ref, pad, proj_at, lanes.start, L)
        sig = sigmoid(pre)
        d_pre = xc[:, lanes] * (sig * (1.0 + pre * (1.0 - sig)))
        for k in range(KERNEL):
            gc_ref[k : k + 1, lanes] = jnp.sum(d_pre * pad[5 + k : 5 + k + L, :], axis=0, keepdims=True)
        gc_ref[4:5, lanes] = jnp.sum(d_pre, axis=0, keepdims=True)
        pad[0:L, :] = d_pre
        pad[L : L + 8, :] = jnp.zeros((8, 128), F32)
        d_in = cw_ref[3:4, lanes] * d_pre
        for k in range(KERNEL - 1):
            d_in = d_in + cw_ref[k : k + 1, lanes] * pad[3 - k : 3 - k + L, :]
        proj_ref[:, pl.ds(proj_at, 128)] = d_in.astype(BF)
        return carry

    lax.fori_loop(0, (G + 2 * STATE) // 128, conv_back, 0)


def column(row):
    return jnp.broadcast_to(row, (128, 128)).T


def rows_loop(rows, body):
    def step(r, carry):
        body(pl.ds(pl.multiple_of(r * TILE, TILE), TILE))
        return carry

    lax.fori_loop(0, rows // TILE, step, 0)


class Group:
    def __init__(self, n_seq, n_wt):
        self.n_seq = n_seq
        self.heads = HEADS // n_seq
        self.runs = n_wt if HEADS % (n_seq * n_wt) == 0 else 1
        self.run_heads = self.heads // self.runs
        self.chans = self.heads * HEAD_DIM
        self.G = -(-self.chans // 128) * 128
        self.CX = self.G + 2 * STATE
        self.NC = 2 * self.G + 2 * STATE + 128
        self.rest = self.G + 2 * STATE + 64
        self.half = (self.G + self.rest) // 2
        self.cut = self.rest // 128 * 64


def head_of(g, here, local_head):
    stride = HEADS // g.runs
    run = local_head // g.run_heads
    return run * stride + here * g.run_heads + (local_head - run * g.run_heads)


def one_hot(found):
    return jnp.where(found, 1.0, 0.0)


def step_select(g, here):
    from_ids = lax.broadcasted_iota(jnp.int32, (128, 128), 0)
    to_ids = lax.broadcasted_iota(jnp.int32, (128, 128), 1)
    return one_hot((from_ids == head_of(g, here, to_ids)) & (to_ids < g.heads))


OUT, GATE, REST, LAST = KINDS = range(4)


class Wire:
    def __init__(self, send_sems, recv_sems):
        self.send_sems, self.recv_sems, self.used = send_sems, recv_sems, 0

    def reserve(self):
        self.used += 1
        return self.used - 1

    def make(self, src, dst, axis, peer, at_send, at_recv):
        return pltpu.make_async_remote_copy(
            src, dst, self.send_sems.at[at_send], self.recv_sems.at[at_recv],
            device_id={axis: peer}, device_id_type=MESH,
        )

    def put(self, src, dst, axis, peer):
        at = self.reserve()
        copy = self.make(src, dst, axis, peer, at, at)
        copy.start()
        return copy


class Maybe:
    def __init__(self, condition, copy):
        self.condition, self.copy = condition, copy

    def start(self):
        pl.when(self.condition)(self.copy.start)
        return self

    def wait_send(self):
        pl.when(self.condition)(self.copy.wait_send)


class PlaneGather:
    def __init__(self, put, n, here, source, block):
        self.put, self.block, self.plane = put, block, n == 4
        mine = block(here, None)
        if not self.plane:
            self.copies = [put(source, mine, SEQ, lax.rem(here + k, n)) for k in range(1, n)]
            return
        self.x = here + 1 - 2 * lax.rem(here, 2)
        self.y = lax.rem(here + 2, 4)
        self.copies = [put(source, mine, SEQ, self.x), put(source, mine, SEQ, self.y)]

    def forward(self, landed=None):
        if self.plane:
            for copy, group, half, peer in (
                (self.copies[0], self.x, 0, self.y),
                (self.copies[1], self.y, 1, self.x),
            ):
                copy.wait_recv()
                part = self.block(group, half)
                self.copies.append(self.put(part, part, SEQ, peer))
                if landed is not None:
                    landed(group)

    def wait_recv(self):
        for copy in self.copies[2:] if self.plane else self.copies:
            copy.wait_recv()

    def wait_send(self):
        for copy in self.copies:
            copy.wait_send()


class PlaneSum:
    def __init__(self, put, n, here, part, got, mid):
        self.put, self.n, self.here, self.part, self.got, self.mid = put, n, here, part, got, mid
        self.plane = n == 4
        self.half = part.shape[1] // 2
        self.peers = [lax.rem(here + k, n) for k in range(1, n)]
        if self.plane:
            self.x = here + 1 - 2 * lax.rem(here, 2)
            self.y = lax.rem(here + 2, 4)
            self.peers = [lax.rem(self.x + 2, 4), self.y, self.x]

    def start(self, product, stat=None, got_stat=None):
        half, part, got = self.half, self.part, self.got
        self.copies = []
        product()
        for k, peer in enumerate(self.peers):
            if not self.plane:
                self.copies.append(self.put(part.at[peer], got.at[k], SEQ, peer))
            elif k == 0:
                self.mids = [
                    self.put(part.at[peer, 0:half], self.mid.at[0], SEQ, self.x),
                    self.put(part.at[peer, half:], self.mid.at[1], SEQ, self.y),
                ]
            elif k == 1:
                self.copies.append(self.put(part.at[peer, half:], got.at[1, half:], SEQ, peer))
            else:
                self.copies.append(self.put(part.at[peer, 0:half], got.at[0, 0:half], SEQ, peer))
            if stat is not None:
                self.copies.append(self.put(stat.at[peer], got_stat.at[k], SEQ, peer))

    def middle(self):
        if not self.plane:
            return
        half, part = self.half, self.part
        for copy in self.mids:
            copy.wait()

        def add(at):
            late = pl.ds(pl.multiple_of(at.start + half, TILE), TILE)
            for peer, rows, slot in ((self.y, at, 0), (self.x, late, 1)):
                total = part[peer, rows, :].astype(F32) + self.mid[slot, at, :].astype(F32)
                part[peer, rows, :] = total.astype(BF)

        rows_loop(half, add)
        self.copies += [
            self.put(part.at[self.y, 0:half], self.got.at[1, 0:half], SEQ, self.y),
            self.put(part.at[self.x, half:], self.got.at[0, half:], SEQ, self.x),
        ]

    def end(self):
        for copy in self.copies:
            copy.wait()

    def total(self, at):
        total = self.part[self.here, at, :].astype(F32)
        for k in range(2 if self.plane else self.n - 1):
            total = total + self.got[k, at, :].astype(F32)
        return total


class Mover:
    def __init__(self, sems):
        self.sems, self.used = sems, 0

    def put(self, src, dst):
        copy = pltpu.make_async_copy(src, dst, self.sems.at[self.used])
        copy.start()
        self.used += 1
        return copy


def meet_all(axes):
    barrier = pltpu.get_barrier_semaphore()
    count = 0
    for axis, n in axes:
        me = lax.axis_index(axis)
        for k in range(1, n):
            pl.semaphore_signal(
                barrier, inc=1, device_id={axis: lax.rem(me + k, n)}, device_id_type=MESH
            )
        count += n - 1
    pl.semaphore_wait(barrier, count)


def column_tiles(first, last, body):
    whole = (last - first) // 256

    def step(t, carry):
        body(pl.ds(pl.multiple_of(first + t * 256, 128), 256))
        return carry

    lax.fori_loop(0, whole, step, 0)
    if first + whole * 256 < last:
        body(slice(first + whole * 256, last))


def four_blocks(part, product):
    count, rows, columns = part.shape

    def step(q, carry):
        at = pl.ds(pl.multiple_of(q * 4 * rows, TILE), 4 * rows)

        def tile(lanes):
            value = product(at, lanes).astype(BF)
            for b in range(4):
                part[q * 4 + b, :, lanes] = value[b * rows : (b + 1) * rows]

        column_tiles(0, columns, tile)
        return carry

    lax.fori_loop(0, count // 4, step, 0)


class ForwardOuts(NamedTuple):
    sec: Any
    pout: Any
    stat0: Any
    h1: Any
    gb_o: Any
    stats: Any
    packs_o: Any
    wf_o: Any
    of_o: Any
    n_o: Any
    proj_o: Any
    mixed_o: Any
    yp_o: Any
    st_o: Any


class ForwardRefs(NamedTuple):
    tokens: Any
    cotangent: Any
    conv_w: Any
    conv_b: Any
    dt_bias: Any
    a_log: Any
    skip_d: Any
    gate_gain: Any
    norm_gain: Any
    w_src: Any
    o_src: Any
    sec: Any
    pout: Any
    stat0: Any
    h1: Any
    gb_o: Any
    stats: Any
    packs_o: Any
    wf_o: Any
    of_o: Any
    n_o: Any
    proj_o: Any
    mixed_o: Any
    yp_o: Any
    st_o: Any
    h0: Any
    cot: Any
    packs: Any
    wf: Any
    of: Any
    normed: Any
    proj: Any
    mixed: Any
    yp: Any
    st: Any
    pad: Any
    xc: Any
    dts: Any
    state: Any
    vg: Any
    ssq: Any
    part: Any
    got: Any
    got_stat: Any
    hbuf: Any
    own_stat: Any
    cols: Any
    mdots: Any
    sel: Any
    pack: Any
    mid: Any
    ss: Any
    rs: Any
    ls: Any


def forward_kernel(g, n, w, rows, *refs):
    r = ForwardRefs(*refs)
    G, NC = g.G, g.NC
    core, here, shard = lax.axis_index(SECTION), lax.axis_index(SEQ), lax.axis_index(WT)
    sibling = 1 - core
    wire, mover = Wire(r.ss, r.rs), Mover(r.ls)
    wf, of, packs = r.wf, r.of, r.packs
    sends, saves = [], []

    def aligned(at, size):
        return pl.ds(pl.multiple_of(at, 16), size)

    def put(src, dst, axis, peer):
        copy = wire.put(src, dst, axis, peer)
        sends.append(copy)
        return copy

    for layer in range(2):
        for first, last in ((g.chans, G), (G + g.chans, 2 * G), (2 * G + 2 * STATE + HEADS, NC)):
            if first < last:
                wf[layer, first:last, :] = jnp.zeros((last - first, D), BF)
    meet_all(((SEQ, n), (WT, w), (SECTION, 2)))
    o_rows = G // w
    lanes_of = D // w
    mine_o = aligned(shard * o_rows, o_rows)
    piece = here if g.runs == w else shard
    o_own = r.o_src.at[aligned(piece * o_rows, o_rows)]
    mine_lanes = pl.ds(pl.multiple_of(shard * lanes_of, 128), lanes_of)
    width = g.run_heads * HEAD_DIM
    runs = []
    for kind_at, source_at in ((0, 0), (G, INNER)):
        for run in range(g.runs):
            source = source_at + run * (INNER // g.runs) + here * width
            runs.append((source, kind_at + run * width, width))
    runs.append((2 * INNER, 2 * G, 2 * STATE))
    runs.append((2 * INNER + 2 * STATE, 2 * G + 2 * STATE, HEADS))
    siblings, locals_ = [], []
    for source, target, size in runs:
        taken = r.w_src.at[aligned(source, size)]
        siblings.append(put(taken, wf.at[core, target : target + size, mine_lanes], SECTION, sibling))
        locals_.append(mover.put(taken, wf.at[core, target : target + size, mine_lanes]))
    others = [put(o_own, of.at[core, mine_o], SECTION, sibling)]
    locals_later = [
        mover.put(o_own, of.at[core, mine_o]),
        mover.put(r.tokens.at[core, 0], r.h0),
        mover.put(r.cotangent.at[core, 0], r.cot),
    ]

    def part_of(layer, kind, at_shard, at_core):
        if kind == OUT:
            return of.at[layer, aligned(at_shard * o_rows + at_core * (o_rows // 2), o_rows // 2)]
        size = (G if kind == GATE else g.rest) // 2
        first = (0 if kind == GATE else G) + at_core * size
        lanes = pl.ds(pl.multiple_of(at_shard * lanes_of, 128), lanes_of)
        return wf.at[layer, aligned(first, size), lanes]

    line = w == 4

    def fetch(layer, kind):
        mine = part_of(layer, kind, shard, core)
        at = [wire.reserve() for _ in range(w)]
        copies = [
            wire.make(mine, mine, WT, lax.rem(shard + k, w), at[k], at[k]) for k in range(1, w)
        ]
        if line:
            copies[1].start()
            sends.append(copies[1])
            sends.append(Maybe(shard != w - 1, copies[0]).start())
            sends.append(Maybe(shard != 0, copies[2]).start())
        else:
            for copy in copies:
                copy.start()
            sends.extend(copies)
        return copies, at

    def far_part(fetched, layer, kind):
        if not line:
            return []
        at = fetched[1]
        fetched[0][1].wait_recv()
        block = part_of(layer, kind, lax.rem(shard + 2, w), core)
        up = wire.make(block, block, WT, lax.rem(shard + 1, w), at[0], at[3])
        down = wire.make(block, block, WT, lax.rem(shard + w - 1, w), at[0], at[1])
        sends.append(Maybe(shard == 2, up).start())
        sends.append(Maybe(shard == 1, down).start())
        return [put(block, block, SECTION, sibling)]

    def near_parts(fetched, layer, kind):
        found = []
        for k in (1, 3) if line else range(1, w):
            fetched[0][k - 1].wait_recv()
            block = part_of(layer, kind, lax.rem(shard + w - k, w), core)
            found.append(put(block, block, SECTION, sibling))
        return found

    def received(copies):
        for copy in copies:
            copy.wait_recv()

    own_rows = aligned(here * rows, rows)

    def gather(whole):
        def block(group, half):
            size = rows if half is None else rows // 2
            return whole.at[aligned(group * rows + (half or 0) * size, size)]

        return PlaneGather(wire.put, n, here, block(here, None), block)

    def save(source, target):
        saves.append(mover.put(source, target))

    def saved():
        while saves:
            saves.pop().wait()

    for copy in locals_:
        copy.wait()
    received(siblings)
    pending = fetch(0, REST)
    gain_at = g.CX + 128 + G
    r.sel[...] = step_select(g, here).astype(BF)
    pack_small(g, here, r.conv_w, r.conv_b, r.dt_bias, r.a_log, r.skip_d, r.gate_gain, r.norm_gain, r.pack)
    others.append(put(r.pack, packs.at[core], SECTION, sibling))
    locals_later.append(mover.put(r.pack, packs.at[core]))
    for copy in locals_later:
        copy.wait()
    received(others)

    def norm(at):
        h = r.h0[at, :]
        inv = lax.rsqrt(jnp.mean(h * h, axis=1, keepdims=True) + EPSILON)
        r.normed[pl.ds(pl.multiple_of(here * rows + at.start, TILE), TILE), :] = (
            h * inv * packs[0, 0:1, gain_at:]
        ).astype(BF)

    rows_loop(rows, norm)
    arriving = gather(r.normed)
    handed = far_part(pending, 0, REST)
    coming = [fetch(0, GATE), fetch(0, OUT)]
    arriving.forward()
    handed += near_parts(pending, 0, REST)

    for layer in range(2):
        proj, mixed, normed = r.proj, r.mixed, r.normed
        conv = packs.at[layer, :, 0 : g.CX]
        head = packs.at[layer, :, g.CX : g.CX + 128]
        wide = packs.at[layer, :, g.CX + 128 : gain_at]

        def project(lanes):
            proj[:, lanes] = dot(normed[...], wf[layer, lanes, :], 1, 1).astype(BF)

        arriving.wait_recv()
        received(handed)
        gathered = arriving
        column_tiles(G, NC, project)
        scan_forward(
            G, proj, conv, head, wide, r.sel, mixed, r.yp, r.st,
            r.pad, r.xc, r.dts, r.state,
        )
        save(mixed, r.mixed_o.at[layer])
        save(r.yp, r.yp_o.at[layer])
        save(r.st, r.st_o.at[layer])
        save(normed, r.n_o.at[layer])
        handed = far_part(coming[0], layer, GATE) + far_part(coming[1], layer, OUT)
        handed += near_parts(coming[0], layer, GATE) + near_parts(coming[1], layer, OUT)
        if layer == 0:
            pending = fetch(1, REST)
        received(handed)
        column_tiles(0, G, project)
        save(proj, r.proj_o.at[layer])
        gate_forward(G, proj, wide, mixed, r.vg, r.ssq)

        def out_product():
            four_blocks(r.part, lambda at, lanes: dot(r.vg[at, :], of[layer, :, lanes], 1, 0))

        saved()
        gathered.wait_send()
        summing = PlaneSum(wire.put, n, here, r.part, r.got, r.mid)
        summing.start(out_product, r.ssq, r.got_stat)
        summing.middle()
        summing.end()
        if layer == 0:
            handed = far_part(pending, 1, REST)
            coming = [fetch(1, GATE), fetch(1, OUT)]
        ssq = r.ssq[here]
        for k in range(n - 1):
            ssq = ssq + r.got_stat[k]
        inv2 = lax.rsqrt(ssq * (1.0 / INNER) + EPSILON)
        r.own_stat[...] = inv2
        r.cols[...] = column(inv2[0:1, :])
        if layer == 0:
            r.stat0[...] = inv2

        def finish(at):
            pout = summing.total(at) * r.cols[at, 0:1]
            whole = pl.ds(pl.multiple_of(here * rows + at.start, TILE), TILE)
            h_in = r.h0[at, :] if layer == 0 else r.hbuf[0, at, :]
            h = h_in + pout
            r.hbuf[layer, at, :] = h
            if layer == 0:
                r.pout[at, :] = pout
                r.h1[at, :] = h
                inv = lax.rsqrt(jnp.mean(h * h, axis=1, keepdims=True) + EPSILON)
                r.normed[whole, :] = (h * inv * packs[1, 0:1, gain_at:]).astype(BF)
            else:
                out = r.cot[at, :].astype(BF)
                dots = jnp.sum(out.astype(F32) * pout, axis=1, keepdims=True)
                r.mdots[at, :] = jnp.broadcast_to(dots * (1.0 / INNER), (TILE, 128))
                r.normed[whole, :] = out

        rows_loop(rows, finish)
        if layer == 0:
            arriving = gather(r.normed)
            arriving.forward()
            handed += near_parts(pending, 1, REST)
    r.stats[here] = r.own_stat[...]
    r.stats[here, 1:2, :] = r.mdots[...].T[0:1, :]
    last_rows = gather(r.normed)
    arriving = []
    for k in range(1, n):
        block = r.stats.at[here]
        arriving.append(put(block, block, SEQ, lax.rem(here + k, n)))
    arriving.append(put(r.hbuf.at[1 - core], r.sec.at[core], SECTION, sibling))
    save(r.hbuf.at[core], r.sec.at[core])
    save(packs, r.packs_o)
    save(wf, r.wf_o)
    save(of, r.of_o)
    last_rows.forward()
    last_rows.wait_recv()
    received(arriving)
    save(r.normed, r.gb_o)
    last_rows.wait_send()
    assert wire.used <= r.ss.shape[0] and mover.used <= r.ls.shape[0]
    for copy in sends:
        copy.wait_send()
    saved()


def forward_call(g, n, w, tokens, cotangent, small, w_src, o_src):
    rows = tokens.shape[2]
    L, G, NC, CX, PK = rows * n, g.G, g.NC, g.CX, g.CX + 128 + g.G + D
    S = jax.ShapeDtypeStruct
    shapes = ForwardOuts(
        sec=S((2, rows, D), F32),
        pout=S((rows, D), F32),
        stat0=S((8, 128), F32),
        h1=S((rows, D), F32),
        gb_o=S((L, D), BF),
        stats=S((n, 8, 128), F32),
        packs_o=S((2, 8, PK), F32),
        wf_o=S((2, NC, D), BF),
        of_o=S((2, G, D), BF),
        n_o=S((2, L, D), BF),
        proj_o=S((2, L, NC), BF),
        mixed_o=S((2, L, G), BF),
        yp_o=S((2, L, G), F32),
        st_o=S((2, L // Q, STATE, G), F32),
    )
    scratch = [
        S((rows, D), F32), S((rows, D), F32), shapes.packs_o, shapes.wf_o, shapes.of_o, S((L, D), BF), S((L, NC), BF), S((L, G), BF),
        S((L, G), F32), S((L // Q, STATE, G), F32), S((8 + L, 128), F32), S((L, CX), F32), S((L, 128), F32), S((STATE, G), F32),
        S((L, G), BF), S((n, 8, 128), F32), S((n, rows, D), BF), S((n - 1, rows, D), BF), S((n - 1, 8, 128), F32),
        S((2, rows, D), F32), S((8, 128), F32), S((rows, 128), F32), S((rows, 128), F32),
        S((128, 128), BF), S((8, PK), F32), S((2, rows // 2, D), BF),
    ]
    remote = 4 + 2 * g.runs + 6 * w + 6 * (w - 1) + 24 + 8 * (n - 1)
    outs = pl.pallas_call(
        functools.partial(forward_kernel, g, n, w, rows),
        out_shape=list(shapes),
        in_specs=[ANY, ANY] + [VM] * len(small) + [ANY, ANY],
        out_specs=[VM] * 4 + [ANY, VM] + [ANY] * 8,
        scratch_shapes=[pltpu.VMEM(s.shape, s.dtype) for s in scratch]
        + [
            pltpu.SemaphoreType.DMA((remote,)),
            pltpu.SemaphoreType.DMA((remote,)),
            pltpu.SemaphoreType.DMA((22 + 2 * g.runs,)),
        ],
        compiler_params=pltpu.CompilerParams(
            collective_id=0, has_side_effects=True, vmem_limit_bytes=FORWARD_VMEM
        ),
        name="forward",
    )(tokens, cotangent, *small, w_src, o_src)
    return ForwardOuts(*outs)


class BackwardOuts(NamedTuple):
    ig: Any
    gi: Any
    go: Any
    gi_sib: Any
    go_sib: Any
    small: Any
    far: Any
    late: Any


class BackwardRefs(NamedTuple):
    packs_i: Any
    wf_i: Any
    of_i: Any
    n_i: Any
    proj_i: Any
    mixed_i: Any
    yp_i: Any
    st_i: Any
    gb_i: Any
    stats1_i: Any
    stat0_i: Any
    pout_i: Any
    h1_i: Any
    tokens_i: Any
    cotangent_i: Any
    ig: Any
    gi: Any
    go: Any
    gi_sib: Any
    go_sib: Any
    small: Any
    far: Any
    late: Any
    packs: Any
    wf: Any
    of: Any
    n: Any
    proj: Any
    mixed: Any
    yp: Any
    st: Any
    gb: Any
    stats: Any
    pout: Any
    h1: Any
    h0: Any
    cot: Any
    dy: Any
    pad: Any
    xc: Any
    dts: Any
    dstate: Any
    part: Any
    got: Any
    own_stat: Any
    mdots: Any
    grads: Any
    gw: Any
    gout: Any
    sib_w: Any
    sib_o: Any
    z_w: Any
    z_o: Any
    relay_w: Any
    relay_o: Any
    sm: Any
    sm_sib: Any
    sm_z: Any
    sm_own: Any
    sel: Any
    gain: Any
    gain_z: Any
    gain_sum: Any
    mid: Any
    ss: Any
    rs: Any
    ls: Any
    free: Any


def backward_kernel(g, n, w, rows, *refs):
    r = BackwardRefs(*refs)
    G, NC, CX = g.G, g.NC, g.CX
    core, here, shard = lax.axis_index(SECTION), lax.axis_index(SEQ), lax.axis_index(WT)
    sibling = 1 - core
    wire, mover = Wire(r.ss, r.rs), Mover(r.ls)
    o_half, lanes_of = G // (2 * w), D // w
    gain_at = CX + 128 + G

    def aligned(at, size):
        return pl.ds(pl.multiple_of(at, 16), size)

    def load(layer, *pairs):
        return [mover.put(source.at[layer], target) for source, target in pairs]

    first = load(1, (r.of_i, r.of), (r.proj_i, r.proj), (r.mixed_i, r.mixed))
    first += [mover.put(r.packs_i, r.packs), mover.put(r.gb_i, r.gb), mover.put(r.stats1_i, r.stats)]
    later = load(1, (r.n_i, r.n), (r.yp_i, r.yp), (r.st_i, r.st), (r.wf_i, r.wf))
    later += [mover.put(r.pout_i, r.pout), mover.put(r.h1_i, r.h1), mover.put(r.stat0_i, r.own_stat)]
    later += [mover.put(r.tokens_i.at[core, 0], r.h0), mover.put(r.cotangent_i.at[core, 0], r.cot)]
    meet_all(((SEQ, n), (WT, w), (SECTION, 2)))
    r.sm[...] = jnp.zeros_like(r.sm)
    r.sel[...] = step_select(g, here).astype(BF)
    r.gain[here] = jnp.zeros((8, D // 4), F32)
    open_sends, record = [], {}
    line = w == 4
    arrivals = r.got if r.got.shape[0] == n - 1 else r.far

    def put(src, dst, axis, peer):
        copy = wire.put(src, dst, axis, peer)
        open_sends.append(copy)
        return copy

    def rows_of(kind):
        return ((0, G), (0, G), (G, g.cut), (G + g.cut, g.rest - g.cut))[kind]

    def kept(kind):
        middle = (G + g.cut) // 2
        return (slice(0, G // (2 * w)), slice(0, G // 2), slice(G // 2, middle), slice(middle, g.half))[kind]

    def buffers(kind):
        if kind == OUT:
            return r.gout, r.sib_o, r.z_o, r.go, r.go_sib
        return r.gw, r.sib_w, r.z_w, r.gi, r.gi_sib

    def block_of(kind, at_shard, at_core):
        if kind == OUT:
            return aligned((2 * at_shard + at_core) * o_half, o_half), slice(0, D)
        first, size = rows_of(kind)
        return (
            aligned(first + at_core * (size // 2), size // 2),
            pl.ds(pl.multiple_of(at_shard * lanes_of, 128), lanes_of),
        )

    def ready(kind):
        for copy in record.pop(kind, ()):
            copy.wait_send()

    def to_sibling(layer, kind):
        grad, sib, _, _, _ = buffers(kind)
        if layer == 0:
            pl.semaphore_wait(r.free.at[kind], 1)
        if kind == OUT:
            pairs = [
                (grad.at[block_of(kind, q, sibling)], sib.at[aligned(q * o_half, o_half)])
                for q in range(w)
            ]
        else:
            first, size = rows_of(kind)
            rows_there = aligned(first + sibling * (size // 2), size // 2)
            pairs = [(grad.at[rows_there], sib.at[kept(kind)])]
        copies = [wire.put(source, target, SECTION, sibling) for source, target in pairs]
        record[kind] = list(copies)
        return copies

    def to_shards(layer, kind, copies):
        grad, sib, z, _, _ = buffers(kind)
        for copy in copies:
            copy.wait_recv()
        if kind == OUT:
            per = o_half // TILE

            def places(t):
                q = t // per
                return (2 * q + core) * o_half + (t - q * per) * TILE, t * TILE

            steps = w * per
        else:
            first, size = rows_of(kind)
            steps = size // 2 // TILE

            def places(t):
                return first + core * (size // 2) + t * TILE, kept(kind).start + t * TILE

        def add(t, carry):
            mine, theirs = (pl.ds(pl.multiple_of(at, TILE), TILE) for at in places(t))
            grad[mine, :] = (grad[mine, :].astype(F32) + sib[theirs, :].astype(F32)).astype(BF)
            return carry

        lax.fori_loop(0, steps, add, 0)
        if layer == 1:
            pl.semaphore_signal(
                r.free.at[kind], inc=1, device_id={SECTION: sibling}, device_id_type=MESH
            )
        at = [wire.reserve() for _ in range(w)]
        found = []
        for k in range(1, w):
            peer = lax.rem(shard + k, w)
            source = grad.at[block_of(kind, peer, core)]
            found.append(wire.make(source, z.at[layer, k - 1, kept(kind)], WT, peer, at[k], at[k]))
        if not line:
            for copy in found:
                copy.start()
            record[kind] += found
            return found, None
        buffer = (r.relay_o if kind == OUT else r.relay_w).at[layer, kept(kind)]
        up = wire.make(grad.at[block_of(kind, w - 1, core)], buffer, WT, 1, at[0], at[0])
        down = wire.make(grad.at[block_of(kind, 0, core)], buffer, WT, w - 2, at[0], at[0])
        inner = (shard == 1) | (shard == 2)
        first = [
            Maybe(shard == 0, up),
            Maybe(shard == w - 1, down),
            Maybe(inner, found[0]),
            Maybe(inner, found[2]),
        ]
        others = [
            Maybe(jnp.logical_not(inner), found[1]),
            Maybe(shard == 0, found[0]),
            Maybe(shard == w - 1, found[2]),
        ]
        record[kind] += [*first, *others, Maybe(inner, found[1])]
        for copy in first:
            copy.start()
        waiting.extend(others)
        arriving = wire.make(buffer, buffer, WT, lax.rem(shard + 1, w), at[0], at[0])
        return found, arriving

    def relay(layer, kind, moving):
        found, arriving = moving
        if not line:
            return
        grad, buffer = (r.gout, r.relay_o) if kind == OUT else (r.gw, r.relay_w)
        rows_here = kept(kind)

        @pl.when((shard == 1) | (shard == 2))
        def _():
            arriving.wait_recv()
            at_rows, at_lanes = block_of(kind, lax.rem(shard + 2, w), core)

            def add(at):
                mine = pl.ds(pl.multiple_of(at_rows.start + at.start, TILE), TILE)
                there = pl.ds(pl.multiple_of(rows_here.start + at.start, TILE), TILE)
                total = grad[mine, at_lanes].astype(F32) + buffer[layer, there, :].astype(F32)
                grad[mine, at_lanes] = total.astype(BF)

            rows_loop(rows_here.stop - rows_here.start, add)
            found[1].start()

    def to_plane(layer, kind, moving):
        grad, _, z, result, _ = buffers(kind)
        copies, _ = moving
        if line:
            pl.when(shard != 0)(copies[0].wait_recv)
            copies[1].wait_recv()
            pl.when(shard != w - 1)(copies[2].wait_recv)
        else:
            for copy in copies:
                copy.wait_recv()
        at_rows, at_lanes = block_of(kind, shard, core)
        here_rows = kept(kind)

        def add(at):
            mine = pl.ds(pl.multiple_of(at_rows.start + at.start, TILE), TILE)
            there = pl.ds(pl.multiple_of(here_rows.start + at.start, TILE), TILE)
            total = grad[mine, at_lanes].astype(F32)
            for k in range(w - 1):
                total = total + z[layer, k, there, :].astype(F32)
            z[layer, 1, there, :] = total.astype(BF)

        def add_end(at, near):
            mine = pl.ds(pl.multiple_of(at_rows.start + at.start, TILE), TILE)
            there = pl.ds(pl.multiple_of(here_rows.start + at.start, TILE), TILE)
            total = grad[mine, at_lanes].astype(F32)
            total = total + z[layer, 1, there, :].astype(F32) + z[layer, near, there, :].astype(F32)
            z[layer, 1, there, :] = total.astype(BF)

        count = here_rows.stop - here_rows.start
        if line:

            @pl.when(shard == 0)
            def _():
                rows_loop(count, lambda at: add_end(at, 2))

            @pl.when(shard == w - 1)
            def _():
                rows_loop(count, lambda at: add_end(at, 0))

            @pl.when((shard == 1) | (shard == 2))
            def _():
                rows_loop(count, add)
        else:
            rows_loop(count, add)
        def target(group, half):
            size = here_rows.stop - here_rows.start
            if half is None:
                return result.at[layer, group, here_rows]
            first = here_rows.start + half * (size // 2)
            return result.at[layer, group, first : first + size // 2]

        block = z.at[layer, 1, here_rows]
        return PlaneGather(put, n, here, block, target), mover.put(block, target(here, None))

    def landed(kind, *arrivals):
        _, _, _, result, target = buffers(kind)
        for found, own in arrivals:
            found.wait_recv()
            own.wait()
        return put(result.at[sibling, :, kept(kind)], target.at[:, kept(kind)], SECTION, sibling)

    def done(copies):
        for copy in copies:
            copy.wait()

    arrived, waiting = {}, []
    for layer in (1, 0):
        conv = r.packs.at[layer, :, 0:CX]
        head = r.packs.at[layer, :, CX : CX + 128]
        wide = r.packs.at[layer, :, CX + 128 : gain_at]
        g_conv = r.sm.at[layer, 0:5, :]
        g_head = r.sm.at[layer, 7:8, 0:256]
        g_wide = r.sm.at[layer, 5:7, 0:G]
        done(first)

        def d_normed(lanes):
            r.xc[:, lanes] = dot(r.gb[...], r.of[lanes, :], 1, 1)

        column_tiles(0, G, d_normed)
        gate_backward(
            G, r.proj, r.mixed, r.xc, r.stats, wide, r.dy, g_wide
        )

        def out_rows(at):
            r.gout[at, :] = dot(r.mixed[:, at], r.gb[...], 0, 0).astype(BF)

        def in_rows(at):
            r.gw[at, :] = dot(r.proj[:, at], r.n[...], 0, 0).astype(BF)

        ready(OUT)
        column_tiles(0, G, out_rows)
        out_sib = to_sibling(layer, OUT)
        done(later)
        ready(GATE)
        column_tiles(0, G, in_rows)
        gate_sib = to_sibling(layer, GATE)
        out_z = to_shards(layer, OUT, out_sib)
        gate_z = to_shards(layer, GATE, gate_sib)
        if layer == 0:
            arrived[1, OUT][0].forward()
            arrived[1, GATE][0].forward()
            arrived[1, REST] = to_plane(1, REST, rest_z[0])
            arrived[1, LAST] = to_plane(1, LAST, rest_z[1])

        def serve():
            for copy in waiting:
                copy.start()

        scan_backward(
            G, r.proj, r.dy, r.yp, r.st, conv, head, wide, r.sel, g_wide, g_conv, g_head,
            r.pad, r.xc, r.dts, r.dstate, serve,
        )
        waiting.clear()
        relay(layer, OUT, out_z)
        relay(layer, GATE, gate_z)
        if layer == 0:
            small_sib = put(r.sm.at[sibling], r.sm_sib, SECTION, sibling)
        if layer == 0:
            arrived[1, REST][0].forward()
            arrived[1, LAST][0].forward()
            small_sib.wait_recv()
            r.sm_own[...] = r.sm[core] + r.sm_sib[...]
            small_z = [
                put(r.sm_own, r.sm_z.at[k - 1], WT, lax.rem(shard + k, w)) for k in range(1, w)
            ]
        if layer == 1:
            first = load(0, (r.of_i, r.of), (r.mixed_i, r.mixed))
            later = load(0, (r.yp_i, r.yp), (r.st_i, r.st))

        def in_product():
            four_blocks(r.part, lambda at, lanes: dot(r.proj[at, :], r.wf[:, lanes], 1, 0))

        summing = PlaneSum(wire.put, n, here, r.part, arrivals, r.mid)

        def rest_gradient():
            ready(REST)
            ready(LAST)
            column_tiles(G, NC, in_rows)
            return to_sibling(layer, REST), to_sibling(layer, LAST)

        def rest_to_shards(copies):
            return to_shards(layer, REST, copies[0]), to_shards(layer, LAST, copies[1])

        if layer == 0:
            rest_sib = rest_gradient()
            summing.start(in_product)
            rest_z = rest_to_shards(rest_sib)
            summing.middle()
        else:
            summing.start(in_product)
            later += load(0, (r.wf_i, r.wf))
            rest_sib = rest_gradient()
            first += load(0, (r.proj_i, r.proj))
            later += load(0, (r.n_i, r.n))
            summing.middle()
            rest_z = rest_to_shards(rest_sib)
        summing.end()
        while waiting:
            waiting.pop(0).start()
        if arrivals is not r.got:
            done(
                [
                    mover.put(arrivals.at[k - 1], r.part.at[lax.rem(here + k, n)])
                    for k in range(1, n)
                ]
            )

        def finish(at):
            if arrivals is r.got:
                d_in = summing.total(at)
            else:
                d_in = r.part[0, at, :].astype(F32)
                for k in range(1, n):
                    d_in = d_in + r.part[k, at, :].astype(F32)
            h = r.h1[at, :] if layer == 1 else r.h0[at, :]
            above = r.cot[at, :] if layer == 1 else r.grads[1, at, :]
            inv = lax.rsqrt(jnp.mean(h * h, axis=1, keepdims=True) + EPSILON)
            normed = h * inv
            gains_here = jnp.sum(d_in * normed, axis=0, keepdims=True)
            for q in range(4):
                row = slice(4 * layer + q, 4 * layer + q + 1)
                r.gain[here, row, :] += gains_here[:, q * (D // 4) : (q + 1) * (D // 4)]
            d_s = d_in * r.packs[layer, 0:1, gain_at:]
            d_h = above + inv * (d_s - normed * jnp.mean(d_s * normed, axis=1, keepdims=True))
            r.grads[layer, at, :] = d_h
            if layer == 1:
                out = d_h.astype(BF)
                whole = pl.ds(pl.multiple_of(here * rows + at.start, TILE), TILE)
                r.gb[whole, :] = out
                dots = jnp.sum(out.astype(F32) * r.pout[at, :], axis=1, keepdims=True)
                r.mdots[at, :] = jnp.broadcast_to(dots * (1.0 / INNER), (TILE, 128))

        rows_loop(rows, finish)
        if layer == 1:
            r.stats[here] = r.own_stat[...]
            r.stats[here, 1:2, :] = r.mdots[...].T[0:1, :]
            own = aligned(here * rows, rows)
            gathering = []

            def rows_of_group(group, half):
                size = rows if half is None else rows // 2
                return r.gb.at[aligned(group * rows + (half or 0) * size, size)]

            grad_rows = PlaneGather(put, n, here, r.gb.at[own], rows_of_group)
            for k in range(1, n):
                peer = lax.rem(here + k, n)
                gathering.append(put(r.stats.at[here], r.stats.at[here], SEQ, peer))
            grad_rows.forward()
            relay(1, REST, rest_z[0])
            relay(1, LAST, rest_z[1])
            arrived[1, OUT] = to_plane(1, OUT, out_z)
            arrived[1, GATE] = to_plane(1, GATE, gate_z)
            grad_rows.wait_recv()
            for copy in gathering:
                copy.wait_recv()
    gains = []
    ends = [put(r.grads.at[sibling], r.ig.at[core], SECTION, sibling)]
    for k in range(1, n):
        gains.append(put(r.gain.at[here], r.gain.at[here], SEQ, lax.rem(here + k, n)))
    local_grad = mover.put(r.grads.at[core], r.ig.at[core])
    relay(0, REST, rest_z[0])
    arrived[0, OUT] = to_plane(0, OUT, out_z)
    arrived[0, GATE] = to_plane(0, GATE, gate_z)
    relay(0, LAST, rest_z[1])
    arrived[0, OUT][0].forward()
    arrived[0, GATE][0].forward()
    for copy in small_z:
        copy.wait_recv()
    total = r.sm_own[...]
    for k in range(w - 1):
        total = total + r.sm_z[k]
    r.small[here] = total
    sums = [
        put(r.small.at[here], r.small.at[here], SEQ, lax.rem(here + k, n)) for k in range(1, n)
    ]
    for copy in gains:
        copy.wait_recv()
    total = r.gain[0]
    for k in range(1, n):
        total = total + r.gain[k]
    r.gain_z[shard] = total
    gains = [
        put(r.gain_z.at[shard], r.gain_z.at[shard], WT, lax.rem(shard + k, w)) for k in range(1, w)
    ]
    arrived[0, REST] = to_plane(0, REST, rest_z[0])
    ends.append(landed(OUT, arrived[1, OUT], arrived[0, OUT]))
    ends.append(landed(GATE, arrived[1, GATE], arrived[0, GATE]))
    arrived[0, LAST] = to_plane(0, LAST, rest_z[1])
    arrived[0, REST][0].forward()
    ends.append(landed(REST, arrived[1, REST], arrived[0, REST]))
    arrived[1, LAST][0].wait_recv()
    arrived[1, LAST][1].wait()
    last, last_own = arrived[0, LAST]

    def hand_over(group):
        source, target = r.gi.at[sibling, group, kept(LAST)], r.gi_sib.at[group, kept(LAST)]
        ends.append(put(source, target, SECTION, sibling))

    last_own.wait()
    hand_over(here)
    if last.plane:
        last.forward(hand_over)
        last.wait_recv()
        hand_over(lax.rem(last.x + 2, 4))
    else:
        last.wait_recv()
        for k in range(1, n):
            hand_over(lax.rem(here + k, n))
    for copy in gains:
        copy.wait_recv()
    total = r.gain_z[0]
    for k in range(1, w):
        total = total + r.gain_z[k]
    r.gain_sum[core] = total
    ends.append(put(r.gain_sum.at[core], r.gain_sum.at[core], SECTION, sibling))
    for copy in ends + sums:
        copy.wait_recv()
    r.late[...] = r.gain_sum[0] + r.gain_sum[1]
    local_grad.wait()
    assert wire.used <= r.ss.shape[0] and mover.used <= r.ls.shape[0]
    for kind in KINDS:
        ready(kind)
    for copy in open_sends:
        copy.wait_send()


def backward_call(g, n, w, fwd, tokens, cotangent):
    rows = tokens.shape[2]
    L, G, NC, CX = rows * n, g.G, g.NC, g.CX
    PK = CX + 128 + G + D
    S = jax.ShapeDtypeStruct
    o_half, lanes_of = G // (2 * w), D // w
    spill = n > 8
    outs = BackwardOuts(
        ig=S((2, rows, D), F32),
        gi=S((2, n, g.half, lanes_of), BF),
        go=S((2, n, o_half, D), BF),
        gi_sib=S((n, g.half, lanes_of), BF),
        go_sib=S((n, o_half, D), BF),
        small=S((n, 8, CX), F32),
        far=S((n - 1, rows, D) if spill else (8, 128), BF),
        late=S((8, D // 4), F32),
    )
    scratch = [
        S((2, 8, PK), F32), S((NC, D), BF), S((G, D), BF), S((L, D), BF), S((L, NC), BF), S((L, G), BF),
        S((L, G), F32), S((L // Q, STATE, G), F32), S((L, D), BF), S((n, 8, 128), F32), S((rows, D), F32),
        S((rows, D), F32), S((rows, D), F32), S((rows, D), F32),
        S((L, G), BF), S((8 + L, 128), F32), S((L, CX), F32), S((L, 128), F32), S((STATE, G), F32),
        S((n, rows, D), BF), S((1 if spill else n - 1, rows, D), BF), S((8, 128), F32), S((rows, 128), F32), S((2, rows, D), F32),
        S((NC, D), BF), S((G, D), BF), S((g.half, D), BF), S((G // 2, D), BF),
        S((2, w - 1, g.half, lanes_of), BF),
        S((2, w - 1, o_half, D), BF), S((2, g.half, lanes_of), BF), S((2, o_half, D), BF), S((2, 8, CX), F32), S((8, CX), F32), S((w - 1, 8, CX), F32), S((8, CX), F32),
        S((128, 128), BF), S((n, 8, D // 4), F32), S((w, 8, D // 4), F32), S((2, 8, D // 4), F32),
        S((2, rows // 2, D), BF),
    ]
    remote = 2 * (4 * (w + w + n) + n - 1) + 2 * (n - 1) + 40 + 2 * (w - 1) + 2 * (n - 1) + n
    args = [
        fwd.packs_o, fwd.wf_o, fwd.of_o, fwd.n_o, fwd.proj_o, fwd.mixed_o, fwd.yp_o, fwd.st_o,
        fwd.gb_o, fwd.stats, fwd.stat0, fwd.pout, fwd.h1, tokens, cotangent,
    ]
    results = pl.pallas_call(
        functools.partial(backward_kernel, g, n, w, rows),
        out_shape=list(outs),
        in_specs=[ANY] * len(args),
        out_specs=[VM, ANY, ANY, ANY, ANY, VM, ANY, VM],
        scratch_shapes=[pltpu.VMEM(s.shape, s.dtype) for s in scratch]
        + [
            pltpu.SemaphoreType.DMA((remote,)),
            pltpu.SemaphoreType.DMA((remote,)),
            pltpu.SemaphoreType.DMA((40 + 2 * n,)),
            pltpu.SemaphoreType.REGULAR((4,)),
        ],
        compiler_params=pltpu.CompilerParams(
            collective_id=1, has_side_effects=True, vmem_limit_bytes=BACKWARD_VMEM
        ),
        name="backward",
    )(*args)
    return BackwardOuts(*results)


def pack_small(g, here, conv_ref, bias_ref, dtb_ref, a_ref, skip_ref, gate_ref, norm_ref, pack_ref):
    G, width = g.G, g.run_heads * HEAD_DIM
    win = -(-(width + 64) // 128) * 128
    start = here * width
    base = pl.multiple_of(start // 128 * 128, 128)
    from_ids = lax.broadcasted_iota(jnp.int32, (win, G), 0)
    to_ids = lax.broadcasted_iota(jnp.int32, (win, G), 1)
    exact = lax.Precision.HIGHEST

    def take(ref, rows):
        total = jnp.zeros((rows, G), F32)
        for run in range(g.runs):
            window = ref[0:rows, pl.ds(pl.multiple_of(base + run * (INNER // g.runs), 128), win)]
            inside = (to_ids >= run * width) & (to_ids < (run + 1) * width)
            pick = one_hot(inside & (from_ids == to_ids - run * width + (start - base)))
            total = total + dot(window, pick, 1, 0, exact)
        return total

    head_from = lax.broadcasted_iota(jnp.int32, (HEADS, 128), 0)
    head_to = lax.broadcasted_iota(jnp.int32, (HEADS, 128), 1)
    head_pick = one_hot((head_from == head_of(g, here, head_to)) & (head_to < g.heads))
    wide_from = lax.broadcasted_iota(jnp.int32, (HEADS, G), 0)
    wide_to = lax.broadcasted_iota(jnp.int32, (HEADS, G), 1)
    wide_pick = (wide_from == head_of(g, here, wide_to // HEAD_DIM)) & (wide_to < g.chans)
    head_at, wide_at, gain_at = g.CX, g.CX + 128, g.CX + 128 + G
    pack_ref[...] = jnp.zeros_like(pack_ref)
    pack_ref[0:KERNEL, 0:G] = take(conv_ref, KERNEL)
    pack_ref[4:5, 0:G] = take(bias_ref, 1)
    pack_ref[0:KERNEL, G:head_at] = conv_ref[:, INNER:]
    pack_ref[4:5, G:head_at] = bias_ref[:, INNER:]
    pack_ref[0:1, head_at:wide_at] = dot(dtb_ref[...], head_pick, 1, 0, exact)
    pack_ref[1:2, head_at:wide_at] = dot(-jnp.exp(a_ref[...]), head_pick, 1, 0, exact)
    pack_ref[0:1, wide_at:gain_at] = take(gate_ref, 1)
    pack_ref[1:2, wide_at:gain_at] = dot(skip_ref[...], one_hot(wide_pick), 1, 0, exact)
    pack_ref[0:1, gain_at:] = norm_ref[...]


def halves_of_heads(g, ref_of, column_at, head):
    parts = []
    for h in (head, head + 1):
        stride = HEADS // g.runs
        group = h % stride // g.run_heads
        local_head = h // stride * g.run_heads + h % g.run_heads
        value = ref_of(group, slice(column_at + local_head // 2 * 128, column_at + local_head // 2 * 128 + 128))
        parts.append(value if local_head % 2 == h % 2 else pltpu.roll(value, HEAD_DIM, 1))
    lanes = lax.broadcasted_iota(jnp.int32, parts[0].shape, 1)
    return jnp.where(lanes < HEAD_DIM, parts[0], parts[1])


def layout_kernel(g, own_ref, sib_ref, own_out_ref, sib_out_ref, small_ref, late_ref, sec_ref, ig_ref, g_in_ref, g_out_ref, sec_out, ig_out, norm_ref, conv_ref, bias_ref, dtb_ref, a_ref, skip_ref, gate_ref):
    n, G = g.n_seq, g.G
    first_core = lax.axis_index(SECTION) == 0

    def all_rows(halves, outs):
        def copy(groups, parts, source, target, size):
            done = 0
            while done < size:
                row = source + done
                first, part_rows, half_at = next(x for x in parts if x[0] <= row < x[0] + x[1])
                half, offset = divmod(row - first, part_rows // 2)
                count = min(size - done, part_rows // 2 - offset)
                at = slice(half_at + offset, half_at + offset + count)
                total = None
                for group in groups:
                    value = halves[half][group, at, :].astype(F32)
                    total = value if total is None else total + value
                g_in_ref[target + done : target + done + count, :] = total
                done += count

        for half in range(2):
            g_out_ref[:, half] = outs[half][...].astype(F32)
        width = g.run_heads * HEAD_DIM
        gate = ((0, G, 0),)
        rest = ((0, g.cut, G // 2), (g.cut, g.rest - g.cut, (G + g.cut) // 2))
        everyone = range(n)
        for run in range(g.runs):
            for group in range(n):
                target = run * (INNER // g.runs) + group * width
                copy([group], gate, run * width, target, width)
                copy([group], rest, run * width, INNER + target, width)
        copy(everyone, rest, G, 2 * INNER, 2 * STATE)
        copy(everyone, rest, G + 2 * STATE, 2 * INNER + 2 * STATE, HEADS)

    sec_out[...] = sec_ref[...]
    ig_out[...] = ig_ref[...]
    own, own_out = own_ref.at[0], own_out_ref.at[0]

    @pl.when(first_core)
    def _():
        all_rows((own, sib_ref), (own_out, sib_out_ref))

    @pl.when(jnp.logical_not(first_core))
    def _():
        all_rows((sib_ref, own), (sib_out_ref, own_out))

    @pl.when(pl.program_id(0) == 0)
    def _():
        from_ids = lax.broadcasted_iota(jnp.int32, (128, HEADS), 0)
        to_ids = lax.broadcasted_iota(jnp.int32, (128, HEADS), 1)
        picks = [one_hot((to_ids == head_of(g, group, from_ids)) & (from_ids < g.heads)) for group in range(n)]
        exact = lax.Precision.HIGHEST
        head_at = g.CX

        def small(group, columns):
            return small_ref[group, :, columns]

        for head in range(0, HEADS, 2):
            at = slice(head * HEAD_DIM, head * HEAD_DIM + 128)
            conv = halves_of_heads(g, small, 0, head)
            conv_ref[:, at] = conv[0:KERNEL]
            bias_ref[:, at] = conv[KERNEL : KERNEL + 1]
            gate_ref[:, at] = conv[5:6]
        conv = small(0, slice(G, head_at))
        for group in range(1, n):
            conv = conv + small(group, slice(G, head_at))
        conv_ref[:, INNER:] = conv[0:KERNEL]
        bias_ref[:, INNER:] = conv[KERNEL : KERNEL + 1]
        for q in range(4):
            late = jnp.where(first_core, late_ref[q : q + 1, :], late_ref[4 + q : 5 + q, :])
            norm_ref[:, q * (D // 4) : (q + 1) * (D // 4)] = late
        biases = jnp.zeros((8, HEADS), F32)
        rates = jnp.zeros((8, HEADS), F32)
        skips = jnp.zeros((8, HEADS), F32)
        wide_from = lax.broadcasted_iota(jnp.int32, (G, HEADS), 0)
        wide_to = lax.broadcasted_iota(jnp.int32, (G, HEADS), 1)
        for group in range(n):
            biases = biases + dot(small(group, slice(0, 128)), picks[group], 1, 0, exact)
            rates = rates + dot(small(group, slice(128, 256)), picks[group], 1, 0, exact)
            pick = (wide_to == head_of(g, group, wide_from // HEAD_DIM)) & (wide_from < g.chans)
            skips = skips + dot(small(group, slice(0, G)), one_hot(pick), 1, 0, exact)
        dtb_ref[...] = biases[7:8]
        a_ref[...] = rates[7:8]
        skip_ref[...] = skips[6:7]


def layout_call(g, core, gi, gi_sib, go, go_sib, small, late, sec, ig):
    _, n, half, lanes = gi.shape
    out_half = go.shape[2]
    steps = lanes // 128
    out_lanes = D // steps
    rows_spec = pl.BlockSpec(sec.shape[:2] + (out_lanes,), lambda t, c: (0, 0, t))
    PK = small.shape[2]
    columns = 2 * INNER + 2 * STATE + HEADS
    S = jax.ShapeDtypeStruct
    shapes = (
        S((columns, lanes), F32), S((n, 2, out_half, D), F32), S(sec.shape, F32), S(ig.shape, F32), S((1, D), F32), S((KERNEL, CONV), F32),
        S((1, CONV), F32), S((1, HEADS), F32), S((1, HEADS), F32), S((1, HEADS), F32), S((1, INNER), F32),
    )
    return pl.pallas_call(
        lambda core_ref, *refs: layout_kernel(g, *refs),
        grid_spec=pltpu.PrefetchScalarGridSpec(
            num_scalar_prefetch=1,
            grid=(steps,),
            in_specs=[
                pl.BlockSpec((1, n, half, 128), lambda t, c: (c[0], 0, 0, t)),
                pl.BlockSpec((n, half, 128), lambda t, c: (0, 0, t)),
                pl.BlockSpec((1, n, out_half, out_lanes), lambda t, c: (c[0], 0, 0, t)),
                pl.BlockSpec((n, out_half, out_lanes), lambda t, c: (0, 0, t)),
                pl.BlockSpec((n, 8, PK), lambda t, c: (0, 0, 0)),
                pl.BlockSpec((8, D // 4), lambda t, c: (0, 0)),
                rows_spec,
                rows_spec,
            ],
            out_specs=[
                pl.BlockSpec((columns, 128), lambda t, c: (0, t)),
                pl.BlockSpec((n, 2, out_half, out_lanes), lambda t, c: (0, 0, 0, t)),
                rows_spec,
                rows_spec,
            ]
            + [pl.BlockSpec(s.shape, lambda t, c: (0, 0)) for s in shapes[4:]],
        ),
        out_shape=shapes,
        compiler_params=pltpu.CompilerParams(vmem_limit_bytes=SMALL_VMEM),
        name="layout",
    )(core, gi, gi_sib, go, go_sib, small, late, sec, ig)


def local(
    tokens, cotangent, norm_gain, w_in, conv_w, conv_b, dt_bias, a_log, skip_d, gate_gain, w_out
):
    n_seq, n_wt = lax.axis_size(SEQ), lax.axis_size(WT)
    here = lax.axis_index(SEQ)
    group = Group(n_seq, n_wt)
    core = lax.axis_index(SECTION).reshape(1)
    G = group.G

    small = (conv_w[0], conv_b, dt_bias, a_log, skip_d, gate_gain, norm_gain)
    w_src = jnp.swapaxes(w_in[0], 0, 1)
    if group.runs == n_wt:
        o_src = w_out[0]
    else:
        o_src = lax.all_gather(w_out[0], WT, axis=0, tiled=True)
        o_src = lax.dynamic_slice_in_dim(o_src, here * group.chans, group.chans, 0)
        o_src = jnp.pad(o_src, ((0, G - group.chans), (0, 0)))
    fwd = forward_call(group, n_seq, n_wt, tokens, cotangent, small, w_src, o_src)
    bwd = backward_call(group, n_seq, n_wt, fwd, tokens, cotangent)
    g_in, g_out, section_out, input_grad, g_norm, g_conv, g_bias, g_dtb, g_a, g_skip, g_gate = layout_call(
        group, core, bwd.gi, bwd.gi_sib, bwd.go, bwd.go_sib, bwd.small, bwd.late, fwd.sec, bwd.ig
    )
    if group.runs == n_wt:
        g_out = g_out.reshape(INNER // n_wt, D)
    else:
        g_out = g_out.astype(BF).reshape(n_seq, G // n_wt, D)
        g_out = lax.all_gather(g_out, WT, axis=1, tiled=True)[:, : group.chans].reshape(INNER, D)
        mine = INNER // n_wt
        g_out = lax.dynamic_slice_in_dim(g_out, lax.axis_index(WT) * mine, mine, 0).astype(F32)
    return (
        section_out[None, :, None],
        input_grad[None, :, None],
        g_norm,
        jnp.swapaxes(g_in, 0, 1)[None],
        g_conv[None],
        g_bias,
        g_dtb,
        g_a,
        g_skip,
        g_gate,
        g_out[None],
    )


def solution(mesh):
    placed = (
        P(None, WT, SEQ, None),
        P(None, WT, SEQ, None),
        P(SECTION, None),
        P(SECTION, WT, None),
        P(SECTION, None, None),
        P(SECTION, None),
        P(SECTION, None),
        P(SECTION, None),
        P(SECTION, None),
        P(SECTION, None),
        P(SECTION, WT, None),
    )
    return jax.shard_map(
        local,
        mesh=mesh,
        in_specs=placed,
        out_specs=(
            P(SECTION, None, WT, SEQ, None),
            P(SECTION, None, WT, SEQ, None),
            P(SECTION, None),
            P(SECTION, WT, None),
            P(SECTION, None, None),
            P(SECTION, None),
            P(SECTION, None),
            P(SECTION, None),
            P(SECTION, None),
            P(SECTION, None),
            P(SECTION, WT, None),
        ),
        check_vma=False,
    )
```

```python
import functools
from typing import Any, NamedTuple

import jax
import jax.numpy as jnp
from jax import lax
from jax.experimental import pallas as pl
from jax.experimental.pallas import tpu as pltpu
from jax.sharding import PartitionSpec as P

D = 1536
HEADS = 48
HEAD_DIM = 64
STATE = 128
KERNEL = 4
INNER = 3072
CONV = 3328
EPSILON = 1e-05

Q = 128
F32 = jnp.float32
BF = jnp.bfloat16
SEQ, WT, SECTION = "seq", "wt", "section"
FORWARD_VMEM = 56 * 2**20
BACKWARD_VMEM = 62 * 2**20
SMALL_VMEM = 60 * 2**20
MESH = pl.DeviceIdType.MESH
VM = pl.BlockSpec(memory_space=pltpu.VMEM)
ANY = pl.BlockSpec(memory_space=pl.ANY)
TILE = 16


def dot(a, b, ca, cb, precision=None):
    return lax.dot_general(a, b, (((ca,), (cb,)), ((), ())), precision=precision, preferred_element_type=F32)

def sigmoid(x):
    return 1.0 / (1.0 + jnp.exp(-x))

def softplus(x):
    return jnp.maximum(x, 0.0) + jnp.log1p(jnp.exp(-jnp.abs(x)))

def lane_mask(rows):
    return lax.broadcasted_iota(jnp.int32, (rows, 128), 1) < HEAD_DIM

def spread(cols, pair, mask):
    a = jnp.broadcast_to(cols[:, 2 * pair : 2 * pair + 1], mask.shape)
    b = jnp.broadcast_to(cols[:, 2 * pair + 1 : 2 * pair + 2], mask.shape)
    return jnp.where(mask, a, b)

def split_pair(u, mask):
    zero = jnp.zeros_like(u)
    return jnp.concatenate([jnp.where(mask, u, zero), jnp.where(mask, zero, u)], axis=0)

def conv_tile(proj_ref, cw_ref, pad, proj_at, conv_at, rows):
    pad[0:8, :] = jnp.zeros((8, 128), F32)
    pad[8 : 8 + rows, :] = proj_ref[:, pl.ds(proj_at, 128)].astype(F32)
    pre = jnp.broadcast_to(cw_ref[4:5, pl.ds(conv_at, 128)], (rows, 128))
    for k in range(KERNEL):
        pre = pre + cw_ref[k : k + 1, pl.ds(conv_at, 128)] * pad[5 + k : 5 + k + rows, :]
    return pre

def step_inputs(proj_ref, at, hp_ref, sel_ref, dt_at):
    return dot(proj_ref[at, dt_at : dt_at + 128], sel_ref[...], 1, 0) + hp_ref[0:1, :]

def chunk_factors(dt, hp_ref):
    rate = dt * hp_ref[1:2, :]
    rows = lax.broadcasted_iota(jnp.int32, (Q, Q), 0)
    cols = lax.broadcasted_iota(jnp.int32, (Q, Q), 1)
    tri = (rows >= cols).astype(F32)
    cum = dot(tri, rate, 1, 0, lax.Precision.HIGHEST)
    return rate, cum, rows >= cols

def decay_pair(cum, cum_t, causal, pair):
    parts = []
    for h in (2 * pair, 2 * pair + 1):
        diff = jnp.broadcast_to(cum[:, h : h + 1], (Q, Q)) - jnp.broadcast_to(cum_t[h : h + 1, :], (Q, Q))
        parts.append(jnp.exp(jnp.where(causal, diff, -1e30)))
    return jnp.concatenate(parts, axis=1)

def scan_forward(G, proj_ref, cw_ref, hp_ref, gw_ref, sel_ref, mixed_ref, yp_ref, st_ref, pad, xc, dts, state):
    L = proj_ref.shape[0]

    def conv(tile, carry):
        lanes = pl.ds(pl.multiple_of(tile * 128, 128), 128)
        pre = conv_tile(proj_ref, cw_ref, pad, pl.multiple_of(G + tile * 128, 128), lanes.start, L)
        xc[:, lanes] = pre * sigmoid(pre)
        return carry

    lax.fori_loop(0, (G + 2 * STATE) // 128, conv, 0)
    dt_at = 2 * G + 2 * STATE
    dts[...] = softplus(step_inputs(proj_ref, slice(0, L), hp_ref, sel_ref, dt_at))
    state[...] = jnp.zeros_like(state)
    mask = lane_mask(Q)

    def chunk(c, _):
        at = pl.ds(pl.multiple_of(c * Q, Q), Q)
        dt = dts[at, :]
        rate, cum, causal = chunk_factors(dt, hp_ref)
        cum_t = cum.T
        last = cum[Q - 1 : Q, :]
        e_cum = jnp.exp(cum)
        tail = jnp.exp(last - cum) * dt
        e_last = jnp.broadcast_to(jnp.exp(last), (8, 128))
        b = xc[at, G : G + STATE].astype(BF)
        cc = xc[at, G + STATE : G + 2 * STATE].astype(BF)
        scores = dot(cc, b, 1, 1)
        scores2 = jnp.concatenate([scores, scores], axis=1)
        for p in range(G // 128):
            lanes = slice(p * 128, p * 128 + 128)
            x = xc[at, lanes]
            u = (x * spread(dt, p, mask)).astype(BF)
            m = (scores2 * decay_pair(cum, cum_t, causal, p)).astype(BF)
            before = state[:, lanes]
            st_ref[c, :, lanes] = before
            y = dot(m, split_pair(u, mask), 1, 0)
            y = y + dot(cc, before.astype(BF), 1, 0) * spread(e_cum, p, mask)
            yp_ref[at, lanes] = y
            after = dot(b, (x * spread(tail, p, mask)).astype(BF), 0, 0)
            state[:, lanes] = before * spread(e_last, p, mask[0:8])[0:1, :] + after
            mixed_ref[at, lanes] = (y + gw_ref[1:2, lanes] * x).astype(BF)
        return 0

    lax.fori_loop(0, L // Q, chunk, 0)


def gate_forward(G, proj_ref, gw_ref, mixed_ref, vg_ref, ssq_ref):
    def chunk(c, _):
        at = pl.ds(pl.multiple_of(c * Q, Q), Q)
        ssq = jnp.zeros((Q, 1), F32)
        for p in range(G // 128):
            lanes = slice(p * 128, p * 128 + 128)
            gate = proj_ref[at, lanes].astype(F32)
            v = mixed_ref[at, lanes].astype(F32) * (gate * sigmoid(gate))
            vg_ref[at, lanes] = (v * gw_ref[0:1, lanes]).astype(BF)
            ssq = ssq + jnp.sum(v * v, axis=1, keepdims=True)
        ssq_ref[c] = jnp.broadcast_to(ssq, (Q, 128)).T[0:8, :]
        return 0

    lax.fori_loop(0, proj_ref.shape[0] // Q, chunk, 0)


def lane_sums(values, pick):
    high = values.astype(BF)
    low = (values - high.astype(F32)).astype(BF)
    return dot(high, pick, 1, 0) + dot(low, pick, 1, 0)


def gate_backward(G, proj_ref, mixed_ref, dn_ref, sc_ref, gw_ref, dy_ref, gg_ref):
    gg_ref[...] = jnp.zeros_like(gg_ref)

    def chunk(c, _):
        at = pl.ds(pl.multiple_of(c * Q, Q), Q)
        sc = jnp.concatenate([sc_ref[c], jnp.zeros((Q - 8, 128), F32)], axis=0).T
        inv2 = jnp.broadcast_to(sc[:, 0:1], (Q, 128))
        mdot = jnp.broadcast_to(sc[:, 1:2], (Q, 128))
        for p in range(G // 128):
            lanes = slice(p * 128, p * 128 + 128)
            gate = proj_ref[at, lanes].astype(F32)
            sig = sigmoid(gate)
            act = gate * sig
            mixed = mixed_ref[at, lanes].astype(F32)
            n2 = mixed * act * inv2
            mixed_ref[at, lanes] = (n2 * gw_ref[0:1, lanes]).astype(BF)
            dn = dn_ref[at, lanes]
            gg_ref[0:1, lanes] += jnp.sum(dn * n2, axis=0, keepdims=True)
            d_v = inv2 * (dn * gw_ref[0:1, lanes] - n2 * mdot)
            dy_ref[at, lanes] = (d_v * act).astype(BF)
            proj_ref[at, lanes] = (d_v * mixed * (sig * (1.0 + gate * (1.0 - sig)))).astype(BF)
        return 0

    lax.fori_loop(0, proj_ref.shape[0] // Q, chunk, 0)


def scan_backward(G, proj_ref, dy_ref, yp_ref, st_ref, cw_ref, hp_ref, gw_ref, sel_ref, gg_ref, gc_ref, gh_ref,
                  pad, xc, dts, dstate, serve):
    L = proj_ref.shape[0]
    nb = L // Q
    mask = lane_mask(Q)

    def conv(tile, carry):
        lanes = pl.ds(pl.multiple_of(tile * 128, 128), 128)
        pre = conv_tile(proj_ref, cw_ref, pad, pl.multiple_of(G + tile * 128, 128), lanes.start, L)
        xc[:, lanes] = pre * sigmoid(pre)
        return carry

    lax.fori_loop(0, (G + 2 * STATE) // 128, conv, 0)
    dt_at = 2 * G + 2 * STATE
    dts[...] = softplus(step_inputs(proj_ref, slice(0, L), hp_ref, sel_ref, dt_at))
    dstate[...] = jnp.zeros_like(dstate)
    gh_ref[...] = jnp.zeros_like(gh_ref)

    def chunk(step, _):
        c = nb - 1 - step
        pl.when(step == nb // 4)(serve)
        at = pl.ds(pl.multiple_of(c * Q, Q), Q)
        dt = dts[at, :]
        rate, cum, causal = chunk_factors(dt, hp_ref)
        cum_t = cum.T
        last = cum[Q - 1 : Q, :]
        e_cum = jnp.exp(cum)
        tail = jnp.exp(last - cum)
        e_last = jnp.broadcast_to(jnp.exp(last), (8, 128))
        b = xc[at, G : G + STATE].astype(BF)
        cc = xc[at, G + STATE : G + 2 * STATE].astype(BF)
        scores = dot(cc, b, 1, 1)
        scores2 = jnp.concatenate([scores, scores], axis=1)
        d_scores = jnp.zeros((Q, Q), F32)
        d_b = jnp.zeros((Q, STATE), F32)
        d_c = jnp.zeros((Q, STATE), F32)
        d_cum = jnp.zeros((Q, 128), F32)
        d_dt = jnp.zeros((Q, 128), F32)
        d_last = jnp.zeros((8, 128), F32)
        lane_ids = lax.broadcasted_iota(jnp.int32, (Q, 128), 1)
        row_ids = lax.broadcasted_iota(jnp.int32, (Q, 128), 0)
        for p in range(G // 128):
            lanes = slice(p * 128, p * 128 + 128)
            dyb = dy_ref[at, lanes]
            d_y = dyb.astype(F32)
            x = xc[at, lanes]
            dt_x = spread(dt, p, mask)
            u = (x * dt_x).astype(BF)
            u2 = split_pair(u, mask)
            uf = u.astype(F32)
            dec = decay_pair(cum, cum_t, causal, p)
            m = (scores2 * dec).astype(BF)
            dm = dot(dyb, u2, 1, 1) * dec
            d_scores = d_scores + dm[:, :Q] + dm[:, Q:]
            both = dot(m, dyb, 0, 0)
            du = jnp.where(mask, both[:Q], both[Q:])
            tail_x = spread(tail, p, mask)
            before = st_ref[c, :, lanes]
            after = dstate[:, lanes]
            afterb = after.astype(BF)
            du_out = tail_x * dot(b, afterb, 1, 0)
            du = du + du_out
            dye = (d_y * spread(e_cum, p, mask)).astype(BF)
            d_c = d_c + dot(dye, before.astype(BF), 1, 1)
            d_b = d_b + dot((uf * tail_x).astype(BF), afterb, 1, 1)
            e_last_x = spread(e_last, p, mask[0:8])
            dstate[:, lanes] = after * e_last_x[0:1, :] + dot(cc, dye, 0, 0)
            z3 = jnp.sum(uf * du_out, axis=0, keepdims=True) + e_last_x[0:1, :] * jnp.sum(before * after, axis=0, keepdims=True)
            z1 = d_y * yp_ref[at, lanes] - uf * du
            z2 = x * du
            pick = jnp.where(lane_ids == 2 * p + jnp.where(row_ids < HEAD_DIM, 0, 1), 1.0, 0.0).astype(BF)
            d_cum = d_cum + lane_sums(z1, pick)
            d_dt = d_dt + lane_sums(z2, pick)
            d_last = d_last + lane_sums(jnp.broadcast_to(z3, (8, 128)), pick)
            xc[at, lanes] = dt_x * du + gw_ref[1:2, lanes] * d_y
            gg_ref[1:2, lanes] += jnp.sum(d_y * x, axis=0, keepdims=True)
        dsb = d_scores.astype(BF)
        xc[at, G : G + STATE] = d_b + dot(dsb, cc, 0, 0)
        xc[at, G + STATE : G + 2 * STATE] = d_c + dot(dsb, b, 1, 0)
        rows = lax.broadcasted_iota(jnp.int32, (Q, Q), 0)
        cols = lax.broadcasted_iota(jnp.int32, (Q, Q), 1)
        upper = (rows <= cols).astype(F32)
        d_rate = dot(upper, d_cum, 1, 0, lax.Precision.HIGHEST) + d_last[0:1, :]
        d_step = d_dt + d_rate * hp_ref[1:2, :]
        d_raw = d_step * sigmoid(step_inputs(proj_ref, at, hp_ref, sel_ref, dt_at))
        proj_ref[at, dt_at : dt_at + 128] = dot(d_raw.astype(BF), sel_ref[...], 1, 1).astype(BF)
        gh_ref[:, 0:128] += jnp.sum(d_raw, axis=0, keepdims=True)
        gh_ref[:, 128:256] += jnp.sum(d_rate * rate, axis=0, keepdims=True)
        return 0

    lax.fori_loop(0, nb, chunk, 0)

    gc_ref[...] = jnp.zeros_like(gc_ref)

    def conv_back(tile, carry):
        lanes = pl.ds(pl.multiple_of(tile * 128, 128), 128)
        proj_at = pl.multiple_of(G + tile * 128, 128)
        pre = conv_tile(proj_ref, cw_ref, pad, proj_at, lanes.start, L)
        sig = sigmoid(pre)
        d_pre = xc[:, lanes] * (sig * (1.0 + pre * (1.0 - sig)))
        for k in range(KERNEL):
            gc_ref[k : k + 1, lanes] = jnp.sum(d_pre * pad[5 + k : 5 + k + L, :], axis=0, keepdims=True)
        gc_ref[4:5, lanes] = jnp.sum(d_pre, axis=0, keepdims=True)
        pad[0:L, :] = d_pre
        pad[L : L + 8, :] = jnp.zeros((8, 128), F32)
        d_in = cw_ref[3:4, lanes] * d_pre
        for k in range(KERNEL - 1):
            d_in = d_in + cw_ref[k : k + 1, lanes] * pad[3 - k : 3 - k + L, :]
        proj_ref[:, pl.ds(proj_at, 128)] = d_in.astype(BF)
        return carry

    lax.fori_loop(0, (G + 2 * STATE) // 128, conv_back, 0)


def column(row):
    return jnp.broadcast_to(row, (128, 128)).T


def rows_loop(rows, body):
    def step(r, carry):
        body(pl.ds(pl.multiple_of(r * TILE, TILE), TILE))
        return carry

    lax.fori_loop(0, rows // TILE, step, 0)


class Group:
    def __init__(self, n_seq, n_wt):
        self.n_seq = n_seq
        self.heads = HEADS // n_seq
        self.runs = n_wt if HEADS % (n_seq * n_wt) == 0 else 1
        self.run_heads = self.heads // self.runs
        self.chans = self.heads * HEAD_DIM
        self.G = -(-self.chans // 128) * 128
        self.CX = self.G + 2 * STATE
        self.NC = 2 * self.G + 2 * STATE + 128
        self.rest = self.G + 2 * STATE + 64
        self.half = (self.G + self.rest) // 2
        self.cut = self.rest * 3 // 256 * 64


def head_of(g, here, local_head):
    stride = HEADS // g.runs
    run = local_head // g.run_heads
    return run * stride + here * g.run_heads + (local_head - run * g.run_heads)


def one_hot(found):
    return jnp.where(found, 1.0, 0.0)


def step_select(g, here):
    from_ids = lax.broadcasted_iota(jnp.int32, (128, 128), 0)
    to_ids = lax.broadcasted_iota(jnp.int32, (128, 128), 1)
    return one_hot((from_ids == head_of(g, here, to_ids)) & (to_ids < g.heads))


OUT, GATE, REST, LAST = KINDS = range(4)


class Wire:
    def __init__(self, send_sems, recv_sems):
        self.send_sems, self.recv_sems, self.used = send_sems, recv_sems, 0

    def reserve(self):
        self.used += 1
        return self.used - 1

    def make(self, src, dst, axis, peer, at_send, at_recv):
        return pltpu.make_async_remote_copy(
            src, dst, self.send_sems.at[at_send], self.recv_sems.at[at_recv],
            device_id={axis: peer}, device_id_type=MESH,
        )

    def put(self, src, dst, axis, peer):
        at = self.reserve()
        copy = self.make(src, dst, axis, peer, at, at)
        copy.start()
        return copy


class Maybe:
    def __init__(self, condition, copy):
        self.condition, self.copy = condition, copy

    def start(self):
        pl.when(self.condition)(self.copy.start)
        return self

    def wait_send(self):
        pl.when(self.condition)(self.copy.wait_send)


class PlaneGather:
    def __init__(self, put, n, here, source, block):
        self.put, self.block, self.plane = put, block, n == 4
        mine = block(here, None)
        if not self.plane:
            self.copies = [put(source, mine, SEQ, lax.rem(here + k, n)) for k in range(1, n)]
            return
        self.x = here + 1 - 2 * lax.rem(here, 2)
        self.y = lax.rem(here + 2, 4)
        self.copies = [put(source, mine, SEQ, self.x), put(source, mine, SEQ, self.y)]

    def forward(self, landed=None):
        if self.plane:
            for copy, group, half, peer in (
                (self.copies[0], self.x, 0, self.y),
                (self.copies[1], self.y, 1, self.x),
            ):
                copy.wait_recv()
                part = self.block(group, half)
                self.copies.append(self.put(part, part, SEQ, peer))
                if landed is not None:
                    landed(group)

    def wait_recv(self):
        for copy in self.copies[2:] if self.plane else self.copies:
            copy.wait_recv()

    def wait_send(self):
        for copy in self.copies:
            copy.wait_send()


class PlaneSum:
    def __init__(self, put, n, here, part, got, mid):
        self.put, self.n, self.here, self.part, self.got, self.mid = put, n, here, part, got, mid
        self.plane = n == 4
        self.half = part.shape[1] // 2
        self.peers = [lax.rem(here + k, n) for k in range(1, n)]
        if self.plane:
            self.x = here + 1 - 2 * lax.rem(here, 2)
            self.y = lax.rem(here + 2, 4)
            self.peers = [lax.rem(self.x + 2, 4), self.y, self.x]

    def start(self, product, stat=None, got_stat=None):
        half, part, got = self.half, self.part, self.got
        self.copies = []
        product()
        for k, peer in enumerate(self.peers):
            if not self.plane:
                self.copies.append(self.put(part.at[peer], got.at[k], SEQ, peer))
            elif k == 0:
                self.mids = [
                    self.put(part.at[peer, 0:half], self.mid.at[0], SEQ, self.x),
                    self.put(part.at[peer, half:], self.mid.at[1], SEQ, self.y),
                ]
            elif k == 1:
                self.copies.append(self.put(part.at[peer, half:], got.at[1, half:], SEQ, peer))
            else:
                self.copies.append(self.put(part.at[peer, 0:half], got.at[0, 0:half], SEQ, peer))
            if stat is not None:
                self.copies.append(self.put(stat.at[peer], got_stat.at[k], SEQ, peer))

    def middle(self):
        if not self.plane:
            return
        half, part = self.half, self.part
        for copy in self.mids:
            copy.wait()

        def add(at):
            late = pl.ds(pl.multiple_of(at.start + half, TILE), TILE)
            for peer, rows, slot in ((self.y, at, 0), (self.x, late, 1)):
                total = part[peer, rows, :].astype(F32) + self.mid[slot, at, :].astype(F32)
                part[peer, rows, :] = total.astype(BF)

        rows_loop(half, add)
        self.copies += [
            self.put(part.at[self.y, 0:half], self.got.at[1, 0:half], SEQ, self.y),
            self.put(part.at[self.x, half:], self.got.at[0, half:], SEQ, self.x),
        ]

    def end(self):
        for copy in self.copies:
            copy.wait()

    def total(self, at):
        total = self.part[self.here, at, :].astype(F32)
        for k in range(2 if self.plane else self.n - 1):
            total = total + self.got[k, at, :].astype(F32)
        return total


class Mover:
    def __init__(self, sems):
        self.sems, self.used = sems, 0

    def put(self, src, dst):
        copy = pltpu.make_async_copy(src, dst, self.sems.at[self.used])
        copy.start()
        self.used += 1
        return copy


def meet_all(axes):
    barrier = pltpu.get_barrier_semaphore()
    count = 0
    for axis, n in axes:
        me = lax.axis_index(axis)
        for k in range(1, n):
            pl.semaphore_signal(
                barrier, inc=1, device_id={axis: lax.rem(me + k, n)}, device_id_type=MESH
            )
        count += n - 1
    pl.semaphore_wait(barrier, count)


def column_tiles(first, last, body):
    whole = (last - first) // 256

    def step(t, carry):
        body(pl.ds(pl.multiple_of(first + t * 256, 128), 256))
        return carry

    lax.fori_loop(0, whole, step, 0)
    if first + whole * 256 < last:
        body(slice(first + whole * 256, last))


def four_blocks(part, product):
    count, rows, columns = part.shape

    def step(q, carry):
        at = pl.ds(pl.multiple_of(q * 4 * rows, TILE), 4 * rows)

        def tile(lanes):
            value = product(at, lanes).astype(BF)
            for b in range(4):
                part[q * 4 + b, :, lanes] = value[b * rows : (b + 1) * rows]

        column_tiles(0, columns, tile)
        return carry

    lax.fori_loop(0, count // 4, step, 0)


class ForwardOuts(NamedTuple):
    sec: Any
    pout: Any
    stat0: Any
    h1: Any
    gb_o: Any
    stats: Any
    packs_o: Any
    wf_o: Any
    of_o: Any
    n_o: Any
    proj_o: Any
    mixed_o: Any
    yp_o: Any
    st_o: Any


class ForwardRefs(NamedTuple):
    tokens: Any
    cotangent: Any
    conv_w: Any
    conv_b: Any
    dt_bias: Any
    a_log: Any
    skip_d: Any
    gate_gain: Any
    norm_gain: Any
    w_src: Any
    o_src: Any
    sec: Any
    pout: Any
    stat0: Any
    h1: Any
    gb_o: Any
    stats: Any
    packs_o: Any
    wf_o: Any
    of_o: Any
    n_o: Any
    proj_o: Any
    mixed_o: Any
    yp_o: Any
    st_o: Any
    h0: Any
    cot: Any
    packs: Any
    wf: Any
    of: Any
    normed: Any
    proj: Any
    mixed: Any
    yp: Any
    st: Any
    pad: Any
    xc: Any
    dts: Any
    state: Any
    vg: Any
    ssq: Any
    part: Any
    got: Any
    got_stat: Any
    hbuf: Any
    own_stat: Any
    cols: Any
    mdots: Any
    sel: Any
    pack: Any
    mid: Any
    ss: Any
    rs: Any
    ls: Any


def forward_kernel(g, n, w, rows, *refs):
    r = ForwardRefs(*refs)
    G, NC = g.G, g.NC
    core, here, shard = lax.axis_index(SECTION), lax.axis_index(SEQ), lax.axis_index(WT)
    sibling = 1 - core
    wire, mover = Wire(r.ss, r.rs), Mover(r.ls)
    wf, of, packs = r.wf, r.of, r.packs
    sends, saves = [], []

    def aligned(at, size):
        return pl.ds(pl.multiple_of(at, 16), size)

    def put(src, dst, axis, peer):
        copy = wire.put(src, dst, axis, peer)
        sends.append(copy)
        return copy

    for layer in range(2):
        for first, last in ((g.chans, G), (G + g.chans, 2 * G), (2 * G + 2 * STATE + HEADS, NC)):
            if first < last:
                wf[layer, first:last, :] = jnp.zeros((last - first, D), BF)
    meet_all(((SEQ, n), (WT, w), (SECTION, 2)))
    o_rows = G // w
    lanes_of = D // w
    mine_o = aligned(shard * o_rows, o_rows)
    piece = here if g.runs == w else shard
    o_own = r.o_src.at[aligned(piece * o_rows, o_rows)]
    mine_lanes = pl.ds(pl.multiple_of(shard * lanes_of, 128), lanes_of)
    width = g.run_heads * HEAD_DIM
    runs = []
    for kind_at, source_at in ((0, 0), (G, INNER)):
        for run in range(g.runs):
            source = source_at + run * (INNER // g.runs) + here * width
            runs.append((source, kind_at + run * width, width))
    runs.append((2 * INNER, 2 * G, 2 * STATE))
    runs.append((2 * INNER + 2 * STATE, 2 * G + 2 * STATE, HEADS))
    siblings, locals_ = [], []
    for source, target, size in runs:
        taken = r.w_src.at[aligned(source, size)]
        siblings.append(put(taken, wf.at[core, target : target + size, mine_lanes], SECTION, sibling))
        locals_.append(mover.put(taken, wf.at[core, target : target + size, mine_lanes]))
    others = [put(o_own, of.at[core, mine_o], SECTION, sibling)]
    locals_later = [
        mover.put(o_own, of.at[core, mine_o]),
        mover.put(r.tokens.at[core, 0], r.h0),
        mover.put(r.cotangent.at[core, 0], r.cot),
    ]

    def part_of(layer, kind, at_shard, at_core):
        if kind == OUT:
            return of.at[layer, aligned(at_shard * o_rows + at_core * (o_rows // 2), o_rows // 2)]
        size = (G if kind == GATE else g.rest) // 2
        first = (0 if kind == GATE else G) + at_core * size
        lanes = pl.ds(pl.multiple_of(at_shard * lanes_of, 128), lanes_of)
        return wf.at[layer, aligned(first, size), lanes]

    line = w == 4

    def fetch(layer, kind):
        mine = part_of(layer, kind, shard, core)
        at = [wire.reserve() for _ in range(w)]
        copies = [
            wire.make(mine, mine, WT, lax.rem(shard + k, w), at[k], at[k]) for k in range(1, w)
        ]
        if line:
            copies[1].start()
            sends.append(copies[1])
            sends.append(Maybe(shard != w - 1, copies[0]).start())
            sends.append(Maybe(shard != 0, copies[2]).start())
        else:
            for copy in copies:
                copy.start()
            sends.extend(copies)
        return copies, at

    def far_part(fetched, layer, kind):
        if not line:
            return []
        at = fetched[1]
        fetched[0][1].wait_recv()
        block = part_of(layer, kind, lax.rem(shard + 2, w), core)
        up = wire.make(block, block, WT, lax.rem(shard + 1, w), at[0], at[3])
        down = wire.make(block, block, WT, lax.rem(shard + w - 1, w), at[0], at[1])
        sends.append(Maybe(shard == 2, up).start())
        sends.append(Maybe(shard == 1, down).start())
        return [put(block, block, SECTION, sibling)]

    def near_parts(fetched, layer, kind):
        found = []
        for k in (1, 3) if line else range(1, w):
            fetched[0][k - 1].wait_recv()
            block = part_of(layer, kind, lax.rem(shard + w - k, w), core)
            found.append(put(block, block, SECTION, sibling))
        return found

    def received(copies):
        for copy in copies:
            copy.wait_recv()

    own_rows = aligned(here * rows, rows)

    def gather(whole):
        def block(group, half):
            size = rows if half is None else rows // 2
            return whole.at[aligned(group * rows + (half or 0) * size, size)]

        return PlaneGather(wire.put, n, here, block(here, None), block)

    def save(source, target):
        saves.append(mover.put(source, target))

    def saved():
        while saves:
            saves.pop().wait()

    for copy in locals_:
        copy.wait()
    received(siblings)
    pending = fetch(0, REST)
    gain_at = g.CX + 128 + G
    r.sel[...] = step_select(g, here).astype(BF)
    pack_small(g, here, r.conv_w, r.conv_b, r.dt_bias, r.a_log, r.skip_d, r.gate_gain, r.norm_gain, r.pack)
    others.append(put(r.pack, packs.at[core], SECTION, sibling))
    locals_later.append(mover.put(r.pack, packs.at[core]))
    for copy in locals_later:
        copy.wait()
    received(others)

    def norm(at):
        h = r.h0[at, :]
        inv = lax.rsqrt(jnp.mean(h * h, axis=1, keepdims=True) + EPSILON)
        r.normed[pl.ds(pl.multiple_of(here * rows + at.start, TILE), TILE), :] = (
            h * inv * packs[0, 0:1, gain_at:]
        ).astype(BF)

    rows_loop(rows, norm)
    arriving = gather(r.normed)
    handed = far_part(pending, 0, REST)
    coming = [fetch(0, GATE), fetch(0, OUT)]
    arriving.forward()
    handed += near_parts(pending, 0, REST)

    for layer in range(2):
        proj, mixed, normed = r.proj, r.mixed, r.normed
        conv = packs.at[layer, :, 0 : g.CX]
        head = packs.at[layer, :, g.CX : g.CX + 128]
        wide = packs.at[layer, :, g.CX + 128 : gain_at]

        def project(lanes):
            proj[:, lanes] = dot(normed[...], wf[layer, lanes, :], 1, 1).astype(BF)

        arriving.wait_recv()
        received(handed)
        gathered = arriving
        column_tiles(G, NC, project)
        scan_forward(
            G, proj, conv, head, wide, r.sel, mixed, r.yp, r.st,
            r.pad, r.xc, r.dts, r.state,
        )
        save(mixed, r.mixed_o.at[layer])
        save(r.yp, r.yp_o.at[layer])
        save(r.st, r.st_o.at[layer])
        save(normed, r.n_o.at[layer])
        handed = far_part(coming[0], layer, GATE) + far_part(coming[1], layer, OUT)
        handed += near_parts(coming[0], layer, GATE) + near_parts(coming[1], layer, OUT)
        if layer == 0:
            pending = fetch(1, REST)
        received(handed)
        column_tiles(0, G, project)
        save(proj, r.proj_o.at[layer])
        gate_forward(G, proj, wide, mixed, r.vg, r.ssq)

        def out_product():
            four_blocks(r.part, lambda at, lanes: dot(r.vg[at, :], of[layer, :, lanes], 1, 0))

        saved()
        gathered.wait_send()
        summing = PlaneSum(wire.put, n, here, r.part, r.got, r.mid)
        summing.start(out_product, r.ssq, r.got_stat)
        summing.middle()
        summing.end()
        if layer == 0:
            handed = far_part(pending, 1, REST)
            coming = [fetch(1, GATE), fetch(1, OUT)]
        ssq = r.ssq[here]
        for k in range(n - 1):
            ssq = ssq + r.got_stat[k]
        inv2 = lax.rsqrt(ssq * (1.0 / INNER) + EPSILON)
        r.own_stat[...] = inv2
        r.cols[...] = column(inv2[0:1, :])
        if layer == 0:
            r.stat0[...] = inv2

        def finish(at):
            pout = summing.total(at) * r.cols[at, 0:1]
            whole = pl.ds(pl.multiple_of(here * rows + at.start, TILE), TILE)
            h_in = r.h0[at, :] if layer == 0 else r.hbuf[0, at, :]
            h = h_in + pout
            r.hbuf[layer, at, :] = h
            if layer == 0:
                r.pout[at, :] = pout
                r.h1[at, :] = h
                inv = lax.rsqrt(jnp.mean(h * h, axis=1, keepdims=True) + EPSILON)
                r.normed[whole, :] = (h * inv * packs[1, 0:1, gain_at:]).astype(BF)
            else:
                out = r.cot[at, :].astype(BF)
                dots = jnp.sum(out.astype(F32) * pout, axis=1, keepdims=True)
                r.mdots[at, :] = jnp.broadcast_to(dots * (1.0 / INNER), (TILE, 128))
                r.normed[whole, :] = out

        rows_loop(rows, finish)
        if layer == 0:
            arriving = gather(r.normed)
            arriving.forward()
            handed += near_parts(pending, 1, REST)
    r.stats[here] = r.own_stat[...]
    r.stats[here, 1:2, :] = r.mdots[...].T[0:1, :]
    last_rows = gather(r.normed)
    arriving = []
    for k in range(1, n):
        block = r.stats.at[here]
        arriving.append(put(block, block, SEQ, lax.rem(here + k, n)))
    arriving.append(put(r.hbuf.at[1 - core], r.sec.at[core], SECTION, sibling))
    save(r.hbuf.at[core], r.sec.at[core])
    save(packs, r.packs_o)
    save(wf, r.wf_o)
    save(of, r.of_o)
    last_rows.forward()
    last_rows.wait_recv()
    received(arriving)
    save(r.normed, r.gb_o)
    last_rows.wait_send()
    assert wire.used <= r.ss.shape[0] and mover.used <= r.ls.shape[0]
    for copy in sends:
        copy.wait_send()
    saved()


def forward_call(g, n, w, tokens, cotangent, small, w_src, o_src):
    rows = tokens.shape[2]
    L, G, NC, CX, PK = rows * n, g.G, g.NC, g.CX, g.CX + 128 + g.G + D
    S = jax.ShapeDtypeStruct
    shapes = ForwardOuts(
        sec=S((2, rows, D), F32),
        pout=S((rows, D), F32),
        stat0=S((8, 128), F32),
        h1=S((rows, D), F32),
        gb_o=S((L, D), BF),
        stats=S((n, 8, 128), F32),
        packs_o=S((2, 8, PK), F32),
        wf_o=S((2, NC, D), BF),
        of_o=S((2, G, D), BF),
        n_o=S((2, L, D), BF),
        proj_o=S((2, L, NC), BF),
        mixed_o=S((2, L, G), BF),
        yp_o=S((2, L, G), F32),
        st_o=S((2, L // Q, STATE, G), F32),
    )
    scratch = [
        S((rows, D), F32), S((rows, D), F32), shapes.packs_o, shapes.wf_o, shapes.of_o, S((L, D), BF), S((L, NC), BF), S((L, G), BF),
        S((L, G), F32), S((L // Q, STATE, G), F32), S((8 + L, 128), F32), S((L, CX), F32), S((L, 128), F32), S((STATE, G), F32),
        S((L, G), BF), S((n, 8, 128), F32), S((n, rows, D), BF), S((n - 1, rows, D), BF), S((n - 1, 8, 128), F32),
        S((2, rows, D), F32), S((8, 128), F32), S((rows, 128), F32), S((rows, 128), F32),
        S((128, 128), BF), S((8, PK), F32), S((2, rows // 2, D), BF),
    ]
    remote = 4 + 2 * g.runs + 6 * w + 6 * (w - 1) + 24 + 8 * (n - 1)
    outs = pl.pallas_call(
        functools.partial(forward_kernel, g, n, w, rows),
        out_shape=list(shapes),
        in_specs=[ANY, ANY] + [VM] * len(small) + [ANY, ANY],
        out_specs=[VM] * 4 + [ANY, VM] + [ANY] * 8,
        scratch_shapes=[pltpu.VMEM(s.shape, s.dtype) for s in scratch]
        + [
            pltpu.SemaphoreType.DMA((remote,)),
            pltpu.SemaphoreType.DMA((remote,)),
            pltpu.SemaphoreType.DMA((22 + 2 * g.runs,)),
        ],
        compiler_params=pltpu.CompilerParams(
            collective_id=0, has_side_effects=True, vmem_limit_bytes=FORWARD_VMEM
        ),
        name="forward",
    )(tokens, cotangent, *small, w_src, o_src)
    return ForwardOuts(*outs)


class BackwardOuts(NamedTuple):
    ig: Any
    gi: Any
    go: Any
    gi_sib: Any
    go_sib: Any
    small: Any
    far: Any
    late: Any


class BackwardRefs(NamedTuple):
    packs_i: Any
    wf_i: Any
    of_i: Any
    n_i: Any
    proj_i: Any
    mixed_i: Any
    yp_i: Any
    st_i: Any
    gb_i: Any
    stats1_i: Any
    stat0_i: Any
    pout_i: Any
    h1_i: Any
    tokens_i: Any
    cotangent_i: Any
    ig: Any
    gi: Any
    go: Any
    gi_sib: Any
    go_sib: Any
    small: Any
    far: Any
    late: Any
    packs: Any
    wf: Any
    of: Any
    n: Any
    proj: Any
    mixed: Any
    yp: Any
    st: Any
    gb: Any
    stats: Any
    pout: Any
    h1: Any
    h0: Any
    cot: Any
    dy: Any
    pad: Any
    xc: Any
    dts: Any
    dstate: Any
    part: Any
    got: Any
    own_stat: Any
    mdots: Any
    grads: Any
    gw: Any
    gout: Any
    sib_w: Any
    sib_o: Any
    z_w: Any
    z_o: Any
    relay_w: Any
    relay_o: Any
    sm: Any
    sm_sib: Any
    sm_z: Any
    sm_own: Any
    sel: Any
    gain: Any
    gain_z: Any
    gain_sum: Any
    mid: Any
    ss: Any
    rs: Any
    ls: Any
    free: Any


def backward_kernel(g, n, w, rows, *refs):
    r = BackwardRefs(*refs)
    G, NC, CX = g.G, g.NC, g.CX
    core, here, shard = lax.axis_index(SECTION), lax.axis_index(SEQ), lax.axis_index(WT)
    sibling = 1 - core
    wire, mover = Wire(r.ss, r.rs), Mover(r.ls)
    o_half, lanes_of = G // (2 * w), D // w
    gain_at = CX + 128 + G

    def aligned(at, size):
        return pl.ds(pl.multiple_of(at, 16), size)

    def load(layer, *pairs):
        return [mover.put(source.at[layer], target) for source, target in pairs]

    first = load(1, (r.of_i, r.of), (r.proj_i, r.proj), (r.mixed_i, r.mixed))
    first += [mover.put(r.packs_i, r.packs), mover.put(r.gb_i, r.gb), mover.put(r.stats1_i, r.stats)]
    later = load(1, (r.n_i, r.n), (r.yp_i, r.yp), (r.st_i, r.st), (r.wf_i, r.wf))
    later += [mover.put(r.pout_i, r.pout), mover.put(r.h1_i, r.h1), mover.put(r.stat0_i, r.own_stat)]
    later += [mover.put(r.tokens_i.at[core, 0], r.h0), mover.put(r.cotangent_i.at[core, 0], r.cot)]
    meet_all(((SEQ, n), (WT, w), (SECTION, 2)))
    r.sm[...] = jnp.zeros_like(r.sm)
    r.sel[...] = step_select(g, here).astype(BF)
    r.gain[here] = jnp.zeros((8, D // 4), F32)
    open_sends, record = [], {}
    line = w == 4
    arrivals = r.got if r.got.shape[0] == n - 1 else r.far

    def put(src, dst, axis, peer):
        copy = wire.put(src, dst, axis, peer)
        open_sends.append(copy)
        return copy

    def rows_of(kind):
        return ((0, G), (0, G), (G, g.cut), (G + g.cut, g.rest - g.cut))[kind]

    def kept(kind):
        middle = (G + g.cut) // 2
        return (slice(0, G // (2 * w)), slice(0, G // 2), slice(G // 2, middle), slice(middle, g.half))[kind]

    def buffers(kind):
        if kind == OUT:
            return r.gout, r.sib_o, r.z_o, r.go, r.go_sib
        return r.gw, r.sib_w, r.z_w, r.gi, r.gi_sib

    def block_of(kind, at_shard, at_core):
        if kind == OUT:
            return aligned((2 * at_shard + at_core) * o_half, o_half), slice(0, D)
        first, size = rows_of(kind)
        return (
            aligned(first + at_core * (size // 2), size // 2),
            pl.ds(pl.multiple_of(at_shard * lanes_of, 128), lanes_of),
        )

    def ready(kind):
        for copy in record.pop(kind, ()):
            copy.wait_send()

    def to_sibling(layer, kind):
        grad, sib, _, _, _ = buffers(kind)
        if layer == 0:
            pl.semaphore_wait(r.free.at[kind], 1)
        if kind == OUT:
            pairs = [
                (grad.at[block_of(kind, q, sibling)], sib.at[aligned(q * o_half, o_half)])
                for q in range(w)
            ]
        else:
            first, size = rows_of(kind)
            rows_there = aligned(first + sibling * (size // 2), size // 2)
            pairs = [(grad.at[rows_there], sib.at[kept(kind)])]
        copies = [wire.put(source, target, SECTION, sibling) for source, target in pairs]
        record[kind] = list(copies)
        return copies

    def to_shards(layer, kind, copies):
        grad, sib, z, _, _ = buffers(kind)
        for copy in copies:
            copy.wait_recv()
        if kind == OUT:
            per = o_half // TILE

            def places(t):
                q = t // per
                return (2 * q + core) * o_half + (t - q * per) * TILE, t * TILE

            steps = w * per
        else:
            first, size = rows_of(kind)
            steps = size // 2 // TILE

            def places(t):
                return first + core * (size // 2) + t * TILE, kept(kind).start + t * TILE

        def add(t, carry):
            mine, theirs = (pl.ds(pl.multiple_of(at, TILE), TILE) for at in places(t))
            grad[mine, :] = (grad[mine, :].astype(F32) + sib[theirs, :].astype(F32)).astype(BF)
            return carry

        lax.fori_loop(0, steps, add, 0)
        if layer == 1:
            pl.semaphore_signal(
                r.free.at[kind], inc=1, device_id={SECTION: sibling}, device_id_type=MESH
            )
        at = [wire.reserve() for _ in range(w)]
        found = []
        for k in range(1, w):
            peer = lax.rem(shard + k, w)
            source = grad.at[block_of(kind, peer, core)]
            found.append(wire.make(source, z.at[layer, k - 1, kept(kind)], WT, peer, at[k], at[k]))
        if not line:
            for copy in found:
                copy.start()
            record[kind] += found
            return found, None
        buffer = (r.relay_o if kind == OUT else r.relay_w).at[layer, kept(kind)]
        up = wire.make(grad.at[block_of(kind, w - 1, core)], buffer, WT, 1, at[0], at[0])
        down = wire.make(grad.at[block_of(kind, 0, core)], buffer, WT, w - 2, at[0], at[0])
        inner = (shard == 1) | (shard == 2)
        first = [
            Maybe(shard == 0, up),
            Maybe(shard == w - 1, down),
            Maybe(inner, found[0]),
            Maybe(inner, found[2]),
        ]
        others = [
            Maybe(jnp.logical_not(inner), found[1]),
            Maybe(shard == 0, found[0]),
            Maybe(shard == w - 1, found[2]),
        ]
        record[kind] += [*first, *others, Maybe(inner, found[1])]
        for copy in first:
            copy.start()
        waiting.extend(others)
        arriving = wire.make(buffer, buffer, WT, lax.rem(shard + 1, w), at[0], at[0])
        return found, arriving

    def relay(layer, kind, moving):
        found, arriving = moving
        if not line:
            return
        grad, buffer = (r.gout, r.relay_o) if kind == OUT else (r.gw, r.relay_w)
        rows_here = kept(kind)

        @pl.when((shard == 1) | (shard == 2))
        def _():
            arriving.wait_recv()
            at_rows, at_lanes = block_of(kind, lax.rem(shard + 2, w), core)

            def add(at):
                mine = pl.ds(pl.multiple_of(at_rows.start + at.start, TILE), TILE)
                there = pl.ds(pl.multiple_of(rows_here.start + at.start, TILE), TILE)
                total = grad[mine, at_lanes].astype(F32) + buffer[layer, there, :].astype(F32)
                grad[mine, at_lanes] = total.astype(BF)

            rows_loop(rows_here.stop - rows_here.start, add)
            found[1].start()

    def to_plane(layer, kind, moving):
        grad, _, z, result, _ = buffers(kind)
        copies, _ = moving
        if line:
            pl.when(shard != 0)(copies[0].wait_recv)
            copies[1].wait_recv()
            pl.when(shard != w - 1)(copies[2].wait_recv)
        else:
            for copy in copies:
                copy.wait_recv()
        at_rows, at_lanes = block_of(kind, shard, core)
        here_rows = kept(kind)

        def add(at):
            mine = pl.ds(pl.multiple_of(at_rows.start + at.start, TILE), TILE)
            there = pl.ds(pl.multiple_of(here_rows.start + at.start, TILE), TILE)
            total = grad[mine, at_lanes].astype(F32)
            for k in range(w - 1):
                total = total + z[layer, k, there, :].astype(F32)
            z[layer, 1, there, :] = total.astype(BF)

        def add_end(at, near):
            mine = pl.ds(pl.multiple_of(at_rows.start + at.start, TILE), TILE)
            there = pl.ds(pl.multiple_of(here_rows.start + at.start, TILE), TILE)
            total = grad[mine, at_lanes].astype(F32)
            total = total + z[layer, 1, there, :].astype(F32) + z[layer, near, there, :].astype(F32)
            z[layer, 1, there, :] = total.astype(BF)

        count = here_rows.stop - here_rows.start
        if line:

            @pl.when(shard == 0)
            def _():
                rows_loop(count, lambda at: add_end(at, 2))

            @pl.when(shard == w - 1)
            def _():
                rows_loop(count, lambda at: add_end(at, 0))

            @pl.when((shard == 1) | (shard == 2))
            def _():
                rows_loop(count, add)
        else:
            rows_loop(count, add)
        def target(group, half):
            size = here_rows.stop - here_rows.start
            if half is None:
                return result.at[layer, group, here_rows]
            first = here_rows.start + half * (size // 2)
            return result.at[layer, group, first : first + size // 2]

        block = z.at[layer, 1, here_rows]
        return PlaneGather(put, n, here, block, target), mover.put(block, target(here, None))

    def landed(kind, *arrivals):
        _, _, _, result, target = buffers(kind)
        for found, own in arrivals:
            found.wait_recv()
            own.wait()
        return put(result.at[sibling, :, kept(kind)], target.at[:, kept(kind)], SECTION, sibling)

    def done(copies):
        for copy in copies:
            copy.wait()

    arrived, waiting = {}, []
    for layer in (1, 0):
        conv = r.packs.at[layer, :, 0:CX]
        head = r.packs.at[layer, :, CX : CX + 128]
        wide = r.packs.at[layer, :, CX + 128 : gain_at]
        g_conv = r.sm.at[layer, 0:5, :]
        g_head = r.sm.at[layer, 7:8, 0:256]
        g_wide = r.sm.at[layer, 5:7, 0:G]
        done(first)

        def d_normed(lanes):
            r.xc[:, lanes] = dot(r.gb[...], r.of[lanes, :], 1, 1)

        column_tiles(0, G, d_normed)
        gate_backward(
            G, r.proj, r.mixed, r.xc, r.stats, wide, r.dy, g_wide
        )

        def out_rows(at):
            r.gout[at, :] = dot(r.mixed[:, at], r.gb[...], 0, 0).astype(BF)

        def in_rows(at):
            r.gw[at, :] = dot(r.proj[:, at], r.n[...], 0, 0).astype(BF)

        ready(OUT)
        column_tiles(0, G, out_rows)
        out_sib = to_sibling(layer, OUT)
        done(later)
        ready(GATE)
        column_tiles(0, G, in_rows)
        gate_sib = to_sibling(layer, GATE)
        out_z = to_shards(layer, OUT, out_sib)
        gate_z = to_shards(layer, GATE, gate_sib)
        if layer == 0:
            arrived[1, OUT][0].forward()
            arrived[1, GATE][0].forward()
            arrived[1, REST] = to_plane(1, REST, rest_z[0])
            arrived[1, LAST] = to_plane(1, LAST, rest_z[1])

        def serve():
            for copy in waiting:
                copy.start()

        scan_backward(
            G, r.proj, r.dy, r.yp, r.st, conv, head, wide, r.sel, g_wide, g_conv, g_head,
            r.pad, r.xc, r.dts, r.dstate, serve,
        )
        waiting.clear()
        relay(layer, OUT, out_z)
        relay(layer, GATE, gate_z)
        if layer == 0:
            small_sib = put(r.sm.at[sibling], r.sm_sib, SECTION, sibling)
        if layer == 0:
            arrived[1, REST][0].forward()
            arrived[1, LAST][0].forward()
            small_sib.wait_recv()
            r.sm_own[...] = r.sm[core] + r.sm_sib[...]
            small_z = [
                put(r.sm_own, r.sm_z.at[k - 1], WT, lax.rem(shard + k, w)) for k in range(1, w)
            ]
        if layer == 1:
            first = load(0, (r.of_i, r.of), (r.mixed_i, r.mixed))
            later = load(0, (r.yp_i, r.yp), (r.st_i, r.st))

        def in_product():
            four_blocks(r.part, lambda at, lanes: dot(r.proj[at, :], r.wf[:, lanes], 1, 0))

        summing = PlaneSum(wire.put, n, here, r.part, arrivals, r.mid)

        def rest_gradient():
            ready(REST)
            ready(LAST)
            column_tiles(G, NC, in_rows)
            return to_sibling(layer, REST), to_sibling(layer, LAST)

        def rest_to_shards(copies):
            return to_shards(layer, REST, copies[0]), to_shards(layer, LAST, copies[1])

        if layer == 0:
            rest_sib = rest_gradient()
            summing.start(in_product)
            rest_z = rest_to_shards(rest_sib)
            summing.middle()
        else:
            summing.start(in_product)
            later += load(0, (r.wf_i, r.wf))
            rest_sib = rest_gradient()
            first += load(0, (r.proj_i, r.proj))
            later += load(0, (r.n_i, r.n))
            summing.middle()
            rest_z = rest_to_shards(rest_sib)
        summing.end()
        while waiting:
            waiting.pop(0).start()
        if arrivals is not r.got:
            done(
                [
                    mover.put(arrivals.at[k - 1], r.part.at[lax.rem(here + k, n)])
                    for k in range(1, n)
                ]
            )

        def finish(at):
            if arrivals is r.got:
                d_in = summing.total(at)
            else:
                d_in = r.part[0, at, :].astype(F32)
                for k in range(1, n):
                    d_in = d_in + r.part[k, at, :].astype(F32)
            h = r.h1[at, :] if layer == 1 else r.h0[at, :]
            above = r.cot[at, :] if layer == 1 else r.grads[1, at, :]
            inv = lax.rsqrt(jnp.mean(h * h, axis=1, keepdims=True) + EPSILON)
            normed = h * inv
            gains_here = jnp.sum(d_in * normed, axis=0, keepdims=True)
            for q in range(4):
                row = slice(4 * layer + q, 4 * layer + q + 1)
                r.gain[here, row, :] += gains_here[:, q * (D // 4) : (q + 1) * (D // 4)]
            d_s = d_in * r.packs[layer, 0:1, gain_at:]
            d_h = above + inv * (d_s - normed * jnp.mean(d_s * normed, axis=1, keepdims=True))
            r.grads[layer, at, :] = d_h
            if layer == 1:
                out = d_h.astype(BF)
                whole = pl.ds(pl.multiple_of(here * rows + at.start, TILE), TILE)
                r.gb[whole, :] = out
                dots = jnp.sum(out.astype(F32) * r.pout[at, :], axis=1, keepdims=True)
                r.mdots[at, :] = jnp.broadcast_to(dots * (1.0 / INNER), (TILE, 128))

        rows_loop(rows, finish)
        if layer == 1:
            r.stats[here] = r.own_stat[...]
            r.stats[here, 1:2, :] = r.mdots[...].T[0:1, :]
            own = aligned(here * rows, rows)
            gathering = []

            def rows_of_group(group, half):
                size = rows if half is None else rows // 2
                return r.gb.at[aligned(group * rows + (half or 0) * size, size)]

            grad_rows = PlaneGather(put, n, here, r.gb.at[own], rows_of_group)
            for k in range(1, n):
                peer = lax.rem(here + k, n)
                gathering.append(put(r.stats.at[here], r.stats.at[here], SEQ, peer))
            grad_rows.forward()
            relay(1, REST, rest_z[0])
            relay(1, LAST, rest_z[1])
            arrived[1, OUT] = to_plane(1, OUT, out_z)
            arrived[1, GATE] = to_plane(1, GATE, gate_z)
            grad_rows.wait_recv()
            for copy in gathering:
                copy.wait_recv()
    gains = []
    ends = [put(r.grads.at[sibling], r.ig.at[core], SECTION, sibling)]
    for k in range(1, n):
        gains.append(put(r.gain.at[here], r.gain.at[here], SEQ, lax.rem(here + k, n)))
    local_grad = mover.put(r.grads.at[core], r.ig.at[core])
    relay(0, REST, rest_z[0])
    arrived[0, OUT] = to_plane(0, OUT, out_z)
    arrived[0, GATE] = to_plane(0, GATE, gate_z)
    relay(0, LAST, rest_z[1])
    arrived[0, OUT][0].forward()
    arrived[0, GATE][0].forward()
    for copy in small_z:
        copy.wait_recv()
    total = r.sm_own[...]
    for k in range(w - 1):
        total = total + r.sm_z[k]
    r.small[here] = total
    sums = [
        put(r.small.at[here], r.small.at[here], SEQ, lax.rem(here + k, n)) for k in range(1, n)
    ]
    for copy in gains:
        copy.wait_recv()
    total = r.gain[0]
    for k in range(1, n):
        total = total + r.gain[k]
    r.gain_z[shard] = total
    gains = [
        put(r.gain_z.at[shard], r.gain_z.at[shard], WT, lax.rem(shard + k, w)) for k in range(1, w)
    ]
    arrived[0, REST] = to_plane(0, REST, rest_z[0])
    ends.append(landed(OUT, arrived[1, OUT], arrived[0, OUT]))
    ends.append(landed(GATE, arrived[1, GATE], arrived[0, GATE]))
    arrived[0, LAST] = to_plane(0, LAST, rest_z[1])
    arrived[0, REST][0].forward()
    ends.append(landed(REST, arrived[1, REST], arrived[0, REST]))
    arrived[1, LAST][0].wait_recv()
    arrived[1, LAST][1].wait()
    last, last_own = arrived[0, LAST]

    def hand_over(group):
        source, target = r.gi.at[sibling, group, kept(LAST)], r.gi_sib.at[group, kept(LAST)]
        ends.append(put(source, target, SECTION, sibling))

    last_own.wait()
    hand_over(here)
    if last.plane:
        last.forward(hand_over)
        last.wait_recv()
        hand_over(lax.rem(last.x + 2, 4))
    else:
        last.wait_recv()
        for k in range(1, n):
            hand_over(lax.rem(here + k, n))
    for copy in gains:
        copy.wait_recv()
    total = r.gain_z[0]
    for k in range(1, w):
        total = total + r.gain_z[k]
    r.gain_sum[core] = total
    ends.append(put(r.gain_sum.at[core], r.gain_sum.at[core], SECTION, sibling))
    for copy in ends + sums:
        copy.wait_recv()
    r.late[...] = r.gain_sum[0] + r.gain_sum[1]
    local_grad.wait()
    assert wire.used <= r.ss.shape[0] and mover.used <= r.ls.shape[0]
    for kind in KINDS:
        ready(kind)
    for copy in open_sends:
        copy.wait_send()


def backward_call(g, n, w, fwd, tokens, cotangent):
    rows = tokens.shape[2]
    L, G, NC, CX = rows * n, g.G, g.NC, g.CX
    PK = CX + 128 + G + D
    S = jax.ShapeDtypeStruct
    o_half, lanes_of = G // (2 * w), D // w
    spill = n > 8
    outs = BackwardOuts(
        ig=S((2, rows, D), F32),
        gi=S((2, n, g.half, lanes_of), BF),
        go=S((2, n, o_half, D), BF),
        gi_sib=S((n, g.half, lanes_of), BF),
        go_sib=S((n, o_half, D), BF),
        small=S((n, 8, CX), F32),
        far=S((n - 1, rows, D) if spill else (8, 128), BF),
        late=S((8, D // 4), F32),
    )
    scratch = [
        S((2, 8, PK), F32), S((NC, D), BF), S((G, D), BF), S((L, D), BF), S((L, NC), BF), S((L, G), BF),
        S((L, G), F32), S((L // Q, STATE, G), F32), S((L, D), BF), S((n, 8, 128), F32), S((rows, D), F32),
        S((rows, D), F32), S((rows, D), F32), S((rows, D), F32),
        S((L, G), BF), S((8 + L, 128), F32), S((L, CX), F32), S((L, 128), F32), S((STATE, G), F32),
        S((n, rows, D), BF), S((1 if spill else n - 1, rows, D), BF), S((8, 128), F32), S((rows, 128), F32), S((2, rows, D), F32),
        S((NC, D), BF), S((G, D), BF), S((g.half, D), BF), S((G // 2, D), BF),
        S((2, w - 1, g.half, lanes_of), BF),
        S((2, w - 1, o_half, D), BF), S((2, g.half, lanes_of), BF), S((2, o_half, D), BF), S((2, 8, CX), F32), S((8, CX), F32), S((w - 1, 8, CX), F32), S((8, CX), F32),
        S((128, 128), BF), S((n, 8, D // 4), F32), S((w, 8, D // 4), F32), S((2, 8, D // 4), F32),
        S((2, rows // 2, D), BF),
    ]
    remote = 2 * (4 * (w + w + n) + n - 1) + 2 * (n - 1) + 40 + 2 * (w - 1) + 2 * (n - 1) + n
    args = [
        fwd.packs_o, fwd.wf_o, fwd.of_o, fwd.n_o, fwd.proj_o, fwd.mixed_o, fwd.yp_o, fwd.st_o,
        fwd.gb_o, fwd.stats, fwd.stat0, fwd.pout, fwd.h1, tokens, cotangent,
    ]
    results = pl.pallas_call(
        functools.partial(backward_kernel, g, n, w, rows),
        out_shape=list(outs),
        in_specs=[ANY] * len(args),
        out_specs=[VM, ANY, ANY, ANY, ANY, VM, ANY, VM],
        scratch_shapes=[pltpu.VMEM(s.shape, s.dtype) for s in scratch]
        + [
            pltpu.SemaphoreType.DMA((remote,)),
            pltpu.SemaphoreType.DMA((remote,)),
            pltpu.SemaphoreType.DMA((40 + 2 * n,)),
            pltpu.SemaphoreType.REGULAR((4,)),
        ],
        compiler_params=pltpu.CompilerParams(
            collective_id=1, has_side_effects=True, vmem_limit_bytes=BACKWARD_VMEM
        ),
        name="backward",
    )(*args)
    return BackwardOuts(*results)


def pack_small(g, here, conv_ref, bias_ref, dtb_ref, a_ref, skip_ref, gate_ref, norm_ref, pack_ref):
    G, width = g.G, g.run_heads * HEAD_DIM
    win = -(-(width + 64) // 128) * 128
    start = here * width
    base = pl.multiple_of(start // 128 * 128, 128)
    from_ids = lax.broadcasted_iota(jnp.int32, (win, G), 0)
    to_ids = lax.broadcasted_iota(jnp.int32, (win, G), 1)
    exact = lax.Precision.HIGHEST

    def take(ref, rows):
        total = jnp.zeros((rows, G), F32)
        for run in range(g.runs):
            window = ref[0:rows, pl.ds(pl.multiple_of(base + run * (INNER // g.runs), 128), win)]
            inside = (to_ids >= run * width) & (to_ids < (run + 1) * width)
            pick = one_hot(inside & (from_ids == to_ids - run * width + (start - base)))
            total = total + dot(window, pick, 1, 0, exact)
        return total

    head_from = lax.broadcasted_iota(jnp.int32, (HEADS, 128), 0)
    head_to = lax.broadcasted_iota(jnp.int32, (HEADS, 128), 1)
    head_pick = one_hot((head_from == head_of(g, here, head_to)) & (head_to < g.heads))
    wide_from = lax.broadcasted_iota(jnp.int32, (HEADS, G), 0)
    wide_to = lax.broadcasted_iota(jnp.int32, (HEADS, G), 1)
    wide_pick = (wide_from == head_of(g, here, wide_to // HEAD_DIM)) & (wide_to < g.chans)
    head_at, wide_at, gain_at = g.CX, g.CX + 128, g.CX + 128 + G
    pack_ref[...] = jnp.zeros_like(pack_ref)
    pack_ref[0:KERNEL, 0:G] = take(conv_ref, KERNEL)
    pack_ref[4:5, 0:G] = take(bias_ref, 1)
    pack_ref[0:KERNEL, G:head_at] = conv_ref[:, INNER:]
    pack_ref[4:5, G:head_at] = bias_ref[:, INNER:]
    pack_ref[0:1, head_at:wide_at] = dot(dtb_ref[...], head_pick, 1, 0, exact)
    pack_ref[1:2, head_at:wide_at] = dot(-jnp.exp(a_ref[...]), head_pick, 1, 0, exact)
    pack_ref[0:1, wide_at:gain_at] = take(gate_ref, 1)
    pack_ref[1:2, wide_at:gain_at] = dot(skip_ref[...], one_hot(wide_pick), 1, 0, exact)
    pack_ref[0:1, gain_at:] = norm_ref[...]


def halves_of_heads(g, ref_of, column_at, head):
    parts = []
    for h in (head, head + 1):
        stride = HEADS // g.runs
        group = h % stride // g.run_heads
        local_head = h // stride * g.run_heads + h % g.run_heads
        value = ref_of(group, slice(column_at + local_head // 2 * 128, column_at + local_head // 2 * 128 + 128))
        parts.append(value if local_head % 2 == h % 2 else pltpu.roll(value, HEAD_DIM, 1))
    lanes = lax.broadcasted_iota(jnp.int32, parts[0].shape, 1)
    return jnp.where(lanes < HEAD_DIM, parts[0], parts[1])


def layout_kernel(g, own_ref, sib_ref, own_out_ref, sib_out_ref, small_ref, late_ref, sec_ref, ig_ref, g_in_ref, g_out_ref, sec_out, ig_out, norm_ref, conv_ref, bias_ref, dtb_ref, a_ref, skip_ref, gate_ref):
    n, G = g.n_seq, g.G
    first_core = lax.axis_index(SECTION) == 0

    def all_rows(halves, outs):
        def copy(groups, parts, source, target, size):
            done = 0
            while done < size:
                row = source + done
                first, part_rows, half_at = next(x for x in parts if x[0] <= row < x[0] + x[1])
                half, offset = divmod(row - first, part_rows // 2)
                count = min(size - done, part_rows // 2 - offset)
                at = slice(half_at + offset, half_at + offset + count)
                total = None
                for group in groups:
                    value = halves[half][group, at, :].astype(F32)
                    total = value if total is None else total + value
                g_in_ref[target + done : target + done + count, :] = total
                done += count

        for half in range(2):
            g_out_ref[:, half] = outs[half][...].astype(F32)
        width = g.run_heads * HEAD_DIM
        gate = ((0, G, 0),)
        rest = ((0, g.cut, G // 2), (g.cut, g.rest - g.cut, (G + g.cut) // 2))
        everyone = range(n)
        for run in range(g.runs):
            for group in range(n):
                target = run * (INNER // g.runs) + group * width
                copy([group], gate, run * width, target, width)
                copy([group], rest, run * width, INNER + target, width)
        copy(everyone, rest, G, 2 * INNER, 2 * STATE)
        copy(everyone, rest, G + 2 * STATE, 2 * INNER + 2 * STATE, HEADS)

    sec_out[...] = sec_ref[...]
    ig_out[...] = ig_ref[...]
    own, own_out = own_ref.at[0], own_out_ref.at[0]

    @pl.when(first_core)
    def _():
        all_rows((own, sib_ref), (own_out, sib_out_ref))

    @pl.when(jnp.logical_not(first_core))
    def _():
        all_rows((sib_ref, own), (sib_out_ref, own_out))

    @pl.when(pl.program_id(0) == 0)
    def _():
        from_ids = lax.broadcasted_iota(jnp.int32, (128, HEADS), 0)
        to_ids = lax.broadcasted_iota(jnp.int32, (128, HEADS), 1)
        picks = [one_hot((to_ids == head_of(g, group, from_ids)) & (from_ids < g.heads)) for group in range(n)]
        exact = lax.Precision.HIGHEST
        head_at = g.CX

        def small(group, columns):
            return small_ref[group, :, columns]

        for head in range(0, HEADS, 2):
            at = slice(head * HEAD_DIM, head * HEAD_DIM + 128)
            conv = halves_of_heads(g, small, 0, head)
            conv_ref[:, at] = conv[0:KERNEL]
            bias_ref[:, at] = conv[KERNEL : KERNEL + 1]
            gate_ref[:, at] = conv[5:6]
        conv = small(0, slice(G, head_at))
        for group in range(1, n):
            conv = conv + small(group, slice(G, head_at))
        conv_ref[:, INNER:] = conv[0:KERNEL]
        bias_ref[:, INNER:] = conv[KERNEL : KERNEL + 1]
        for q in range(4):
            late = jnp.where(first_core, late_ref[q : q + 1, :], late_ref[4 + q : 5 + q, :])
            norm_ref[:, q * (D // 4) : (q + 1) * (D // 4)] = late
        biases = jnp.zeros((8, HEADS), F32)
        rates = jnp.zeros((8, HEADS), F32)
        skips = jnp.zeros((8, HEADS), F32)
        wide_from = lax.broadcasted_iota(jnp.int32, (G, HEADS), 0)
        wide_to = lax.broadcasted_iota(jnp.int32, (G, HEADS), 1)
        for group in range(n):
            biases = biases + dot(small(group, slice(0, 128)), picks[group], 1, 0, exact)
            rates = rates + dot(small(group, slice(128, 256)), picks[group], 1, 0, exact)
            pick = (wide_to == head_of(g, group, wide_from // HEAD_DIM)) & (wide_from < g.chans)
            skips = skips + dot(small(group, slice(0, G)), one_hot(pick), 1, 0, exact)
        dtb_ref[...] = biases[7:8]
        a_ref[...] = rates[7:8]
        skip_ref[...] = skips[6:7]


def layout_call(g, core, gi, gi_sib, go, go_sib, small, late, sec, ig):
    _, n, half, lanes = gi.shape
    out_half = go.shape[2]
    steps = lanes // 128
    out_lanes = D // steps
    rows_spec = pl.BlockSpec(sec.shape[:2] + (out_lanes,), lambda t, c: (0, 0, t))
    PK = small.shape[2]
    columns = 2 * INNER + 2 * STATE + HEADS
    S = jax.ShapeDtypeStruct
    shapes = (
        S((columns, lanes), F32), S((n, 2, out_half, D), F32), S(sec.shape, F32), S(ig.shape, F32), S((1, D), F32), S((KERNEL, CONV), F32),
        S((1, CONV), F32), S((1, HEADS), F32), S((1, HEADS), F32), S((1, HEADS), F32), S((1, INNER), F32),
    )
    return pl.pallas_call(
        lambda core_ref, *refs: layout_kernel(g, *refs),
        grid_spec=pltpu.PrefetchScalarGridSpec(
            num_scalar_prefetch=1,
            grid=(steps,),
            in_specs=[
                pl.BlockSpec((1, n, half, 128), lambda t, c: (c[0], 0, 0, t)),
                pl.BlockSpec((n, half, 128), lambda t, c: (0, 0, t)),
                pl.BlockSpec((1, n, out_half, out_lanes), lambda t, c: (c[0], 0, 0, t)),
                pl.BlockSpec((n, out_half, out_lanes), lambda t, c: (0, 0, t)),
                pl.BlockSpec((n, 8, PK), lambda t, c: (0, 0, 0)),
                pl.BlockSpec((8, D // 4), lambda t, c: (0, 0)),
                rows_spec,
                rows_spec,
            ],
            out_specs=[
                pl.BlockSpec((columns, 128), lambda t, c: (0, t)),
                pl.BlockSpec((n, 2, out_half, out_lanes), lambda t, c: (0, 0, 0, t)),
                rows_spec,
                rows_spec,
            ]
            + [pl.BlockSpec(s.shape, lambda t, c: (0, 0)) for s in shapes[4:]],
        ),
        out_shape=shapes,
        compiler_params=pltpu.CompilerParams(vmem_limit_bytes=SMALL_VMEM),
        name="layout",
    )(core, gi, gi_sib, go, go_sib, small, late, sec, ig)


def local(
    tokens, cotangent, norm_gain, w_in, conv_w, conv_b, dt_bias, a_log, skip_d, gate_gain, w_out
):
    n_seq, n_wt = lax.axis_size(SEQ), lax.axis_size(WT)
    here = lax.axis_index(SEQ)
    group = Group(n_seq, n_wt)
    core = lax.axis_index(SECTION).reshape(1)
    G = group.G

    small = (conv_w[0], conv_b, dt_bias, a_log, skip_d, gate_gain, norm_gain)
    w_src = jnp.swapaxes(w_in[0], 0, 1)
    if group.runs == n_wt:
        o_src = w_out[0]
    else:
        o_src = lax.all_gather(w_out[0], WT, axis=0, tiled=True)
        o_src = lax.dynamic_slice_in_dim(o_src, here * group.chans, group.chans, 0)
        o_src = jnp.pad(o_src, ((0, G - group.chans), (0, 0)))
    fwd = forward_call(group, n_seq, n_wt, tokens, cotangent, small, w_src, o_src)
    bwd = backward_call(group, n_seq, n_wt, fwd, tokens, cotangent)
    g_in, g_out, section_out, input_grad, g_norm, g_conv, g_bias, g_dtb, g_a, g_skip, g_gate = layout_call(
        group, core, bwd.gi, bwd.gi_sib, bwd.go, bwd.go_sib, bwd.small, bwd.late, fwd.sec, bwd.ig
    )
    if group.runs == n_wt:
        g_out = g_out.reshape(INNER // n_wt, D)
    else:
        g_out = g_out.astype(BF).reshape(n_seq, G // n_wt, D)
        g_out = lax.all_gather(g_out, WT, axis=1, tiled=True)[:, : group.chans].reshape(INNER, D)
        mine = INNER // n_wt
        g_out = lax.dynamic_slice_in_dim(g_out, lax.axis_index(WT) * mine, mine, 0).astype(F32)
    return (
        section_out[None, :, None],
        input_grad[None, :, None],
        g_norm,
        jnp.swapaxes(g_in, 0, 1)[None],
        g_conv[None],
        g_bias,
        g_dtb,
        g_a,
        g_skip,
        g_gate,
        g_out[None],
    )


def solution(mesh):
    placed = (
        P(None, WT, SEQ, None),
        P(None, WT, SEQ, None),
        P(SECTION, None),
        P(SECTION, WT, None),
        P(SECTION, None, None),
        P(SECTION, None),
        P(SECTION, None),
        P(SECTION, None),
        P(SECTION, None),
        P(SECTION, None),
        P(SECTION, WT, None),
    )
    return jax.shard_map(
        local,
        mesh=mesh,
        in_specs=placed,
        out_specs=(
            P(SECTION, None, WT, SEQ, None),
            P(SECTION, None, WT, SEQ, None),
            P(SECTION, None),
            P(SECTION, WT, None),
            P(SECTION, None, None),
            P(SECTION, None),
            P(SECTION, None),
            P(SECTION, None),
            P(SECTION, None),
            P(SECTION, None),
            P(SECTION, WT, None),
        ),
        check_vma=False,
    )
```
